32 devices in a mesh: dp: 16 (over z, x, core), exp: 2 (over y).
Axes of the slice: x: 2, y: 2, z: 4, core: 2. Of those that a mesh axis runs over, the one named last changes fastest.
Arguments:
- tokens: bfloat16 [4096, 1024], P(('dp', 'exp')), may hold values from -6 to 6
- cotangent: bfloat16 [4096, 1024], P(('dp', 'exp')), may hold values from -6 to 6
- doc_lengths: int32 [64, 3], P(('dp', 'exp')), may hold values from 1 to 48, 64 in all within a row
- routes: int32 [4096, 8], P(('dp', 'exp')), may hold values from 0 to 15, all different within a row; in each aligned block of 64 rows (0 to 63, 64 to 127, ...) at most 40 rows name the same one
- qkv_weight: float32 [1024, 2048], P(('dp', 'exp')), may hold values from -0.25 to 0.25
- qkv_mean: float32 [1024, 2048], P(('dp', 'exp')), may hold values from -128 to 128
- qkv_square: float32 [1024, 2048], P(('dp', 'exp')), may hold values from 1843.2 to 7372.8
- out_weight: float32 [1024, 1024], P(('dp', 'exp')), may hold values from -0.5 to 0.5
- out_mean: float32 [1024, 1024], P(('dp', 'exp')), may hold values from -40 to 40
- out_square: float32 [1024, 1024], P(('dp', 'exp')), may hold values from 163.84 to 655.36
- router_weight: float32 [1024, 16], P(('dp', 'exp')), may hold values from -0.09375 to 0.09375
- router_mean: float32 [1024, 16], P(('dp', 'exp')), may hold values from -512 to 512
- router_square: float32 [1024, 16], P(('dp', 'exp')), may hold values from 34816 to 139264
- norm_gains: float32 [1024, 2], P(('dp', 'exp')), may hold values from 0.5 to 1.5
- gains_mean: float32 [1024, 2], P(('dp', 'exp')), may hold values from -160 to 160
- gains_square: float32 [1024, 2], P(('dp', 'exp')), may hold values from 3276.8 to 13107.2
- in_weight: float32 [16, 1024, 1024], P('exp', 'dp'), may hold values from -0.1875 to 0.1875
- in_mean: float32 [16, 1024, 1024], P('exp', 'dp'), may hold values from -20 to 20
- in_square: float32 [16, 1024, 1024], P('exp', 'dp'), may hold values from 51.2 to 204.8
- down_weight: float32 [16, 1024, 512], P('exp', 'dp'), may hold values from -2 to 2
- down_mean: float32 [16, 1024, 512], P('exp', 'dp'), may hold values from -5 to 5
- down_square: float32 [16, 1024, 512], P('exp', 'dp'), may hold values from 0.57344 to 2.2528
Outputs:
- block_out: bfloat16 [4096, 1024], P(('dp', 'exp'))
- input_grad: bfloat16 [4096, 1024], P(('dp', 'exp'))
- new_qkv: float32 [1024, 2048], P(('dp', 'exp'))
- new_qkv_mean: float32 [1024, 2048], P(('dp', 'exp'))
- new_qkv_square: float32 [1024, 2048], P(('dp', 'exp'))
- new_out: float32 [1024, 1024], P(('dp', 'exp'))
- new_out_mean: float32 [1024, 1024], P(('dp', 'exp'))
- new_out_square: float32 [1024, 1024], P(('dp', 'exp'))
- new_router: float32 [1024, 16], P(('dp', 'exp'))
- new_router_mean: float32 [1024, 16], P(('dp', 'exp'))
- new_router_square: float32 [1024, 16], P(('dp', 'exp'))
- new_gains: float32 [1024, 2], P(('dp', 'exp'))
- new_gains_mean: float32 [1024, 2], P(('dp', 'exp'))
- new_gains_square: float32 [1024, 2], P(('dp', 'exp'))
- new_in: float32 [16, 1024, 1024], P('exp', 'dp')
- new_in_mean: float32 [16, 1024, 1024], P('exp', 'dp')
- new_in_square: float32 [16, 1024, 1024], P('exp', 'dp')
- new_down: float32 [16, 1024, 512], P('exp', 'dp')
- new_down_mean: float32 [16, 1024, 512], P('exp', 'dp')
- new_down_square: float32 [16, 1024, 512], P('exp', 'dp')
The draws below stay inside these ranges and needn't reach their ends.
Inputs may be any that keep to these rules, and one draw needn't show every extreme that they name: `doc_lengths`: row b lists the lengths of the 3 documents of block b in order; they sum to 64, and the longest is exactly 48. `routes`: each row names 8 different experts. In each aligned block of 64 rows (one micro-batch of one device) no expert is named by more than 40 rows, a bound that some block reaches.
All inputs are finite; a program needn't handle non-finite values.
Results may differ from the reference program's by a relative error of at most 0.02.
Values may be sent and summed in bfloat16 or wider, within the bound.
No kernel may reach another device: no remote copies, remote signals or barrier semaphores. Data moves between devices by JAX's collectives and lax.ppermute only.
A program may use at most 192 MiB of HBM per device.

```python
import math
import jax
import jax.numpy as jnp
import numpy as np
from jax import lax

D = 1024
QUERY_HEADS = 16
KEY_VALUE_HEADS = 8
HEAD_DIMENSION = 64
FF = 512
TOP = 8
EXPERTS = 16
TOK_MB = 64
MICRO = 2
DOCS = 3
STEP = 10
QKV = 2048
CAP = 40
DOC_MOST = 48
BLOCKS = 64
TOKENS = 4096
ROUTED = 2048
N_DP = 16
N_EXP = 2


def block_scale(rng, dims, cuts, smallest, high):
    loudness, own = 1.0, jax.random.fold_in(rng, 6)
    for dim, parts in cuts:
        heights = jnp.exp(jax.random.uniform(jax.random.fold_in(own, dim), (parts,), jnp.float32, smallest / len(cuts), high / len(cuts)))
        loudness = loudness * jnp.repeat(heights, dims[dim] // parts).reshape([-1 if axis == dim else 1 for axis in range(len(dims))])
    return loudness


def split_up(amount, total, limit, lean):
    portions = [(1 << 20) // math.isqrt(rank ** lean) + 1 for rank in range(2, amount + 1)]
    rest, counts = total - limit - (amount - 1), [1] * (amount - 1)
    while rest > 0:
        candidates = [i for i in range(amount - 1) if counts[i] < limit]
        mass, budget = sum([portions[i] for i in candidates]), rest
        for i in candidates:
            extra = min(limit - counts[i], max(1, budget * portions[i] // mass), rest)
            counts[i] = counts[i] + extra
            rest = rest - extra
    return np.array([limit] + counts)


def uneven(rng, number_of, total, most, slope):
    if number_of == 2:
        one = jax.random.randint(rng, (), max(1, total - most), min(most, total - 1) + 1)
        return jnp.stack([one, total - one])
    sizes = jnp.asarray(split_up(number_of, total, most, slope), jnp.int32)
    pairs = (number_of - 1) // 2
    giver, taker = sizes[1:1 + 2 * pairs:2], sizes[2:2 + 2 * pairs:2]
    slack = jnp.minimum(giver - 1, most - taker)
    shifted = jax.random.randint(jax.random.fold_in(rng, 1), (pairs,), 0, 1 << 20) % (slack + 1)
    sizes = sizes.at[1:1 + 2 * pairs:2].set(giver - shifted).at[2:2 + 2 * pairs:2].set(taker + shifted)
    return sizes[jax.random.permutation(jax.random.fold_in(rng, 2), number_of)]


def deal_out(key, own, number, rows, count, top, bound, slope):
    sequence = jax.random.permutation(key, count)
    crowded, common = load_shares(count, rows * top, bound, slope, True), load_shares(count, rows * top, bound, slope, False)
    places = jnp.arange(count)

    def named(sizes, turn):
        used = int((sizes > 0).sum())
        fixed = max(1, used // 4)
        moved = fixed + (places - fixed + turn * (used - fixed)) % max(1, count - fixed)
        return jnp.zeros((count,), jnp.int32).at[sequence[jnp.where(places < fixed, places, moved)]].set(jnp.asarray(sizes, jnp.int32))

    sizes = jnp.where(number % 4 == 0, named(crowded, number // 4), named(common, number - number // 4 - 1))
    mixed = jax.random.permutation(jax.random.fold_in(own, 3), count)
    giver, receiver = mixed[0:count // 2 * 2:2], mixed[1:count // 2 * 2:2]
    room = jnp.minimum(sizes[giver] - 1, bound - sizes[receiver]) // 2
    room = jnp.where((giver == sequence[0]) | (receiver == sequence[0]) | (sizes[receiver] == 0), 0, jnp.maximum(room, 0))
    moved = jax.random.randint(jax.random.fold_in(own, 4), (count // 2,), 0, 1 << 20) % (room + 1)
    sizes = sizes.at[giver].add(-moved).at[receiver].add(moved)
    labels = jnp.searchsorted(jnp.cumsum(sizes), jnp.arange(rows * top), side="right").astype(jnp.int32)
    grid = labels.reshape(top, rows).T
    grid = grid[jax.random.permutation(jax.random.fold_in(own, 1), rows)]
    turn = jax.random.randint(jax.random.fold_in(own, 2), (rows, 1), 0, top)
    return jnp.take_along_axis(grid, (jnp.arange(top)[None, :] + turn) % top, axis=1)


def load_shares(count, total, limit, lean, full):
    portions = [(1 << 20) // math.isqrt(grade ** lean) + 1 for grade in range(1, count + 1)]
    largest = limit if full else min(limit, max(-(-total // count), total * portions[0] // sum(portions)))
    least = 1 if total - largest >= count - 1 else 0
    counts, surplus = [largest] + [least] * (count - 1), total - largest - least * (count - 1)
    while surplus > 0:
        candidates = [i for i in range(1, count) if counts[i] < largest] or [i for i in range(1, count) if counts[i] < limit]
        pool, left = sum([portions[i] for i in candidates]), surplus
        for i in candidates:
            extra = min(limit - counts[i], max(1, left * portions[i] // pool), surplus)
            counts[i] = counts[i] + extra
            surplus = surplus - extra
    return np.array(counts)


def normal_values(own_key, extent, width, most, split=(), kind=jnp.bfloat16):
    array = jax.random.normal(own_key, extent, jnp.float32) * width
    if len(split) > 0:
        array = block_scale(own_key, extent, split, -0.22, 0.18) * array
    return jnp.clip(array, min=-most, max=most).astype(kind)


def setup_inputs(seed: int = 0) -> dict:
    splits = jax.random.split(jax.random.key(seed), 23)
    tokens = normal_values(splits[0], (TOKENS, D), 1.0, 6.0, ((0, 32),))
    cotangent = normal_values(splits[1], (TOKENS, D), 1.0, 6.0, ((0, 32),))
    doc_lengths = jax.vmap(lambda own: uneven(own, DOCS, TOK_MB, DOC_MOST, 2))(jax.random.split(splits[2], BLOCKS)).reshape((BLOCKS, DOCS)).astype(jnp.int32)
    routes_keys = jax.random.split(jax.random.fold_in(splits[3], 1), TOKENS // TOK_MB)
    routes_turns = jax.random.permutation(jax.random.fold_in(splits[3], 3), TOKENS // TOK_MB)
    routes = jax.vmap(lambda own, number: deal_out(jax.random.fold_in(splits[3], 2), own, number, TOK_MB, EXPERTS, TOP, CAP, 2))(routes_keys, routes_turns).reshape((TOKENS, TOP))
    qkv_weight = normal_values(splits[4], (D, QKV), (D // 2) ** -0.5, 0.25, ((0, 32),), jnp.float32)
    qkv_mean = normal_values(splits[5], (D, QKV), (0.33 * TOKENS ** 0.5), 128.0, ((0, 32),), jnp.float32)
    qkv_square = jnp.clip(jnp.exp(math.log(7372.8) - 1.3862944 * jax.random.uniform(splits[6], (D, QKV), jnp.float32) ** block_scale(splits[6], (D, QKV), ((0, 32),), -0.2, 0.2)), 1843.2, 7372.8)
    out_weight = normal_values(splits[7], (D, QUERY_HEADS * HEAD_DIMENSION), (QUERY_HEADS * HEAD_DIMENSION // 8) ** -0.5, 0.5, ((0, 32),), jnp.float32)
    out_mean = normal_values(splits[8], (D, QUERY_HEADS * HEAD_DIMENSION), (0.1 * TOKENS ** 0.5), 40.0, ((0, 32),), jnp.float32)
    out_square = jnp.clip(jnp.exp(math.log(655.36) - 1.3862944 * jax.random.uniform(splits[9], (D, QUERY_HEADS * HEAD_DIMENSION), jnp.float32) ** block_scale(splits[9], (D, QUERY_HEADS * HEAD_DIMENSION), ((0, 32),), -0.2, 0.2)), 163.84, 655.36)
    router_weight = normal_values(splits[10], (D, EXPERTS), (4 * D) ** -0.5, 0.09375, ((0, 32),), jnp.float32)
    router_mean = normal_values(splits[11], (D, EXPERTS), (1.4 * TOKENS ** 0.5), 512.0, ((0, 32),), jnp.float32)
    router_square = jnp.clip(jnp.exp(math.log(139264.0) - 1.3862944 * jax.random.uniform(splits[12], (D, EXPERTS), jnp.float32) ** block_scale(splits[12], (D, EXPERTS), ((0, 32),), -0.2, 0.2)), 34816.0, 139264.0)
    norm_gains = jnp.clip(1.0 + 0.1 * jax.random.normal(splits[13], (D, 2), jnp.float32), 0.5, 1.5)
    gains_mean = normal_values(splits[14], (D, 2), (0.44 * TOKENS ** 0.5), 160.0, ((0, 32),), jnp.float32)
    gains_square = jnp.clip(jnp.exp(math.log(13107.2) - 1.3862944 * jax.random.uniform(splits[15], (D, 2), jnp.float32) ** block_scale(splits[15], (D, 2), ((0, 32),), -0.2, 0.2)), 3276.8, 13107.2)
    in_weight = normal_values(splits[16], (EXPERTS, D, 2 * FF), D ** -0.5, 0.1875, ((0, 2), (1, 16)), jnp.float32)
    in_mean = normal_values(splits[17], (EXPERTS, D, 2 * FF), (0.077 * ROUTED ** 0.5), 20.0, ((0, 2), (1, 16)), jnp.float32)
    in_square = jnp.clip(jnp.exp(math.log(204.8) - 1.3862944 * jax.random.uniform(splits[18], (EXPERTS, D, 2 * FF), jnp.float32) ** block_scale(splits[18], (EXPERTS, D, 2 * FF), ((0, 2), (1, 16)), -0.2, 0.2)), 51.2, 204.8)
    down_weight = normal_values(splits[19], (EXPERTS, D, FF), (max(FF // 64, 1)) ** -0.5, 2.0, ((0, 2), (1, 16)), jnp.float32)
    down_mean = normal_values(splits[20], (EXPERTS, D, FF), (0.008 * ROUTED ** 0.5), 5.0, ((0, 2), (1, 16)), jnp.float32)
    down_square = jnp.clip(jnp.exp(math.log(2.2528) - 1.3682758234896075 * jax.random.uniform(splits[21], (EXPERTS, D, FF), jnp.float32) ** block_scale(splits[21], (EXPERTS, D, FF), ((0, 2), (1, 16)), -0.2, 0.2)), 0.57344, 2.2528)
    return {"tokens": tokens, "cotangent": cotangent, "doc_lengths": doc_lengths, "routes": routes, "qkv_weight": qkv_weight, "qkv_mean": qkv_mean, "qkv_square": qkv_square, "out_weight": out_weight, "out_mean": out_mean, "out_square": out_square, "router_weight": router_weight, "router_mean": router_mean, "router_square": router_square, "norm_gains": norm_gains, "gains_mean": gains_mean, "gains_square": gains_square, "in_weight": in_weight, "in_mean": in_mean, "in_square": in_square, "down_weight": down_weight, "down_mean": down_mean, "down_square": down_square}


@jax.custom_vjp
def low(v):
    return lax.optimization_barrier(v.astype(jnp.bfloat16)).astype(jnp.float32)

@jax.custom_vjp
def low_back(v):
    return v

def low_keep(v):
    return (low(v), None)

def low_pass(kept, grad):
    return (grad,)

def back_keep(v):
    return (v, None)

def back_low(kept, grad):
    return (low(grad),)
low.defvjp(low_keep, low_pass)
low_back.defvjp(back_keep, back_low)
norm_eps = 1e-06
rope_base = 10000.0
mask_fill = -1e+30
beta_one = 0.9
beta_two = 0.95
adam_eps = 1e-08
decay_rate = 0.1
highest = lax.Precision.HIGHEST

def rms_scale(values):
    return lax.rsqrt(lax.optimization_barrier(jnp.mean(values * values, axis=-1, keepdims=True)) + norm_eps)

def doc_layout(doc_lens, sequence_length):
    row_index = jnp.arange(sequence_length, dtype=jnp.int32)
    doc_ends = jnp.cumsum(doc_lens, dtype=jnp.int32)
    passed = (row_index[:, None] >= doc_ends[None, :]).astype(jnp.int32)
    segment = lax.optimization_barrier(jnp.sum(passed, axis=1, dtype=jnp.int32))
    starts = lax.optimization_barrier(jnp.sum(passed * doc_lens[None, :], axis=1, dtype=jnp.int32))
    return ((row_index - starts).astype(jnp.float32), segment)

def rope_tables(positions, head_size):
    half_size = head_size // 2
    freq_index = jnp.arange(half_size, dtype=jnp.float32)
    inverse = jnp.exp(freq_index * (-2.0 * math.log(rope_base) / head_size))
    angles = positions[:, None] * inverse[None, :]
    return (jnp.cos(angles)[:, None, :], jnp.sin(angles)[:, None, :])

def rotary_apply(values, cosine_table, sine_table):
    half_size = values.shape[-1] // 2
    lower_half = values[..., :half_size]
    upper_half = values[..., half_size:]
    return jnp.concatenate([lower_half * cosine_table - upper_half * sine_table, upper_half * cosine_table + lower_half * sine_table], axis=-1)

@jax.checkpoint
def attend(query_rows, key_matrix_rows, value_matrix_rows, segment):
    sequence_length = query_rows.shape[0]
    grouped_heads = query_rows.reshape(sequence_length, KEY_VALUE_HEADS, QUERY_HEADS // KEY_VALUE_HEADS, HEAD_DIMENSION)
    scores = low_back(jnp.einsum('tkgd,skd->kgts', grouped_heads, key_matrix_rows, precision=highest) * HEAD_DIMENSION ** (-0.5))
    row_index = jnp.arange(sequence_length, dtype=jnp.int32)
    allowed = (segment[:, None] == segment[None, :]) & (row_index[None, :] <= row_index[:, None])
    scores = jnp.where(allowed, scores, mask_fill)
    attention_weights = jax.nn.softmax(scores, axis=-1)
    combined = jnp.einsum('kgts,skd->tkgd', low(attention_weights), value_matrix_rows, precision=highest)
    return combined.reshape(sequence_length, QUERY_HEADS * HEAD_DIMENSION)

def block_forward(params, tokens_block, doc_lens, token_routes):
    qkv_matrix, out_matrix, router_matrix, gain_pair, in_matrix, down_matrix = params
    sequence_length = tokens_block.shape[0]
    model_width = tokens_block.shape[1]
    positions, segment = doc_layout(doc_lens, sequence_length)
    cosine_table, sine_table = rope_tables(positions, HEAD_DIMENSION)
    query_total_width = QUERY_HEADS * HEAD_DIMENSION
    key_value_width = KEY_VALUE_HEADS * HEAD_DIMENSION
    normed = low(tokens_block * rms_scale(tokens_block) * gain_pair[:, 0])
    projected_output = low_back(jnp.dot(normed, qkv_matrix, precision=highest))
    query_rows = low(rotary_apply(projected_output[:, :query_total_width].reshape(sequence_length, QUERY_HEADS, HEAD_DIMENSION), cosine_table, sine_table))
    key_matrix_rows = low(rotary_apply(projected_output[:, query_total_width:query_total_width + key_value_width].reshape(sequence_length, KEY_VALUE_HEADS, HEAD_DIMENSION), cosine_table, sine_table))
    value_matrix_rows = low(projected_output[:, query_total_width + key_value_width:].reshape(sequence_length, KEY_VALUE_HEADS, HEAD_DIMENSION))
    attended = low_back(low(attend(query_rows, key_matrix_rows, value_matrix_rows, segment)))
    branch = low_back(jnp.dot(attended, out_matrix.T, precision=highest))
    hidden = tokens_block + branch
    normed_two = low(hidden * rms_scale(hidden) * gain_pair[:, 1])
    logits = low_back(jnp.dot(normed_two, router_matrix, precision=highest))
    picked = (token_routes[:, :, None] == jnp.arange(EXPERTS, dtype=jnp.int32)[None, None, :]).astype(jnp.float32)
    gates = jax.nn.softmax(lax.optimization_barrier(jnp.sum(picked * logits[:, None, :], axis=-1)), axis=-1)
    pair_count = sequence_length * TOP
    flat_routes = token_routes.reshape(pair_count)
    expert_hits = (flat_routes[:, None] == jnp.arange(EXPERTS, dtype=jnp.int32)[None, :]).astype(jnp.int32)
    earlier_hits = jnp.cumsum(expert_hits, axis=0, dtype=jnp.int32) - expert_hits
    slot_of_pair = (flat_routes * CAP + lax.optimization_barrier(jnp.sum(earlier_hits * expert_hits, axis=1, dtype=jnp.int32))).astype(jnp.int32)
    copies = low_back(jnp.repeat(normed_two, TOP, axis=0))
    slot_rows = jnp.zeros((EXPERTS * CAP, model_width), jnp.float32).at[slot_of_pair].set(copies)
    slot_rows = slot_rows.reshape(EXPERTS, CAP, model_width)
    inner_sums = low_back(jnp.einsum('ecd,edf->ecf', slot_rows, in_matrix, precision=highest))
    activation = low(jax.nn.silu(inner_sums[..., :FF]) * inner_sums[..., FF:])
    results = low_back(low(jnp.einsum('ecf,edf->ecd', activation, down_matrix, precision=highest)))
    returned = results.reshape(EXPERTS * CAP, model_width)[slot_of_pair].reshape(sequence_length, TOP, model_width)
    return hidden + lax.optimization_barrier(jnp.sum(gates[:, :, None] * returned, axis=1))

def adamw(weight, gradient, mean_old, square_old, step_rate, weight_decay):
    mean_new = beta_one * mean_old + (1.0 - beta_one) * gradient
    square_new = beta_two * square_old + (1.0 - beta_two) * gradient * gradient
    corrected = mean_new / (1.0 - beta_one ** STEP) / (jnp.sqrt(square_new / (1.0 - beta_two ** STEP)) + adam_eps)
    return (weight - step_rate * (corrected + weight_decay * weight), mean_new, square_new)

def add_arrays(former, latter):
    return former + latter

def reference(tokens, cotangent, doc_lengths, routes, qkv_weight, qkv_mean, qkv_square, out_weight, out_mean, out_square, router_weight, router_mean, router_square, norm_gains, gains_mean, gains_square, in_weight, in_mean, in_square, down_weight, down_mean, down_square):
    params = (low(qkv_weight), low(out_weight), low(router_weight), low(norm_gains), low(in_weight), low(down_weight))
    blocks = MICRO * N_DP * N_EXP
    group_size = math.gcd(blocks, max(1, 4096 // TOK_MB))
    rounds = blocks // group_size
    model_width = tokens.shape[1]
    token_blocks = tokens.astype(jnp.float32).reshape(rounds, group_size, TOK_MB, model_width)
    cot_blocks = cotangent.astype(jnp.float32).reshape(rounds, group_size, TOK_MB, model_width)
    length_blocks = doc_lengths.reshape(rounds, group_size, DOCS)
    route_blocks = routes.reshape(rounds, group_size, TOK_MB, TOP)

    def scan_step(totals, inputs):
        token_group, cot_group, length_group, route_group = inputs

        def run_group(weights_in, tokens_in):
            return jax.vmap(block_forward, in_axes=(None, 0, 0, 0))(weights_in, tokens_in, length_group, route_group)
        produced, pullback = jax.vjp(run_group, params, token_group)
        weight_grads, token_grads = pullback(cot_group)
        totals = jax.tree.map(add_arrays, totals, weight_grads)
        return (totals, (produced.astype(jnp.bfloat16), token_grads.astype(jnp.bfloat16)))
    start_totals = tuple((jnp.zeros_like(member) for member in params))
    totals, (produced_all, grads_all) = lax.scan(scan_step, start_totals, (token_blocks, cot_blocks, length_blocks, route_blocks))
    block_out = produced_all.reshape(-1, model_width)
    input_grad = grads_all.reshape(-1, model_width)
    d_qkv, d_out, d_router, d_gains, d_in, d_down = totals
    new_qkv, new_qkv_mean, new_qkv_square = adamw(qkv_weight, d_qkv, qkv_mean, qkv_square, 0.15, decay_rate)
    new_out, new_out_mean, new_out_square = adamw(out_weight, d_out, out_mean, out_square, 0.3, decay_rate)
    new_router, new_router_mean, new_router_square = adamw(router_weight, d_router, router_mean, router_square, 0.05, decay_rate)
    new_gains, new_gains_mean, new_gains_square = adamw(norm_gains, d_gains, gains_mean, gains_square, 0.8, 0.0)
    new_in, new_in_mean, new_in_square = adamw(in_weight, d_in, in_mean, in_square, 0.1, decay_rate)
    new_down, new_down_mean, new_down_square = adamw(down_weight, d_down, down_mean, down_square, 1.0, decay_rate)
    return (block_out, input_grad, new_qkv, new_qkv_mean, new_qkv_square, new_out, new_out_mean, new_out_square, new_router, new_router_mean, new_router_square, new_gains, new_gains_mean, new_gains_square, new_in, new_in_mean, new_in_square, new_down, new_down_mean, new_down_square)
```

```python
import math

import jax
import jax.numpy as jnp
import numpy as np
from jax import lax
from jax.sharding import Mesh
from jax.sharding import PartitionSpec as P

QUERY_HEADS = 16
KEY_VALUE_HEADS = 8
HEAD_DIMENSION = 64
FF = 512
STEP = 10
EXPERTS = 16
LANES = 128


norm_eps = 1e-06
rope_base = 10000.0
mask_fill = -1e30
beta_one = 0.9
beta_two = 0.95
adam_eps = 1e-08
decay_rate = 0.1


def rms_scale(values):
    return lax.rsqrt(jnp.mean(values * values, axis=-1, keepdims=True) + norm_eps)


def doc_layout(doc_lens, sequence_length):
    row_index = jnp.arange(sequence_length, dtype=jnp.int32)
    doc_ends = jnp.cumsum(doc_lens, dtype=jnp.int32)
    passed = (row_index[:, None] >= doc_ends[None, :]).astype(jnp.int32)
    segment = jnp.sum(passed, axis=1, dtype=jnp.int32)
    starts = jnp.sum(passed * doc_lens[None, :], axis=1, dtype=jnp.int32)
    return ((row_index - starts).astype(jnp.float32), segment)


def rope_tables(positions, head_size):
    half_size = head_size // 2
    freq_index = jnp.arange(half_size, dtype=jnp.float32)
    inverse = jnp.exp(freq_index * (-2.0 * math.log(rope_base) / head_size))
    angles = positions[:, None] * inverse[None, :]
    return (jnp.cos(angles)[:, None, :], jnp.sin(angles)[:, None, :])


def rotary_apply(values, cosine_table, sine_table):
    half_size = values.shape[-1] // 2
    lower_half = values[..., :half_size]
    upper_half = values[..., half_size:]
    return jnp.concatenate(
        [
            lower_half * cosine_table - upper_half * sine_table,
            upper_half * cosine_table + lower_half * sine_table,
        ],
        axis=-1,
    )


def rotate_back(values, cosine_table, sine_table):
    half_size = values.shape[-1] // 2
    lower_half = values[..., :half_size]
    upper_half = values[..., half_size:]
    return jnp.concatenate(
        [
            lower_half * cosine_table + upper_half * sine_table,
            upper_half * cosine_table - lower_half * sine_table,
        ],
        axis=-1,
    )


def adamw(weight, gradient, mean_old, square_old, step_rate, weight_decay):
    mean_new = beta_one * mean_old + (1.0 - beta_one) * gradient
    square_new = beta_two * square_old + (1.0 - beta_two) * gradient * gradient
    corrected = (
        mean_new
        / (1.0 - beta_one**STEP)
        / (jnp.sqrt(square_new / (1.0 - beta_two**STEP)) + adam_eps)
    )
    return (weight - step_rate * (corrected + weight_decay * weight), mean_new, square_new)


def order_of(kind, sizes):
    axes = {"home": (0, 1, 2, 3, 4), "dense": (2, 1, 3, 0, 4), "expert": (1, 2, 0, 3, 4)}[kind]
    return np.arange(math.prod(sizes), dtype=np.int32).reshape(sizes).transpose(axes).reshape(-1)


def reorder_matrix(before, after):
    return (jnp.asarray(before)[:, None] == jnp.asarray(after)[None, :]).astype(jnp.bfloat16)


def spread(values, axes):
    count = lax.axis_size(axes)
    copies = jnp.broadcast_to(values[None], (count,) + values.shape)
    return lax.all_to_all(copies, axes, split_axis=0, concat_axis=0, tiled=True)


def collect(values, axes):
    count = lax.axis_size(axes)
    parts = values.reshape((count, values.shape[0] // count) + values.shape[1:])
    parts = lax.all_to_all(parts, axes, split_axis=0, concat_axis=0, tiled=True)
    return jnp.sum(parts.astype(jnp.float32), axis=0)


def gather_dense(rows):
    width = rows.shape[1]
    rows = spread(rows, "a").reshape(-1, width)
    rows = spread(rows, ("r", "exp")).reshape(-1, width)
    return spread(rows, "core").reshape(-1, width)


def reduce_dense(grad):
    grad = collect(grad.astype(jnp.bfloat16), "core").astype(jnp.bfloat16)
    grad = collect(grad, ("r", "exp")).astype(jnp.bfloat16)
    return collect(grad, "a")


def body(
    tokens,
    cotangent,
    doc_lengths,
    routes,
    qkv_weight,
    qkv_mean,
    qkv_square,
    out_weight,
    out_mean,
    out_square,
    router_weight,
    router_mean,
    router_square,
    norm_gains,
    gains_mean,
    gains_square,
    in_weight,
    in_mean,
    in_square,
    down_weight,
    down_mean,
    down_square,
):
    f32, bf16 = jnp.float32, jnp.bfloat16
    n_a, n_r, n_c, n_e = (lax.axis_size(name) for name in ("a", "r", "core", "exp"))
    rows, width = tokens.shape
    experts = router_weight.shape[1]
    local_count = in_weight.shape[0]
    group_rows = n_c * n_a * rows
    sizes = (n_a, n_r, n_c, n_e, width // (n_a * n_r * n_c * n_e))
    home, dense, expert = (order_of(kind, sizes) for kind in ("home", "dense", "expert"))
    query_width = QUERY_HEADS * HEAD_DIMENSION
    key_width = KEY_VALUE_HEADS * HEAD_DIMENSION
    qkv_width = query_width + 2 * key_width
    fold = QUERY_HEADS // KEY_VALUE_HEADS
    score_scale = HEAD_DIMENSION ** (-0.5)

    local_rows = qkv_weight.shape[0]
    extra = jnp.zeros((local_rows, LANES - experts - 2), bf16)
    first_pack = jnp.concatenate(
        [qkv_weight.astype(bf16), router_weight.astype(bf16), norm_gains.astype(bf16), extra], axis=1
    )
    first_full = gather_dense(first_pack)
    out_full = gather_dense(out_weight.astype(bf16))
    to_dense = reorder_matrix(home, dense)
    cot_expert = jnp.dot(
        cotangent, reorder_matrix(home, expert), preferred_element_type=f32
    ).astype(bf16)
    cot_group = lax.all_gather(cot_expert, ("core", "a"), axis=0, tiled=True)
    expert_pack = jnp.concatenate([in_weight.astype(bf16), down_weight.astype(bf16)], axis=2)
    expert_pack = lax.all_to_all(expert_pack, ("core", "a"), split_axis=0, concat_axis=0, tiled=True)
    expert_full = lax.all_gather(expert_pack, ("exp", "r"), axis=0, tiled=True).reshape(
        n_e, width, 3 * FF
    )

    residual = jnp.dot(tokens, to_dense, preferred_element_type=f32)
    upstream = jnp.dot(cotangent, to_dense, preferred_element_type=f32)
    positions, segment = doc_layout(doc_lengths.reshape(-1), rows)
    cosine_table, sine_table = rope_tables(positions, HEAD_DIMENSION)
    row_index = jnp.arange(rows, dtype=jnp.int32)
    allowed = (segment[:, None] == segment[None, :]) & (row_index[None, :] <= row_index[:, None])
    qkv_full = first_full[:, :qkv_width]
    router_full = first_full[:, qkv_width : qkv_width + experts]
    gain_pair = first_full[:, qkv_width + experts : qkv_width + experts + 2].astype(f32)
    first_gain = gain_pair[:, 0]
    second_gain = gain_pair[:, 1]
    first_scale = rms_scale(residual)
    normed = (residual * first_scale * first_gain).astype(bf16)
    projected = jnp.dot(normed, qkv_full, preferred_element_type=f32)
    query_rows = (
        rotary_apply(
            projected[:, :query_width].reshape(rows, QUERY_HEADS, HEAD_DIMENSION),
            cosine_table,
            sine_table,
        )
        .astype(bf16)
        .reshape(rows, KEY_VALUE_HEADS, fold, HEAD_DIMENSION)
    )
    key_rows = rotary_apply(
        projected[:, query_width : query_width + key_width].reshape(
            rows, KEY_VALUE_HEADS, HEAD_DIMENSION
        ),
        cosine_table,
        sine_table,
    ).astype(bf16)
    value_rows = (
        projected[:, query_width + key_width :]
        .reshape(rows, KEY_VALUE_HEADS, HEAD_DIMENSION)
        .astype(bf16)
    )
    scores = (
        jnp.einsum("tkgd,skd->kgts", query_rows, key_rows, preferred_element_type=f32) * score_scale
    )
    scores = jnp.where(allowed, scores, mask_fill)
    row_peak = jnp.max(scores, axis=-1, keepdims=True)
    log_total = row_peak + jnp.log(jnp.sum(jnp.exp(scores - row_peak), axis=-1, keepdims=True))
    weights = jnp.exp(scores - log_total)
    attended = jnp.einsum(
        "kgts,skd->tkgd", weights.astype(bf16), value_rows, preferred_element_type=f32
    )
    attended = attended.reshape(rows, query_width).astype(bf16)
    hidden = residual + jnp.einsum("th,dh->td", attended, out_full, preferred_element_type=f32)
    second_scale = rms_scale(hidden)
    normed_two = (hidden * second_scale * second_gain).astype(bf16)
    logits = jnp.dot(normed_two, router_full, preferred_element_type=f32)
    expert_index = jnp.arange(experts, dtype=jnp.int32)
    used = jnp.any(routes[:, :, None] == expert_index[None, None, :], axis=1)
    gates = jax.nn.softmax(jnp.where(used, logits, -jnp.inf), axis=-1)
    gates_high = gates.astype(bf16)
    gates_low = (gates - gates_high.astype(f32)).astype(bf16)

    normed_expert = jnp.dot(
        normed_two, reorder_matrix(dense, expert), preferred_element_type=f32
    ).astype(bf16)
    sent = jnp.concatenate(
        [normed_expert, gates_high, gates_low, jnp.zeros((rows, LANES - 2 * experts), bf16)], axis=1
    )
    arrived = spread(sent, "a").reshape(n_a * rows, width + LANES)
    arrived = spread(arrived, "core").reshape(group_rows, width + LANES)
    group_normed = arrived[:, :width]
    group_gates = arrived[:, width:].astype(f32)
    place = lax.axis_index("core") * n_a + lax.axis_index("a")
    lane = jnp.arange(LANES, dtype=jnp.int32)
    cot_rows = cot_group.astype(f32)
    part_out = jnp.zeros((group_rows, width), f32)
    part_back = jnp.zeros((group_rows, width), f32)
    part_dots = jnp.zeros((group_rows, LANES), f32)
    expert_grads = []
    for index in range(n_e):
        number = index * local_count + place
        chosen = (lane % experts == number) & (lane < 2 * experts)
        gate = jnp.sum(jnp.where(chosen[None, :], group_gates, 0.0), axis=1, keepdims=True)
        in_full = expert_full[index, :, : 2 * FF]
        down_full = expert_full[index, :, 2 * FF :]
        inner = jnp.dot(group_normed, in_full, preferred_element_type=f32)
        gate_part = inner[:, :FF]
        up_part = inner[:, FF:]
        gate_sigmoid = jax.nn.sigmoid(gate_part)
        gate_silu = gate_part * gate_sigmoid
        activation = (gate_silu * up_part).astype(bf16)
        result = (
            jnp.einsum("tf,df->td", activation, down_full, preferred_element_type=f32)
            .astype(bf16)
            .astype(f32)
        )
        part_out = part_out + gate * result
        dots = jnp.sum(cot_rows * result, axis=1, keepdims=True)
        dots_high = dots.astype(bf16).astype(f32)
        part_dots = part_dots + jnp.where(
            (lane == number)[None, :],
            dots_high,
            jnp.where((lane == number + experts)[None, :], dots - dots_high, 0.0),
        )
        result_grad = (gate * cot_rows).astype(bf16)
        activation_grad = jnp.dot(result_grad, down_full, preferred_element_type=f32)
        inner_grad = jnp.concatenate(
            [
                activation_grad * up_part * gate_sigmoid * (1.0 + gate_part * (1.0 - gate_sigmoid)),
                activation_grad * gate_silu,
            ],
            axis=-1,
        ).astype(bf16)
        part_back = part_back + jnp.einsum(
            "tf,df->td", inner_grad, in_full, preferred_element_type=f32
        )
        in_grad = jnp.einsum("td,tf->df", group_normed, inner_grad, preferred_element_type=f32)
        down_grad = jnp.einsum("td,tf->df", result_grad, activation, preferred_element_type=f32)
        expert_grads.append(
            jnp.concatenate([in_grad.astype(bf16), down_grad.astype(bf16)], axis=1)
        )
    parts = jnp.concatenate(
        [part_out.astype(bf16), part_back.astype(bf16), part_dots.astype(bf16)], axis=1
    )
    parts = collect(parts, "core").astype(bf16).reshape(n_a, rows, 2 * width + LANES)
    parts = lax.all_to_all(parts, "a", split_axis=0, concat_axis=0, tiled=True)

    expert_grad = jnp.stack(expert_grads).reshape(n_e * n_r, n_c * n_a, width // (n_r * n_c * n_a), 3 * FF)
    expert_grad = collect(expert_grad, ("exp", "r")).astype(bf16)
    expert_grad = lax.all_to_all(
        expert_grad.reshape((local_count,) + expert_grad.shape[-2:]),
        ("core", "a"),
        split_axis=0,
        concat_axis=0,
        tiled=True,
    ).astype(f32)
    d_in = expert_grad[:, :, : 2 * FF]
    d_down = expert_grad[:, :, 2 * FF :]

    back = reorder_matrix(expert, dense)
    mixed = jnp.einsum("std,de->te", parts[:, :, :width], back, preferred_element_type=f32)
    copies_grad = jnp.einsum(
        "std,de->te", parts[:, :, width : 2 * width], back, preferred_element_type=f32
    )
    dots = jnp.sum(parts[:, :, 2 * width :].astype(f32), axis=0)
    gate_grad = dots[:, :experts] + dots[:, experts : 2 * experts]
    from_dense = reorder_matrix(dense, home)
    block_out = jnp.dot(
        (hidden + mixed).astype(bf16), from_dense, preferred_element_type=f32
    ).astype(bf16)
    logit_grad = (
        gates * (gate_grad - jnp.sum(gates * gate_grad, axis=-1, keepdims=True))
    ).astype(bf16)
    normed_two_grad = copies_grad + jnp.einsum(
        "te,de->td", logit_grad, router_full, preferred_element_type=f32
    )
    scaled_two = normed_two_grad * second_gain
    second_gain_grad = jnp.sum(normed_two_grad * hidden * second_scale, axis=0)
    hidden_grad = (
        upstream
        + second_scale * scaled_two
        - hidden * second_scale**3 * jnp.mean(scaled_two * hidden, axis=-1, keepdims=True)
    )
    branch_grad = hidden_grad.astype(bf16)
    out_grad = jnp.einsum("td,th->dh", branch_grad, attended, preferred_element_type=f32)
    router_grad = jnp.einsum("td,te->de", normed_two, logit_grad, preferred_element_type=f32)
    out_total = reduce_dense(
        jnp.concatenate(
            [
                out_grad.astype(bf16),
                router_grad.astype(bf16),
                second_gain_grad.astype(bf16)[:, None],
                jnp.zeros((width, LANES - experts - 1), bf16),
            ],
            axis=1,
        )
    )
    d_out = out_total[:, :query_width]
    d_router = out_total[:, query_width : query_width + experts]

    attended_grad = (
        jnp.einsum("td,dh->th", branch_grad, out_full, preferred_element_type=f32)
        .astype(bf16)
        .reshape(rows, KEY_VALUE_HEADS, fold, HEAD_DIMENSION)
    )
    value_grad = jnp.einsum(
        "kgts,tkgd->skd", weights.astype(bf16), attended_grad, preferred_element_type=f32
    )
    weight_grad = jnp.einsum(
        "tkgd,skd->kgts", attended_grad, value_rows, preferred_element_type=f32
    )
    row_delta = jnp.sum(weights * weight_grad, axis=-1, keepdims=True)
    score_grad = (weights * (weight_grad - row_delta)).astype(bf16)
    query_grad = (
        jnp.einsum("kgts,skd->tkgd", score_grad, key_rows, preferred_element_type=f32) * score_scale
    )
    key_grad = (
        jnp.einsum("kgts,tkgd->skd", score_grad, query_rows, preferred_element_type=f32)
        * score_scale
    )
    query_grad = rotate_back(
        query_grad.reshape(rows, QUERY_HEADS, HEAD_DIMENSION), cosine_table, sine_table
    ).reshape(rows, query_width)
    key_grad = rotate_back(key_grad, cosine_table, sine_table).reshape(rows, key_width)
    projected_grad = jnp.concatenate(
        [query_grad, key_grad, value_grad.reshape(rows, key_width)], axis=-1
    ).astype(bf16)
    qkv_grad = jnp.einsum("td,tf->df", normed, projected_grad, preferred_element_type=f32)
    normed_grad = jnp.einsum("tf,df->td", projected_grad, qkv_full, preferred_element_type=f32)
    scaled_one = normed_grad * first_gain
    first_gain_grad = jnp.sum(normed_grad * residual * first_scale, axis=0)
    qkv_total = reduce_dense(
        jnp.concatenate(
            [
                qkv_grad.astype(bf16),
                first_gain_grad.astype(bf16)[:, None],
                jnp.zeros((width, LANES - 1), bf16),
            ],
            axis=1,
        )
    )
    d_qkv = qkv_total[:, :qkv_width]
    d_gains = jnp.concatenate(
        [
            qkv_total[:, qkv_width : qkv_width + 1],
            out_total[:, query_width + experts : query_width + experts + 1],
        ],
        axis=1,
    )
    input_grad = (
        hidden_grad
        + first_scale * scaled_one
        - residual * first_scale**3 * jnp.mean(scaled_one * residual, axis=-1, keepdims=True)
    ).astype(bf16)
    input_grad = jnp.dot(input_grad, from_dense, preferred_element_type=f32).astype(bf16)
    new_qkv, new_qkv_mean, new_qkv_square = adamw(
        qkv_weight, d_qkv, qkv_mean, qkv_square, 0.15, decay_rate
    )
    new_out, new_out_mean, new_out_square = adamw(
        out_weight, d_out, out_mean, out_square, 0.3, decay_rate
    )
    new_router, new_router_mean, new_router_square = adamw(
        router_weight, d_router, router_mean, router_square, 0.05, decay_rate
    )
    new_gains, new_gains_mean, new_gains_square = adamw(
        norm_gains, d_gains, gains_mean, gains_square, 0.8, 0.0
    )
    new_in, new_in_mean, new_in_square = adamw(in_weight, d_in, in_mean, in_square, 0.1, decay_rate)
    new_down, new_down_mean, new_down_square = adamw(
        down_weight, d_down, down_mean, down_square, 1.0, decay_rate
    )
    return (
        block_out,
        input_grad,
        new_qkv,
        new_qkv_mean,
        new_qkv_square,
        new_out,
        new_out_mean,
        new_out_square,
        new_router,
        new_router_mean,
        new_router_square,
        new_gains,
        new_gains_mean,
        new_gains_square,
        new_in,
        new_in_mean,
        new_in_square,
        new_down,
        new_down_mean,
        new_down_square,
    )


def solution(mesh):
    n_dp, n_exp = mesh.shape["dp"], mesh.shape["exp"]
    n_a = EXPERTS // n_exp // 2
    mesh = Mesh(
        mesh.devices.reshape(n_a, n_dp // (2 * n_a), 2, n_exp), ("a", "r", "core", "exp")
    )
    placed = (
        P(("a", "r", "core", "exp"), None),
        P(("a", "r", "core", "exp"), None),
        P(("a", "r", "core", "exp"), None),
        P(("a", "r", "core", "exp"), None),
        P(("a", "r", "core", "exp"), None),
        P(("a", "r", "core", "exp"), None),
        P(("a", "r", "core", "exp"), None),
        P(("a", "r", "core", "exp"), None),
        P(("a", "r", "core", "exp"), None),
        P(("a", "r", "core", "exp"), None),
        P(("a", "r", "core", "exp"), None),
        P(("a", "r", "core", "exp"), None),
        P(("a", "r", "core", "exp"), None),
        P(("a", "r", "core", "exp"), None),
        P(("a", "r", "core", "exp"), None),
        P(("a", "r", "core", "exp"), None),
        P("exp", ("a", "r", "core"), None),
        P("exp", ("a", "r", "core"), None),
        P("exp", ("a", "r", "core"), None),
        P("exp", ("a", "r", "core"), None),
        P("exp", ("a", "r", "core"), None),
        P("exp", ("a", "r", "core"), None),
    )
    return jax.shard_map(
        body,
        mesh=mesh,
        in_specs=placed,
        out_specs=(
            P(("a", "r", "core", "exp"), None),
            P(("a", "r", "core", "exp"), None),
            P(("a", "r", "core", "exp"), None),
            P(("a", "r", "core", "exp"), None),
            P(("a", "r", "core", "exp"), None),
            P(("a", "r", "core", "exp"), None),
            P(("a", "r", "core", "exp"), None),
            P(("a", "r", "core", "exp"), None),
            P(("a", "r", "core", "exp"), None),
            P(("a", "r", "core", "exp"), None),
            P(("a", "r", "core", "exp"), None),
            P(("a", "r", "core", "exp"), None),
            P(("a", "r", "core", "exp"), None),
            P(("a", "r", "core", "exp"), None),
            P("exp", ("a", "r", "core"), None),
            P("exp", ("a", "r", "core"), None),
            P("exp", ("a", "r", "core"), None),
            P("exp", ("a", "r", "core"), None),
            P("exp", ("a", "r", "core"), None),
            P("exp", ("a", "r", "core"), None),
        ),
        check_vma=False,
    )
```

```python
import functools
import math

import jax
import jax.numpy as jnp
import numpy as np
from jax import lax
from jax.experimental import pallas as pl
from jax.experimental.pallas import tpu as pltpu
from jax.sharding import Mesh
from jax.sharding import PartitionSpec as P

QUERY_HEADS = 16
KEY_VALUE_HEADS = 8
HEAD_DIMENSION = 64
FF = 512
STEP = 10
EXPERTS = 16
LANES = 128
VMEM_BYTES = 48 * 1024 * 1024


norm_eps = 1e-06
rope_base = 10000.0
mask_fill = -1e30
beta_one = 0.9
beta_two = 0.95
adam_eps = 1e-08
decay_rate = 0.1


def rms_scale(values):
    return lax.rsqrt(jnp.mean(values * values, axis=-1, keepdims=True) + norm_eps)


def doc_layout(doc_lens, sequence_length):
    row_index = jnp.arange(sequence_length, dtype=jnp.int32)
    doc_ends = jnp.cumsum(doc_lens, dtype=jnp.int32)
    passed = (row_index[:, None] >= doc_ends[None, :]).astype(jnp.int32)
    segment = jnp.sum(passed, axis=1, dtype=jnp.int32)
    starts = jnp.sum(passed * doc_lens[None, :], axis=1, dtype=jnp.int32)
    return ((row_index - starts).astype(jnp.float32), segment)


def rope_tables(positions, head_size):
    half_size = head_size // 2
    freq_index = jnp.arange(half_size, dtype=jnp.float32)
    inverse = jnp.exp(freq_index * (-2.0 * math.log(rope_base) / head_size))
    angles = positions[:, None] * inverse[None, :]
    return (jnp.cos(angles), jnp.sin(angles))


def adamw(weight, gradient, mean_old, square_old, step_rate, weight_decay):
    mean_new = beta_one * mean_old + (1.0 - beta_one) * gradient
    square_new = beta_two * square_old + (1.0 - beta_two) * gradient * gradient
    corrected = (
        mean_new
        / (1.0 - beta_one**STEP)
        / (jnp.sqrt(square_new / (1.0 - beta_two**STEP)) + adam_eps)
    )
    return (weight - step_rate * (corrected + weight_decay * weight), mean_new, square_new)

def dot_nn(left, right):
    return jnp.dot(left, right, preferred_element_type=jnp.float32)


def dot_nt(left, right):
    return lax.dot_general(left, right, (((1,), (1,)), ((), ())), preferred_element_type=jnp.float32)


def dot_tn(left, right):
    return lax.dot_general(left, right, (((0,), (0,)), ((), ())), preferred_element_type=jnp.float32)


def lane_iota(rows):
    return lax.broadcasted_iota(jnp.int32, (rows, LANES), 1)


def gain_rows(extra, experts):
    row = lax.broadcasted_iota(jnp.int32, (8, LANES), 0)
    pick = (lane_iota(8) == row + experts).astype(jnp.bfloat16)
    return dot_nt(jnp.where(row < 2, pick, jnp.zeros_like(pick)), extra)


def swap_halves(values):
    half = HEAD_DIMENSION // 2
    lower = lane_iota(values.shape[0]) % HEAD_DIMENSION < half
    return jnp.where(lower, pltpu.roll(values, LANES - half, 1), pltpu.roll(values, half, 1))


def column_sums(values, lane):
    high = values.astype(jnp.bfloat16)
    low = (values - high.astype(jnp.float32)).astype(jnp.bfloat16)
    place = (lane_iota(values.shape[0]) == lane).astype(jnp.bfloat16)
    return dot_tn(high, place) + dot_tn(low, place)


def head_block(index):
    return slice(index * HEAD_DIMENSION, (index + 1) * HEAD_DIMENSION)


def attention_forward(
    experts,
    copies,
    x_ref,
    w_ref,
    cos_ref,
    sin_ref,
    allow_ref,
    used_ref,
    order_ref,
    hidden_ref,
    normed_ref,
    qkv_ref,
    lse_ref,
    att_ref,
    second_ref,
    gates_ref,
    sent_ref,
):
    f32, bf16 = jnp.float32, jnp.bfloat16
    width = x_ref.shape[1]
    rows = x_ref.shape[0]
    qkv_width = qkv_ref.shape[1]
    query_width = QUERY_HEADS * HEAD_DIMENSION
    key_width = KEY_VALUE_HEADS * HEAD_DIMENSION
    extra = w_ref[:, qkv_width + width :]
    gains = gain_rows(extra, experts)
    x = x_ref[...].astype(f32)
    normed = (x * rms_scale(x) * gains[0:1]).astype(bf16)
    normed_ref[...] = normed
    cosine, sine = cos_ref[...], sin_ref[...]
    for start in range(0, qkv_width, 512):
        part = dot_nn(normed, w_ref[:, start : start + 512])
        for inner in range(0, 512, LANES):
            piece = part[:, inner : inner + LANES]
            if start + inner < query_width + key_width:
                piece = piece * cosine + swap_halves(piece) * sine
            qkv_ref[:, start + inner : start + inner + LANES] = piece.astype(bf16)
    allowed = allow_ref[...] > 0.0
    lane = lane_iota(rows)
    logs = jnp.zeros((rows, LANES), f32)
    fold = QUERY_HEADS // KEY_VALUE_HEADS
    for group in range(KEY_VALUE_HEADS):
        keys = qkv_ref[:, query_width + group * HEAD_DIMENSION : query_width + (group + 1) * HEAD_DIMENSION]
        values = qkv_ref[
            :,
            query_width + key_width + group * HEAD_DIMENSION : query_width
            + key_width
            + (group + 1) * HEAD_DIMENSION,
        ]
        outs = []
        for head in range(group * fold, (group + 1) * fold):
            scores = dot_nt(qkv_ref[:, head_block(head)], keys) * HEAD_DIMENSION ** (-0.5)
            scores = jnp.where(allowed, scores, mask_fill)
            peak = jnp.max(scores, axis=1, keepdims=True)
            log_total = peak + jnp.log(jnp.sum(jnp.exp(scores - peak), axis=1, keepdims=True))
            logs = jnp.where(lane == head, log_total, logs)
            outs.append(dot_nn(jnp.exp(scores - log_total).astype(bf16), values))
        att_ref[:, group * fold * HEAD_DIMENSION : (group + 1) * fold * HEAD_DIMENSION] = (
            jnp.concatenate(outs, axis=1).astype(bf16)
        )
    lse_ref[...] = logs
    hidden = x + dot_nt(att_ref[...], w_ref[:, qkv_width : qkv_width + width])
    hidden_ref[...] = hidden
    second = (hidden * rms_scale(hidden) * gains[1:2]).astype(bf16)
    second_ref[...] = second
    used = used_ref[...] > 0.0
    logits = jnp.where(used, dot_nn(second, extra), mask_fill)
    powers = jnp.where(used, jnp.exp(logits - jnp.max(logits, axis=1, keepdims=True)), 0.0)
    gates = powers / jnp.sum(powers, axis=1, keepdims=True)
    gates_ref[...] = gates
    high = gates.astype(bf16).astype(f32)
    lanes = (high + pltpu.roll(gates - high, experts, 1)).astype(bf16)
    moved = dot_nn(second, order_ref[...]).astype(bf16)
    for copy in range(copies):
        sent_ref[copy, :, :width] = moved
        sent_ref[copy, :, width:] = lanes


def experts_forward(
    experts,
    local_count,
    place_ref,
    rows_ref,
    cot_ref,
    w_ref,
    out_ref,
    dots_ref,
    inner_ref,
    sum_ref,
    dots_sum_ref,
):
    f32, bf16 = jnp.float32, jnp.bfloat16
    index, chunk = pl.program_id(0), pl.program_id(1)
    count, width = cot_ref.shape
    number = index * local_count + place_ref[0]
    lane = lane_iota(count)
    chosen = (lane == number) | (lane == number + experts)
    gate = jnp.sum(
        jnp.where(chosen, rows_ref[:, width:].astype(f32), 0.0), axis=1, keepdims=True
    )
    inner = dot_nn(rows_ref[:, :width], w_ref[0, :, : 2 * FF])
    inner_ref[0] = inner
    gate_part = inner[:, :FF]
    activation = (gate_part * jax.nn.sigmoid(gate_part) * inner[:, FF:]).astype(bf16)
    result = dot_nt(activation, w_ref[0, :, 2 * FF :]).astype(bf16).astype(f32)
    dots = jnp.sum(cot_ref[...].astype(f32) * result, axis=1, keepdims=True)
    dots_high = dots.astype(bf16).astype(f32)
    lanes = jnp.where(lane == number, dots_high, 0.0) + jnp.where(
        lane == number + experts, dots - dots_high, 0.0
    )
    here = pl.ds(pl.multiple_of(chunk * count, count), count)

    @pl.when(index == 0)
    def _():
        sum_ref[here, :] = gate * result
        dots_sum_ref[here, :] = lanes

    @pl.when(index > 0)
    def _():
        sum_ref[here, :] += gate * result
        dots_sum_ref[here, :] += lanes

    out_ref[...] = sum_ref[here, :].astype(bf16)
    dots_ref[...] = dots_sum_ref[here, :].astype(bf16)


def experts_backward(
    experts,
    local_count,
    place_ref,
    gates_ref,
    cot_ref,
    w_ref,
    inner_ref,
    dots_ref,
    back_ref,
    inner_grad_ref,
    act_ref,
    result_grad_ref,
    sum_ref,
):
    f32, bf16 = jnp.float32, jnp.bfloat16
    index, chunk = pl.program_id(0), pl.program_id(1)
    count, width = cot_ref.shape
    number = index * local_count + place_ref[0]
    lane = lane_iota(count)
    chosen = (lane == number) | (lane == number + experts)
    gate = jnp.sum(jnp.where(chosen, gates_ref[...].astype(f32), 0.0), axis=1, keepdims=True)
    result_grad = (gate * cot_ref[...].astype(f32)).astype(bf16)
    result_grad_ref[0] = result_grad
    act_grad = dot_nn(result_grad, w_ref[0, :, 2 * FF :])
    gate_part = inner_ref[0, :, :FF]
    up_part = inner_ref[0, :, FF:]
    gate_sigmoid = jax.nn.sigmoid(gate_part)
    gate_silu = gate_part * gate_sigmoid
    act_ref[0] = (gate_silu * up_part).astype(bf16)
    inner_grad_ref[0, :, :FF] = (
        act_grad * up_part * gate_sigmoid * (1.0 + gate_part * (1.0 - gate_sigmoid))
    ).astype(bf16)
    inner_grad_ref[0, :, FF:] = (act_grad * gate_silu).astype(bf16)
    copy_grad = dot_nt(inner_grad_ref[0], w_ref[0, :, : 2 * FF])
    here = pl.ds(pl.multiple_of(chunk * count, count), count)

    @pl.when(index == 0)
    def _():
        sum_ref[here, :] = copy_grad

    @pl.when(index > 0)
    def _():
        sum_ref[here, :] += copy_grad

    back_ref[:, :width] = sum_ref[here, :].astype(bf16)
    back_ref[:, width:] = dots_ref[...]


def experts_weights(rows_ref, inner_grad_ref, result_grad_ref, act_ref, grad_ref):
    grad_ref[0, :, : 2 * FF] = dot_tn(rows_ref[...], inner_grad_ref[0]).astype(jnp.bfloat16)
    grad_ref[0, :, 2 * FF :] = dot_tn(result_grad_ref[0], act_ref[0]).astype(jnp.bfloat16)


def home_backward(
    experts,
    parts_ref,
    order_ref,
    cot_ref,
    hidden_ref,
    second_ref,
    gates_ref,
    w_ref,
    att_ref,
    hidden_grad_ref,
    branch_grad_ref,
    out_grad_ref,
):
    f32, bf16 = jnp.float32, jnp.bfloat16
    rows, width = cot_ref.shape
    sources = parts_ref.shape[0]
    extra = w_ref[:, w_ref.shape[1] - LANES :]
    second_gain = gain_rows(extra, experts)[1:2]
    dots = jnp.zeros((rows, LANES), f32)
    second_grad = jnp.zeros((rows, width), f32)
    for source in range(sources):
        dots = dots + parts_ref[source, :, width:].astype(f32)
        second_grad = second_grad + dot_nn(parts_ref[source, :, :width], order_ref[...])
    dots = dots + pltpu.roll(dots, LANES - experts, 1)
    gates = gates_ref[...]
    logit_grad = (gates * (dots - jnp.sum(gates * dots, axis=1, keepdims=True))).astype(bf16)
    second_grad = second_grad + dot_nt(logit_grad, extra)
    hidden = hidden_ref[...]
    scale = rms_scale(hidden)
    scaled = second_grad * second_gain
    hidden_grad = (
        cot_ref[...].astype(f32)
        + scale * scaled
        - hidden * (scale * scale * scale) * jnp.mean(scaled * hidden, axis=1, keepdims=True)
    )
    hidden_grad_ref[...] = hidden_grad
    branch_grad = hidden_grad.astype(bf16)
    branch_grad_ref[...] = branch_grad
    for start in range(0, width, 512):
        out_grad_ref[:, start : start + 512] = dot_tn(
            branch_grad, att_ref[:, start : start + 512]
        ).astype(bf16)
    out_grad_ref[:, width:] = (
        dot_tn(second_ref[...], logit_grad) + column_sums(second_grad * hidden * scale, experts)
    ).astype(bf16)


def attention_backward(
    experts,
    branch_grad_ref,
    hidden_grad_ref,
    w_ref,
    qkv_ref,
    lse_ref,
    normed_ref,
    x_ref,
    cos_ref,
    sin_ref,
    allow_ref,
    qkv_grad_ref,
    input_grad_ref,
    mid_ref,
    proj_ref,
):
    f32, bf16 = jnp.float32, jnp.bfloat16
    rows, width = x_ref.shape
    qkv_width = qkv_ref.shape[1]
    query_width = QUERY_HEADS * HEAD_DIMENSION
    key_width = KEY_VALUE_HEADS * HEAD_DIMENSION
    fold = QUERY_HEADS // KEY_VALUE_HEADS
    score_scale = HEAD_DIMENSION ** (-0.5)
    first_gain = gain_rows(w_ref[:, qkv_width + width :], experts)[0:1]
    mid_ref[...] = dot_nn(branch_grad_ref[...], w_ref[:, qkv_width : qkv_width + width]).astype(bf16)
    cosine, sine = cos_ref[...], sin_ref[...]
    allowed = allow_ref[...] > 0.0
    lane = lane_iota(rows)
    logs = lse_ref[...]

    def turned_back(values):
        return (values * cosine - swap_halves(values) * sine).astype(bf16)

    key_grads, value_grads = [], []
    for group in range(KEY_VALUE_HEADS):
        keys = qkv_ref[:, query_width + group * HEAD_DIMENSION : query_width + (group + 1) * HEAD_DIMENSION]
        values = qkv_ref[
            :,
            query_width + key_width + group * HEAD_DIMENSION : query_width
            + key_width
            + (group + 1) * HEAD_DIMENSION,
        ]
        query_grads = []
        key_grad = jnp.zeros((rows, HEAD_DIMENSION), f32)
        value_grad = jnp.zeros((rows, HEAD_DIMENSION), f32)
        for head in range(group * fold, (group + 1) * fold):
            queries = qkv_ref[:, head_block(head)]
            mid = mid_ref[:, head_block(head)]
            log_total = jnp.sum(jnp.where(lane == head, logs, 0.0), axis=1, keepdims=True)
            scores = jnp.where(allowed, dot_nt(queries, keys) * score_scale, mask_fill)
            weights = jnp.exp(scores - log_total)
            weight_grad = dot_nt(mid, values)
            delta = jnp.sum(weights * weight_grad, axis=1, keepdims=True)
            score_grad = (weights * (weight_grad - delta)).astype(bf16)
            query_grads.append(dot_nn(score_grad, keys) * score_scale)
            key_grad = key_grad + dot_tn(score_grad, queries)
            value_grad = value_grad + dot_tn(weights.astype(bf16), mid)
        proj_ref[:, group * LANES : (group + 1) * LANES] = turned_back(
            jnp.concatenate(query_grads, axis=1)
        )
        key_grads.append(key_grad * score_scale)
        value_grads.append(value_grad)
        if group % 2 == 1:
            start = query_width + (group // 2) * LANES
            proj_ref[:, start : start + LANES] = turned_back(
                jnp.concatenate(key_grads[-2:], axis=1)
            )
            start = start + key_width
            proj_ref[:, start : start + LANES] = jnp.concatenate(value_grads[-2:], axis=1).astype(
                bf16
            )
    normed = normed_ref[...]
    for start in range(0, qkv_width, 512):
        qkv_grad_ref[:, start : start + 512] = dot_tn(
            normed, proj_ref[:, start : start + 512]
        ).astype(bf16)
    normed_grad = dot_nt(proj_ref[...], w_ref[:, :qkv_width])
    x = x_ref[...].astype(f32)
    scale = rms_scale(x)
    scaled = normed_grad * first_gain
    qkv_grad_ref[:, qkv_width:] = column_sums(normed_grad * x * scale, 0).astype(bf16)
    input_grad_ref[...] = (
        hidden_grad_ref[...]
        + scale * scaled
        - x * (scale * scale * scale) * jnp.mean(scaled * x, axis=1, keepdims=True)
    ).astype(bf16)


def whole_call(kernel, outputs, operands, flops, scratch=()):
    moved = sum(math.prod(item.shape) * item.dtype.itemsize for item in list(outputs) + list(operands))
    return pl.pallas_call(
        kernel,
        out_shape=outputs,
        in_specs=[pl.BlockSpec(memory_space=pltpu.VMEM)] * len(operands),
        out_specs=[pl.BlockSpec(memory_space=pltpu.VMEM)] * len(outputs),
        scratch_shapes=list(scratch),
        compiler_params=pltpu.CompilerParams(vmem_limit_bytes=VMEM_BYTES),
        cost_estimate=pl.CostEstimate(flops=flops, bytes_accessed=moved, transcendentals=0),
    )(*operands)


def order_of(kind, sizes):
    axes = {"home": (0, 1, 2, 3, 4), "dense": (2, 1, 3, 0, 4), "expert": (1, 2, 0, 3, 4)}[kind]
    return np.arange(math.prod(sizes), dtype=np.int32).reshape(sizes).transpose(axes).reshape(-1)


def reorder_matrix(before, after):
    return (jnp.asarray(before)[:, None] == jnp.asarray(after)[None, :]).astype(jnp.bfloat16)


def exchange(values, axes):
    return lax.all_to_all(values, axes, split_axis=0, concat_axis=0, tiled=True)


def spread(values, axes):
    count = lax.axis_size(axes)
    copies = exchange(jnp.broadcast_to(values[None], (count,) + values.shape), axes)
    return copies.reshape((count * values.shape[0],) + values.shape[1:])


def collect(values, axes):
    count = lax.axis_size(axes)
    parts = exchange(values.reshape((count, values.shape[0] // count) + values.shape[1:]), axes)
    total = parts[0].astype(jnp.float32)
    for index in range(1, count):
        total = total + parts[index].astype(jnp.float32)
    return total


def reduce_dense(grad):
    grad = collect(grad, "core").astype(jnp.bfloat16)
    grad = collect(grad, ("r", "exp")).astype(jnp.bfloat16)
    return collect(grad, "a")


def run_experts(place, arrived, cot_group, expert_full, experts, local_count):
    f32, bf16 = jnp.float32, jnp.bfloat16
    shape = jax.ShapeDtypeStruct
    n_e, width, _ = expert_full.shape
    group_rows = arrived.shape[0]
    count = min(256, group_rows)
    chunks = group_rows // count
    params = pltpu.CompilerParams(vmem_limit_bytes=VMEM_BYTES)
    scalar = pl.BlockSpec(memory_space=pltpu.SMEM)
    cot_spec = pl.BlockSpec((count, width), lambda k, i: (i, 0))
    w_spec = pl.BlockSpec((1, width, 3 * FF), lambda k, i: (k, 0, 0))
    inner_spec = pl.BlockSpec((1, count, 2 * FF), lambda k, i: (k, i, 0))
    dots_spec = pl.BlockSpec((count, LANES), lambda k, i: (i, 0))
    rows_spec = pl.BlockSpec((count, width + LANES), lambda k, i: (i, 0))
    flops = 2 * n_e * group_rows * width * 3 * FF
    weight_bytes = n_e * width * 3 * FF * 2
    out, dots, inner = pl.pallas_call(
        functools.partial(experts_forward, experts, local_count),
        grid=(n_e, chunks),
        out_shape=[
            shape((group_rows, width), bf16),
            shape((group_rows, LANES), bf16),
            shape((n_e, group_rows, 2 * FF), f32),
        ],
        in_specs=[scalar, rows_spec, cot_spec, w_spec],
        out_specs=[cot_spec, dots_spec, inner_spec],
        scratch_shapes=[pltpu.VMEM((group_rows, width), f32), pltpu.VMEM((group_rows, LANES), f32)],
        compiler_params=params,
        cost_estimate=pl.CostEstimate(
            flops=flops,
            bytes_accessed=weight_bytes + n_e * group_rows * width * 10,
            transcendentals=n_e * group_rows * FF,
        ),
    )(place, arrived, cot_group, expert_full)
    back, inner_grad, activation, result_grad = pl.pallas_call(
        functools.partial(experts_backward, experts, local_count),
        grid=(n_e, chunks),
        out_shape=[
            shape((group_rows, width + LANES), bf16),
            shape((n_e, group_rows, 2 * FF), bf16),
            shape((n_e, group_rows, FF), bf16),
            shape((n_e, group_rows, width), bf16),
        ],
        in_specs=[
            scalar,
            pl.BlockSpec((count, LANES), lambda k, i: (i, width // LANES)),
            cot_spec,
            w_spec,
            inner_spec,
            dots_spec,
        ],
        out_specs=[
            rows_spec,
            inner_spec,
            pl.BlockSpec((1, count, FF), lambda k, i: (k, i, 0)),
            pl.BlockSpec((1, count, width), lambda k, i: (k, i, 0)),
        ],
        scratch_shapes=[pltpu.VMEM((group_rows, width), f32)],
        compiler_params=params,
        cost_estimate=pl.CostEstimate(
            flops=flops,
            bytes_accessed=weight_bytes + n_e * group_rows * width * 13,
            transcendentals=n_e * group_rows * FF,
        ),
    )(place, arrived, cot_group, expert_full, inner, dots)
    part = min(256, width)
    grads = pl.pallas_call(
        experts_weights,
        grid=(n_e, width // part),
        out_shape=shape((n_e, width, 3 * FF), bf16),
        in_specs=[
            pl.BlockSpec((group_rows, part), lambda k, j: (0, j)),
            pl.BlockSpec((1, group_rows, 2 * FF), lambda k, j: (k, 0, 0)),
            pl.BlockSpec((1, group_rows, part), lambda k, j: (k, 0, j)),
            pl.BlockSpec((1, group_rows, FF), lambda k, j: (k, 0, 0)),
        ],
        out_specs=pl.BlockSpec((1, part, 3 * FF), lambda k, j: (k, j, 0)),
        compiler_params=params,
        cost_estimate=pl.CostEstimate(
            flops=flops,
            bytes_accessed=weight_bytes + n_e * group_rows * width * 7,
            transcendentals=0,
        ),
    )(arrived, inner_grad, result_grad, activation)
    return out, back, grads


def body(
    tokens,
    cotangent,
    doc_lengths,
    routes,
    qkv_weight,
    qkv_mean,
    qkv_square,
    out_weight,
    out_mean,
    out_square,
    router_weight,
    router_mean,
    router_square,
    norm_gains,
    gains_mean,
    gains_square,
    in_weight,
    in_mean,
    in_square,
    down_weight,
    down_mean,
    down_square,
):
    f32, bf16 = jnp.float32, jnp.bfloat16
    shape = jax.ShapeDtypeStruct
    n_a, n_r, n_c, n_e = (lax.axis_size(name) for name in ("a", "r", "core", "exp"))
    rows, width = tokens.shape
    experts = router_weight.shape[1]
    local_count = in_weight.shape[0]
    sizes = (n_a, n_r, n_c, n_e, width // (n_a * n_r * n_c * n_e))
    home, dense, expert = (order_of(kind, sizes) for kind in ("home", "dense", "expert"))
    query_width = QUERY_HEADS * HEAD_DIMENSION
    qkv_width = query_width + 2 * KEY_VALUE_HEADS * HEAD_DIMENSION

    local_rows = qkv_weight.shape[0]
    extra = jnp.zeros((local_rows, LANES - experts - 2), bf16)
    pack = jnp.concatenate(
        [
            qkv_weight.astype(bf16),
            out_weight.astype(bf16),
            router_weight.astype(bf16),
            norm_gains.astype(bf16),
            extra,
        ],
        axis=1,
    )
    pack = spread(pack, "a")
    cot_expert = dot_nn(cotangent, reorder_matrix(home, expert)).astype(bf16)
    cot_group = lax.all_gather(cot_expert, ("core", "a"), axis=0, tiled=True)
    expert_pack = jnp.concatenate([in_weight.astype(bf16), down_weight.astype(bf16)], axis=2)
    pack, expert_pack = lax.optimization_barrier((pack, expert_pack))
    expert_pack = exchange(expert_pack, ("core", "a"))
    expert_full = lax.all_gather(expert_pack, ("exp", "r"), axis=0, tiled=True).reshape(
        n_e, width, 3 * FF
    )
    dense_full = spread(spread(pack, ("r", "exp")), "core")

    to_dense = reorder_matrix(home, dense)
    x_dense = dot_nn(tokens, to_dense).astype(bf16)
    cot_dense = dot_nn(cotangent, to_dense).astype(bf16)
    positions, segment = doc_layout(doc_lengths.reshape(-1), rows)
    cosine, sine = rope_tables(positions, HEAD_DIMENSION)
    repeat = LANES // HEAD_DIMENSION
    cosine = jnp.concatenate([cosine, cosine] * repeat, axis=1)
    sine = jnp.concatenate([-sine, sine] * repeat, axis=1)
    row_index = jnp.arange(rows, dtype=jnp.int32)
    allowed = (segment[:, None] == segment[None, :]) & (row_index[None, :] <= row_index[:, None])
    allowed = allowed.astype(f32)
    used = jnp.any(
        routes[:, :, None] == jnp.arange(LANES, dtype=jnp.int32)[None, None, :], axis=1
    ).astype(f32)
    hidden, normed, qkv, logs, attended, second, gates, sent = whole_call(
        functools.partial(attention_forward, experts, n_a),
        [
            shape((rows, width), f32),
            shape((rows, width), bf16),
            shape((rows, qkv_width), bf16),
            shape((rows, LANES), f32),
            shape((rows, query_width), bf16),
            shape((rows, width), bf16),
            shape((rows, LANES), f32),
            shape((n_a, rows, width + LANES), bf16),
        ],
        [x_dense, dense_full, cosine, sine, allowed, used, reorder_matrix(dense, expert)],
        flops=2 * rows * width * (qkv_width + 2 * width + 2 * rows),
    )

    arrived = exchange(sent, "a").reshape(n_a * rows, width + LANES)
    arrived = spread(arrived, "core")
    place = (lax.axis_index("core") * n_a + lax.axis_index("a")).astype(jnp.int32).reshape(1)
    out, back, expert_grad = run_experts(
        place, arrived, cot_group, expert_full, experts, local_count
    )
    out = exchange(collect(out, "core").astype(bf16).reshape(n_a, rows, width), "a")
    back = exchange(collect(back, "core").astype(bf16).reshape(n_a, rows, width + LANES), "a")

    from_expert = reorder_matrix(expert, dense)
    hidden_grad, branch_grad, out_grad = whole_call(
        functools.partial(home_backward, experts),
        [
            shape((rows, width), f32),
            shape((rows, width), bf16),
            shape((width, query_width + LANES), bf16),
        ],
        [back, from_expert, cot_dense, hidden, second, gates, dense_full, attended],
        flops=2 * rows * width * (n_a * width + query_width),
    )
    out_total = reduce_dense(out_grad)
    qkv_grad, input_grad = whole_call(
        functools.partial(attention_backward, experts),
        [shape((width, qkv_width + LANES), bf16), shape((rows, width), bf16)],
        [
            branch_grad,
            hidden_grad,
            dense_full,
            qkv,
            logs,
            normed,
            x_dense,
            cosine,
            sine,
            allowed,
        ],
        flops=2 * rows * width * (2 * qkv_width + width + 4 * rows),
        scratch=[pltpu.VMEM((rows, query_width), bf16), pltpu.VMEM((rows, qkv_width), bf16)],
    )
    qkv_total = reduce_dense(qkv_grad)

    expert_grad = expert_grad.reshape(
        n_e * n_r * n_c * n_a, width // (n_r * n_c * n_a), 3 * FF
    )
    expert_grad = exchange(collect(expert_grad, ("exp", "r")).astype(bf16), ("core", "a"))
    expert_grad = expert_grad.astype(f32)
    d_in = expert_grad[:, :, : 2 * FF]
    d_down = expert_grad[:, :, 2 * FF :]

    from_dense = reorder_matrix(dense, home)
    mixed = dot_nn(out[0], from_expert)
    for index in range(1, n_a):
        mixed = mixed + dot_nn(out[index], from_expert)
    block_out = dot_nn((hidden + mixed).astype(bf16), from_dense).astype(bf16)
    input_grad = dot_nn(input_grad, from_dense).astype(bf16)
    d_out = out_total[:, :query_width]
    d_router = out_total[:, query_width : query_width + experts]
    d_qkv = qkv_total[:, :qkv_width]
    d_gains = jnp.concatenate(
        [
            qkv_total[:, qkv_width : qkv_width + 1],
            out_total[:, query_width + experts : query_width + experts + 1],
        ],
        axis=1,
    )
    new_qkv, new_qkv_mean, new_qkv_square = adamw(
        qkv_weight, d_qkv, qkv_mean, qkv_square, 0.15, decay_rate
    )
    new_out, new_out_mean, new_out_square = adamw(
        out_weight, d_out, out_mean, out_square, 0.3, decay_rate
    )
    new_router, new_router_mean, new_router_square = adamw(
        router_weight, d_router, router_mean, router_square, 0.05, decay_rate
    )
    new_gains, new_gains_mean, new_gains_square = adamw(
        norm_gains, d_gains, gains_mean, gains_square, 0.8, 0.0
    )
    new_in, new_in_mean, new_in_square = adamw(in_weight, d_in, in_mean, in_square, 0.1, decay_rate)
    new_down, new_down_mean, new_down_square = adamw(
        down_weight, d_down, down_mean, down_square, 1.0, decay_rate
    )
    return (
        block_out,
        input_grad,
        new_qkv,
        new_qkv_mean,
        new_qkv_square,
        new_out,
        new_out_mean,
        new_out_square,
        new_router,
        new_router_mean,
        new_router_square,
        new_gains,
        new_gains_mean,
        new_gains_square,
        new_in,
        new_in_mean,
        new_in_square,
        new_down,
        new_down_mean,
        new_down_square,
    )


def solution(mesh):
    n_dp, n_exp = mesh.shape["dp"], mesh.shape["exp"]
    n_a = EXPERTS // n_exp // 2
    mesh = Mesh(
        mesh.devices.reshape(n_a, n_dp // (2 * n_a), 2, n_exp), ("a", "r", "core", "exp")
    )
    placed = (
        P(("a", "r", "core", "exp"), None),
        P(("a", "r", "core", "exp"), None),
        P(("a", "r", "core", "exp"), None),
        P(("a", "r", "core", "exp"), None),
        P(("a", "r", "core", "exp"), None),
        P(("a", "r", "core", "exp"), None),
        P(("a", "r", "core", "exp"), None),
        P(("a", "r", "core", "exp"), None),
        P(("a", "r", "core", "exp"), None),
        P(("a", "r", "core", "exp"), None),
        P(("a", "r", "core", "exp"), None),
        P(("a", "r", "core", "exp"), None),
        P(("a", "r", "core", "exp"), None),
        P(("a", "r", "core", "exp"), None),
        P(("a", "r", "core", "exp"), None),
        P(("a", "r", "core", "exp"), None),
        P("exp", ("a", "r", "core"), None),
        P("exp", ("a", "r", "core"), None),
        P("exp", ("a", "r", "core"), None),
        P("exp", ("a", "r", "core"), None),
        P("exp", ("a", "r", "core"), None),
        P("exp", ("a", "r", "core"), None),
    )
    return jax.shard_map(
        body,
        mesh=mesh,
        in_specs=placed,
        out_specs=(
            P(("a", "r", "core", "exp"), None),
            P(("a", "r", "core", "exp"), None),
            P(("a", "r", "core", "exp"), None),
            P(("a", "r", "core", "exp"), None),
            P(("a", "r", "core", "exp"), None),
            P(("a", "r", "core", "exp"), None),
            P(("a", "r", "core", "exp"), None),
            P(("a", "r", "core", "exp"), None),
            P(("a", "r", "core", "exp"), None),
            P(("a", "r", "core", "exp"), None),
            P(("a", "r", "core", "exp"), None),
            P(("a", "r", "core", "exp"), None),
            P(("a", "r", "core", "exp"), None),
            P(("a", "r", "core", "exp"), None),
            P("exp", ("a", "r", "core"), None),
            P("exp", ("a", "r", "core"), None),
            P("exp", ("a", "r", "core"), None),
            P("exp", ("a", "r", "core"), None),
            P("exp", ("a", "r", "core"), None),
            P("exp", ("a", "r", "core"), None),
        ),
        check_vma=False,
    )
```

```python
import functools
import math

import jax
import jax.numpy as jnp
import numpy as np
from jax import lax
from jax.experimental import pallas as pl
from jax.experimental.pallas import tpu as pltpu
from jax.sharding import Mesh
from jax.sharding import PartitionSpec as P

QUERY_HEADS = 16
KEY_VALUE_HEADS = 8
HEAD_DIMENSION = 64
FF = 512
STEP = 10
EXPERTS = 16
LANES = 128
MESH_AXES = ("a", "r", "core", "exp")
VMEM_BYTES = 48 * 1024 * 1024


norm_eps = 1e-06
rope_base = 10000.0
mask_fill = -1e30
beta_one = 0.9
beta_two = 0.95
adam_eps = 1e-08
decay_rate = 0.1


def rms_scale(values):
    return lax.rsqrt(jnp.mean(values * values, axis=-1, keepdims=True) + norm_eps)


def doc_layout(doc_lens, sequence_length):
    row_index = jnp.arange(sequence_length, dtype=jnp.int32)
    doc_ends = jnp.cumsum(doc_lens, dtype=jnp.int32)
    passed = (row_index[:, None] >= doc_ends[None, :]).astype(jnp.int32)
    segment = jnp.sum(passed, axis=1, dtype=jnp.int32)
    starts = jnp.sum(passed * doc_lens[None, :], axis=1, dtype=jnp.int32)
    return ((row_index - starts).astype(jnp.float32), segment)


def rope_tables(positions, head_size):
    half_size = head_size // 2
    freq_index = jnp.arange(half_size, dtype=jnp.float32)
    inverse = jnp.exp(freq_index * (-2.0 * math.log(rope_base) / head_size))
    angles = positions[:, None] * inverse[None, :]
    return (jnp.cos(angles), jnp.sin(angles))


def adamw(weight, gradient, mean_old, square_old, step_rate, weight_decay):
    mean_new = beta_one * mean_old + (1.0 - beta_one) * gradient
    square_new = beta_two * square_old + (1.0 - beta_two) * gradient * gradient
    corrected = (
        mean_new
        / (1.0 - beta_one**STEP)
        / (jnp.sqrt(square_new / (1.0 - beta_two**STEP)) + adam_eps)
    )
    return (weight - step_rate * (corrected + weight_decay * weight), mean_new, square_new)

def dot_nn(left, right):
    return jnp.dot(left, right, preferred_element_type=jnp.float32)


def dot_nt(left, right):
    return lax.dot_general(left, right, (((1,), (1,)), ((), ())), preferred_element_type=jnp.float32)


def dot_tn(left, right):
    return lax.dot_general(left, right, (((0,), (0,)), ((), ())), preferred_element_type=jnp.float32)


def lane_iota(rows):
    return lax.broadcasted_iota(jnp.int32, (rows, LANES), 1)


def gain_rows(extra, experts):
    row = lax.broadcasted_iota(jnp.int32, (8, LANES), 0)
    pick = (lane_iota(8) == row + experts).astype(jnp.bfloat16)
    return dot_nt(jnp.where(row < 2, pick, jnp.zeros_like(pick)), extra)


def swap_halves(values):
    half = HEAD_DIMENSION // 2
    lower = lane_iota(values.shape[0]) % HEAD_DIMENSION < half
    return jnp.where(lower, pltpu.roll(values, LANES - half, 1), pltpu.roll(values, half, 1))


def column_sums(values, lane):
    high = values.astype(jnp.bfloat16)
    low = (values - high.astype(jnp.float32)).astype(jnp.bfloat16)
    place = (lane_iota(values.shape[0]) == lane).astype(jnp.bfloat16)
    return dot_tn(high, place) + dot_tn(low, place)


def head_block(index):
    return slice(index * HEAD_DIMENSION, (index + 1) * HEAD_DIMENSION)


def attention_forward(
    experts,
    copies,
    x_ref,
    w_ref,
    cos_ref,
    sin_ref,
    allow_ref,
    used_ref,
    order_ref,
    hidden_ref,
    normed_ref,
    qkv_ref,
    lse_ref,
    att_ref,
    second_ref,
    gates_ref,
    sent_ref,
):
    f32, bf16 = jnp.float32, jnp.bfloat16
    width = x_ref.shape[1]
    rows = x_ref.shape[0]
    qkv_width = qkv_ref.shape[1]
    query_width = QUERY_HEADS * HEAD_DIMENSION
    key_width = KEY_VALUE_HEADS * HEAD_DIMENSION
    extra = w_ref[:, qkv_width + width :]
    gains = gain_rows(extra, experts)
    x = x_ref[...].astype(f32)
    normed = (x * rms_scale(x) * gains[0:1]).astype(bf16)
    normed_ref[...] = normed
    cosine, sine = cos_ref[...], sin_ref[...]
    for start in range(0, qkv_width, 512):
        part = dot_nn(normed, w_ref[:, start : start + 512])
        for inner in range(0, 512, LANES):
            piece = part[:, inner : inner + LANES]
            if start + inner < query_width + key_width:
                piece = piece * cosine + swap_halves(piece) * sine
            qkv_ref[:, start + inner : start + inner + LANES] = piece.astype(bf16)
    allowed = allow_ref[...] > 0.0
    lane = lane_iota(rows)
    logs = jnp.zeros((rows, LANES), f32)
    fold = QUERY_HEADS // KEY_VALUE_HEADS
    for group in range(KEY_VALUE_HEADS):
        keys = qkv_ref[:, query_width + group * HEAD_DIMENSION : query_width + (group + 1) * HEAD_DIMENSION]
        values = qkv_ref[
            :,
            query_width + key_width + group * HEAD_DIMENSION : query_width
            + key_width
            + (group + 1) * HEAD_DIMENSION,
        ]
        outs = []
        for head in range(group * fold, (group + 1) * fold):
            scores = dot_nt(qkv_ref[:, head_block(head)], keys) * HEAD_DIMENSION ** (-0.5)
            scores = jnp.where(allowed, scores, mask_fill)
            peak = jnp.max(scores, axis=1, keepdims=True)
            log_total = peak + jnp.log(jnp.sum(jnp.exp(scores - peak), axis=1, keepdims=True))
            logs = jnp.where(lane == head, log_total, logs)
            outs.append(dot_nn(jnp.exp(scores - log_total).astype(bf16), values))
        att_ref[:, group * fold * HEAD_DIMENSION : (group + 1) * fold * HEAD_DIMENSION] = (
            jnp.concatenate(outs, axis=1).astype(bf16)
        )
    lse_ref[...] = logs
    hidden = x + dot_nt(att_ref[...], w_ref[:, qkv_width : qkv_width + width])
    hidden_ref[...] = hidden
    second = (hidden * rms_scale(hidden) * gains[1:2]).astype(bf16)
    second_ref[...] = second
    used = used_ref[...] > 0.0
    logits = jnp.where(used, dot_nn(second, extra), mask_fill)
    powers = jnp.where(used, jnp.exp(logits - jnp.max(logits, axis=1, keepdims=True)), 0.0)
    gates = powers / jnp.sum(powers, axis=1, keepdims=True)
    gates_ref[...] = gates
    high = gates.astype(bf16).astype(f32)
    lanes = (high + pltpu.roll(gates - high, experts, 1)).astype(bf16)
    moved = dot_nn(second, order_ref[...]).astype(bf16)
    for copy in range(copies):
        sent_ref[copy, :, :width] = moved
        sent_ref[copy, :, width:] = lanes


def own_gate(lanes, number, experts):
    lane = lane_iota(lanes.shape[0])
    chosen = (lane == number) | (lane == number + experts)
    return jnp.sum(jnp.where(chosen, lanes.astype(jnp.float32), 0.0), axis=1, keepdims=True)


def experts_forward(
    experts, local_count, place_ref, rows_ref, w_ref, out_ref, inner_ref, sum_ref
):
    f32, bf16 = jnp.float32, jnp.bfloat16
    index, chunk = pl.program_id(0), pl.program_id(1)
    count, width = out_ref.shape
    gate = own_gate(rows_ref[:, width:], index * local_count + place_ref[0], experts)
    inner = dot_nn(rows_ref[:, :width], w_ref[0, :, : 2 * FF])
    inner_ref[0] = inner
    gate_part = inner[:, :FF]
    activation = (gate_part * jax.nn.sigmoid(gate_part) * inner[:, FF:]).astype(bf16)
    result = dot_nt(activation, w_ref[0, :, 2 * FF :]).astype(bf16).astype(f32)
    here = pl.ds(pl.multiple_of(chunk * count, count), count)

    @pl.when(index == 0)
    def _():
        sum_ref[here, :] = gate * result

    @pl.when(index > 0)
    def _():
        sum_ref[here, :] += gate * result

    out_ref[...] = sum_ref[here, :].astype(bf16)


def experts_backward(
    experts,
    local_count,
    place_ref,
    gates_ref,
    cot_ref,
    w_ref,
    inner_ref,
    back_ref,
    inner_grad_ref,
    act_ref,
    sum_ref,
    dots_sum_ref,
):
    f32, bf16 = jnp.float32, jnp.bfloat16
    index, chunk = pl.program_id(0), pl.program_id(1)
    count, width = cot_ref.shape
    number = index * local_count + place_ref[0]
    gate = own_gate(gates_ref[...], number, experts)
    gate_part = inner_ref[0, :, :FF]
    up_part = inner_ref[0, :, FF:]
    gate_sigmoid = jax.nn.sigmoid(gate_part)
    gate_silu = gate_part * gate_sigmoid
    activation = (gate_silu * up_part).astype(bf16).astype(f32)
    act_ref[0] = (gate * activation).astype(bf16)
    act_grad = dot_nn(cot_ref[...], w_ref[0, :, 2 * FF :])
    dots = jnp.sum(activation * act_grad, axis=1, keepdims=True)
    dots_high = dots.astype(bf16).astype(f32)
    lane = lane_iota(count)
    lanes = jnp.where(lane == number, dots_high, 0.0) + jnp.where(
        lane == number + experts, dots - dots_high, 0.0
    )
    act_grad = gate * act_grad
    inner_grad_ref[0, :, :FF] = (
        act_grad * up_part * gate_sigmoid * (1.0 + gate_part * (1.0 - gate_sigmoid))
    ).astype(bf16)
    inner_grad_ref[0, :, FF:] = (act_grad * gate_silu).astype(bf16)
    copy_grad = dot_nt(inner_grad_ref[0], w_ref[0, :, : 2 * FF])
    here = pl.ds(pl.multiple_of(chunk * count, count), count)

    @pl.when(index == 0)
    def _():
        sum_ref[here, :] = copy_grad
        dots_sum_ref[here, :] = lanes

    @pl.when(index > 0)
    def _():
        sum_ref[here, :] += copy_grad
        dots_sum_ref[here, :] += lanes

    back_ref[:, :width] = sum_ref[here, :].astype(bf16)
    back_ref[:, width:] = dots_sum_ref[here, :].astype(bf16)


def experts_weights(where_ref, rows_ref, inner_grad_ref, cot_ref, act_ref, grad_ref):
    grad_ref[:, : 2 * FF] = dot_tn(rows_ref[...], inner_grad_ref[0]).astype(jnp.bfloat16)
    grad_ref[:, 2 * FF :] = dot_tn(cot_ref[...], act_ref[0]).astype(jnp.bfloat16)


def home_backward(
    experts,
    parts_ref,
    order_ref,
    cot_ref,
    hidden_ref,
    second_ref,
    gates_ref,
    w_ref,
    att_ref,
    qkv_ref,
    lse_ref,
    normed_ref,
    x_ref,
    cos_ref,
    sin_ref,
    allow_ref,
    grad_ref,
    input_grad_ref,
    mid_ref,
    proj_ref,
):
    f32, bf16 = jnp.float32, jnp.bfloat16
    rows, width = x_ref.shape
    sources = parts_ref.shape[0]
    qkv_width = qkv_ref.shape[1]
    query_width = QUERY_HEADS * HEAD_DIMENSION
    key_width = KEY_VALUE_HEADS * HEAD_DIMENSION
    fold = QUERY_HEADS // KEY_VALUE_HEADS
    score_scale = HEAD_DIMENSION ** (-0.5)
    extra = w_ref[:, qkv_width + width :]
    gains = gain_rows(extra, experts)
    dots = jnp.zeros((rows, LANES), f32)
    second_grad = jnp.zeros((rows, width), f32)
    for source in range(sources):
        dots = dots + parts_ref[source, :, width:].astype(f32)
        second_grad = second_grad + dot_nn(parts_ref[source, :, :width], order_ref[...])
    dots = dots + pltpu.roll(dots, LANES - experts, 1)
    gates = gates_ref[...]
    logit_grad = (gates * (dots - jnp.sum(gates * dots, axis=1, keepdims=True))).astype(bf16)
    second_grad = second_grad + dot_nt(logit_grad, extra)
    hidden = hidden_ref[...]
    scale = rms_scale(hidden)
    scaled = second_grad * gains[1:2]
    hidden_grad = (
        cot_ref[...].astype(f32)
        + scale * scaled
        - hidden * (scale * scale * scale) * jnp.mean(scaled * hidden, axis=1, keepdims=True)
    )
    branch_grad = hidden_grad.astype(bf16)
    for start in range(0, width, 512):
        grad_ref[:, qkv_width + start : qkv_width + start + 512] = dot_tn(
            branch_grad, att_ref[:, start : start + 512]
        ).astype(bf16)
    small_grad = dot_tn(second_ref[...], logit_grad) + column_sums(
        second_grad * hidden * scale, experts + 1
    )
    mid_ref[...] = dot_nn(branch_grad, w_ref[:, qkv_width : qkv_width + width]).astype(bf16)
    cosine, sine = cos_ref[...], sin_ref[...]
    allowed = allow_ref[...] > 0.0
    lane = lane_iota(rows)
    logs = lse_ref[...]

    def turned_back(values):
        return (values * cosine - swap_halves(values) * sine).astype(bf16)

    key_grads, value_grads = [], []
    for group in range(KEY_VALUE_HEADS):
        keys = qkv_ref[:, query_width + group * HEAD_DIMENSION : query_width + (group + 1) * HEAD_DIMENSION]
        values = qkv_ref[
            :,
            query_width + key_width + group * HEAD_DIMENSION : query_width
            + key_width
            + (group + 1) * HEAD_DIMENSION,
        ]
        query_grads = []
        key_grad = jnp.zeros((rows, HEAD_DIMENSION), f32)
        value_grad = jnp.zeros((rows, HEAD_DIMENSION), f32)
        for head in range(group * fold, (group + 1) * fold):
            queries = qkv_ref[:, head_block(head)]
            mid = mid_ref[:, head_block(head)]
            log_total = jnp.sum(jnp.where(lane == head, logs, 0.0), axis=1, keepdims=True)
            scores = jnp.where(allowed, dot_nt(queries, keys) * score_scale, mask_fill)
            weights = jnp.exp(scores - log_total)
            weight_grad = dot_nt(mid, values)
            delta = jnp.sum(weights * weight_grad, axis=1, keepdims=True)
            score_grad = (weights * (weight_grad - delta)).astype(bf16)
            query_grads.append(dot_nn(score_grad, keys) * score_scale)
            key_grad = key_grad + dot_tn(score_grad, queries)
            value_grad = value_grad + dot_tn(weights.astype(bf16), mid)
        proj_ref[:, group * LANES : (group + 1) * LANES] = turned_back(
            jnp.concatenate(query_grads, axis=1)
        )
        key_grads.append(key_grad * score_scale)
        value_grads.append(value_grad)
        if group % 2 == 1:
            start = query_width + (group // 2) * LANES
            proj_ref[:, start : start + LANES] = turned_back(
                jnp.concatenate(key_grads[-2:], axis=1)
            )
            start = start + key_width
            proj_ref[:, start : start + LANES] = jnp.concatenate(value_grads[-2:], axis=1).astype(
                bf16
            )
    normed = normed_ref[...]
    for start in range(0, qkv_width, 512):
        grad_ref[:, start : start + 512] = dot_tn(normed, proj_ref[:, start : start + 512]).astype(
            bf16
        )
    normed_grad = dot_nt(proj_ref[...], w_ref[:, :qkv_width])
    x = x_ref[...].astype(f32)
    scale = rms_scale(x)
    scaled = normed_grad * gains[0:1]
    small_grad = small_grad + column_sums(normed_grad * x * scale, experts)
    grad_ref[:, qkv_width + width :] = small_grad.astype(bf16)
    input_grad_ref[...] = (
        hidden_grad
        + scale * scaled
        - x * (scale * scale * scale) * jnp.mean(scaled * x, axis=1, keepdims=True)
    ).astype(bf16)


def whole_call(kernel, outputs, operands, flops, scratch=(), earlier=()):
    operands_read = len(operands)

    def run(*refs):
        kernel(*refs[:operands_read], *refs[operands_read + len(earlier) :])

    moved = sum(math.prod(item.shape) * item.dtype.itemsize for item in list(outputs) + list(operands))
    return pl.pallas_call(
        run,
        out_shape=outputs,
        in_specs=[pl.BlockSpec(memory_space=pltpu.VMEM)] * len(operands)
        + [pl.BlockSpec(memory_space=pl.ANY)] * len(earlier),
        out_specs=[pl.BlockSpec(memory_space=pltpu.VMEM)] * len(outputs),
        scratch_shapes=list(scratch),
        compiler_params=pltpu.CompilerParams(vmem_limit_bytes=VMEM_BYTES),
        cost_estimate=pl.CostEstimate(flops=flops, bytes_accessed=moved, transcendentals=0),
    )(*operands, *earlier)


def order_of(kind, sizes):
    axes = {"home": (0, 1, 2, 3, 4), "dense": (2, 1, 3, 0, 4), "expert": (1, 2, 0, 3, 4)}[kind]
    return np.arange(math.prod(sizes), dtype=np.int32).reshape(sizes).transpose(axes).reshape(-1)


def reorder_matrix(before, after):
    return (jnp.asarray(before)[:, None] == jnp.asarray(after)[None, :]).astype(jnp.bfloat16)


def exchange(values, axes):
    return lax.all_to_all(values, axes, split_axis=0, concat_axis=0, tiled=True)


def spread(values, axes):
    count = lax.axis_size(axes)
    copies = exchange(jnp.broadcast_to(values[None], (count,) + values.shape), axes)
    return copies.reshape((count * values.shape[0],) + values.shape[1:])


def collect(values, axes):
    count = lax.axis_size(axes)
    parts = exchange(values.reshape((count, values.shape[0] // count) + values.shape[1:]), axes)
    total = parts[0].astype(jnp.float32)
    for index in range(1, count):
        total = total + parts[index].astype(jnp.float32)
    return total


def partner(values, axes, step):
    names = (axes,) if isinstance(axes, str) else axes
    steps = {}
    for name in reversed(names):
        step, steps[name] = divmod(step, lax.axis_size(name))
    names = tuple(name for name in MESH_AXES if name in names)
    flat = 0
    for name in names:
        flat = flat * lax.axis_size(name) + steps[name]
    pairs = [(index, index ^ flat) for index in range(lax.axis_size(names))]
    return lax.ppermute(values, names, pairs)


def piece_of(values, index):
    return lax.dynamic_index_in_dim(values, index, 0, keepdims=False)


def in_order(own, received, me):
    result = jnp.zeros((len(received) + 1,) + own.shape, own.dtype)
    for step, part in enumerate([own] + received):
        result = lax.dynamic_update_index_in_dim(result, part, me ^ step, 0)
    return result


def spread_aside(values, axes):
    count = lax.axis_size(axes)
    received = [partner(values, axes, step) for step in range(1, count)]
    result = in_order(values, received, lax.axis_index(axes))
    return result.reshape((count * values.shape[0],) + values.shape[1:])


def exchange_aside(values, axes):
    me = lax.axis_index(axes)
    received = [
        partner(piece_of(values, me ^ step), axes, step) for step in range(1, values.shape[0])
    ]
    return in_order(piece_of(values, me), received, me)


def collect_aside(values, axes):
    me = lax.axis_index(axes)
    count = lax.axis_size(axes)
    values = values.reshape((count, values.shape[0] // count) + values.shape[1:])
    total = piece_of(values, me).astype(jnp.float32)
    for step in range(1, count):
        total = total + partner(piece_of(values, me ^ step), axes, step).astype(jnp.float32)
    return total


def expert_specs(n_e, group_rows, width):
    count = min(256, group_rows)
    return dict(
        grid=(n_e, group_rows // count),
        scalar=pl.BlockSpec(memory_space=pltpu.SMEM),
        wide=pl.BlockSpec((count, width), lambda k, i: (i, 0)),
        wider=pl.BlockSpec((count, width + LANES), lambda k, i: (i, 0)),
        lanes=pl.BlockSpec((count, LANES), lambda k, i: (i, width // LANES)),
        weight=pl.BlockSpec((1, width, 3 * FF), lambda k, i: (k, 0, 0)),
        inner=pl.BlockSpec((1, count, 2 * FF), lambda k, i: (k, i, 0)),
        act=pl.BlockSpec((1, count, FF), lambda k, i: (k, i, 0)),
    )


def run_forward(place, arrived, expert_full, experts, local_count):
    n_e, width, _ = expert_full.shape
    group_rows = arrived.shape[0]
    specs = expert_specs(n_e, group_rows, width)
    return pl.pallas_call(
        functools.partial(experts_forward, experts, local_count),
        grid=specs["grid"],
        out_shape=[
            jax.ShapeDtypeStruct((group_rows, width), jnp.bfloat16),
            jax.ShapeDtypeStruct((n_e, group_rows, 2 * FF), jnp.float32),
        ],
        in_specs=[specs["scalar"], specs["wider"], specs["weight"]],
        out_specs=[specs["wide"], specs["inner"]],
        scratch_shapes=[pltpu.VMEM((group_rows, width), jnp.float32)],
        compiler_params=pltpu.CompilerParams(vmem_limit_bytes=VMEM_BYTES),
        cost_estimate=pl.CostEstimate(
            flops=2 * n_e * group_rows * width * 3 * FF,
            bytes_accessed=n_e * width * (3 * FF * 2 + group_rows * 8),
            transcendentals=n_e * group_rows * FF,
        ),
    )(place, arrived, expert_full)


def run_backward(place, arrived, cot_group, expert_full, inner, experts, local_count):
    bf16 = jnp.bfloat16
    n_e, width, _ = expert_full.shape
    group_rows = arrived.shape[0]
    specs = expert_specs(n_e, group_rows, width)
    return pl.pallas_call(
        functools.partial(experts_backward, experts, local_count),
        grid=specs["grid"],
        out_shape=[
            jax.ShapeDtypeStruct((group_rows, width + LANES), bf16),
            jax.ShapeDtypeStruct((n_e, group_rows, 2 * FF), bf16),
            jax.ShapeDtypeStruct((n_e, group_rows, FF), bf16),
        ],
        in_specs=[
            specs["scalar"],
            specs["lanes"],
            specs["wide"],
            specs["weight"],
            specs["inner"],
        ],
        out_specs=[specs["wider"], specs["inner"], specs["act"]],
        scratch_shapes=[
            pltpu.VMEM((group_rows, width), jnp.float32),
            pltpu.VMEM((group_rows, LANES), jnp.float32),
        ],
        compiler_params=pltpu.CompilerParams(vmem_limit_bytes=VMEM_BYTES),
        cost_estimate=pl.CostEstimate(
            flops=2 * n_e * group_rows * width * 3 * FF,
            bytes_accessed=n_e * width * (3 * FF * 2 + group_rows * 10),
            transcendentals=n_e * group_rows * FF,
        ),
    )(place, arrived, cot_group, expert_full, inner)


def run_weights(arrived, inner_grad, cot_group, act, slot, first, blocks, part):
    group_rows = arrived.shape[0]
    where = jnp.stack([slot, first]).astype(jnp.int32)
    return pl.pallas_call(
        experts_weights,
        grid_spec=pltpu.PrefetchScalarGridSpec(
            num_scalar_prefetch=1,
            grid=(blocks,),
            in_specs=[
                pl.BlockSpec((group_rows, part), lambda j, at: (0, at[1] + j)),
                pl.BlockSpec((1, group_rows, 2 * FF), lambda j, at: (at[0], 0, 0)),
                pl.BlockSpec((group_rows, part), lambda j, at: (0, at[1] + j)),
                pl.BlockSpec((1, group_rows, FF), lambda j, at: (at[0], 0, 0)),
            ],
            out_specs=pl.BlockSpec((part, 3 * FF), lambda j, at: (j, 0)),
        ),
        out_shape=jax.ShapeDtypeStruct((blocks * part, 3 * FF), jnp.bfloat16),
        compiler_params=pltpu.CompilerParams(vmem_limit_bytes=VMEM_BYTES),
        cost_estimate=pl.CostEstimate(
            flops=2 * blocks * part * group_rows * 3 * FF,
            bytes_accessed=group_rows * 6 * FF + blocks * part * (group_rows * 4 + 6 * FF),
            transcendentals=0,
        ),
    )(where, arrived, inner_grad, cot_group, act)


def in_pieces(n_e, n_r, width):
    return n_e * n_r <= 8 and width // n_r % min(256, width) == 0


def weight_grads(arrived, inner_grad, cot_group, act, n_e, n_r):
    width = cot_group.shape[1]
    part = min(256, width)
    factors = (arrived, inner_grad, cot_group, act)
    if in_pieces(n_e, n_r, width):
        me = lax.axis_index(("exp", "r"))
        blocks = width // n_r // part
        grads = []
        for step in reversed(range(n_e * n_r)):
            goal = me ^ step
            grads.append(run_weights(*factors, goal // n_r, goal % n_r * blocks, blocks, part))
        return grads[::-1]
    blocks = width // part
    return [
        run_weights(*factors, jnp.int32(slot), jnp.int32(0), blocks, part) for slot in range(n_e)
    ]


def reduce_experts(grads, n_e, n_r, width):
    axes = ("exp", "r")
    if not in_pieces(n_e, n_r, width):
        return collect(jnp.concatenate(grads, axis=0), axes)
    total = grads[0].astype(jnp.float32)
    for step in reversed(range(1, len(grads))):
        total = total + partner(grads[step], axes, step).astype(jnp.float32)
    return total


def body(
    tokens,
    cotangent,
    doc_lengths,
    routes,
    qkv_weight,
    qkv_mean,
    qkv_square,
    out_weight,
    out_mean,
    out_square,
    router_weight,
    router_mean,
    router_square,
    norm_gains,
    gains_mean,
    gains_square,
    in_weight,
    in_mean,
    in_square,
    down_weight,
    down_mean,
    down_square,
):
    f32, bf16 = jnp.float32, jnp.bfloat16
    shape = jax.ShapeDtypeStruct
    n_a, n_r, n_c, n_e = (lax.axis_size(name) for name in ("a", "r", "core", "exp"))
    rows, width = tokens.shape
    experts = router_weight.shape[1]
    local_count = in_weight.shape[0]
    sizes = (n_a, n_r, n_c, n_e, width // (n_a * n_r * n_c * n_e))
    home, dense, expert = (order_of(kind, sizes) for kind in ("home", "dense", "expert"))
    query_width = QUERY_HEADS * HEAD_DIMENSION
    qkv_width = query_width + 2 * KEY_VALUE_HEADS * HEAD_DIMENSION

    local_rows = qkv_weight.shape[0]
    extra = jnp.zeros((local_rows, LANES - experts - 2), bf16)
    pack = jnp.concatenate(
        [
            qkv_weight.astype(bf16),
            out_weight.astype(bf16),
            router_weight.astype(bf16),
            norm_gains.astype(bf16),
            extra,
        ],
        axis=1,
    )
    pack = spread(pack, "a")
    cot_expert = dot_nn(cotangent, reorder_matrix(home, expert)).astype(bf16)
    expert_pack = jnp.concatenate([in_weight.astype(bf16), down_weight.astype(bf16)], axis=2)
    pack, expert_pack = lax.optimization_barrier((pack, expert_pack))
    expert_pack = exchange_aside(expert_pack, ("core", "a"))
    cot_expert, expert_pack = lax.optimization_barrier((cot_expert, expert_pack))
    cot_group = spread_aside(spread_aside(cot_expert, "a"), "core")
    expert_full = lax.all_gather(expert_pack, ("exp", "r"), axis=0, tiled=True).reshape(
        n_e, width, 3 * FF
    )
    dense_full = spread(spread(pack, ("r", "exp")), "core")

    to_dense = reorder_matrix(home, dense)
    x_dense = dot_nn(tokens, to_dense).astype(bf16)
    cot_dense = dot_nn(cotangent, to_dense).astype(bf16)
    positions, segment = doc_layout(doc_lengths.reshape(-1), rows)
    cosine, sine = rope_tables(positions, HEAD_DIMENSION)
    repeat = LANES // HEAD_DIMENSION
    cosine = jnp.concatenate([cosine, cosine] * repeat, axis=1)
    sine = jnp.concatenate([-sine, sine] * repeat, axis=1)
    row_index = jnp.arange(rows, dtype=jnp.int32)
    allowed = (segment[:, None] == segment[None, :]) & (row_index[None, :] <= row_index[:, None])
    allowed = allowed.astype(f32)
    used = jnp.any(
        routes[:, :, None] == jnp.arange(LANES, dtype=jnp.int32)[None, None, :], axis=1
    ).astype(f32)
    hidden, normed, qkv, logs, attended, second, gates, sent = whole_call(
        functools.partial(attention_forward, experts, n_a),
        [
            shape((rows, width), f32),
            shape((rows, width), bf16),
            shape((rows, qkv_width), bf16),
            shape((rows, LANES), f32),
            shape((rows, query_width), bf16),
            shape((rows, width), bf16),
            shape((rows, LANES), f32),
            shape((n_a, rows, width + LANES), bf16),
        ],
        [x_dense, dense_full, cosine, sine, allowed, used, reorder_matrix(dense, expert)],
        flops=2 * rows * width * (qkv_width + 2 * width + 2 * rows),
    )

    arrived = exchange(sent, "a").reshape(n_a * rows, width + LANES)
    arrived = spread(arrived, "core")
    place = (lax.axis_index("core") * n_a + lax.axis_index("a")).astype(jnp.int32).reshape(1)
    out, inner = run_forward(place, arrived, expert_full, experts, local_count)
    back, inner_grad, activation = run_backward(
        place, arrived, cot_group, expert_full, inner, experts, local_count
    )
    back = exchange(collect(back, "core").astype(bf16).reshape(n_a, rows, width + LANES), "a")
    out = collect_aside(out, "core").astype(bf16).reshape(n_a, rows, width)
    back, out = lax.optimization_barrier((back, out))
    out = exchange_aside(out, "a")

    expert_grads = weight_grads(arrived, inner_grad, cot_group, activation, n_e, n_r)
    expert_grad = reduce_experts(expert_grads, n_e, n_r, width).astype(bf16)
    expert_grad = expert_grad.reshape(n_c * n_a, width // (n_r * n_c * n_a), 3 * FF)

    from_expert = reorder_matrix(expert, dense)
    dense_grad, input_grad = whole_call(
        functools.partial(home_backward, experts),
        [shape((width, qkv_width + width + LANES), bf16), shape((rows, width), bf16)],
        [
            back,
            from_expert,
            cot_dense,
            hidden,
            second,
            gates,
            dense_full,
            attended,
            qkv,
            logs,
            normed,
            x_dense,
            cosine,
            sine,
            allowed,
        ],
        earlier=expert_grads,
        flops=2 * rows * width * (n_a * width + 2 * qkv_width + 2 * width + 4 * rows),
        scratch=[pltpu.VMEM((rows, query_width), bf16), pltpu.VMEM((rows, qkv_width), bf16)],
    )
    dense_grad = collect(dense_grad, "core").astype(bf16)
    dense_grad, expert_grad, out = lax.optimization_barrier((dense_grad, expert_grad, out))
    expert_grad = exchange_aside(expert_grad, ("core", "a")).astype(f32)
    d_in = expert_grad[:, :, : 2 * FF]
    d_down = expert_grad[:, :, 2 * FF :]
    dense_total = collect(collect(dense_grad, ("r", "exp")).astype(bf16), "a")

    from_dense = reorder_matrix(dense, home)
    mixed = dot_nn(out[0], from_expert)
    for index in range(1, n_a):
        mixed = mixed + dot_nn(out[index], from_expert)
    block_out = dot_nn((hidden + mixed).astype(bf16), from_dense).astype(bf16)
    input_grad = dot_nn(input_grad, from_dense).astype(bf16)
    d_qkv = dense_total[:, :qkv_width]
    d_out = dense_total[:, qkv_width : qkv_width + query_width]
    small_total = dense_total[:, qkv_width + query_width :]
    d_router = small_total[:, :experts]
    d_gains = small_total[:, experts : experts + 2]
    new_qkv, new_qkv_mean, new_qkv_square = adamw(
        qkv_weight, d_qkv, qkv_mean, qkv_square, 0.15, decay_rate
    )
    new_out, new_out_mean, new_out_square = adamw(
        out_weight, d_out, out_mean, out_square, 0.3, decay_rate
    )
    new_router, new_router_mean, new_router_square = adamw(
        router_weight, d_router, router_mean, router_square, 0.05, decay_rate
    )
    new_gains, new_gains_mean, new_gains_square = adamw(
        norm_gains, d_gains, gains_mean, gains_square, 0.8, 0.0
    )
    new_in, new_in_mean, new_in_square = adamw(in_weight, d_in, in_mean, in_square, 0.1, decay_rate)
    new_down, new_down_mean, new_down_square = adamw(
        down_weight, d_down, down_mean, down_square, 1.0, decay_rate
    )
    return (
        block_out,
        input_grad,
        new_qkv,
        new_qkv_mean,
        new_qkv_square,
        new_out,
        new_out_mean,
        new_out_square,
        new_router,
        new_router_mean,
        new_router_square,
        new_gains,
        new_gains_mean,
        new_gains_square,
        new_in,
        new_in_mean,
        new_in_square,
        new_down,
        new_down_mean,
        new_down_square,
    )


def solution(mesh):
    n_dp, n_exp = mesh.shape["dp"], mesh.shape["exp"]
    n_a = EXPERTS // n_exp // 2
    mesh = Mesh(
        mesh.devices.reshape(n_a, n_dp // (2 * n_a), 2, n_exp), MESH_AXES
    )
    placed = (
        P(("a", "r", "core", "exp"), None),
        P(("a", "r", "core", "exp"), None),
        P(("a", "r", "core", "exp"), None),
        P(("a", "r", "core", "exp"), None),
        P(("a", "r", "core", "exp"), None),
        P(("a", "r", "core", "exp"), None),
        P(("a", "r", "core", "exp"), None),
        P(("a", "r", "core", "exp"), None),
        P(("a", "r", "core", "exp"), None),
        P(("a", "r", "core", "exp"), None),
        P(("a", "r", "core", "exp"), None),
        P(("a", "r", "core", "exp"), None),
        P(("a", "r", "core", "exp"), None),
        P(("a", "r", "core", "exp"), None),
        P(("a", "r", "core", "exp"), None),
        P(("a", "r", "core", "exp"), None),
        P("exp", ("a", "r", "core"), None),
        P("exp", ("a", "r", "core"), None),
        P("exp", ("a", "r", "core"), None),
        P("exp", ("a", "r", "core"), None),
        P("exp", ("a", "r", "core"), None),
        P("exp", ("a", "r", "core"), None),
    )
    return jax.shard_map(
        body,
        mesh=mesh,
        in_specs=placed,
        out_specs=(
            P(("a", "r", "core", "exp"), None),
            P(("a", "r", "core", "exp"), None),
            P(("a", "r", "core", "exp"), None),
            P(("a", "r", "core", "exp"), None),
            P(("a", "r", "core", "exp"), None),
            P(("a", "r", "core", "exp"), None),
            P(("a", "r", "core", "exp"), None),
            P(("a", "r", "core", "exp"), None),
            P(("a", "r", "core", "exp"), None),
            P(("a", "r", "core", "exp"), None),
            P(("a", "r", "core", "exp"), None),
            P(("a", "r", "core", "exp"), None),
            P(("a", "r", "core", "exp"), None),
            P(("a", "r", "core", "exp"), None),
            P("exp", ("a", "r", "core"), None),
            P("exp", ("a", "r", "core"), None),
            P("exp", ("a", "r", "core"), None),
            P("exp", ("a", "r", "core"), None),
            P("exp", ("a", "r", "core"), None),
            P("exp", ("a", "r", "core"), None),
        ),
        check_vma=False,
    )
```

```python
import functools
import math

import jax
import jax.numpy as jnp
import numpy as np
from jax import lax
from jax.experimental import pallas as pl
from jax.experimental.pallas import tpu as pltpu
from jax.sharding import Mesh
from jax.sharding import PartitionSpec as P

QUERY_HEADS = 16
KEY_VALUE_HEADS = 8
HEAD_DIMENSION = 64
FF = 512
STEP = 10
EXPERTS = 16
LANES = 128
MESH_AXES = ("a", "r", "core", "exp")
VMEM_BYTES = 48 * 1024 * 1024


norm_eps = 1e-06
rope_base = 10000.0
mask_fill = -1e30
beta_one = 0.9
beta_two = 0.95
adam_eps = 1e-08
decay_rate = 0.1


def rms_scale(values):
    return lax.rsqrt(jnp.mean(values * values, axis=-1, keepdims=True) + norm_eps)


def doc_layout(doc_lens, sequence_length):
    row_index = jnp.arange(sequence_length, dtype=jnp.int32)
    doc_ends = jnp.cumsum(doc_lens, dtype=jnp.int32)
    passed = (row_index[:, None] >= doc_ends[None, :]).astype(jnp.int32)
    segment = jnp.sum(passed, axis=1, dtype=jnp.int32)
    starts = jnp.sum(passed * doc_lens[None, :], axis=1, dtype=jnp.int32)
    return ((row_index - starts).astype(jnp.float32), segment)


def rope_tables(positions, head_size):
    half_size = head_size // 2
    freq_index = jnp.arange(half_size, dtype=jnp.float32)
    inverse = jnp.exp(freq_index * (-2.0 * math.log(rope_base) / head_size))
    angles = positions[:, None] * inverse[None, :]
    return (jnp.cos(angles), jnp.sin(angles))


def adamw(weight, gradient, mean_old, square_old, step_rate, weight_decay):
    mean_new = beta_one * mean_old + (1.0 - beta_one) * gradient
    square_new = beta_two * square_old + (1.0 - beta_two) * gradient * gradient
    corrected = (
        mean_new
        / (1.0 - beta_one**STEP)
        / (jnp.sqrt(square_new / (1.0 - beta_two**STEP)) + adam_eps)
    )
    return (weight - step_rate * (corrected + weight_decay * weight), mean_new, square_new)

def dot_nn(left, right):
    return jnp.dot(left, right, preferred_element_type=jnp.float32)


def dot_nt(left, right):
    return lax.dot_general(left, right, (((1,), (1,)), ((), ())), preferred_element_type=jnp.float32)


def dot_tn(left, right):
    return lax.dot_general(left, right, (((0,), (0,)), ((), ())), preferred_element_type=jnp.float32)


def lane_iota(rows):
    return lax.broadcasted_iota(jnp.int32, (rows, LANES), 1)


def gain_rows(extra, experts):
    row = lax.broadcasted_iota(jnp.int32, (8, LANES), 0)
    pick = (lane_iota(8) == row + experts).astype(jnp.bfloat16)
    return dot_nt(jnp.where(row < 2, pick, jnp.zeros_like(pick)), extra)


def swap_halves(values):
    half = HEAD_DIMENSION // 2
    lower = lane_iota(values.shape[0]) % HEAD_DIMENSION < half
    return jnp.where(lower, pltpu.roll(values, LANES - half, 1), pltpu.roll(values, half, 1))


def column_sums(values, lane):
    high = values.astype(jnp.bfloat16)
    low = (values - high.astype(jnp.float32)).astype(jnp.bfloat16)
    place = (lane_iota(values.shape[0]) == lane).astype(jnp.bfloat16)
    return dot_tn(high, place) + dot_tn(low, place)


def head_block(index):
    return slice(index * HEAD_DIMENSION, (index + 1) * HEAD_DIMENSION)


def attention_forward(
    experts,
    copies,
    x_ref,
    w_ref,
    cos_ref,
    sin_ref,
    allow_ref,
    used_ref,
    order_ref,
    wide_ref,
    qkv_ref,
    sent_ref,
):
    f32, bf16 = jnp.float32, jnp.bfloat16
    rows, width = x_ref.shape
    query_width = QUERY_HEADS * HEAD_DIMENSION
    key_width = KEY_VALUE_HEADS * HEAD_DIMENSION
    qkv_width = query_width + 2 * key_width
    extra = w_ref[:, qkv_width + width :]
    gains = gain_rows(extra, experts)
    x = x_ref[...].astype(f32)
    normed = (x * rms_scale(x) * gains[0:1]).astype(bf16)
    cosine, sine = cos_ref[...], sin_ref[...]
    for start in range(0, qkv_width, 512):
        part = dot_nn(normed, w_ref[:, start : start + 512])
        for inner in range(0, 512, LANES):
            piece = part[:, inner : inner + LANES]
            if start + inner < query_width + key_width:
                piece = piece * cosine + swap_halves(piece) * sine
            qkv_ref[:, start + inner : start + inner + LANES] = piece.astype(bf16)
    allowed = allow_ref[...] > 0.0
    lane = lane_iota(rows)
    logs = jnp.zeros((rows, LANES), f32)
    fold = QUERY_HEADS // KEY_VALUE_HEADS
    for group in range(KEY_VALUE_HEADS):
        keys = qkv_ref[:, query_width + group * HEAD_DIMENSION : query_width + (group + 1) * HEAD_DIMENSION]
        values = qkv_ref[
            :,
            query_width + key_width + group * HEAD_DIMENSION : query_width
            + key_width
            + (group + 1) * HEAD_DIMENSION,
        ]
        outs = []
        for head in range(group * fold, (group + 1) * fold):
            scores = dot_nt(qkv_ref[:, head_block(head)], keys) * HEAD_DIMENSION ** (-0.5)
            scores = jnp.where(allowed, scores, mask_fill)
            peak = jnp.max(scores, axis=1, keepdims=True)
            log_total = peak + jnp.log(jnp.sum(jnp.exp(scores - peak), axis=1, keepdims=True))
            logs = jnp.where(lane == head, log_total, logs)
            outs.append(dot_nn(jnp.exp(scores - log_total).astype(bf16), values))
        start = qkv_width + group * LANES
        qkv_ref[:, start : start + LANES] = jnp.concatenate(outs, axis=1).astype(bf16)
    wide_ref[:, width : width + LANES] = logs
    hidden = x + dot_nt(qkv_ref[:, qkv_width:], w_ref[:, qkv_width : qkv_width + width])
    wide_ref[:, :width] = hidden
    second = (hidden * rms_scale(hidden) * gains[1:2]).astype(bf16)
    used = used_ref[...] > 0.0
    logits = jnp.where(used, dot_nn(second, extra), mask_fill)
    powers = jnp.where(used, jnp.exp(logits - jnp.max(logits, axis=1, keepdims=True)), 0.0)
    gates = powers / jnp.sum(powers, axis=1, keepdims=True)
    wide_ref[:, width + LANES :] = gates
    high = gates.astype(bf16).astype(f32)
    lanes = (high + pltpu.roll(gates - high, experts, 1)).astype(bf16)
    moved = dot_nn(second, order_ref[...]).astype(bf16)
    for copy in range(copies):
        sent_ref[copy, :, :width] = moved
        sent_ref[copy, :, width:] = lanes


def own_gate(lanes, number, experts):
    lane = lane_iota(lanes.shape[0])
    chosen = (lane == number) | (lane == number + experts)
    return jnp.sum(jnp.where(chosen, lanes.astype(jnp.float32), 0.0), axis=1, keepdims=True)


def experts_forward(
    experts, local_count, place_ref, rows_ref, w_ref, out_ref, inner_ref, sum_ref
):
    f32, bf16 = jnp.float32, jnp.bfloat16
    index, chunk = pl.program_id(0), pl.program_id(1)
    count, width = out_ref.shape
    gate = own_gate(rows_ref[:, width:], index * local_count + place_ref[0], experts)
    inner = dot_nn(rows_ref[:, :width], w_ref[0, :, : 2 * FF])
    inner_ref[0] = inner
    gate_part = inner[:, :FF]
    activation = (gate_part * jax.nn.sigmoid(gate_part) * inner[:, FF:]).astype(bf16)
    result = dot_nt(activation, w_ref[0, :, 2 * FF :]).astype(bf16).astype(f32)
    here = pl.ds(pl.multiple_of(chunk * count, count), count)

    @pl.when(index == 0)
    def _():
        sum_ref[here, :] = gate * result

    @pl.when(index > 0)
    def _():
        sum_ref[here, :] += gate * result

    out_ref[...] = sum_ref[here, :].astype(bf16)


def experts_backward(
    experts,
    local_count,
    place_ref,
    gates_ref,
    cot_ref,
    w_ref,
    inner_ref,
    back_ref,
    inner_grad_ref,
    act_ref,
    sum_ref,
    dots_sum_ref,
):
    f32, bf16 = jnp.float32, jnp.bfloat16
    index, chunk = pl.program_id(0), pl.program_id(1)
    count, width = cot_ref.shape
    number = index * local_count + place_ref[0]
    gate = own_gate(gates_ref[...], number, experts)
    gate_part = inner_ref[0, :, :FF]
    up_part = inner_ref[0, :, FF:]
    gate_sigmoid = jax.nn.sigmoid(gate_part)
    gate_silu = gate_part * gate_sigmoid
    activation = (gate_silu * up_part).astype(bf16).astype(f32)
    act_ref[0] = (gate * activation).astype(bf16)
    act_grad = dot_nn(cot_ref[...], w_ref[0, :, 2 * FF :])
    dots = jnp.sum(activation * act_grad, axis=1, keepdims=True)
    dots_high = dots.astype(bf16).astype(f32)
    lane = lane_iota(count)
    lanes = jnp.where(lane == number, dots_high, 0.0) + jnp.where(
        lane == number + experts, dots - dots_high, 0.0
    )
    act_grad = gate * act_grad
    inner_grad_ref[0, :, :FF] = (
        act_grad * up_part * gate_sigmoid * (1.0 + gate_part * (1.0 - gate_sigmoid))
    ).astype(bf16)
    inner_grad_ref[0, :, FF:] = (act_grad * gate_silu).astype(bf16)
    copy_grad = dot_nt(inner_grad_ref[0], w_ref[0, :, : 2 * FF])
    here = pl.ds(pl.multiple_of(chunk * count, count), count)

    @pl.when(index == 0)
    def _():
        sum_ref[here, :] = copy_grad
        dots_sum_ref[here, :] = lanes

    @pl.when(index > 0)
    def _():
        sum_ref[here, :] += copy_grad
        dots_sum_ref[here, :] += lanes

    back_ref[:, :width] = sum_ref[here, :].astype(bf16)
    back_ref[:, width:] = dots_sum_ref[here, :].astype(bf16)


def experts_weights(where_ref, rows_ref, inner_grad_ref, cot_ref, act_ref, grad_ref):
    grad_ref[:, : 2 * FF] = dot_tn(rows_ref[...], inner_grad_ref[0]).astype(jnp.bfloat16)
    grad_ref[:, 2 * FF :] = dot_tn(cot_ref[...], act_ref[0]).astype(jnp.bfloat16)


def home_backward(
    experts,
    parts_ref,
    order_ref,
    cot_ref,
    wide_ref,
    w_ref,
    qkv_ref,
    x_ref,
    cos_ref,
    sin_ref,
    allow_ref,
    grad_ref,
    input_grad_ref,
    mid_ref,
    proj_ref,
):
    f32, bf16 = jnp.float32, jnp.bfloat16
    rows, width = x_ref.shape
    sources = parts_ref.shape[0]
    query_width = QUERY_HEADS * HEAD_DIMENSION
    key_width = KEY_VALUE_HEADS * HEAD_DIMENSION
    qkv_width = query_width + 2 * key_width
    fold = QUERY_HEADS // KEY_VALUE_HEADS
    score_scale = HEAD_DIMENSION ** (-0.5)
    extra = w_ref[:, qkv_width + width :]
    gains = gain_rows(extra, experts)
    dots = jnp.zeros((rows, LANES), f32)
    second_grad = jnp.zeros((rows, width), f32)
    for source in range(sources):
        dots = dots + parts_ref[source, :, width:].astype(f32)
        second_grad = second_grad + dot_nn(parts_ref[source, :, :width], order_ref[...])
    dots = dots + pltpu.roll(dots, LANES - experts, 1)
    gates = wide_ref[:, width + LANES :]
    logit_grad = (gates * (dots - jnp.sum(gates * dots, axis=1, keepdims=True))).astype(bf16)
    second_grad = second_grad + dot_nt(logit_grad, extra)
    hidden = wide_ref[:, :width]
    scale = rms_scale(hidden)
    second = (hidden * scale * gains[1:2]).astype(bf16)
    scaled = second_grad * gains[1:2]
    hidden_grad = (
        cot_ref[...].astype(f32)
        + scale * scaled
        - hidden * (scale * scale * scale) * jnp.mean(scaled * hidden, axis=1, keepdims=True)
    )
    branch_grad = hidden_grad.astype(bf16)
    for start in range(0, width, 512):
        grad_ref[:, qkv_width + start : qkv_width + start + 512] = dot_tn(
            branch_grad, qkv_ref[:, qkv_width + start : qkv_width + start + 512]
        ).astype(bf16)
    small_grad = dot_tn(second, logit_grad) + column_sums(
        second_grad * hidden * scale, experts + 1
    )
    mid_ref[...] = dot_nn(branch_grad, w_ref[:, qkv_width : qkv_width + width]).astype(bf16)
    cosine, sine = cos_ref[...], sin_ref[...]
    allowed = allow_ref[...] > 0.0
    lane = lane_iota(rows)
    logs = wide_ref[:, width : width + LANES]

    def turned_back(values):
        return (values * cosine - swap_halves(values) * sine).astype(bf16)

    key_grads, value_grads = [], []
    for group in range(KEY_VALUE_HEADS):
        keys = qkv_ref[:, query_width + group * HEAD_DIMENSION : query_width + (group + 1) * HEAD_DIMENSION]
        values = qkv_ref[
            :,
            query_width + key_width + group * HEAD_DIMENSION : query_width
            + key_width
            + (group + 1) * HEAD_DIMENSION,
        ]
        query_grads = []
        key_grad = jnp.zeros((rows, HEAD_DIMENSION), f32)
        value_grad = jnp.zeros((rows, HEAD_DIMENSION), f32)
        for head in range(group * fold, (group + 1) * fold):
            queries = qkv_ref[:, head_block(head)]
            mid = mid_ref[:, head_block(head)]
            log_total = jnp.sum(jnp.where(lane == head, logs, 0.0), axis=1, keepdims=True)
            scores = jnp.where(allowed, dot_nt(queries, keys) * score_scale, mask_fill)
            weights = jnp.exp(scores - log_total)
            weight_grad = dot_nt(mid, values)
            delta = jnp.sum(weights * weight_grad, axis=1, keepdims=True)
            score_grad = (weights * (weight_grad - delta)).astype(bf16)
            query_grads.append(dot_nn(score_grad, keys) * score_scale)
            key_grad = key_grad + dot_tn(score_grad, queries)
            value_grad = value_grad + dot_tn(weights.astype(bf16), mid)
        proj_ref[:, group * LANES : (group + 1) * LANES] = turned_back(
            jnp.concatenate(query_grads, axis=1)
        )
        key_grads.append(key_grad * score_scale)
        value_grads.append(value_grad)
        if group % 2 == 1:
            start = query_width + (group // 2) * LANES
            proj_ref[:, start : start + LANES] = turned_back(
                jnp.concatenate(key_grads[-2:], axis=1)
            )
            start = start + key_width
            proj_ref[:, start : start + LANES] = jnp.concatenate(value_grads[-2:], axis=1).astype(
                bf16
            )
    x = x_ref[...].astype(f32)
    scale = rms_scale(x)
    normed = (x * scale * gains[0:1]).astype(bf16)
    for start in range(0, qkv_width, 512):
        grad_ref[:, start : start + 512] = dot_tn(normed, proj_ref[:, start : start + 512]).astype(
            bf16
        )
    normed_grad = dot_nt(proj_ref[...], w_ref[:, :qkv_width])
    scaled = normed_grad * gains[0:1]
    small_grad = small_grad + column_sums(normed_grad * x * scale, experts)
    grad_ref[:, qkv_width + width :] = small_grad.astype(bf16)
    input_grad_ref[...] = (
        hidden_grad
        + scale * scaled
        - x * (scale * scale * scale) * jnp.mean(scaled * x, axis=1, keepdims=True)
    ).astype(bf16)


def dense_update(parts_ref, *refs):
    total = parts_ref[0].astype(jnp.float32)
    for source in range(1, parts_ref.shape[0]):
        total = total + parts_ref[source].astype(jnp.float32)
    start = 0
    rates = ((0.15, decay_rate), (0.3, decay_rate), (0.05, decay_rate), (0.8, 0.0))
    for index, (rate, decay) in enumerate(rates):
        weight_ref, mean_ref, square_ref = refs[3 * index : 3 * index + 3]
        columns = weight_ref.shape[1]
        values = adamw(
            weight_ref[...],
            total[:, start : start + columns],
            mean_ref[...],
            square_ref[...],
            rate,
            decay,
        )
        for out_ref, value in zip(refs[3 * index + 12 : 3 * index + 15], values):
            out_ref[...] = value
        start += columns


def whole_call(kernel, outputs, operands, flops, scratch=(), earlier=()):
    operands_read = len(operands)

    def run(*refs):
        kernel(*refs[:operands_read], *refs[operands_read + len(earlier) :])

    moved = sum(math.prod(item.shape) * item.dtype.itemsize for item in list(outputs) + list(operands))
    moved = moved if flops > 1 else 1
    return pl.pallas_call(
        run,
        out_shape=outputs,
        in_specs=[pl.BlockSpec(memory_space=pltpu.VMEM)] * len(operands)
        + [pl.BlockSpec(memory_space=pl.ANY)] * len(earlier),
        out_specs=[pl.BlockSpec(memory_space=pltpu.VMEM)] * len(outputs),
        scratch_shapes=list(scratch),
        compiler_params=pltpu.CompilerParams(vmem_limit_bytes=VMEM_BYTES),
        cost_estimate=pl.CostEstimate(flops=flops, bytes_accessed=moved, transcendentals=0),
    )(*operands, *earlier)


def order_of(kind, sizes):
    axes = {"home": (0, 1, 2, 3, 4), "dense": (2, 1, 3, 0, 4), "expert": (1, 2, 0, 3, 4)}[kind]
    return np.arange(math.prod(sizes), dtype=np.int32).reshape(sizes).transpose(axes).reshape(-1)


def reorder_matrix(before, after):
    return (jnp.asarray(before)[:, None] == jnp.asarray(after)[None, :]).astype(jnp.bfloat16)


def exchange(values, axes):
    return lax.all_to_all(values, axes, split_axis=0, concat_axis=0, tiled=True)


def spread(values, axes):
    count = lax.axis_size(axes)
    copies = exchange(jnp.broadcast_to(values[None], (count,) + values.shape), axes)
    return copies.reshape((count * values.shape[0],) + values.shape[1:])


def collect(values, axes):
    count = lax.axis_size(axes)
    parts = exchange(values.reshape((count, values.shape[0] // count) + values.shape[1:]), axes)
    total = parts[0].astype(jnp.float32)
    for index in range(1, count):
        total = total + parts[index].astype(jnp.float32)
    return total


def partner(values, axes, step):
    names = (axes,) if isinstance(axes, str) else axes
    steps = {}
    for name in reversed(names):
        step, steps[name] = divmod(step, lax.axis_size(name))
    names = tuple(name for name in MESH_AXES if name in names)
    flat = 0
    for name in names:
        flat = flat * lax.axis_size(name) + steps[name]
    pairs = [(index, index ^ flat) for index in range(lax.axis_size(names))]
    return lax.ppermute(values, names, pairs)


def piece_of(values, index):
    return lax.dynamic_index_in_dim(values, index, 0, keepdims=False)


def in_order(own, received, me):
    result = jnp.zeros((len(received) + 1,) + own.shape, own.dtype)
    for step, part in enumerate([own] + received):
        result = lax.dynamic_update_index_in_dim(result, part, me ^ step, 0)
    return result


def spread_aside(values, axes):
    count = lax.axis_size(axes)
    received = [partner(values, axes, step) for step in range(1, count)]
    result = in_order(values, received, lax.axis_index(axes))
    return result.reshape((count * values.shape[0],) + values.shape[1:])


def exchange_aside(values, axes):
    me = lax.axis_index(axes)
    received = [
        partner(piece_of(values, me ^ step), axes, step) for step in range(1, values.shape[0])
    ]
    return in_order(piece_of(values, me), received, me)


def expert_specs(n_e, group_rows, width):
    count = min(256, group_rows)
    return dict(
        grid=(n_e, group_rows // count),
        scalar=pl.BlockSpec(memory_space=pltpu.SMEM),
        wide=pl.BlockSpec((count, width), lambda k, i: (i, 0)),
        wider=pl.BlockSpec((count, width + LANES), lambda k, i: (i, 0)),
        lanes=pl.BlockSpec((count, LANES), lambda k, i: (i, width // LANES)),
        weight=pl.BlockSpec((1, width, 3 * FF), lambda k, i: (k, 0, 0)),
        inner=pl.BlockSpec((1, count, 2 * FF), lambda k, i: (k, i, 0)),
        act=pl.BlockSpec((1, count, FF), lambda k, i: (k, i, 0)),
    )


def run_forward(place, arrived, expert_full, experts, local_count):
    n_e, width, _ = expert_full.shape
    group_rows = arrived.shape[0]
    specs = expert_specs(n_e, group_rows, width)
    return pl.pallas_call(
        functools.partial(experts_forward, experts, local_count),
        grid=specs["grid"],
        out_shape=[
            jax.ShapeDtypeStruct((group_rows, width), jnp.bfloat16),
            jax.ShapeDtypeStruct((n_e, group_rows, 2 * FF), jnp.float32),
        ],
        in_specs=[specs["scalar"], specs["wider"], specs["weight"]],
        out_specs=[specs["wide"], specs["inner"]],
        scratch_shapes=[pltpu.VMEM((group_rows, width), jnp.float32)],
        compiler_params=pltpu.CompilerParams(vmem_limit_bytes=VMEM_BYTES),
        cost_estimate=pl.CostEstimate(
            flops=2 * n_e * group_rows * width * 3 * FF,
            bytes_accessed=n_e * width * (3 * FF * 2 + group_rows * 8),
            transcendentals=n_e * group_rows * FF,
        ),
    )(place, arrived, expert_full)


def run_backward(place, arrived, cot_group, expert_full, inner, experts, local_count):
    bf16 = jnp.bfloat16
    n_e, width, _ = expert_full.shape
    group_rows = arrived.shape[0]
    specs = expert_specs(n_e, group_rows, width)
    return pl.pallas_call(
        functools.partial(experts_backward, experts, local_count),
        grid=specs["grid"],
        out_shape=[
            jax.ShapeDtypeStruct((group_rows, width + LANES), bf16),
            jax.ShapeDtypeStruct((n_e, group_rows, 2 * FF), bf16),
            jax.ShapeDtypeStruct((n_e, group_rows, FF), bf16),
        ],
        in_specs=[
            specs["scalar"],
            specs["lanes"],
            specs["wide"],
            specs["weight"],
            specs["inner"],
        ],
        out_specs=[specs["wider"], specs["inner"], specs["act"]],
        scratch_shapes=[
            pltpu.VMEM((group_rows, width), jnp.float32),
            pltpu.VMEM((group_rows, LANES), jnp.float32),
        ],
        compiler_params=pltpu.CompilerParams(vmem_limit_bytes=VMEM_BYTES),
        cost_estimate=pl.CostEstimate(
            flops=2 * n_e * group_rows * width * 3 * FF,
            bytes_accessed=n_e * width * (3 * FF * 2 + group_rows * 10),
            transcendentals=n_e * group_rows * FF,
        ),
    )(place, arrived, cot_group, expert_full, inner)


def run_weights(arrived, inner_grad, cot_group, act, slot, first, blocks, part):
    group_rows = arrived.shape[0]
    where = jnp.stack([slot, first]).astype(jnp.int32)
    return pl.pallas_call(
        experts_weights,
        grid_spec=pltpu.PrefetchScalarGridSpec(
            num_scalar_prefetch=1,
            grid=(blocks,),
            in_specs=[
                pl.BlockSpec((group_rows, part), lambda j, at: (0, at[1] + j)),
                pl.BlockSpec((1, group_rows, 2 * FF), lambda j, at: (at[0], 0, 0)),
                pl.BlockSpec((group_rows, part), lambda j, at: (0, at[1] + j)),
                pl.BlockSpec((1, group_rows, FF), lambda j, at: (at[0], 0, 0)),
            ],
            out_specs=pl.BlockSpec((part, 3 * FF), lambda j, at: (j, 0)),
        ),
        out_shape=jax.ShapeDtypeStruct((blocks * part, 3 * FF), jnp.bfloat16),
        compiler_params=pltpu.CompilerParams(vmem_limit_bytes=VMEM_BYTES),
        cost_estimate=pl.CostEstimate(
            flops=2 * blocks * part * group_rows * 3 * FF,
            bytes_accessed=group_rows * 6 * FF + blocks * part * (group_rows * 4 + 6 * FF),
            transcendentals=0,
        ),
    )(where, arrived, inner_grad, cot_group, act)


def in_pieces(n_e, n_r, width):
    return n_e * n_r <= 8 and width // n_r % min(256, width) == 0


def weight_grads(back, factors, n_e, n_r):
    width = factors[2].shape[1]
    part = min(256, width)
    if in_pieces(n_e, n_r, width):
        me = lax.axis_index(("exp", "r"))
        blocks = width // n_r // part
        grads = []
        for step in reversed(range(n_e * n_r)):
            goal = me ^ step
            grads.append(run_weights(*factors, goal // n_r, goal % n_r * blocks, blocks, part))
            if len(grads) == 1:
                back, me = lax.optimization_barrier((back, me))
        return back, grads[::-1]
    blocks = width // part
    return back, [
        run_weights(*factors, jnp.int32(slot), jnp.int32(0), blocks, part) for slot in range(n_e)
    ]


def send_grads(grads, n_e, n_r, width):
    axes = ("exp", "r")
    if not in_pieces(n_e, n_r, width):
        grads = jnp.concatenate(grads, axis=0)
        return list(exchange(grads.reshape((n_e * n_r, -1) + grads.shape[1:]), axes))
    return [grads[0]] + [
        partner(grads[step], axes, step) for step in reversed(range(1, len(grads)))
    ]


def body(
    tokens,
    cotangent,
    doc_lengths,
    routes,
    qkv_weight,
    qkv_mean,
    qkv_square,
    out_weight,
    out_mean,
    out_square,
    router_weight,
    router_mean,
    router_square,
    norm_gains,
    gains_mean,
    gains_square,
    in_weight,
    in_mean,
    in_square,
    down_weight,
    down_mean,
    down_square,
):
    f32, bf16 = jnp.float32, jnp.bfloat16
    shape = jax.ShapeDtypeStruct
    n_a, n_r, n_c, n_e = (lax.axis_size(name) for name in ("a", "r", "core", "exp"))
    rows, width = tokens.shape
    experts = router_weight.shape[1]
    local_count = in_weight.shape[0]
    sizes = (n_a, n_r, n_c, n_e, width // (n_a * n_r * n_c * n_e))
    home, dense, expert = (order_of(kind, sizes) for kind in ("home", "dense", "expert"))
    query_width = QUERY_HEADS * HEAD_DIMENSION
    qkv_width = query_width + 2 * KEY_VALUE_HEADS * HEAD_DIMENSION

    local_rows = qkv_weight.shape[0]
    extra = jnp.zeros((local_rows, LANES - experts - 2), bf16)
    pack = jnp.concatenate(
        [
            qkv_weight.astype(bf16),
            out_weight.astype(bf16),
            router_weight.astype(bf16),
            norm_gains.astype(bf16),
            extra,
        ],
        axis=1,
    )
    pack = spread(pack, "a")
    cot_expert = dot_nn(cotangent, reorder_matrix(home, expert)).astype(bf16)
    expert_pack = jnp.concatenate([in_weight.astype(bf16), down_weight.astype(bf16)], axis=2)
    pack, expert_pack = lax.optimization_barrier((pack, expert_pack))
    pack = spread(pack, ("r", "exp"))
    expert_pack = exchange_aside(expert_pack, ("core", "a"))
    pack, expert_pack = lax.optimization_barrier((pack, expert_pack))
    cot_expert, expert_pack = lax.optimization_barrier((cot_expert, expert_pack))
    cot_group = spread_aside(spread_aside(cot_expert, "a"), "core")
    expert_full = lax.all_gather(expert_pack, ("exp", "r"), axis=0, tiled=True).reshape(
        n_e, width, 3 * FF
    )
    dense_full = spread(pack, "core")

    to_dense = reorder_matrix(home, dense)
    x_dense = dot_nn(tokens, to_dense).astype(bf16)
    cot_dense = dot_nn(cotangent, to_dense).astype(bf16)
    positions, segment = doc_layout(doc_lengths.reshape(-1), rows)
    cosine, sine = rope_tables(positions, HEAD_DIMENSION)
    repeat = LANES // HEAD_DIMENSION
    cosine = jnp.concatenate([cosine, cosine] * repeat, axis=1)
    sine = jnp.concatenate([-sine, sine] * repeat, axis=1)
    row_index = jnp.arange(rows, dtype=jnp.int32)
    allowed = (segment[:, None] == segment[None, :]) & (row_index[None, :] <= row_index[:, None])
    allowed = allowed.astype(f32)
    used = jnp.any(
        routes[:, :, None] == jnp.arange(LANES, dtype=jnp.int32)[None, None, :], axis=1
    ).astype(f32)
    wide, qkv, sent = whole_call(
        functools.partial(attention_forward, experts, n_a),
        [
            shape((rows, width + 2 * LANES), f32),
            shape((rows, qkv_width + query_width), bf16),
            shape((n_a, rows, width + LANES), bf16),
        ],
        [x_dense, dense_full, cosine, sine, allowed, used, reorder_matrix(dense, expert)],
        flops=2 * rows * width * (qkv_width + 2 * width + 2 * rows),
    )

    arrived = exchange(sent, "a").reshape(n_a * rows, width + LANES)
    arrived = spread(arrived, "core")
    place = (lax.axis_index("core") * n_a + lax.axis_index("a")).astype(jnp.int32).reshape(1)
    out, inner = run_forward(place, arrived, expert_full, experts, local_count)
    back, inner_grad, activation = run_backward(
        place, arrived, cot_group, expert_full, inner, experts, local_count
    )
    back = collect(back, "core").astype(bf16)

    factors = (arrived, inner_grad, cot_group, activation)
    back, expert_grads = weight_grads(back, factors, n_e, n_r)
    back = exchange(back.reshape(n_a, rows, width + LANES), "a")
    back, out = lax.optimization_barrier((back, out))
    out = lax.psum_scatter(out, ("core", "a"), scatter_dimension=0, tiled=True)
    received = send_grads(expert_grads, n_e, n_r, width)

    from_expert = reorder_matrix(expert, dense)
    dense_grad, input_grad = whole_call(
        functools.partial(home_backward, experts),
        [shape((width, qkv_width + width + LANES), bf16), shape((rows, width), bf16)],
        [
            back,
            from_expert,
            cot_dense,
            wide,
            dense_full,
            qkv,
            x_dense,
            cosine,
            sine,
            allowed,
        ],
        earlier=expert_grads,
        flops=1,
        scratch=[pltpu.VMEM((rows, query_width), bf16), pltpu.VMEM((rows, qkv_width), bf16)],
    )
    dense_grad = collect(dense_grad, "core").astype(bf16)
    dense_grad, *received = lax.optimization_barrier((dense_grad, *received))
    expert_grad = received[0].astype(f32)
    for part in received[1:]:
        expert_grad = expert_grad + part.astype(f32)
    expert_grad = expert_grad.astype(bf16).reshape(
        n_c * n_a, width // (n_r * n_c * n_a), 3 * FF
    )
    expert_grad = exchange_aside(expert_grad, ("core", "a")).astype(f32)
    d_in = expert_grad[:, :, : 2 * FF]
    d_down = expert_grad[:, :, 2 * FF :]
    dense_grad = collect(dense_grad, ("r", "exp")).astype(bf16)
    dense_grad = exchange(dense_grad.reshape((n_a, local_rows) + dense_grad.shape[1:]), "a")

    from_dense = reorder_matrix(dense, home)
    mixed = dot_nn(out, from_expert)
    block_out = dot_nn((wide[:, :width] + mixed).astype(bf16), from_dense).astype(bf16)
    input_grad = dot_nn(input_grad, from_dense).astype(bf16)
    dense_state = [
        qkv_weight,
        qkv_mean,
        qkv_square,
        out_weight,
        out_mean,
        out_square,
        router_weight,
        router_mean,
        router_square,
        norm_gains,
        gains_mean,
        gains_square,
    ]
    (
        new_qkv,
        new_qkv_mean,
        new_qkv_square,
        new_out,
        new_out_mean,
        new_out_square,
        new_router,
        new_router_mean,
        new_router_square,
        new_gains,
        new_gains_mean,
        new_gains_square,
    ) = whole_call(
        dense_update,
        [shape(item.shape, f32) for item in dense_state],
        [dense_grad] + dense_state,
        flops=20 * local_rows * (qkv_width + width),
    )
    new_in, new_in_mean, new_in_square = adamw(in_weight, d_in, in_mean, in_square, 0.1, decay_rate)
    new_down, new_down_mean, new_down_square = adamw(
        down_weight, d_down, down_mean, down_square, 1.0, decay_rate
    )
    return (
        block_out,
        input_grad,
        new_qkv,
        new_qkv_mean,
        new_qkv_square,
        new_out,
        new_out_mean,
        new_out_square,
        new_router,
        new_router_mean,
        new_router_square,
        new_gains,
        new_gains_mean,
        new_gains_square,
        new_in,
        new_in_mean,
        new_in_square,
        new_down,
        new_down_mean,
        new_down_square,
    )


def solution(mesh):
    n_dp, n_exp = mesh.shape["dp"], mesh.shape["exp"]
    n_a = EXPERTS // n_exp // 2
    mesh = Mesh(
        mesh.devices.reshape(n_a, n_dp // (2 * n_a), 2, n_exp), MESH_AXES
    )
    placed = (
        P(("a", "r", "core", "exp"), None),
        P(("a", "r", "core", "exp"), None),
        P(("a", "r", "core", "exp"), None),
        P(("a", "r", "core", "exp"), None),
        P(("a", "r", "core", "exp"), None),
        P(("a", "r", "core", "exp"), None),
        P(("a", "r", "core", "exp"), None),
        P(("a", "r", "core", "exp"), None),
        P(("a", "r", "core", "exp"), None),
        P(("a", "r", "core", "exp"), None),
        P(("a", "r", "core", "exp"), None),
        P(("a", "r", "core", "exp"), None),
        P(("a", "r", "core", "exp"), None),
        P(("a", "r", "core", "exp"), None),
        P(("a", "r", "core", "exp"), None),
        P(("a", "r", "core", "exp"), None),
        P("exp", ("a", "r", "core"), None),
        P("exp", ("a", "r", "core"), None),
        P("exp", ("a", "r", "core"), None),
        P("exp", ("a", "r", "core"), None),
        P("exp", ("a", "r", "core"), None),
        P("exp", ("a", "r", "core"), None),
    )
    return jax.shard_map(
        body,
        mesh=mesh,
        in_specs=placed,
        out_specs=(
            P(("a", "r", "core", "exp"), None),
            P(("a", "r", "core", "exp"), None),
            P(("a", "r", "core", "exp"), None),
            P(("a", "r", "core", "exp"), None),
            P(("a", "r", "core", "exp"), None),
            P(("a", "r", "core", "exp"), None),
            P(("a", "r", "core", "exp"), None),
            P(("a", "r", "core", "exp"), None),
            P(("a", "r", "core", "exp"), None),
            P(("a", "r", "core", "exp"), None),
            P(("a", "r", "core", "exp"), None),
            P(("a", "r", "core", "exp"), None),
            P(("a", "r", "core", "exp"), None),
            P(("a", "r", "core", "exp"), None),
            P("exp", ("a", "r", "core"), None),
            P("exp", ("a", "r", "core"), None),
            P("exp", ("a", "r", "core"), None),
            P("exp", ("a", "r", "core"), None),
            P("exp", ("a", "r", "core"), None),
            P("exp", ("a", "r", "core"), None),
        ),
        check_vma=False,
    )
```

```python
import functools
import math

import jax
import jax.numpy as jnp
import numpy as np
from jax import lax
from jax.experimental import pallas as pl
from jax.experimental.pallas import tpu as pltpu
from jax.sharding import Mesh
from jax.sharding import PartitionSpec as P

QUERY_HEADS = 16
KEY_VALUE_HEADS = 8
HEAD_DIMENSION = 64
FF = 512
STEP = 10
EXPERTS = 16
LANES = 128
MESH_AXES = ("a", "r", "core", "exp")
VMEM_BYTES = 26 * 1024 * 1024


norm_eps = 1e-06
rope_base = 10000.0
mask_fill = -1e30
beta_one = 0.9
beta_two = 0.95
adam_eps = 1e-08
decay_rate = 0.1


def rms_scale(values):
    return lax.rsqrt(jnp.mean(values * values, axis=-1, keepdims=True) + norm_eps)


def doc_layout(doc_lens, sequence_length):
    row_index = jnp.arange(sequence_length, dtype=jnp.int32)
    doc_ends = jnp.cumsum(doc_lens, dtype=jnp.int32)
    passed = (row_index[:, None] >= doc_ends[None, :]).astype(jnp.int32)
    segment = jnp.sum(passed, axis=1, dtype=jnp.int32)
    starts = jnp.sum(passed * doc_lens[None, :], axis=1, dtype=jnp.int32)
    return ((row_index - starts).astype(jnp.float32), segment)


def rope_tables(positions, head_size):
    half_size = head_size // 2
    freq_index = jnp.arange(half_size, dtype=jnp.float32)
    inverse = jnp.exp(freq_index * (-2.0 * math.log(rope_base) / head_size))
    angles = positions[:, None] * inverse[None, :]
    return (jnp.cos(angles), jnp.sin(angles))


def adamw(weight, gradient, mean_old, square_old, step_rate, weight_decay):
    mean_new = beta_one * mean_old + (1.0 - beta_one) * gradient
    square_new = beta_two * square_old + (1.0 - beta_two) * gradient * gradient
    corrected = (
        mean_new
        / (1.0 - beta_one**STEP)
        / (jnp.sqrt(square_new / (1.0 - beta_two**STEP)) + adam_eps)
    )
    return (weight - step_rate * (corrected + weight_decay * weight), mean_new, square_new)

def dot_nn(left, right):
    return jnp.dot(left, right, preferred_element_type=jnp.float32)


def dot_nt(left, right):
    return lax.dot_general(left, right, (((1,), (1,)), ((), ())), preferred_element_type=jnp.float32)


def dot_tn(left, right):
    return lax.dot_general(left, right, (((0,), (0,)), ((), ())), preferred_element_type=jnp.float32)


def lane_iota(rows):
    return lax.broadcasted_iota(jnp.int32, (rows, LANES), 1)


def gain_rows(extra, experts):
    row = lax.broadcasted_iota(jnp.int32, (8, LANES), 0)
    pick = (lane_iota(8) == row + experts).astype(jnp.bfloat16)
    return dot_nt(jnp.where(row < 2, pick, jnp.zeros_like(pick)), extra)


def swap_halves(values):
    half = HEAD_DIMENSION // 2
    lower = lane_iota(values.shape[0]) % HEAD_DIMENSION < half
    return jnp.where(lower, pltpu.roll(values, LANES - half, 1), pltpu.roll(values, half, 1))


def column_sums(values, lane):
    high = values.astype(jnp.bfloat16)
    low = (values - high.astype(jnp.float32)).astype(jnp.bfloat16)
    place = (lane_iota(values.shape[0]) == lane).astype(jnp.bfloat16)
    return dot_tn(high, place) + dot_tn(low, place)


def head_block(index):
    return slice(index * HEAD_DIMENSION, (index + 1) * HEAD_DIMENSION)


def attention_forward(
    experts,
    copies,
    x_ref,
    w_ref,
    cos_ref,
    sin_ref,
    allow_ref,
    used_ref,
    order_ref,
    wide_ref,
    qkv_ref,
    sent_ref,
):
    f32, bf16 = jnp.float32, jnp.bfloat16
    rows, width = x_ref.shape
    query_width = QUERY_HEADS * HEAD_DIMENSION
    key_width = KEY_VALUE_HEADS * HEAD_DIMENSION
    qkv_width = query_width + 2 * key_width
    extra = w_ref[:, qkv_width + width :]
    gains = gain_rows(extra, experts)
    x = x_ref[...].astype(f32)
    normed = (x * rms_scale(x) * gains[0:1]).astype(bf16)
    cosine, sine = cos_ref[...], sin_ref[...]
    for start in range(0, qkv_width, 512):
        part = dot_nn(normed, w_ref[:, start : start + 512])
        for inner in range(0, 512, LANES):
            piece = part[:, inner : inner + LANES]
            if start + inner < query_width + key_width:
                piece = piece * cosine + swap_halves(piece) * sine
            qkv_ref[:, start + inner : start + inner + LANES] = piece.astype(bf16)
    allowed = allow_ref[...] > 0.0
    lane = lane_iota(rows)
    logs = jnp.zeros((rows, LANES), f32)
    fold = QUERY_HEADS // KEY_VALUE_HEADS
    for group in range(KEY_VALUE_HEADS):
        keys = qkv_ref[:, query_width + group * HEAD_DIMENSION : query_width + (group + 1) * HEAD_DIMENSION]
        values = qkv_ref[
            :,
            query_width + key_width + group * HEAD_DIMENSION : query_width
            + key_width
            + (group + 1) * HEAD_DIMENSION,
        ]
        outs = []
        for head in range(group * fold, (group + 1) * fold):
            scores = dot_nt(qkv_ref[:, head_block(head)], keys) * HEAD_DIMENSION ** (-0.5)
            scores = jnp.where(allowed, scores, mask_fill)
            peak = jnp.max(scores, axis=1, keepdims=True)
            log_total = peak + jnp.log(jnp.sum(jnp.exp(scores - peak), axis=1, keepdims=True))
            logs = jnp.where(lane == head, log_total, logs)
            outs.append(dot_nn(jnp.exp(scores - log_total).astype(bf16), values))
        start = qkv_width + group * LANES
        qkv_ref[:, start : start + LANES] = jnp.concatenate(outs, axis=1).astype(bf16)
    wide_ref[:, width : width + LANES] = logs
    hidden = x + dot_nt(qkv_ref[:, qkv_width:], w_ref[:, qkv_width : qkv_width + width])
    wide_ref[:, :width] = hidden
    second = (hidden * rms_scale(hidden) * gains[1:2]).astype(bf16)
    used = used_ref[...] > 0.0
    logits = jnp.where(used, dot_nn(second, extra), mask_fill)
    powers = jnp.where(used, jnp.exp(logits - jnp.max(logits, axis=1, keepdims=True)), 0.0)
    gates = powers / jnp.sum(powers, axis=1, keepdims=True)
    wide_ref[:, width + LANES :] = gates
    high = gates.astype(bf16).astype(f32)
    lanes = (high + pltpu.roll(gates - high, experts, 1)).astype(bf16)
    moved = dot_nn(second, order_ref[...]).astype(bf16)
    for copy in range(copies):
        sent_ref[copy, :, :width] = moved
        sent_ref[copy, :, width:] = lanes


def own_gate(lanes, number, experts):
    lane = lane_iota(lanes.shape[0])
    chosen = (lane == number) | (lane == number + experts)
    return jnp.sum(jnp.where(chosen, lanes.astype(jnp.float32), 0.0), axis=1, keepdims=True)


def experts_forward(
    experts, local_count, place_ref, rows_ref, w_ref, out_ref, inner_ref, sum_ref
):
    f32, bf16 = jnp.float32, jnp.bfloat16
    index, chunk = pl.program_id(0), pl.program_id(1)
    count, width = out_ref.shape
    gate = own_gate(rows_ref[:, width:], index * local_count + place_ref[0], experts)
    inner = dot_nn(rows_ref[:, :width], w_ref[0, :, : 2 * FF])
    inner_ref[0] = inner
    gate_part = inner[:, :FF]
    activation = (gate_part * jax.nn.sigmoid(gate_part) * inner[:, FF:]).astype(bf16)
    result = dot_nt(activation, w_ref[0, :, 2 * FF :]).astype(bf16).astype(f32)
    here = pl.ds(pl.multiple_of(chunk * count, count), count)

    @pl.when(index == 0)
    def _():
        sum_ref[here, :] = gate * result

    @pl.when(index > 0)
    def _():
        sum_ref[here, :] += gate * result

    out_ref[...] = sum_ref[here, :].astype(bf16)


def experts_backward(
    experts,
    local_count,
    place_ref,
    gates_ref,
    cot_ref,
    w_ref,
    inner_ref,
    back_ref,
    inner_grad_ref,
    act_ref,
    sum_ref,
    dots_sum_ref,
):
    f32, bf16 = jnp.float32, jnp.bfloat16
    index, chunk = pl.program_id(0), pl.program_id(1)
    count, width = cot_ref.shape
    number = index * local_count + place_ref[0]
    gate = own_gate(gates_ref[...], number, experts)
    gate_part = inner_ref[0, :, :FF]
    up_part = inner_ref[0, :, FF:]
    gate_sigmoid = jax.nn.sigmoid(gate_part)
    gate_silu = gate_part * gate_sigmoid
    activation = (gate_silu * up_part).astype(bf16).astype(f32)
    act_ref[0] = (gate * activation).astype(bf16)
    act_grad = dot_nn(cot_ref[...], w_ref[0, :, 2 * FF :])
    dots = jnp.sum(activation * act_grad, axis=1, keepdims=True)
    dots_high = dots.astype(bf16).astype(f32)
    lane = lane_iota(count)
    lanes = jnp.where(lane == number, dots_high, 0.0) + jnp.where(
        lane == number + experts, dots - dots_high, 0.0
    )
    act_grad = gate * act_grad
    inner_grad_ref[0, :, :FF] = (
        act_grad * up_part * gate_sigmoid * (1.0 + gate_part * (1.0 - gate_sigmoid))
    ).astype(bf16)
    inner_grad_ref[0, :, FF:] = (act_grad * gate_silu).astype(bf16)
    copy_grad = dot_nt(inner_grad_ref[0], w_ref[0, :, : 2 * FF])
    here = pl.ds(pl.multiple_of(chunk * count, count), count)

    @pl.when(index == 0)
    def _():
        sum_ref[here, :] = copy_grad
        dots_sum_ref[here, :] = lanes

    @pl.when(index > 0)
    def _():
        sum_ref[here, :] += copy_grad
        dots_sum_ref[here, :] += lanes

    back_ref[:, :width] = sum_ref[here, :].astype(bf16)
    back_ref[:, width:] = dots_sum_ref[here, :].astype(bf16)


def experts_weights(where_ref, rows_ref, inner_grad_ref, cot_ref, act_ref, grad_ref):
    grad_ref[:, : 2 * FF] = dot_tn(rows_ref[...], inner_grad_ref[0]).astype(jnp.bfloat16)
    grad_ref[:, 2 * FF :] = dot_tn(cot_ref[...], act_ref[0]).astype(jnp.bfloat16)


def home_backward(
    experts,
    parts_ref,
    order_ref,
    cot_ref,
    wide_ref,
    w_ref,
    qkv_ref,
    x_ref,
    cos_ref,
    sin_ref,
    allow_ref,
    grad_ref,
    input_grad_ref,
    mid_ref,
    proj_ref,
):
    f32, bf16 = jnp.float32, jnp.bfloat16
    rows, width = x_ref.shape
    sources = parts_ref.shape[0]
    query_width = QUERY_HEADS * HEAD_DIMENSION
    key_width = KEY_VALUE_HEADS * HEAD_DIMENSION
    qkv_width = query_width + 2 * key_width
    fold = QUERY_HEADS // KEY_VALUE_HEADS
    score_scale = HEAD_DIMENSION ** (-0.5)
    extra = w_ref[:, qkv_width + width :]
    gains = gain_rows(extra, experts)
    dots = jnp.zeros((rows, LANES), f32)
    second_grad = jnp.zeros((rows, width), f32)
    for source in range(sources):
        dots = dots + parts_ref[source, :, width:].astype(f32)
        second_grad = second_grad + dot_nn(parts_ref[source, :, :width], order_ref[...])
    dots = dots + pltpu.roll(dots, LANES - experts, 1)
    gates = wide_ref[:, width + LANES :]
    logit_grad = (gates * (dots - jnp.sum(gates * dots, axis=1, keepdims=True))).astype(bf16)
    second_grad = second_grad + dot_nt(logit_grad, extra)
    hidden = wide_ref[:, :width]
    scale = rms_scale(hidden)
    second = (hidden * scale * gains[1:2]).astype(bf16)
    scaled = second_grad * gains[1:2]
    hidden_grad = (
        cot_ref[...].astype(f32)
        + scale * scaled
        - hidden * (scale * scale * scale) * jnp.mean(scaled * hidden, axis=1, keepdims=True)
    )
    branch_grad = hidden_grad.astype(bf16)
    for start in range(0, width, 512):
        grad_ref[:, qkv_width + start : qkv_width + start + 512] = dot_tn(
            branch_grad, qkv_ref[:, qkv_width + start : qkv_width + start + 512]
        ).astype(bf16)
    small_grad = dot_tn(second, logit_grad) + column_sums(
        second_grad * hidden * scale, experts + 1
    )
    mid_ref[...] = dot_nn(branch_grad, w_ref[:, qkv_width : qkv_width + width]).astype(bf16)
    cosine, sine = cos_ref[...], sin_ref[...]
    allowed = allow_ref[...] > 0.0
    lane = lane_iota(rows)
    logs = wide_ref[:, width : width + LANES]

    def turned_back(values):
        return (values * cosine - swap_halves(values) * sine).astype(bf16)

    key_grads, value_grads = [], []
    for group in range(KEY_VALUE_HEADS):
        keys = qkv_ref[:, query_width + group * HEAD_DIMENSION : query_width + (group + 1) * HEAD_DIMENSION]
        values = qkv_ref[
            :,
            query_width + key_width + group * HEAD_DIMENSION : query_width
            + key_width
            + (group + 1) * HEAD_DIMENSION,
        ]
        query_grads = []
        key_grad = jnp.zeros((rows, HEAD_DIMENSION), f32)
        value_grad = jnp.zeros((rows, HEAD_DIMENSION), f32)
        for head in range(group * fold, (group + 1) * fold):
            queries = qkv_ref[:, head_block(head)]
            mid = mid_ref[:, head_block(head)]
            log_total = jnp.sum(jnp.where(lane == head, logs, 0.0), axis=1, keepdims=True)
            scores = jnp.where(allowed, dot_nt(queries, keys) * score_scale, mask_fill)
            weights = jnp.exp(scores - log_total)
            weight_grad = dot_nt(mid, values)
            delta = jnp.sum(weights * weight_grad, axis=1, keepdims=True)
            score_grad = (weights * (weight_grad - delta)).astype(bf16)
            query_grads.append(dot_nn(score_grad, keys) * score_scale)
            key_grad = key_grad + dot_tn(score_grad, queries)
            value_grad = value_grad + dot_tn(weights.astype(bf16), mid)
        proj_ref[:, group * LANES : (group + 1) * LANES] = turned_back(
            jnp.concatenate(query_grads, axis=1)
        )
        key_grads.append(key_grad * score_scale)
        value_grads.append(value_grad)
        if group % 2 == 1:
            start = query_width + (group // 2) * LANES
            proj_ref[:, start : start + LANES] = turned_back(
                jnp.concatenate(key_grads[-2:], axis=1)
            )
            start = start + key_width
            proj_ref[:, start : start + LANES] = jnp.concatenate(value_grads[-2:], axis=1).astype(
                bf16
            )
    x = x_ref[...].astype(f32)
    scale = rms_scale(x)
    normed = (x * scale * gains[0:1]).astype(bf16)
    for start in range(0, qkv_width, 512):
        grad_ref[:, start : start + 512] = dot_tn(normed, proj_ref[:, start : start + 512]).astype(
            bf16
        )
    normed_grad = dot_nt(proj_ref[...], w_ref[:, :qkv_width])
    scaled = normed_grad * gains[0:1]
    small_grad = small_grad + column_sums(normed_grad * x * scale, experts)
    grad_ref[:, qkv_width + width :] = small_grad.astype(bf16)
    input_grad_ref[...] = (
        hidden_grad
        + scale * scaled
        - x * (scale * scale * scale) * jnp.mean(scaled * x, axis=1, keepdims=True)
    ).astype(bf16)


def dense_update(parts_ref, *refs):
    total = parts_ref[0].astype(jnp.float32)
    for source in range(1, parts_ref.shape[0]):
        total = total + parts_ref[source].astype(jnp.float32)
    start = total.shape[1] - LANES
    small = jnp.transpose(total[:, start:])
    experts = refs[6].shape[0]
    qkv_width = refs[0].shape[1]
    grads = (
        total[:, :qkv_width],
        total[:, qkv_width:start],
        small[:experts],
        small[experts : experts + 2],
    )
    rates = ((0.15, decay_rate), (0.3, decay_rate), (0.05, decay_rate), (0.8, 0.0))
    for index, (rate, decay) in enumerate(rates):
        weight_ref, mean_ref, square_ref = refs[3 * index : 3 * index + 3]
        values = adamw(weight_ref[...], grads[index], mean_ref[...], square_ref[...], rate, decay)
        for out_ref, value in zip(refs[3 * index + 12 : 3 * index + 15], values):
            out_ref[...] = value


def whole_call(kernel, outputs, operands, flops, scratch=(), earlier=()):
    operands_read = len(operands)

    def run(*refs):
        kernel(*refs[:operands_read], *refs[operands_read + len(earlier) :])

    moved = sum(math.prod(item.shape) * item.dtype.itemsize for item in list(outputs) + list(operands))
    moved = moved if flops > 1 else 1
    return pl.pallas_call(
        run,
        out_shape=outputs,
        in_specs=[pl.BlockSpec(memory_space=pltpu.VMEM)] * len(operands)
        + [pl.BlockSpec(memory_space=pl.ANY)] * len(earlier),
        out_specs=[pl.BlockSpec(memory_space=pltpu.VMEM)] * len(outputs),
        scratch_shapes=list(scratch),
        compiler_params=pltpu.CompilerParams(vmem_limit_bytes=VMEM_BYTES),
        cost_estimate=pl.CostEstimate(flops=flops, bytes_accessed=moved, transcendentals=0),
    )(*operands, *earlier)


def order_of(kind, sizes):
    axes = {"home": (0, 1, 2, 3, 4), "dense": (2, 1, 3, 0, 4), "expert": (1, 2, 0, 3, 4)}[kind]
    return np.arange(math.prod(sizes), dtype=np.int32).reshape(sizes).transpose(axes).reshape(-1)


def reorder_matrix(before, after):
    return (jnp.asarray(before)[:, None] == jnp.asarray(after)[None, :]).astype(jnp.bfloat16)


def exchange(values, axes):
    return lax.all_to_all(values, axes, split_axis=0, concat_axis=0, tiled=True)


def spread(values, axes):
    count = lax.axis_size(axes)
    copies = exchange(jnp.broadcast_to(values[None], (count,) + values.shape), axes)
    return copies.reshape((count * values.shape[0],) + values.shape[1:])


def collect(values, axes):
    count = lax.axis_size(axes)
    parts = exchange(values.reshape((count, values.shape[0] // count) + values.shape[1:]), axes)
    total = parts[0].astype(jnp.float32)
    for index in range(1, count):
        total = total + parts[index].astype(jnp.float32)
    return total


def partner(values, axes, step):
    names = (axes,) if isinstance(axes, str) else axes
    steps = {}
    for name in reversed(names):
        step, steps[name] = divmod(step, lax.axis_size(name))
    names = tuple(name for name in MESH_AXES if name in names)
    flat = 0
    for name in names:
        flat = flat * lax.axis_size(name) + steps[name]
    pairs = [(index, index ^ flat) for index in range(lax.axis_size(names))]
    return lax.ppermute(values, names, pairs)


def piece_of(values, index):
    return lax.dynamic_index_in_dim(values, index, 0, keepdims=False)


def in_order(own, received, me):
    result = jnp.zeros((len(received) + 1,) + own.shape, own.dtype)
    for step, part in enumerate([own] + received):
        result = lax.dynamic_update_index_in_dim(result, part, me ^ step, 0)
    return result


def spread_aside(values, axes):
    count = lax.axis_size(axes)
    received = [partner(values, axes, step) for step in range(1, count)]
    result = in_order(values, received, lax.axis_index(axes))
    return result.reshape((count * values.shape[0],) + values.shape[1:])


def pieces_for(values, axes):
    me = lax.axis_index(axes)
    return [piece_of(values, me ^ step) for step in range(values.shape[0])]


def exchange_aside(pieces, axes):
    received = [partner(piece, axes, step) for step, piece in enumerate(pieces) if step > 0]
    return in_order(pieces[0], received, lax.axis_index(axes))


def collect_aside(values, axes):
    count = lax.axis_size(axes)
    pieces = pieces_for(values.reshape((count, values.shape[0] // count) + values.shape[1:]), axes)
    total = pieces[0].astype(jnp.float32)
    for step in range(1, count):
        total = total + partner(pieces[step], axes, step).astype(jnp.float32)
    return total


def expert_specs(n_e, group_rows, width):
    count = min(256, group_rows)
    return dict(
        grid=(n_e, group_rows // count),
        scalar=pl.BlockSpec(memory_space=pltpu.SMEM),
        wide=pl.BlockSpec((count, width), lambda k, i: (i, 0)),
        wider=pl.BlockSpec((count, width + LANES), lambda k, i: (i, 0)),
        lanes=pl.BlockSpec((count, LANES), lambda k, i: (i, width // LANES)),
        weight=pl.BlockSpec((1, width, 3 * FF), lambda k, i: (k, 0, 0)),
        inner=pl.BlockSpec((1, count, 2 * FF), lambda k, i: (k, i, 0)),
        act=pl.BlockSpec((1, count, FF), lambda k, i: (k, i, 0)),
    )


def run_forward(place, arrived, expert_full, experts, local_count):
    n_e, width, _ = expert_full.shape
    group_rows = arrived.shape[0]
    specs = expert_specs(n_e, group_rows, width)
    return pl.pallas_call(
        functools.partial(experts_forward, experts, local_count),
        grid=specs["grid"],
        out_shape=[
            jax.ShapeDtypeStruct((group_rows, width), jnp.bfloat16),
            jax.ShapeDtypeStruct((n_e, group_rows, 2 * FF), jnp.float32),
        ],
        in_specs=[specs["scalar"], specs["wider"], specs["weight"]],
        out_specs=[specs["wide"], specs["inner"]],
        scratch_shapes=[pltpu.VMEM((group_rows, width), jnp.float32)],
        compiler_params=pltpu.CompilerParams(vmem_limit_bytes=VMEM_BYTES),
        cost_estimate=pl.CostEstimate(
            flops=2 * n_e * group_rows * width * 3 * FF,
            bytes_accessed=n_e * width * (3 * FF * 2 + group_rows * 8),
            transcendentals=n_e * group_rows * FF,
        ),
    )(place, arrived, expert_full)


def run_backward(place, arrived, cot_group, expert_full, inner, experts, local_count):
    bf16 = jnp.bfloat16
    n_e, width, _ = expert_full.shape
    group_rows = arrived.shape[0]
    specs = expert_specs(n_e, group_rows, width)
    return pl.pallas_call(
        functools.partial(experts_backward, experts, local_count),
        grid=specs["grid"],
        out_shape=[
            jax.ShapeDtypeStruct((group_rows, width + LANES), bf16),
            jax.ShapeDtypeStruct((n_e, group_rows, 2 * FF), bf16),
            jax.ShapeDtypeStruct((n_e, group_rows, FF), bf16),
        ],
        in_specs=[
            specs["scalar"],
            specs["lanes"],
            specs["wide"],
            specs["weight"],
            specs["inner"],
        ],
        out_specs=[specs["wider"], specs["inner"], specs["act"]],
        scratch_shapes=[
            pltpu.VMEM((group_rows, width), jnp.float32),
            pltpu.VMEM((group_rows, LANES), jnp.float32),
        ],
        compiler_params=pltpu.CompilerParams(vmem_limit_bytes=VMEM_BYTES),
        cost_estimate=pl.CostEstimate(
            flops=2 * n_e * group_rows * width * 3 * FF,
            bytes_accessed=n_e * width * (3 * FF * 2 + group_rows * 10),
            transcendentals=n_e * group_rows * FF,
        ),
    )(place, arrived, cot_group, expert_full, inner)


def run_weights(arrived, inner_grad, cot_group, act, slot, first, blocks, part):
    group_rows = arrived.shape[0]
    where = jnp.stack([slot, first]).astype(jnp.int32)
    return pl.pallas_call(
        experts_weights,
        grid_spec=pltpu.PrefetchScalarGridSpec(
            num_scalar_prefetch=1,
            grid=(blocks,),
            in_specs=[
                pl.BlockSpec((group_rows, part), lambda j, at: (0, at[1] + j)),
                pl.BlockSpec((1, group_rows, 2 * FF), lambda j, at: (at[0], 0, 0)),
                pl.BlockSpec((group_rows, part), lambda j, at: (0, at[1] + j)),
                pl.BlockSpec((1, group_rows, FF), lambda j, at: (at[0], 0, 0)),
            ],
            out_specs=pl.BlockSpec((part, 3 * FF), lambda j, at: (j, 0)),
        ),
        out_shape=jax.ShapeDtypeStruct((blocks * part, 3 * FF), jnp.bfloat16),
        compiler_params=pltpu.CompilerParams(vmem_limit_bytes=VMEM_BYTES),
        cost_estimate=pl.CostEstimate(
            flops=2 * blocks * part * group_rows * 3 * FF,
            bytes_accessed=group_rows * 6 * FF + blocks * part * (group_rows * 4 + 6 * FF),
            transcendentals=0,
        ),
    )(where, arrived, inner_grad, cot_group, act)


def in_pieces(n_e, n_r, width):
    return n_e * n_r <= 8 and width // n_r % min(256, width) == 0


def weight_grads(back, factors, n_e, n_r):
    width = factors[2].shape[1]
    part = min(256, width)
    if in_pieces(n_e, n_r, width):
        me = lax.axis_index(("exp", "r"))
        blocks = width // n_r // part
        grads = []
        for step in reversed(range(n_e * n_r)):
            goal = me ^ step
            grads.append(run_weights(*factors, goal // n_r, goal % n_r * blocks, blocks, part))
            if len(grads) == 1:
                back, me = lax.optimization_barrier((back, me))
        return back, grads[::-1]
    blocks = width // part
    return back, [
        run_weights(*factors, jnp.int32(slot), jnp.int32(0), blocks, part) for slot in range(n_e)
    ]


def send_grads(grads, n_e, n_r, width):
    axes = ("exp", "r")
    if not in_pieces(n_e, n_r, width):
        grads = jnp.concatenate(grads, axis=0)
        return list(exchange(grads.reshape((n_e * n_r, -1) + grads.shape[1:]), axes))
    return [grads[0]] + [
        partner(grads[step], axes, step) for step in reversed(range(1, len(grads)))
    ]


def body(
    tokens,
    cotangent,
    doc_lengths,
    routes,
    qkv_weight,
    qkv_mean,
    qkv_square,
    out_weight,
    out_mean,
    out_square,
    router_weight,
    router_mean,
    router_square,
    norm_gains,
    gains_mean,
    gains_square,
    in_weight,
    in_mean,
    in_square,
    down_weight,
    down_mean,
    down_square,
):
    f32, bf16 = jnp.float32, jnp.bfloat16
    shape = jax.ShapeDtypeStruct
    n_a, n_r, n_c, n_e = (lax.axis_size(name) for name in ("a", "r", "core", "exp"))
    rows, width = tokens.shape
    experts = router_weight.shape[1]
    local_count = in_weight.shape[0]
    sizes = (n_a, n_r, n_c, n_e, width // (n_a * n_r * n_c * n_e))
    home, dense, expert = (order_of(kind, sizes) for kind in ("home", "dense", "expert"))
    query_width = QUERY_HEADS * HEAD_DIMENSION
    qkv_width = query_width + 2 * KEY_VALUE_HEADS * HEAD_DIMENSION

    local_rows = qkv_weight.shape[0]
    extra = jnp.zeros((local_rows, LANES - experts - 2), bf16)
    pack = jnp.concatenate(
        [
            qkv_weight.astype(bf16),
            out_weight.astype(bf16),
            router_weight.astype(bf16),
            norm_gains.astype(bf16),
            extra,
        ],
        axis=1,
    )
    pack = spread(pack, "a")

    to_dense = reorder_matrix(home, dense)
    x_dense = dot_nn(tokens, to_dense).astype(bf16)
    cot_dense = dot_nn(cotangent, to_dense).astype(bf16)
    positions, segment = doc_layout(doc_lengths.reshape(-1), rows)
    cosine, sine = rope_tables(positions, HEAD_DIMENSION)
    repeat = LANES // HEAD_DIMENSION
    cosine = jnp.concatenate([cosine, cosine] * repeat, axis=1)
    sine = jnp.concatenate([-sine, sine] * repeat, axis=1)
    row_index = jnp.arange(rows, dtype=jnp.int32)
    allowed = (segment[:, None] == segment[None, :]) & (row_index[None, :] <= row_index[:, None])
    allowed = allowed.astype(f32)
    used = jnp.any(
        routes[:, :, None] == jnp.arange(LANES, dtype=jnp.int32)[None, None, :], axis=1
    ).astype(f32)

    cot_expert = dot_nn(cotangent, reorder_matrix(home, expert)).astype(bf16)
    expert_pack = jnp.concatenate([in_weight.astype(bf16), down_weight.astype(bf16)], axis=2)
    to_expert = reorder_matrix(dense, expert)
    pieces = pieces_for(expert_pack, ("core", "a"))
    pack, x_dense, cot_dense, cosine, sine, allowed, used, to_expert, *pieces = (
        lax.optimization_barrier(
            (pack, x_dense, cot_dense, cosine, sine, allowed, used, to_expert, *pieces)
        )
    )
    pack = spread(pack, ("r", "exp"))
    expert_pack = exchange_aside(pieces, ("core", "a"))
    pack, expert_pack = lax.optimization_barrier((pack, expert_pack))
    cot_expert, expert_pack = lax.optimization_barrier((cot_expert, expert_pack))
    cot_group = spread_aside(spread_aside(cot_expert, "a"), "core")
    expert_full = lax.all_gather(expert_pack, ("exp", "r"), axis=0, tiled=True).reshape(
        n_e, width, 3 * FF
    )
    dense_full = spread(pack, "core")

    wide, qkv, sent = whole_call(
        functools.partial(attention_forward, experts, n_a),
        [
            shape((rows, width + 2 * LANES), f32),
            shape((rows, qkv_width + query_width), bf16),
            shape((n_a, rows, width + LANES), bf16),
        ],
        [x_dense, dense_full, cosine, sine, allowed, used, to_expert],
        flops=2 * rows * width * (qkv_width + 2 * width + 2 * rows),
    )

    arrived = exchange(sent, "a").reshape(n_a * rows, width + LANES)
    arrived = spread(arrived, "core")
    place = (lax.axis_index("core") * n_a + lax.axis_index("a")).astype(jnp.int32).reshape(1)
    out, inner = run_forward(place, arrived, expert_full, experts, local_count)
    back, inner_grad, activation = run_backward(
        place, arrived, cot_group, expert_full, inner, experts, local_count
    )
    out = collect_aside(out, "core").astype(bf16).reshape(n_a, rows, width)
    back = collect(back, "core").astype(bf16)

    factors = (arrived, inner_grad, cot_group, activation)
    back, expert_grads = weight_grads(back, factors, n_e, n_r)
    back = exchange(back.reshape(n_a, rows, width + LANES), "a")
    back, out = lax.optimization_barrier((back, out))
    out = exchange(out, "a")
    received = send_grads(expert_grads, n_e, n_r, width)

    from_expert = reorder_matrix(expert, dense)
    dense_grad, input_grad = whole_call(
        functools.partial(home_backward, experts),
        [shape((width, qkv_width + width + LANES), bf16), shape((rows, width), bf16)],
        [
            back,
            from_expert,
            cot_dense,
            wide,
            dense_full,
            qkv,
            x_dense,
            cosine,
            sine,
            allowed,
        ],
        earlier=expert_grads,
        flops=1,
        scratch=[pltpu.VMEM((rows, query_width), bf16), pltpu.VMEM((rows, qkv_width), bf16)],
    )
    dense_grad, out = lax.optimization_barrier((dense_grad, out))
    dense_grad = collect(dense_grad, "core").astype(bf16)
    dense_grad, *received = lax.optimization_barrier((dense_grad, *received))
    expert_grad = received[0].astype(f32)
    for part in received[1:]:
        expert_grad = expert_grad + part.astype(f32)
    expert_grad = expert_grad.astype(bf16).reshape(
        n_c * n_a, width // (n_r * n_c * n_a), 3 * FF
    )
    expert_grad = exchange_aside(
        pieces_for(expert_grad, ("core", "a")), ("core", "a")
    ).astype(f32)
    d_in = expert_grad[:, :, : 2 * FF]
    d_down = expert_grad[:, :, 2 * FF :]
    dense_grad = collect(dense_grad, ("r", "exp")).astype(bf16)
    from_dense = reorder_matrix(dense, home)
    mixed = dot_nn(out[0], from_expert)
    for index in range(1, n_a):
        mixed = mixed + dot_nn(out[index], from_expert)
    block_out = dot_nn((wide[:, :width] + mixed).astype(bf16), from_dense).astype(bf16)
    input_grad = dot_nn(input_grad, from_dense).astype(bf16)
    dense_grad, block_out, input_grad = lax.optimization_barrier(
        (dense_grad, block_out, input_grad)
    )
    dense_grad = exchange(dense_grad.reshape((n_a, local_rows) + dense_grad.shape[1:]), "a")

    dense_state = [
        qkv_weight,
        qkv_mean,
        qkv_square,
        out_weight,
        out_mean,
        out_square,
        router_weight.T,
        router_mean.T,
        router_square.T,
        norm_gains.T,
        gains_mean.T,
        gains_square.T,
    ]
    (
        new_qkv,
        new_qkv_mean,
        new_qkv_square,
        new_out,
        new_out_mean,
        new_out_square,
        new_router,
        new_router_mean,
        new_router_square,
        new_gains,
        new_gains_mean,
        new_gains_square,
    ) = whole_call(
        dense_update,
        [shape(item.shape, f32) for item in dense_state],
        [dense_grad] + dense_state,
        flops=20 * local_rows * (qkv_width + width),
    )
    new_router, new_router_mean, new_router_square = (
        item.T for item in (new_router, new_router_mean, new_router_square)
    )
    new_gains, new_gains_mean, new_gains_square = (
        item.T for item in (new_gains, new_gains_mean, new_gains_square)
    )
    new_in, new_in_mean, new_in_square = adamw(in_weight, d_in, in_mean, in_square, 0.1, decay_rate)
    new_down, new_down_mean, new_down_square = adamw(
        down_weight, d_down, down_mean, down_square, 1.0, decay_rate
    )
    return (
        block_out,
        input_grad,
        new_qkv,
        new_qkv_mean,
        new_qkv_square,
        new_out,
        new_out_mean,
        new_out_square,
        new_router,
        new_router_mean,
        new_router_square,
        new_gains,
        new_gains_mean,
        new_gains_square,
        new_in,
        new_in_mean,
        new_in_square,
        new_down,
        new_down_mean,
        new_down_square,
    )


def solution(mesh):
    n_dp, n_exp = mesh.shape["dp"], mesh.shape["exp"]
    n_a = EXPERTS // n_exp // 2
    mesh = Mesh(
        mesh.devices.reshape(n_a, n_dp // (2 * n_a), 2, n_exp), MESH_AXES
    )
    placed = (
        P(("a", "r", "core", "exp"), None),
        P(("a", "r", "core", "exp"), None),
        P(("a", "r", "core", "exp"), None),
        P(("a", "r", "core", "exp"), None),
        P(("a", "r", "core", "exp"), None),
        P(("a", "r", "core", "exp"), None),
        P(("a", "r", "core", "exp"), None),
        P(("a", "r", "core", "exp"), None),
        P(("a", "r", "core", "exp"), None),
        P(("a", "r", "core", "exp"), None),
        P(("a", "r", "core", "exp"), None),
        P(("a", "r", "core", "exp"), None),
        P(("a", "r", "core", "exp"), None),
        P(("a", "r", "core", "exp"), None),
        P(("a", "r", "core", "exp"), None),
        P(("a", "r", "core", "exp"), None),
        P("exp", ("a", "r", "core"), None),
        P("exp", ("a", "r", "core"), None),
        P("exp", ("a", "r", "core"), None),
        P("exp", ("a", "r", "core"), None),
        P("exp", ("a", "r", "core"), None),
        P("exp", ("a", "r", "core"), None),
    )
    return jax.shard_map(
        body,
        mesh=mesh,
        in_specs=placed,
        out_specs=(
            P(("a", "r", "core", "exp"), None),
            P(("a", "r", "core", "exp"), None),
            P(("a", "r", "core", "exp"), None),
            P(("a", "r", "core", "exp"), None),
            P(("a", "r", "core", "exp"), None),
            P(("a", "r", "core", "exp"), None),
            P(("a", "r", "core", "exp"), None),
            P(("a", "r", "core", "exp"), None),
            P(("a", "r", "core", "exp"), None),
            P(("a", "r", "core", "exp"), None),
            P(("a", "r", "core", "exp"), None),
            P(("a", "r", "core", "exp"), None),
            P(("a", "r", "core", "exp"), None),
            P(("a", "r", "core", "exp"), None),
            P("exp", ("a", "r", "core"), None),
            P("exp", ("a", "r", "core"), None),
            P("exp", ("a", "r", "core"), None),
            P("exp", ("a", "r", "core"), None),
            P("exp", ("a", "r", "core"), None),
            P("exp", ("a", "r", "core"), None),
        ),
        check_vma=False,
    )
```

```python
import functools
import math

import jax
import jax.numpy as jnp
import numpy as np
from jax import lax
from jax.experimental import pallas as pl
from jax.experimental.pallas import tpu as pltpu
from jax.sharding import Mesh
from jax.sharding import PartitionSpec as P

QUERY_HEADS = 16
KEY_VALUE_HEADS = 8
HEAD_DIMENSION = 64
FF = 512
STEP = 10
EXPERTS = 16
LANES = 128
MESH_AXES = ("a", "r", "core", "exp")
VMEM_BYTES = 26 * 1024 * 1024


norm_eps = 1e-06
rope_base = 10000.0
mask_fill = -1e30
beta_one = 0.9
beta_two = 0.95
adam_eps = 1e-08
decay_rate = 0.1


def rms_scale(values):
    return lax.rsqrt(jnp.mean(values * values, axis=-1, keepdims=True) + norm_eps)


def doc_layout(doc_lens, sequence_length):
    row_index = jnp.arange(sequence_length, dtype=jnp.int32)
    doc_ends = jnp.cumsum(doc_lens, dtype=jnp.int32)
    passed = (row_index[:, None] >= doc_ends[None, :]).astype(jnp.int32)
    segment = jnp.sum(passed, axis=1, dtype=jnp.int32)
    starts = jnp.sum(passed * doc_lens[None, :], axis=1, dtype=jnp.int32)
    return ((row_index - starts).astype(jnp.float32), segment)


def rope_tables(positions, head_size):
    half_size = head_size // 2
    freq_index = jnp.arange(half_size, dtype=jnp.float32)
    inverse = jnp.exp(freq_index * (-2.0 * math.log(rope_base) / head_size))
    angles = positions[:, None] * inverse[None, :]
    return (jnp.cos(angles), jnp.sin(angles))


def adamw(weight, gradient, mean_old, square_old, step_rate, weight_decay):
    mean_new = beta_one * mean_old + (1.0 - beta_one) * gradient
    square_new = beta_two * square_old + (1.0 - beta_two) * gradient * gradient
    corrected = (
        mean_new
        / (1.0 - beta_one**STEP)
        / (jnp.sqrt(square_new / (1.0 - beta_two**STEP)) + adam_eps)
    )
    return (weight - step_rate * (corrected + weight_decay * weight), mean_new, square_new)

def dot_nn(left, right):
    return jnp.dot(left, right, preferred_element_type=jnp.float32)


def dot_nt(left, right):
    return lax.dot_general(left, right, (((1,), (1,)), ((), ())), preferred_element_type=jnp.float32)


def dot_tn(left, right):
    return lax.dot_general(left, right, (((0,), (0,)), ((), ())), preferred_element_type=jnp.float32)


def lane_iota(rows):
    return lax.broadcasted_iota(jnp.int32, (rows, LANES), 1)


def gain_rows(extra, experts):
    row = lax.broadcasted_iota(jnp.int32, (8, LANES), 0)
    pick = (lane_iota(8) == row + experts).astype(jnp.bfloat16)
    return dot_nt(jnp.where(row < 2, pick, jnp.zeros_like(pick)), extra)


def swap_halves(values):
    half = HEAD_DIMENSION // 2
    lower = lane_iota(values.shape[0]) % HEAD_DIMENSION < half
    return jnp.where(lower, pltpu.roll(values, LANES - half, 1), pltpu.roll(values, half, 1))


def column_sums(values, lane):
    high = values.astype(jnp.bfloat16)
    low = (values - high.astype(jnp.float32)).astype(jnp.bfloat16)
    place = (lane_iota(values.shape[0]) == lane).astype(jnp.bfloat16)
    return dot_tn(high, place) + dot_tn(low, place)


def head_block(index):
    return slice(index * HEAD_DIMENSION, (index + 1) * HEAD_DIMENSION)


def attention_forward(
    experts,
    copies,
    x_ref,
    w_ref,
    cos_ref,
    sin_ref,
    allow_ref,
    used_ref,
    order_ref,
    wide_ref,
    qkv_ref,
    sent_ref,
):
    f32, bf16 = jnp.float32, jnp.bfloat16
    rows, width = x_ref.shape
    query_width = QUERY_HEADS * HEAD_DIMENSION
    key_width = KEY_VALUE_HEADS * HEAD_DIMENSION
    qkv_width = query_width + 2 * key_width
    extra = w_ref[:, qkv_width + width :]
    gains = gain_rows(extra, experts)
    x = x_ref[...].astype(f32)
    normed = (x * rms_scale(x) * gains[0:1]).astype(bf16)
    cosine, sine = cos_ref[...], sin_ref[...]
    for start in range(0, qkv_width, 512):
        part = dot_nn(normed, w_ref[:, start : start + 512])
        for inner in range(0, 512, LANES):
            piece = part[:, inner : inner + LANES]
            if start + inner < query_width + key_width:
                piece = piece * cosine + swap_halves(piece) * sine
            qkv_ref[:, start + inner : start + inner + LANES] = piece.astype(bf16)
    allowed = allow_ref[...] > 0.0
    lane = lane_iota(rows)
    logs = jnp.zeros((rows, LANES), f32)
    fold = QUERY_HEADS // KEY_VALUE_HEADS
    for group in range(KEY_VALUE_HEADS):
        keys = qkv_ref[:, query_width + group * HEAD_DIMENSION : query_width + (group + 1) * HEAD_DIMENSION]
        values = qkv_ref[
            :,
            query_width + key_width + group * HEAD_DIMENSION : query_width
            + key_width
            + (group + 1) * HEAD_DIMENSION,
        ]
        outs = []
        for head in range(group * fold, (group + 1) * fold):
            scores = dot_nt(qkv_ref[:, head_block(head)], keys) * HEAD_DIMENSION ** (-0.5)
            scores = jnp.where(allowed, scores, mask_fill)
            peak = jnp.max(scores, axis=1, keepdims=True)
            log_total = peak + jnp.log(jnp.sum(jnp.exp(scores - peak), axis=1, keepdims=True))
            logs = jnp.where(lane == head, log_total, logs)
            outs.append(dot_nn(jnp.exp(scores - log_total).astype(bf16), values))
        start = qkv_width + group * LANES
        qkv_ref[:, start : start + LANES] = jnp.concatenate(outs, axis=1).astype(bf16)
    wide_ref[:, width : width + LANES] = logs
    hidden = x + dot_nt(qkv_ref[:, qkv_width:], w_ref[:, qkv_width : qkv_width + width])
    wide_ref[:, :width] = hidden
    second = (hidden * rms_scale(hidden) * gains[1:2]).astype(bf16)
    used = used_ref[...] > 0.0
    logits = jnp.where(used, dot_nn(second, extra), mask_fill)
    powers = jnp.where(used, jnp.exp(logits - jnp.max(logits, axis=1, keepdims=True)), 0.0)
    gates = powers / jnp.sum(powers, axis=1, keepdims=True)
    wide_ref[:, width + LANES :] = gates
    high = gates.astype(bf16).astype(f32)
    lanes = (high + pltpu.roll(gates - high, experts, 1)).astype(bf16)
    moved = dot_nn(second, order_ref[...]).astype(bf16)
    for copy in range(copies):
        sent_ref[copy, :, :width] = moved
        sent_ref[copy, :, width:] = lanes


def own_gate(lanes, number, experts):
    lane = lane_iota(lanes.shape[0])
    chosen = (lane == number) | (lane == number + experts)
    return jnp.sum(jnp.where(chosen, lanes.astype(jnp.float32), 0.0), axis=1, keepdims=True)


def experts_forward(
    experts, local_count, place_ref, rows_ref, w_ref, out_ref, inner_ref, sum_ref
):
    f32, bf16 = jnp.float32, jnp.bfloat16
    index, chunk = pl.program_id(0), pl.program_id(1)
    count, width = out_ref.shape
    gate = own_gate(rows_ref[:, width:], index * local_count + place_ref[0], experts)
    inner = dot_nn(rows_ref[:, :width], w_ref[0, :, : 2 * FF])
    inner_ref[0] = inner
    gate_part = inner[:, :FF]
    activation = (gate_part * jax.nn.sigmoid(gate_part) * inner[:, FF:]).astype(bf16)
    result = dot_nt(activation, w_ref[0, :, 2 * FF :]).astype(bf16).astype(f32)
    here = pl.ds(pl.multiple_of(chunk * count, count), count)

    @pl.when(index == 0)
    def _():
        sum_ref[here, :] = gate * result

    @pl.when(index > 0)
    def _():
        sum_ref[here, :] += gate * result

    out_ref[...] = sum_ref[here, :].astype(bf16)


def experts_backward(
    experts,
    local_count,
    place_ref,
    gates_ref,
    cot_ref,
    w_ref,
    inner_ref,
    back_ref,
    inner_grad_ref,
    act_ref,
    sum_ref,
    dots_sum_ref,
):
    f32, bf16 = jnp.float32, jnp.bfloat16
    index, chunk = pl.program_id(0), pl.program_id(1)
    count, width = cot_ref.shape
    number = index * local_count + place_ref[0]
    gate = own_gate(gates_ref[...], number, experts)
    gate_part = inner_ref[0, :, :FF]
    up_part = inner_ref[0, :, FF:]
    gate_sigmoid = jax.nn.sigmoid(gate_part)
    gate_silu = gate_part * gate_sigmoid
    activation = (gate_silu * up_part).astype(bf16).astype(f32)
    act_ref[0] = (gate * activation).astype(bf16)
    act_grad = dot_nn(cot_ref[...], w_ref[0, :, 2 * FF :])
    dots = jnp.sum(activation * act_grad, axis=1, keepdims=True)
    dots_high = dots.astype(bf16).astype(f32)
    lane = lane_iota(count)
    lanes = jnp.where(lane == number, dots_high, 0.0) + jnp.where(
        lane == number + experts, dots - dots_high, 0.0
    )
    act_grad = gate * act_grad
    inner_grad_ref[0, :, :FF] = (
        act_grad * up_part * gate_sigmoid * (1.0 + gate_part * (1.0 - gate_sigmoid))
    ).astype(bf16)
    inner_grad_ref[0, :, FF:] = (act_grad * gate_silu).astype(bf16)
    copy_grad = dot_nt(inner_grad_ref[0], w_ref[0, :, : 2 * FF])
    here = pl.ds(pl.multiple_of(chunk * count, count), count)

    @pl.when(index == 0)
    def _():
        sum_ref[here, :] = copy_grad
        dots_sum_ref[here, :] = lanes

    @pl.when(index > 0)
    def _():
        sum_ref[here, :] += copy_grad
        dots_sum_ref[here, :] += lanes

    back_ref[:, :width] = sum_ref[here, :].astype(bf16)
    back_ref[:, width:] = dots_sum_ref[here, :].astype(bf16)


def experts_weights(where_ref, rows_ref, inner_grad_ref, cot_ref, act_ref, *grad_refs):
    goal = pl.program_id(0)
    inner = dot_tn(rows_ref[...], inner_grad_ref[0]).astype(jnp.bfloat16)
    down = dot_tn(cot_ref[...], act_ref[0]).astype(jnp.bfloat16)
    for index, grad_ref in enumerate(grad_refs):

        @pl.when(goal == index)
        def _(grad_ref=grad_ref):
            grad_ref[:, : 2 * FF] = inner
            grad_ref[:, 2 * FF :] = down


def home_backward(
    experts,
    parts_ref,
    order_ref,
    cot_ref,
    wide_ref,
    w_ref,
    qkv_ref,
    x_ref,
    cos_ref,
    sin_ref,
    allow_ref,
    grad_ref,
    input_grad_ref,
    mid_ref,
    proj_ref,
):
    f32, bf16 = jnp.float32, jnp.bfloat16
    rows, width = x_ref.shape
    sources = parts_ref.shape[0]
    query_width = QUERY_HEADS * HEAD_DIMENSION
    key_width = KEY_VALUE_HEADS * HEAD_DIMENSION
    qkv_width = query_width + 2 * key_width
    fold = QUERY_HEADS // KEY_VALUE_HEADS
    score_scale = HEAD_DIMENSION ** (-0.5)
    extra = w_ref[:, qkv_width + width :]
    gains = gain_rows(extra, experts)
    dots = jnp.zeros((rows, LANES), f32)
    second_grad = jnp.zeros((rows, width), f32)
    for source in range(sources):
        dots = dots + parts_ref[source, :, width:].astype(f32)
        second_grad = second_grad + dot_nn(parts_ref[source, :, :width], order_ref[...])
    dots = dots + pltpu.roll(dots, LANES - experts, 1)
    gates = wide_ref[:, width + LANES :]
    logit_grad = (gates * (dots - jnp.sum(gates * dots, axis=1, keepdims=True))).astype(bf16)
    second_grad = second_grad + dot_nt(logit_grad, extra)
    hidden = wide_ref[:, :width]
    scale = rms_scale(hidden)
    second = (hidden * scale * gains[1:2]).astype(bf16)
    scaled = second_grad * gains[1:2]
    hidden_grad = (
        cot_ref[...].astype(f32)
        + scale * scaled
        - hidden * (scale * scale * scale) * jnp.mean(scaled * hidden, axis=1, keepdims=True)
    )
    branch_grad = hidden_grad.astype(bf16)
    for start in range(0, width, 512):
        grad_ref[:, qkv_width + start : qkv_width + start + 512] = dot_tn(
            branch_grad, qkv_ref[:, qkv_width + start : qkv_width + start + 512]
        ).astype(bf16)
    small_grad = dot_tn(second, logit_grad) + column_sums(
        second_grad * hidden * scale, experts + 1
    )
    mid_ref[...] = dot_nn(branch_grad, w_ref[:, qkv_width : qkv_width + width]).astype(bf16)
    cosine, sine = cos_ref[...], sin_ref[...]
    allowed = allow_ref[...] > 0.0
    lane = lane_iota(rows)
    logs = wide_ref[:, width : width + LANES]

    def turned_back(values):
        return (values * cosine - swap_halves(values) * sine).astype(bf16)

    key_grads, value_grads = [], []
    for group in range(KEY_VALUE_HEADS):
        keys = qkv_ref[:, query_width + group * HEAD_DIMENSION : query_width + (group + 1) * HEAD_DIMENSION]
        values = qkv_ref[
            :,
            query_width + key_width + group * HEAD_DIMENSION : query_width
            + key_width
            + (group + 1) * HEAD_DIMENSION,
        ]
        query_grads = []
        key_grad = jnp.zeros((rows, HEAD_DIMENSION), f32)
        value_grad = jnp.zeros((rows, HEAD_DIMENSION), f32)
        for head in range(group * fold, (group + 1) * fold):
            queries = qkv_ref[:, head_block(head)]
            mid = mid_ref[:, head_block(head)]
            log_total = jnp.sum(jnp.where(lane == head, logs, 0.0), axis=1, keepdims=True)
            scores = jnp.where(allowed, dot_nt(queries, keys) * score_scale, mask_fill)
            weights = jnp.exp(scores - log_total)
            weight_grad = dot_nt(mid, values)
            delta = jnp.sum(weights * weight_grad, axis=1, keepdims=True)
            score_grad = (weights * (weight_grad - delta)).astype(bf16)
            query_grads.append(dot_nn(score_grad, keys) * score_scale)
            key_grad = key_grad + dot_tn(score_grad, queries)
            value_grad = value_grad + dot_tn(weights.astype(bf16), mid)
        proj_ref[:, group * LANES : (group + 1) * LANES] = turned_back(
            jnp.concatenate(query_grads, axis=1)
        )
        key_grads.append(key_grad * score_scale)
        value_grads.append(value_grad)
        if group % 2 == 1:
            start = query_width + (group // 2) * LANES
            proj_ref[:, start : start + LANES] = turned_back(
                jnp.concatenate(key_grads[-2:], axis=1)
            )
            start = start + key_width
            proj_ref[:, start : start + LANES] = jnp.concatenate(value_grads[-2:], axis=1).astype(
                bf16
            )
    x = x_ref[...].astype(f32)
    scale = rms_scale(x)
    normed = (x * scale * gains[0:1]).astype(bf16)
    for start in range(0, qkv_width, 512):
        grad_ref[:, start : start + 512] = dot_tn(normed, proj_ref[:, start : start + 512]).astype(
            bf16
        )
    normed_grad = dot_nt(proj_ref[...], w_ref[:, :qkv_width])
    scaled = normed_grad * gains[0:1]
    small_grad = small_grad + column_sums(normed_grad * x * scale, experts)
    grad_ref[:, qkv_width + width :] = small_grad.astype(bf16)
    input_grad_ref[...] = (
        hidden_grad
        + scale * scaled
        - x * (scale * scale * scale) * jnp.mean(scaled * x, axis=1, keepdims=True)
    ).astype(bf16)


def dense_update(parts_ref, *refs):
    total = parts_ref[0].astype(jnp.float32)
    for source in range(1, parts_ref.shape[0]):
        total = total + parts_ref[source].astype(jnp.float32)
    start = total.shape[1] - LANES
    small = jnp.transpose(total[:, start:])
    experts = refs[6].shape[0]
    qkv_width = refs[0].shape[1]
    grads = (
        total[:, :qkv_width],
        total[:, qkv_width:start],
        small[:experts],
        small[experts : experts + 2],
    )
    rates = ((0.15, decay_rate), (0.3, decay_rate), (0.05, decay_rate), (0.8, 0.0))
    for index, (rate, decay) in enumerate(rates):
        weight_ref, mean_ref, square_ref = refs[3 * index : 3 * index + 3]
        values = adamw(weight_ref[...], grads[index], mean_ref[...], square_ref[...], rate, decay)
        for out_ref, value in zip(refs[3 * index + 12 : 3 * index + 15], values):
            out_ref[...] = value


def whole_call(kernel, outputs, operands, flops, scratch=(), earlier=()):
    operands_read = len(operands)

    def run(*refs):
        kernel(*refs[:operands_read], *refs[operands_read + len(earlier) :])

    moved = sum(math.prod(item.shape) * item.dtype.itemsize for item in list(outputs) + list(operands))
    moved = moved if flops > 1 else 1
    return pl.pallas_call(
        run,
        out_shape=outputs,
        in_specs=[pl.BlockSpec(memory_space=pltpu.VMEM)] * len(operands)
        + [pl.BlockSpec(memory_space=pl.ANY)] * len(earlier),
        out_specs=[pl.BlockSpec(memory_space=pltpu.VMEM)] * len(outputs),
        scratch_shapes=list(scratch),
        compiler_params=pltpu.CompilerParams(vmem_limit_bytes=VMEM_BYTES),
        cost_estimate=pl.CostEstimate(flops=flops, bytes_accessed=moved, transcendentals=0),
    )(*operands, *earlier)


def order_of(kind, sizes):
    axes = {"home": (0, 1, 2, 3, 4), "dense": (2, 1, 3, 0, 4), "expert": (1, 2, 0, 3, 4)}[kind]
    return np.arange(math.prod(sizes), dtype=np.int32).reshape(sizes).transpose(axes).reshape(-1)


def reorder_matrix(before, after):
    return (jnp.asarray(before)[:, None] == jnp.asarray(after)[None, :]).astype(jnp.bfloat16)


def exchange(values, axes):
    return lax.all_to_all(values, axes, split_axis=0, concat_axis=0, tiled=True)


def spread(values, axes):
    count = lax.axis_size(axes)
    copies = exchange(jnp.broadcast_to(values[None], (count,) + values.shape), axes)
    return copies.reshape((count * values.shape[0],) + values.shape[1:])


def collect(values, axes):
    count = lax.axis_size(axes)
    parts = exchange(values.reshape((count, values.shape[0] // count) + values.shape[1:]), axes)
    total = parts[0].astype(jnp.float32)
    for index in range(1, count):
        total = total + parts[index].astype(jnp.float32)
    return total


def partner(values, axes, step):
    names = (axes,) if isinstance(axes, str) else axes
    steps = {}
    for name in reversed(names):
        step, steps[name] = divmod(step, lax.axis_size(name))
    names = tuple(name for name in MESH_AXES if name in names)
    flat = 0
    for name in names:
        flat = flat * lax.axis_size(name) + steps[name]
    pairs = [(index, index ^ flat) for index in range(lax.axis_size(names))]
    return lax.ppermute(values, names, pairs)


def piece_of(values, index):
    return lax.dynamic_index_in_dim(values, index, 0, keepdims=False)


def in_order(own, received, me):
    result = jnp.zeros((len(received) + 1,) + own.shape, own.dtype)
    for step, part in enumerate([own] + received):
        result = lax.dynamic_update_index_in_dim(result, part, me ^ step, 0)
    return result


def spread_aside(values, axes):
    count = lax.axis_size(axes)
    received = [partner(values, axes, step) for step in range(1, count)]
    result = in_order(values, received, lax.axis_index(axes))
    return result.reshape((count * values.shape[0],) + values.shape[1:])


def pieces_for(values, axes):
    me = lax.axis_index(axes)
    return [piece_of(values, me ^ step) for step in range(values.shape[0])]


def exchange_aside(pieces, axes):
    received = [partner(piece, axes, step) for step, piece in enumerate(pieces) if step > 0]
    return in_order(pieces[0], received, lax.axis_index(axes))


def collect_aside(values, axes):
    count = lax.axis_size(axes)
    pieces = pieces_for(values.reshape((count, values.shape[0] // count) + values.shape[1:]), axes)
    total = pieces[0].astype(jnp.float32)
    for step in range(1, count):
        total = total + partner(pieces[step], axes, step).astype(jnp.float32)
    return total


def expert_specs(n_e, group_rows, width):
    count = min(256, group_rows)
    return dict(
        grid=(n_e, group_rows // count),
        scalar=pl.BlockSpec(memory_space=pltpu.SMEM),
        wide=pl.BlockSpec((count, width), lambda k, i: (i, 0)),
        wider=pl.BlockSpec((count, width + LANES), lambda k, i: (i, 0)),
        lanes=pl.BlockSpec((count, LANES), lambda k, i: (i, width // LANES)),
        weight=pl.BlockSpec((1, width, 3 * FF), lambda k, i: (k, 0, 0)),
        inner=pl.BlockSpec((1, count, 2 * FF), lambda k, i: (k, i, 0)),
        act=pl.BlockSpec((1, count, FF), lambda k, i: (k, i, 0)),
    )


def run_forward(place, arrived, expert_full, experts, local_count):
    n_e, width, _ = expert_full.shape
    group_rows = arrived.shape[0]
    specs = expert_specs(n_e, group_rows, width)
    return pl.pallas_call(
        functools.partial(experts_forward, experts, local_count),
        grid=specs["grid"],
        out_shape=[
            jax.ShapeDtypeStruct((group_rows, width), jnp.bfloat16),
            jax.ShapeDtypeStruct((n_e, group_rows, 2 * FF), jnp.float32),
        ],
        in_specs=[specs["scalar"], specs["wider"], specs["weight"]],
        out_specs=[specs["wide"], specs["inner"]],
        scratch_shapes=[pltpu.VMEM((group_rows, width), jnp.float32)],
        compiler_params=pltpu.CompilerParams(vmem_limit_bytes=VMEM_BYTES),
        cost_estimate=pl.CostEstimate(
            flops=2 * n_e * group_rows * width * 3 * FF,
            bytes_accessed=n_e * width * (3 * FF * 2 + group_rows * 8),
            transcendentals=n_e * group_rows * FF,
        ),
    )(place, arrived, expert_full)


def run_backward(place, arrived, cot_group, expert_full, inner, experts, local_count):
    bf16 = jnp.bfloat16
    n_e, width, _ = expert_full.shape
    group_rows = arrived.shape[0]
    specs = expert_specs(n_e, group_rows, width)
    return pl.pallas_call(
        functools.partial(experts_backward, experts, local_count),
        grid=specs["grid"],
        out_shape=[
            jax.ShapeDtypeStruct((group_rows, width + LANES), bf16),
            jax.ShapeDtypeStruct((n_e, group_rows, 2 * FF), bf16),
            jax.ShapeDtypeStruct((n_e, group_rows, FF), bf16),
        ],
        in_specs=[
            specs["scalar"],
            specs["lanes"],
            specs["wide"],
            specs["weight"],
            specs["inner"],
        ],
        out_specs=[specs["wider"], specs["inner"], specs["act"]],
        scratch_shapes=[
            pltpu.VMEM((group_rows, width), jnp.float32),
            pltpu.VMEM((group_rows, LANES), jnp.float32),
        ],
        compiler_params=pltpu.CompilerParams(vmem_limit_bytes=VMEM_BYTES),
        cost_estimate=pl.CostEstimate(
            flops=2 * n_e * group_rows * width * 3 * FF,
            bytes_accessed=n_e * width * (3 * FF * 2 + group_rows * 10),
            transcendentals=n_e * group_rows * FF,
        ),
    )(place, arrived, cot_group, expert_full, inner)


def run_weights(arrived, inner_grad, cot_group, act, slots, firsts, blocks, part):
    group_rows = arrived.shape[0]
    goals = len(slots)
    where = jnp.stack(slots + firsts).astype(jnp.int32)

    def block_of(index):
        return lambda g, j, at: (jnp.where(g == index, j, jnp.where(g < index, 0, blocks - 1)), 0)

    return pl.pallas_call(
        experts_weights,
        grid_spec=pltpu.PrefetchScalarGridSpec(
            num_scalar_prefetch=1,
            grid=(goals, blocks),
            in_specs=[
                pl.BlockSpec((group_rows, part), lambda g, j, at: (0, at[goals + g] + j)),
                pl.BlockSpec((1, group_rows, 2 * FF), lambda g, j, at: (at[g], 0, 0)),
                pl.BlockSpec((group_rows, part), lambda g, j, at: (0, at[goals + g] + j)),
                pl.BlockSpec((1, group_rows, FF), lambda g, j, at: (at[g], 0, 0)),
            ],
            out_specs=[pl.BlockSpec((part, 3 * FF), block_of(index)) for index in range(goals)],
        ),
        out_shape=[jax.ShapeDtypeStruct((blocks * part, 3 * FF), jnp.bfloat16)] * goals,
        compiler_params=pltpu.CompilerParams(vmem_limit_bytes=VMEM_BYTES),
        cost_estimate=pl.CostEstimate(
            flops=2 * goals * blocks * part * group_rows * 3 * FF,
            bytes_accessed=goals * (group_rows * 6 * FF + blocks * part * (group_rows * 4 + 6 * FF)),
            transcendentals=0,
        ),
    )(where, arrived, inner_grad, cot_group, act)


def in_pieces(n_e, n_r, width):
    return n_e * n_r <= 8 and width // n_r % min(256, width) == 0


def weight_grads(factors, n_e, n_r):
    width = factors[2].shape[1]
    part = min(256, width)
    if in_pieces(n_e, n_r, width):
        me = lax.axis_index(("exp", "r"))
        blocks = width // n_r // part
        goals = [me ^ step for step in range(n_e * n_r)]
        slots = [goal // n_r for goal in goals]
        firsts = [goal % n_r * blocks for goal in goals]
        return run_weights(*factors, slots, firsts, blocks, part)
    grads = []
    for slot in range(n_e):
        grads += run_weights(*factors, [jnp.int32(slot)], [jnp.int32(0)], width // part, part)
    return grads


def send_grads(grads, n_e, n_r, width):
    axes = ("exp", "r")
    if not in_pieces(n_e, n_r, width):
        grads = jnp.concatenate(grads, axis=0)
        return list(exchange(grads.reshape((n_e * n_r, -1) + grads.shape[1:]), axes))
    return [grads[0]] + [
        partner(grads[step], axes, step) for step in reversed(range(1, len(grads)))
    ]


def body(
    tokens,
    cotangent,
    doc_lengths,
    routes,
    qkv_weight,
    qkv_mean,
    qkv_square,
    out_weight,
    out_mean,
    out_square,
    router_weight,
    router_mean,
    router_square,
    norm_gains,
    gains_mean,
    gains_square,
    in_weight,
    in_mean,
    in_square,
    down_weight,
    down_mean,
    down_square,
):
    f32, bf16 = jnp.float32, jnp.bfloat16
    shape = jax.ShapeDtypeStruct
    n_a, n_r, n_c, n_e = (lax.axis_size(name) for name in ("a", "r", "core", "exp"))
    rows, width = tokens.shape
    experts = router_weight.shape[1]
    local_count = in_weight.shape[0]
    sizes = (n_a, n_r, n_c, n_e, width // (n_a * n_r * n_c * n_e))
    home, dense, expert = (order_of(kind, sizes) for kind in ("home", "dense", "expert"))
    query_width = QUERY_HEADS * HEAD_DIMENSION
    qkv_width = query_width + 2 * KEY_VALUE_HEADS * HEAD_DIMENSION

    local_rows = qkv_weight.shape[0]
    extra = jnp.zeros((local_rows, LANES - experts - 2), bf16)
    pack = jnp.concatenate(
        [
            qkv_weight.astype(bf16),
            out_weight.astype(bf16),
            router_weight.astype(bf16),
            norm_gains.astype(bf16),
            extra,
        ],
        axis=1,
    )
    pack = spread(pack, "a")

    to_dense = reorder_matrix(home, dense)
    x_dense = dot_nn(tokens, to_dense).astype(bf16)
    cot_dense = dot_nn(cotangent, to_dense).astype(bf16)
    positions, segment = doc_layout(doc_lengths.reshape(-1), rows)
    cosine, sine = rope_tables(positions, HEAD_DIMENSION)
    repeat = LANES // HEAD_DIMENSION
    cosine = jnp.concatenate([cosine, cosine] * repeat, axis=1)
    sine = jnp.concatenate([-sine, sine] * repeat, axis=1)
    row_index = jnp.arange(rows, dtype=jnp.int32)
    allowed = (segment[:, None] == segment[None, :]) & (row_index[None, :] <= row_index[:, None])
    allowed = allowed.astype(f32)
    used = jnp.any(
        routes[:, :, None] == jnp.arange(LANES, dtype=jnp.int32)[None, None, :], axis=1
    ).astype(f32)

    cot_expert = dot_nn(cotangent, reorder_matrix(home, expert)).astype(bf16)
    expert_pack = jnp.concatenate([in_weight.astype(bf16), down_weight.astype(bf16)], axis=2)
    to_expert = reorder_matrix(dense, expert)
    pieces = pieces_for(expert_pack, ("core", "a"))
    pack, x_dense, cot_dense, cosine, sine, allowed, used, to_expert, *pieces = (
        lax.optimization_barrier(
            (pack, x_dense, cot_dense, cosine, sine, allowed, used, to_expert, *pieces)
        )
    )
    pack = spread(pack, ("r", "exp"))
    expert_pack = exchange_aside(pieces, ("core", "a"))
    pack, expert_pack = lax.optimization_barrier((pack, expert_pack))
    cot_expert, expert_pack = lax.optimization_barrier((cot_expert, expert_pack))
    cot_group = spread_aside(spread_aside(cot_expert, "a"), "core")
    expert_full = lax.all_gather(expert_pack, ("exp", "r"), axis=0, tiled=True).reshape(
        n_e, width, 3 * FF
    )
    dense_full = spread(pack, "core")

    wide, qkv, sent = whole_call(
        functools.partial(attention_forward, experts, n_a),
        [
            shape((rows, width + 2 * LANES), f32),
            shape((rows, qkv_width + query_width), bf16),
            shape((n_a, rows, width + LANES), bf16),
        ],
        [x_dense, dense_full, cosine, sine, allowed, used, to_expert],
        flops=2 * rows * width * (qkv_width + 2 * width + 2 * rows),
    )

    arrived = exchange(sent, "a").reshape(n_a * rows, width + LANES)
    arrived = spread(arrived, "core")
    place = (lax.axis_index("core") * n_a + lax.axis_index("a")).astype(jnp.int32).reshape(1)
    out, inner = run_forward(place, arrived, expert_full, experts, local_count)
    back, inner_grad, activation = run_backward(
        place, arrived, cot_group, expert_full, inner, experts, local_count
    )
    out = collect_aside(out, "core").astype(bf16).reshape(n_a, rows, width)
    back = collect(back, "core").astype(bf16)

    factors = (arrived, inner_grad, cot_group, activation)
    expert_grads = list(weight_grads(factors, n_e, n_r))
    back = exchange(back.reshape(n_a, rows, width + LANES), "a")
    received = send_grads(expert_grads, n_e, n_r, width)
    back, out, expert_grads[0] = lax.optimization_barrier((back, out, expert_grads[0]))
    out = exchange(out, "a")

    from_expert = reorder_matrix(expert, dense)
    dense_grad, input_grad = whole_call(
        functools.partial(home_backward, experts),
        [shape((width, qkv_width + width + LANES), bf16), shape((rows, width), bf16)],
        [
            back,
            from_expert,
            cot_dense,
            wide,
            dense_full,
            qkv,
            x_dense,
            cosine,
            sine,
            allowed,
        ],
        earlier=expert_grads[:1],
        flops=1,
        scratch=[pltpu.VMEM((rows, query_width), bf16), pltpu.VMEM((rows, qkv_width), bf16)],
    )
    dense_grad, out = lax.optimization_barrier((dense_grad, out))
    dense_grad = collect(dense_grad, "core").astype(bf16)
    dense_grad, *received = lax.optimization_barrier((dense_grad, *received))
    expert_grad = received[0].astype(f32)
    for part in received[1:]:
        expert_grad = expert_grad + part.astype(f32)
    expert_grad = expert_grad.astype(bf16).reshape(
        n_c * n_a, width // (n_r * n_c * n_a), 3 * FF
    )
    expert_grad = exchange_aside(
        pieces_for(expert_grad, ("core", "a")), ("core", "a")
    ).astype(f32)
    d_in = expert_grad[:, :, : 2 * FF]
    d_down = expert_grad[:, :, 2 * FF :]
    dense_grad = collect(dense_grad, ("r", "exp")).astype(bf16)
    from_dense = reorder_matrix(dense, home)
    mixed = dot_nn(out[0], from_expert)
    for index in range(1, n_a):
        mixed = mixed + dot_nn(out[index], from_expert)
    block_out = dot_nn((wide[:, :width] + mixed).astype(bf16), from_dense).astype(bf16)
    input_grad = dot_nn(input_grad, from_dense).astype(bf16)
    dense_grad, block_out, input_grad = lax.optimization_barrier(
        (dense_grad, block_out, input_grad)
    )
    dense_grad = exchange(dense_grad.reshape((n_a, local_rows) + dense_grad.shape[1:]), "a")

    dense_state = [
        qkv_weight,
        qkv_mean,
        qkv_square,
        out_weight,
        out_mean,
        out_square,
        router_weight.T,
        router_mean.T,
        router_square.T,
        norm_gains.T,
        gains_mean.T,
        gains_square.T,
    ]
    (
        new_qkv,
        new_qkv_mean,
        new_qkv_square,
        new_out,
        new_out_mean,
        new_out_square,
        new_router,
        new_router_mean,
        new_router_square,
        new_gains,
        new_gains_mean,
        new_gains_square,
    ) = whole_call(
        dense_update,
        [shape(item.shape, f32) for item in dense_state],
        [dense_grad] + dense_state,
        flops=20 * local_rows * (qkv_width + width),
    )
    new_router, new_router_mean, new_router_square = (
        item.T for item in (new_router, new_router_mean, new_router_square)
    )
    new_gains, new_gains_mean, new_gains_square = (
        item.T for item in (new_gains, new_gains_mean, new_gains_square)
    )
    new_in, new_in_mean, new_in_square = adamw(in_weight, d_in, in_mean, in_square, 0.1, decay_rate)
    new_down, new_down_mean, new_down_square = adamw(
        down_weight, d_down, down_mean, down_square, 1.0, decay_rate
    )
    return (
        block_out,
        input_grad,
        new_qkv,
        new_qkv_mean,
        new_qkv_square,
        new_out,
        new_out_mean,
        new_out_square,
        new_router,
        new_router_mean,
        new_router_square,
        new_gains,
        new_gains_mean,
        new_gains_square,
        new_in,
        new_in_mean,
        new_in_square,
        new_down,
        new_down_mean,
        new_down_square,
    )


def solution(mesh):
    n_dp, n_exp = mesh.shape["dp"], mesh.shape["exp"]
    n_a = EXPERTS // n_exp // 2
    mesh = Mesh(
        mesh.devices.reshape(n_a, n_dp // (2 * n_a), 2, n_exp), MESH_AXES
    )
    placed = (
        P(("a", "r", "core", "exp"), None),
        P(("a", "r", "core", "exp"), None),
        P(("a", "r", "core", "exp"), None),
        P(("a", "r", "core", "exp"), None),
        P(("a", "r", "core", "exp"), None),
        P(("a", "r", "core", "exp"), None),
        P(("a", "r", "core", "exp"), None),
        P(("a", "r", "core", "exp"), None),
        P(("a", "r", "core", "exp"), None),
        P(("a", "r", "core", "exp"), None),
        P(("a", "r", "core", "exp"), None),
        P(("a", "r", "core", "exp"), None),
        P(("a", "r", "core", "exp"), None),
        P(("a", "r", "core", "exp"), None),
        P(("a", "r", "core", "exp"), None),
        P(("a", "r", "core", "exp"), None),
        P("exp", ("a", "r", "core"), None),
        P("exp", ("a", "r", "core"), None),
        P("exp", ("a", "r", "core"), None),
        P("exp", ("a", "r", "core"), None),
        P("exp", ("a", "r", "core"), None),
        P("exp", ("a", "r", "core"), None),
    )
    return jax.shard_map(
        body,
        mesh=mesh,
        in_specs=placed,
        out_specs=(
            P(("a", "r", "core", "exp"), None),
            P(("a", "r", "core", "exp"), None),
            P(("a", "r", "core", "exp"), None),
            P(("a", "r", "core", "exp"), None),
            P(("a", "r", "core", "exp"), None),
            P(("a", "r", "core", "exp"), None),
            P(("a", "r", "core", "exp"), None),
            P(("a", "r", "core", "exp"), None),
            P(("a", "r", "core", "exp"), None),
            P(("a", "r", "core", "exp"), None),
            P(("a", "r", "core", "exp"), None),
            P(("a", "r", "core", "exp"), None),
            P(("a", "r", "core", "exp"), None),
            P(("a", "r", "core", "exp"), None),
            P("exp", ("a", "r", "core"), None),
            P("exp", ("a", "r", "core"), None),
            P("exp", ("a", "r", "core"), None),
            P("exp", ("a", "r", "core"), None),
            P("exp", ("a", "r", "core"), None),
            P("exp", ("a", "r", "core"), None),
        ),
        check_vma=False,
    )
```

```python
import functools
import math

import jax
import jax.numpy as jnp
import numpy as np
from jax import lax
from jax.experimental import pallas as pl
from jax.experimental.pallas import tpu as pltpu
from jax.sharding import Mesh
from jax.sharding import PartitionSpec as P

QUERY_HEADS = 16
KEY_VALUE_HEADS = 8
HEAD_DIMENSION = 64
FF = 512
STEP = 10
EXPERTS = 16
LANES = 128
MESH_AXES = ("a", "r", "core", "exp")
VMEM_BYTES = 26 * 1024 * 1024


norm_eps = 1e-06
rope_base = 10000.0
mask_fill = -1e30
beta_one = 0.9
beta_two = 0.95
adam_eps = 1e-08
decay_rate = 0.1


def rms_scale(values):
    return lax.rsqrt(jnp.mean(values * values, axis=-1, keepdims=True) + norm_eps)


def doc_layout(doc_lens, sequence_length):
    row_index = jnp.arange(sequence_length, dtype=jnp.int32)
    doc_ends = jnp.cumsum(doc_lens, dtype=jnp.int32)
    passed = (row_index[:, None] >= doc_ends[None, :]).astype(jnp.int32)
    segment = jnp.sum(passed, axis=1, dtype=jnp.int32)
    starts = jnp.sum(passed * doc_lens[None, :], axis=1, dtype=jnp.int32)
    return ((row_index - starts).astype(jnp.float32), segment)


def rope_tables(positions, head_size):
    half_size = head_size // 2
    freq_index = jnp.arange(half_size, dtype=jnp.float32)
    inverse = jnp.exp(freq_index * (-2.0 * math.log(rope_base) / head_size))
    angles = positions[:, None] * inverse[None, :]
    return (jnp.cos(angles), jnp.sin(angles))


def adamw(weight, gradient, mean_old, square_old, step_rate, weight_decay):
    mean_new = beta_one * mean_old + (1.0 - beta_one) * gradient
    square_new = beta_two * square_old + (1.0 - beta_two) * gradient * gradient
    corrected = (
        mean_new
        / (1.0 - beta_one**STEP)
        / (jnp.sqrt(square_new / (1.0 - beta_two**STEP)) + adam_eps)
    )
    return (weight - step_rate * (corrected + weight_decay * weight), mean_new, square_new)

def dot_nn(left, right):
    return jnp.dot(left, right, preferred_element_type=jnp.float32)


def dot_nt(left, right):
    return lax.dot_general(left, right, (((1,), (1,)), ((), ())), preferred_element_type=jnp.float32)


def dot_tn(left, right):
    return lax.dot_general(left, right, (((0,), (0,)), ((), ())), preferred_element_type=jnp.float32)


def lane_iota(rows):
    return lax.broadcasted_iota(jnp.int32, (rows, LANES), 1)


def gain_rows(extra, experts):
    row = lax.broadcasted_iota(jnp.int32, (8, LANES), 0)
    pick = (lane_iota(8) == row + experts).astype(jnp.bfloat16)
    return dot_nt(jnp.where(row < 2, pick, jnp.zeros_like(pick)), extra)


def swap_halves(values):
    half = HEAD_DIMENSION // 2
    lower = lane_iota(values.shape[0]) % HEAD_DIMENSION < half
    return jnp.where(lower, pltpu.roll(values, LANES - half, 1), pltpu.roll(values, half, 1))


def column_sums(values, lane):
    high = values.astype(jnp.bfloat16)
    low = (values - high.astype(jnp.float32)).astype(jnp.bfloat16)
    place = (lane_iota(values.shape[0]) == lane).astype(jnp.bfloat16)
    return dot_tn(high, place) + dot_tn(low, place)


def head_block(index):
    return slice(index * HEAD_DIMENSION, (index + 1) * HEAD_DIMENSION)


def attention_forward(
    experts,
    copies,
    x_ref,
    w_ref,
    cos_ref,
    sin_ref,
    allow_ref,
    used_ref,
    order_ref,
    wide_ref,
    qkv_ref,
    sent_ref,
):
    f32, bf16 = jnp.float32, jnp.bfloat16
    rows, width = x_ref.shape
    query_width = QUERY_HEADS * HEAD_DIMENSION
    key_width = KEY_VALUE_HEADS * HEAD_DIMENSION
    qkv_width = query_width + 2 * key_width
    extra = w_ref[:, qkv_width + width :]
    gains = gain_rows(extra, experts)
    x = x_ref[...].astype(f32)
    normed = (x * rms_scale(x) * gains[0:1]).astype(bf16)
    cosine, sine = cos_ref[...], sin_ref[...]
    for start in range(0, qkv_width, 512):
        part = dot_nn(normed, w_ref[:, start : start + 512])
        for inner in range(0, 512, LANES):
            piece = part[:, inner : inner + LANES]
            if start + inner < query_width + key_width:
                piece = piece * cosine + swap_halves(piece) * sine
            qkv_ref[:, start + inner : start + inner + LANES] = piece.astype(bf16)
    allowed = allow_ref[...] > 0.0
    lane = lane_iota(rows)
    logs = jnp.zeros((rows, LANES), f32)
    fold = QUERY_HEADS // KEY_VALUE_HEADS
    for group in range(KEY_VALUE_HEADS):
        keys = qkv_ref[:, query_width + group * HEAD_DIMENSION : query_width + (group + 1) * HEAD_DIMENSION]
        values = qkv_ref[
            :,
            query_width + key_width + group * HEAD_DIMENSION : query_width
            + key_width
            + (group + 1) * HEAD_DIMENSION,
        ]
        outs = []
        for head in range(group * fold, (group + 1) * fold):
            scores = dot_nt(qkv_ref[:, head_block(head)], keys) * HEAD_DIMENSION ** (-0.5)
            scores = jnp.where(allowed, scores, mask_fill)
            peak = jnp.max(scores, axis=1, keepdims=True)
            log_total = peak + jnp.log(jnp.sum(jnp.exp(scores - peak), axis=1, keepdims=True))
            logs = jnp.where(lane == head, log_total, logs)
            outs.append(dot_nn(jnp.exp(scores - log_total).astype(bf16), values))
        start = qkv_width + group * LANES
        qkv_ref[:, start : start + LANES] = jnp.concatenate(outs, axis=1).astype(bf16)
    wide_ref[:, width : width + LANES] = logs
    hidden = x + dot_nt(qkv_ref[:, qkv_width:], w_ref[:, qkv_width : qkv_width + width])
    wide_ref[:, :width] = hidden
    second = (hidden * rms_scale(hidden) * gains[1:2]).astype(bf16)
    used = used_ref[...] > 0.0
    logits = jnp.where(used, dot_nn(second, extra), mask_fill)
    powers = jnp.where(used, jnp.exp(logits - jnp.max(logits, axis=1, keepdims=True)), 0.0)
    gates = powers / jnp.sum(powers, axis=1, keepdims=True)
    wide_ref[:, width + LANES :] = gates
    high = gates.astype(bf16).astype(f32)
    lanes = (high + pltpu.roll(gates - high, experts, 1)).astype(bf16)
    moved = dot_nn(second, order_ref[...]).astype(bf16)
    for copy in range(copies):
        sent_ref[copy, :, :width] = moved
        sent_ref[copy, :, width:] = lanes


def own_gate(lanes, number, experts):
    lane = lane_iota(lanes.shape[0])
    chosen = (lane == number) | (lane == number + experts)
    return jnp.sum(jnp.where(chosen, lanes.astype(jnp.float32), 0.0), axis=1, keepdims=True)


def experts_forward(
    experts, local_count, place_ref, rows_ref, w_ref, out_ref, inner_ref, sum_ref
):
    f32, bf16 = jnp.float32, jnp.bfloat16
    index, chunk = pl.program_id(0), pl.program_id(1)
    count, width = out_ref.shape
    gate = own_gate(rows_ref[:, width:], index * local_count + place_ref[0], experts)
    inner = dot_nn(rows_ref[:, :width], w_ref[0, :, : 2 * FF])
    inner_ref[0] = inner
    gate_part = inner[:, :FF]
    activation = (gate_part * jax.nn.sigmoid(gate_part) * inner[:, FF:]).astype(bf16)
    result = dot_nt(activation, w_ref[0, :, 2 * FF :]).astype(bf16).astype(f32)
    here = pl.ds(pl.multiple_of(chunk * count, count), count)

    @pl.when(index == 0)
    def _():
        sum_ref[here, :] = gate * result

    @pl.when(index > 0)
    def _():
        sum_ref[here, :] += gate * result

    out_ref[...] = sum_ref[here, :].astype(bf16)


def experts_backward(
    experts,
    local_count,
    place_ref,
    gates_ref,
    cot_ref,
    w_ref,
    inner_ref,
    back_ref,
    inner_grad_ref,
    act_ref,
    sum_ref,
    dots_sum_ref,
):
    f32, bf16 = jnp.float32, jnp.bfloat16
    index, chunk = pl.program_id(0), pl.program_id(1)
    count, width = cot_ref.shape
    number = index * local_count + place_ref[0]
    gate = own_gate(gates_ref[...], number, experts)
    gate_part = inner_ref[0, :, :FF]
    up_part = inner_ref[0, :, FF:]
    gate_sigmoid = jax.nn.sigmoid(gate_part)
    gate_silu = gate_part * gate_sigmoid
    activation = (gate_silu * up_part).astype(bf16).astype(f32)
    act_ref[0] = (gate * activation).astype(bf16)
    act_grad = dot_nn(cot_ref[...], w_ref[0, :, 2 * FF :])
    dots = jnp.sum(activation * act_grad, axis=1, keepdims=True)
    dots_high = dots.astype(bf16).astype(f32)
    lane = lane_iota(count)
    lanes = jnp.where(lane == number, dots_high, 0.0) + jnp.where(
        lane == number + experts, dots - dots_high, 0.0
    )
    act_grad = gate * act_grad
    inner_grad_ref[0, :, :FF] = (
        act_grad * up_part * gate_sigmoid * (1.0 + gate_part * (1.0 - gate_sigmoid))
    ).astype(bf16)
    inner_grad_ref[0, :, FF:] = (act_grad * gate_silu).astype(bf16)
    copy_grad = dot_nt(inner_grad_ref[0], w_ref[0, :, : 2 * FF])
    here = pl.ds(pl.multiple_of(chunk * count, count), count)

    @pl.when(index == 0)
    def _():
        sum_ref[here, :] = copy_grad
        dots_sum_ref[here, :] = lanes

    @pl.when(index > 0)
    def _():
        sum_ref[here, :] += copy_grad
        dots_sum_ref[here, :] += lanes

    back_ref[:, :width] = sum_ref[here, :].astype(bf16)
    back_ref[:, width:] = dots_sum_ref[here, :].astype(bf16)


def experts_weights(where_ref, rows_ref, inner_grad_ref, cot_ref, act_ref, *grad_refs):
    goal = pl.program_id(0)
    inner = dot_tn(rows_ref[...], inner_grad_ref[0]).astype(jnp.bfloat16)
    down = dot_tn(cot_ref[...], act_ref[0]).astype(jnp.bfloat16)
    for index, grad_ref in enumerate(grad_refs):

        @pl.when(goal == index)
        def _(grad_ref=grad_ref):
            grad_ref[:, : 2 * FF] = inner
            grad_ref[:, 2 * FF :] = down


def home_backward(
    experts,
    parts_ref,
    order_ref,
    cot_ref,
    wide_ref,
    w_ref,
    qkv_ref,
    x_ref,
    cos_ref,
    sin_ref,
    allow_ref,
    grad_ref,
    input_grad_ref,
    mid_ref,
    proj_ref,
):
    f32, bf16 = jnp.float32, jnp.bfloat16
    rows, width = x_ref.shape
    sources = parts_ref.shape[0]
    query_width = QUERY_HEADS * HEAD_DIMENSION
    key_width = KEY_VALUE_HEADS * HEAD_DIMENSION
    qkv_width = query_width + 2 * key_width
    fold = QUERY_HEADS // KEY_VALUE_HEADS
    score_scale = HEAD_DIMENSION ** (-0.5)
    extra = w_ref[:, qkv_width + width :]
    gains = gain_rows(extra, experts)
    dots = jnp.zeros((rows, LANES), f32)
    second_grad = jnp.zeros((rows, width), f32)
    for source in range(sources):
        dots = dots + parts_ref[source, :, width:].astype(f32)
        second_grad = second_grad + dot_nn(parts_ref[source, :, :width], order_ref[...])
    dots = dots + pltpu.roll(dots, LANES - experts, 1)
    gates = wide_ref[:, width + LANES :]
    logit_grad = (gates * (dots - jnp.sum(gates * dots, axis=1, keepdims=True))).astype(bf16)
    second_grad = second_grad + dot_nt(logit_grad, extra)
    hidden = wide_ref[:, :width]
    scale = rms_scale(hidden)
    second = (hidden * scale * gains[1:2]).astype(bf16)
    scaled = second_grad * gains[1:2]
    hidden_grad = (
        cot_ref[...].astype(f32)
        + scale * scaled
        - hidden * (scale * scale * scale) * jnp.mean(scaled * hidden, axis=1, keepdims=True)
    )
    branch_grad = hidden_grad.astype(bf16)
    for start in range(0, width, 512):
        grad_ref[:, qkv_width + start : qkv_width + start + 512] = dot_tn(
            branch_grad, qkv_ref[:, qkv_width + start : qkv_width + start + 512]
        ).astype(bf16)
    small_grad = dot_tn(second, logit_grad) + column_sums(
        second_grad * hidden * scale, experts + 1
    )
    mid_ref[...] = dot_nn(branch_grad, w_ref[:, qkv_width : qkv_width + width]).astype(bf16)
    cosine, sine = cos_ref[...], sin_ref[...]
    allowed = allow_ref[...] > 0.0
    lane = lane_iota(rows)
    logs = wide_ref[:, width : width + LANES]

    def turned_back(values):
        return (values * cosine - swap_halves(values) * sine).astype(bf16)

    key_grads, value_grads = [], []
    for group in range(KEY_VALUE_HEADS):
        keys = qkv_ref[:, query_width + group * HEAD_DIMENSION : query_width + (group + 1) * HEAD_DIMENSION]
        values = qkv_ref[
            :,
            query_width + key_width + group * HEAD_DIMENSION : query_width
            + key_width
            + (group + 1) * HEAD_DIMENSION,
        ]
        query_grads = []
        key_grad = jnp.zeros((rows, HEAD_DIMENSION), f32)
        value_grad = jnp.zeros((rows, HEAD_DIMENSION), f32)
        for head in range(group * fold, (group + 1) * fold):
            queries = qkv_ref[:, head_block(head)]
            mid = mid_ref[:, head_block(head)]
            log_total = jnp.sum(jnp.where(lane == head, logs, 0.0), axis=1, keepdims=True)
            scores = jnp.where(allowed, dot_nt(queries, keys) * score_scale, mask_fill)
            weights = jnp.exp(scores - log_total)
            weight_grad = dot_nt(mid, values)
            delta = jnp.sum(weights * weight_grad, axis=1, keepdims=True)
            score_grad = (weights * (weight_grad - delta)).astype(bf16)
            query_grads.append(dot_nn(score_grad, keys) * score_scale)
            key_grad = key_grad + dot_tn(score_grad, queries)
            value_grad = value_grad + dot_tn(weights.astype(bf16), mid)
        proj_ref[:, group * LANES : (group + 1) * LANES] = turned_back(
            jnp.concatenate(query_grads, axis=1)
        )
        key_grads.append(key_grad * score_scale)
        value_grads.append(value_grad)
        if group % 2 == 1:
            start = query_width + (group // 2) * LANES
            proj_ref[:, start : start + LANES] = turned_back(
                jnp.concatenate(key_grads[-2:], axis=1)
            )
            start = start + key_width
            proj_ref[:, start : start + LANES] = jnp.concatenate(value_grads[-2:], axis=1).astype(
                bf16
            )
    x = x_ref[...].astype(f32)
    scale = rms_scale(x)
    normed = (x * scale * gains[0:1]).astype(bf16)
    for start in range(0, qkv_width, 512):
        grad_ref[:, start : start + 512] = dot_tn(normed, proj_ref[:, start : start + 512]).astype(
            bf16
        )
    normed_grad = dot_nt(proj_ref[...], w_ref[:, :qkv_width])
    scaled = normed_grad * gains[0:1]
    small_grad = small_grad + column_sums(normed_grad * x * scale, experts)
    grad_ref[:, qkv_width + width :] = small_grad.astype(bf16)
    input_grad_ref[...] = (
        hidden_grad
        + scale * scaled
        - x * (scale * scale * scale) * jnp.mean(scaled * x, axis=1, keepdims=True)
    ).astype(bf16)


def dense_update(parts_ref, *refs):
    total = parts_ref[0].astype(jnp.float32)
    for source in range(1, parts_ref.shape[0]):
        total = total + parts_ref[source].astype(jnp.float32)
    start = total.shape[1] - LANES
    small = jnp.transpose(total[:, start:])
    experts = refs[6].shape[0]
    qkv_width = refs[0].shape[1]
    grads = (
        total[:, :qkv_width],
        total[:, qkv_width:start],
        small[:experts],
        small[experts : experts + 2],
    )
    rates = ((0.15, decay_rate), (0.3, decay_rate), (0.05, decay_rate), (0.8, 0.0))
    for index, (rate, decay) in enumerate(rates):
        weight_ref, mean_ref, square_ref = refs[3 * index : 3 * index + 3]
        values = adamw(weight_ref[...], grads[index], mean_ref[...], square_ref[...], rate, decay)
        for out_ref, value in zip(refs[3 * index + 12 : 3 * index + 15], values):
            out_ref[...] = value


def whole_call(kernel, outputs, operands, flops, scratch=(), earlier=()):
    operands_read = len(operands)

    def run(*refs):
        kernel(*refs[:operands_read], *refs[operands_read + len(earlier) :])

    moved = sum(math.prod(item.shape) * item.dtype.itemsize for item in list(outputs) + list(operands))
    moved = moved if flops > 1 else 1
    return pl.pallas_call(
        run,
        out_shape=outputs,
        in_specs=[pl.BlockSpec(memory_space=pltpu.VMEM)] * len(operands)
        + [pl.BlockSpec(memory_space=pl.ANY)] * len(earlier),
        out_specs=[pl.BlockSpec(memory_space=pltpu.VMEM)] * len(outputs),
        scratch_shapes=list(scratch),
        compiler_params=pltpu.CompilerParams(vmem_limit_bytes=VMEM_BYTES),
        cost_estimate=pl.CostEstimate(flops=flops, bytes_accessed=moved, transcendentals=0),
    )(*operands, *earlier)


def order_of(kind, sizes):
    axes = {"home": (0, 1, 2, 3, 4), "dense": (2, 1, 3, 0, 4), "expert": (1, 2, 0, 3, 4)}[kind]
    return np.arange(math.prod(sizes), dtype=np.int32).reshape(sizes).transpose(axes).reshape(-1)


def reorder_matrix(before, after):
    return (jnp.asarray(before)[:, None] == jnp.asarray(after)[None, :]).astype(jnp.bfloat16)


def exchange(values, axes):
    return lax.all_to_all(values, axes, split_axis=0, concat_axis=0, tiled=True)


def spread(values, axes):
    count = lax.axis_size(axes)
    copies = exchange(jnp.broadcast_to(values[None], (count,) + values.shape), axes)
    return copies.reshape((count * values.shape[0],) + values.shape[1:])


def collect(values, axes):
    count = lax.axis_size(axes)
    parts = exchange(values.reshape((count, values.shape[0] // count) + values.shape[1:]), axes)
    total = parts[0].astype(jnp.float32)
    for index in range(1, count):
        total = total + parts[index].astype(jnp.float32)
    return total


def partner(values, axes, step):
    names = (axes,) if isinstance(axes, str) else axes
    steps = {}
    for name in reversed(names):
        step, steps[name] = divmod(step, lax.axis_size(name))
    names = tuple(name for name in MESH_AXES if name in names)
    flat = 0
    for name in names:
        flat = flat * lax.axis_size(name) + steps[name]
    pairs = [(index, index ^ flat) for index in range(lax.axis_size(names))]
    return lax.ppermute(values, names, pairs)


def piece_of(values, index):
    return lax.dynamic_index_in_dim(values, index, 0, keepdims=False)


def in_order(own, received, me):
    result = jnp.zeros((len(received) + 1,) + own.shape, own.dtype)
    for step, part in enumerate([own] + received):
        result = lax.dynamic_update_index_in_dim(result, part, me ^ step, 0)
    return result


def spread_aside(values, axes):
    count = lax.axis_size(axes)
    received = [partner(values, axes, step) for step in range(1, count)]
    result = in_order(values, received, lax.axis_index(axes))
    return result.reshape((count * values.shape[0],) + values.shape[1:])


def pieces_for(values, axes):
    me = lax.axis_index(axes)
    return [piece_of(values, me ^ step) for step in range(values.shape[0])]


def exchange_aside(pieces, axes):
    received = [partner(piece, axes, step) for step, piece in enumerate(pieces) if step > 0]
    return in_order(pieces[0], received, lax.axis_index(axes))


def collect_aside(values, axes):
    count = lax.axis_size(axes)
    pieces = pieces_for(values.reshape((count, values.shape[0] // count) + values.shape[1:]), axes)
    total = pieces[0].astype(jnp.float32)
    for step in range(1, count):
        total = total + partner(pieces[step], axes, step).astype(jnp.float32)
    return total


def expert_specs(n_e, group_rows, width):
    count = min(256, group_rows)
    return dict(
        grid=(n_e, group_rows // count),
        scalar=pl.BlockSpec(memory_space=pltpu.SMEM),
        wide=pl.BlockSpec((count, width), lambda k, i: (i, 0)),
        wider=pl.BlockSpec((count, width + LANES), lambda k, i: (i, 0)),
        lanes=pl.BlockSpec((count, LANES), lambda k, i: (i, width // LANES)),
        weight=pl.BlockSpec((1, width, 3 * FF), lambda k, i: (k, 0, 0)),
        inner=pl.BlockSpec((1, count, 2 * FF), lambda k, i: (k, i, 0)),
        act=pl.BlockSpec((1, count, FF), lambda k, i: (k, i, 0)),
    )


def run_forward(place, arrived, expert_full, experts, local_count):
    n_e, width, _ = expert_full.shape
    group_rows = arrived.shape[0]
    specs = expert_specs(n_e, group_rows, width)
    return pl.pallas_call(
        functools.partial(experts_forward, experts, local_count),
        grid=specs["grid"],
        out_shape=[
            jax.ShapeDtypeStruct((group_rows, width), jnp.bfloat16),
            jax.ShapeDtypeStruct((n_e, group_rows, 2 * FF), jnp.float32),
        ],
        in_specs=[specs["scalar"], specs["wider"], specs["weight"]],
        out_specs=[specs["wide"], specs["inner"]],
        scratch_shapes=[pltpu.VMEM((group_rows, width), jnp.float32)],
        compiler_params=pltpu.CompilerParams(vmem_limit_bytes=VMEM_BYTES),
        cost_estimate=pl.CostEstimate(
            flops=2 * n_e * group_rows * width * 3 * FF,
            bytes_accessed=n_e * width * (3 * FF * 2 + group_rows * 8),
            transcendentals=n_e * group_rows * FF,
        ),
    )(place, arrived, expert_full)


def run_backward(place, arrived, cot_group, expert_full, inner, experts, local_count):
    bf16 = jnp.bfloat16
    n_e, width, _ = expert_full.shape
    group_rows = arrived.shape[0]
    specs = expert_specs(n_e, group_rows, width)
    return pl.pallas_call(
        functools.partial(experts_backward, experts, local_count),
        grid=specs["grid"],
        out_shape=[
            jax.ShapeDtypeStruct((group_rows, width + LANES), bf16),
            jax.ShapeDtypeStruct((n_e, group_rows, 2 * FF), bf16),
            jax.ShapeDtypeStruct((n_e, group_rows, FF), bf16),
        ],
        in_specs=[
            specs["scalar"],
            specs["lanes"],
            specs["wide"],
            specs["weight"],
            specs["inner"],
        ],
        out_specs=[specs["wider"], specs["inner"], specs["act"]],
        scratch_shapes=[
            pltpu.VMEM((group_rows, width), jnp.float32),
            pltpu.VMEM((group_rows, LANES), jnp.float32),
        ],
        compiler_params=pltpu.CompilerParams(vmem_limit_bytes=VMEM_BYTES),
        cost_estimate=pl.CostEstimate(
            flops=2 * n_e * group_rows * width * 3 * FF,
            bytes_accessed=n_e * width * (3 * FF * 2 + group_rows * 10),
            transcendentals=n_e * group_rows * FF,
        ),
    )(place, arrived, cot_group, expert_full, inner)


def run_weights(arrived, inner_grad, cot_group, act, slots, firsts, blocks, part):
    group_rows = arrived.shape[0]
    goals = len(slots)
    where = jnp.stack(slots + firsts).astype(jnp.int32)

    def block_of(index):
        return lambda g, j, at: (jnp.where(g == index, j, jnp.where(g < index, 0, blocks - 1)), 0)

    return pl.pallas_call(
        experts_weights,
        grid_spec=pltpu.PrefetchScalarGridSpec(
            num_scalar_prefetch=1,
            grid=(goals, blocks),
            in_specs=[
                pl.BlockSpec((group_rows, part), lambda g, j, at: (0, at[goals + g] + j)),
                pl.BlockSpec((1, group_rows, 2 * FF), lambda g, j, at: (at[g], 0, 0)),
                pl.BlockSpec((group_rows, part), lambda g, j, at: (0, at[goals + g] + j)),
                pl.BlockSpec((1, group_rows, FF), lambda g, j, at: (at[g], 0, 0)),
            ],
            out_specs=[pl.BlockSpec((part, 3 * FF), block_of(index)) for index in range(goals)],
        ),
        out_shape=[jax.ShapeDtypeStruct((blocks * part, 3 * FF), jnp.bfloat16)] * goals,
        compiler_params=pltpu.CompilerParams(vmem_limit_bytes=VMEM_BYTES),
        cost_estimate=pl.CostEstimate(
            flops=2 * goals * blocks * part * group_rows * 3 * FF,
            bytes_accessed=goals * (group_rows * 6 * FF + blocks * part * (group_rows * 4 + 6 * FF)),
            transcendentals=0,
        ),
    )(where, arrived, inner_grad, cot_group, act)


def in_pieces(n_e, n_r, width):
    return n_e * n_r <= 8 and width // n_r % min(256, width) == 0


def weight_grads(factors, n_e, n_r):
    width = factors[2].shape[1]
    part = min(256, width)
    if in_pieces(n_e, n_r, width):
        me = lax.axis_index(("exp", "r"))
        blocks = width // n_r // part
        goals = [me ^ step for step in range(n_e * n_r)]
        slots = [goal // n_r for goal in goals]
        firsts = [goal % n_r * blocks for goal in goals]
        return run_weights(*factors, slots, firsts, blocks, part)
    grads = []
    for slot in range(n_e):
        grads += run_weights(*factors, [jnp.int32(slot)], [jnp.int32(0)], width // part, part)
    return grads


def send_grads(grads, n_e, n_r, width):
    axes = ("exp", "r")
    if not in_pieces(n_e, n_r, width):
        grads = jnp.concatenate(grads, axis=0)
        return list(exchange(grads.reshape((n_e * n_r, -1) + grads.shape[1:]), axes))
    return [grads[0]] + [
        partner(grads[step], axes, step) for step in reversed(range(1, len(grads)))
    ]


def body(
    tokens,
    cotangent,
    doc_lengths,
    routes,
    qkv_weight,
    qkv_mean,
    qkv_square,
    out_weight,
    out_mean,
    out_square,
    router_weight,
    router_mean,
    router_square,
    norm_gains,
    gains_mean,
    gains_square,
    in_weight,
    in_mean,
    in_square,
    down_weight,
    down_mean,
    down_square,
):
    f32, bf16 = jnp.float32, jnp.bfloat16
    shape = jax.ShapeDtypeStruct
    n_a, n_r, n_c, n_e = (lax.axis_size(name) for name in ("a", "r", "core", "exp"))
    rows, width = tokens.shape
    experts = router_weight.shape[1]
    local_count = in_weight.shape[0]
    sizes = (n_a, n_r, n_c, n_e, width // (n_a * n_r * n_c * n_e))
    home, dense, expert = (order_of(kind, sizes) for kind in ("home", "dense", "expert"))
    query_width = QUERY_HEADS * HEAD_DIMENSION
    qkv_width = query_width + 2 * KEY_VALUE_HEADS * HEAD_DIMENSION

    local_rows = qkv_weight.shape[0]
    extra = jnp.zeros((local_rows, LANES - experts - 2), bf16)
    pack = jnp.concatenate(
        [
            qkv_weight.astype(bf16),
            out_weight.astype(bf16),
            router_weight.astype(bf16),
            norm_gains.astype(bf16),
            extra,
        ],
        axis=1,
    )
    pack = spread(pack, "a")

    to_dense = reorder_matrix(home, dense)
    x_dense = dot_nn(tokens, to_dense).astype(bf16)
    cot_dense = dot_nn(cotangent, to_dense).astype(bf16)
    positions, segment = doc_layout(doc_lengths.reshape(-1), rows)
    cosine, sine = rope_tables(positions, HEAD_DIMENSION)
    repeat = LANES // HEAD_DIMENSION
    cosine = jnp.concatenate([cosine, cosine] * repeat, axis=1)
    sine = jnp.concatenate([-sine, sine] * repeat, axis=1)
    row_index = jnp.arange(rows, dtype=jnp.int32)
    allowed = (segment[:, None] == segment[None, :]) & (row_index[None, :] <= row_index[:, None])
    allowed = allowed.astype(f32)
    used = jnp.any(
        routes[:, :, None] == jnp.arange(LANES, dtype=jnp.int32)[None, None, :], axis=1
    ).astype(f32)

    cot_expert = dot_nn(cotangent, reorder_matrix(home, expert)).astype(bf16)
    expert_pack = jnp.concatenate([in_weight.astype(bf16), down_weight.astype(bf16)], axis=2)
    to_expert = reorder_matrix(dense, expert)
    pieces = pieces_for(expert_pack, ("core", "a"))
    pack, x_dense, cot_dense, cosine, sine, allowed, used, to_expert, *pieces = (
        lax.optimization_barrier(
            (pack, x_dense, cot_dense, cosine, sine, allowed, used, to_expert, *pieces)
        )
    )
    pack = spread(pack, ("r", "exp"))
    expert_pack = exchange_aside(pieces, ("core", "a"))
    pack, expert_pack = lax.optimization_barrier((pack, expert_pack))
    cot_expert, expert_pack = lax.optimization_barrier((cot_expert, expert_pack))
    cot_group = spread_aside(spread_aside(cot_expert, "a"), "core")
    expert_full = lax.all_gather(expert_pack, ("exp", "r"), axis=0, tiled=True).reshape(
        n_e, width, 3 * FF
    )
    dense_full = spread(pack, "core")

    wide, qkv, sent = whole_call(
        functools.partial(attention_forward, experts, n_a),
        [
            shape((rows, width + 2 * LANES), f32),
            shape((rows, qkv_width + query_width), bf16),
            shape((n_a, rows, width + LANES), bf16),
        ],
        [x_dense, dense_full, cosine, sine, allowed, used, to_expert],
        flops=2 * rows * width * (qkv_width + 2 * width + 2 * rows),
    )

    arrived = exchange(sent, "a").reshape(n_a * rows, width + LANES)
    arrived = spread(arrived, "core")
    place = (lax.axis_index("core") * n_a + lax.axis_index("a")).astype(jnp.int32).reshape(1)
    out, inner = run_forward(place, arrived, expert_full, experts, local_count)
    back, inner_grad, activation = run_backward(
        place, arrived, cot_group, expert_full, inner, experts, local_count
    )
    out = collect_aside(out, "core").astype(bf16).reshape(n_a, rows, width)
    back = collect(back, "core").astype(bf16)

    factors = (arrived, inner_grad, cot_group, activation)
    expert_grads = list(weight_grads(factors, n_e, n_r))
    back = exchange(back.reshape(n_a, rows, width + LANES), "a")
    received = send_grads(expert_grads, n_e, n_r, width)
    back, out, expert_grads[0] = lax.optimization_barrier((back, out, expert_grads[0]))
    out = exchange(out, "a")

    from_expert = reorder_matrix(expert, dense)
    dense_grad, input_grad = whole_call(
        functools.partial(home_backward, experts),
        [shape((width, qkv_width + width + LANES), bf16), shape((rows, width), bf16)],
        [
            back,
            from_expert,
            cot_dense,
            wide,
            dense_full,
            qkv,
            x_dense,
            cosine,
            sine,
            allowed,
        ],
        earlier=expert_grads[:1],
        flops=1,
        scratch=[pltpu.VMEM((rows, query_width), bf16), pltpu.VMEM((rows, qkv_width), bf16)],
    )
    dense_grad, out = lax.optimization_barrier((dense_grad, out))
    dense_grad = collect(dense_grad, "core").astype(bf16)
    dense_grad, *received = lax.optimization_barrier((dense_grad, *received))
    expert_grad = received[0].astype(f32)
    for part in received[1:]:
        expert_grad = expert_grad + part.astype(f32)
    expert_grad = expert_grad.astype(bf16).reshape(
        n_c * n_a, width // (n_r * n_c * n_a), 3 * FF
    )
    expert_grad = exchange_aside(
        pieces_for(expert_grad, ("core", "a")), ("core", "a")
    ).astype(f32)
    d_in = expert_grad[:, :, : 2 * FF]
    d_down = expert_grad[:, :, 2 * FF :]
    dense_grad = collect(dense_grad, ("r", "exp")).astype(bf16)
    from_dense = reorder_matrix(dense, home)
    mixed = dot_nn(out[0], from_expert)
    for index in range(1, n_a):
        mixed = mixed + dot_nn(out[index], from_expert)
    block_out = dot_nn((wide[:, :width] + mixed).astype(bf16), from_dense).astype(bf16)
    input_grad = dot_nn(input_grad, from_dense).astype(bf16)
    dense_grad, block_out, input_grad = lax.optimization_barrier(
        (dense_grad, block_out, input_grad)
    )
    dense_grad = exchange(dense_grad.reshape((n_a, local_rows) + dense_grad.shape[1:]), "a")

    dense_state = [
        qkv_weight,
        qkv_mean,
        qkv_square,
        out_weight,
        out_mean,
        out_square,
        router_weight.T,
        router_mean.T,
        router_square.T,
        norm_gains.T,
        gains_mean.T,
        gains_square.T,
    ]
    (
        new_qkv,
        new_qkv_mean,
        new_qkv_square,
        new_out,
        new_out_mean,
        new_out_square,
        new_router,
        new_router_mean,
        new_router_square,
        new_gains,
        new_gains_mean,
        new_gains_square,
    ) = whole_call(
        dense_update,
        [shape(item.shape, f32) for item in dense_state],
        [dense_grad] + dense_state,
        flops=20 * local_rows * (qkv_width + width),
    )
    new_router, new_router_mean, new_router_square = (
        item.T for item in (new_router, new_router_mean, new_router_square)
    )
    new_gains, new_gains_mean, new_gains_square = (
        item.T for item in (new_gains, new_gains_mean, new_gains_square)
    )
    new_in, new_in_mean, new_in_square = adamw(in_weight, d_in, in_mean, in_square, 0.1, decay_rate)
    new_down, new_down_mean, new_down_square = adamw(
        down_weight, d_down, down_mean, down_square, 1.0, decay_rate
    )
    return (
        block_out,
        input_grad,
        new_qkv,
        new_qkv_mean,
        new_qkv_square,
        new_out,
        new_out_mean,
        new_out_square,
        new_router,
        new_router_mean,
        new_router_square,
        new_gains,
        new_gains_mean,
        new_gains_square,
        new_in,
        new_in_mean,
        new_in_square,
        new_down,
        new_down_mean,
        new_down_square,
    )


def attend_heads(experts, x_ref, w_ref, table_ref, allow_ref, qkv_ref, lse_ref, att_ref):
    f32, bf16 = jnp.float32, jnp.bfloat16
    rows = x_ref.shape[0]
    width = w_ref.shape[0]
    gains = gain_rows(w_ref[:, 2 * LANES :], experts)
    x = x_ref[:, :width].astype(f32)
    normed = (x * rms_scale(x) * gains[0:1]).astype(bf16)
    projected = dot_nn(normed, w_ref[:, : 2 * LANES])
    lane = lane_iota(rows)
    cosine, sine = table_ref[:, :LANES], table_ref[:, LANES:]
    queries, others = projected[:, :LANES], projected[:, LANES:]
    turned = others * cosine + swap_halves(others) * sine
    qkv_ref[:, :LANES] = (queries * cosine + swap_halves(queries) * sine).astype(bf16)
    qkv_ref[:, LANES:] = jnp.where(lane < HEAD_DIMENSION, turned, others).astype(bf16)
    keys = qkv_ref[:, LANES : LANES + HEAD_DIMENSION]
    values = qkv_ref[:, LANES + HEAD_DIMENSION :]
    allowed = allow_ref[0] > 0.0
    logs = jnp.zeros((rows, LANES), f32)
    outs = []
    for head in range(QUERY_HEADS // KEY_VALUE_HEADS):
        scores = dot_nt(qkv_ref[:, head_block(head)], keys) * HEAD_DIMENSION ** (-0.5)
        scores = jnp.where(allowed, scores, mask_fill)
        peak = jnp.max(scores, axis=1, keepdims=True)
        log_total = peak + jnp.log(jnp.sum(jnp.exp(scores - peak), axis=1, keepdims=True))
        logs = jnp.where(lane == head, log_total, logs)
        outs.append(dot_nn(jnp.exp(scores - log_total).astype(bf16), values))
    lse_ref[...] = logs
    att_ref[0] = jnp.concatenate(outs, axis=1).astype(bf16)


def home_forward(
    experts, copies, x_ref, att_ref, out_ref, extra_ref, used_ref, order_ref, wide_ref, sent_ref
):
    f32, bf16 = jnp.float32, jnp.bfloat16
    width = x_ref.shape[1]
    extra = extra_ref[...]
    hidden = x_ref[...].astype(f32)
    for place in range(att_ref.shape[0]):
        hidden = hidden + dot_nt(att_ref[place], out_ref[:, place * LANES : (place + 1) * LANES])
    wide_ref[:, :width] = hidden
    second = (hidden * rms_scale(hidden) * gain_rows(extra, experts)[1:2]).astype(bf16)
    used = used_ref[...] > 0.0
    logits = jnp.where(used, dot_nn(second, extra), mask_fill)
    powers = jnp.where(used, jnp.exp(logits - jnp.max(logits, axis=1, keepdims=True)), 0.0)
    gates = powers / jnp.sum(powers, axis=1, keepdims=True)
    wide_ref[:, width:] = gates
    high = gates.astype(bf16).astype(f32)
    lanes = (high + pltpu.roll(gates - high, experts, 1)).astype(bf16)
    moved = dot_nn(second, order_ref[...]).astype(bf16)
    for copy in range(copies):
        sent_ref[copy, :, :width] = moved
        sent_ref[copy, :, width:] = lanes


def home_back(
    experts,
    parts_ref,
    order_ref,
    cot_ref,
    wide_ref,
    extra_ref,
    out_ref,
    att_ref,
    split_ref,
    hidden_grad_ref,
    mid_ref,
    grad_ref,
):
    f32, bf16 = jnp.float32, jnp.bfloat16
    rows, width = cot_ref.shape
    extra = extra_ref[...]
    split = split_ref[...]
    dots = jnp.zeros((rows, LANES), f32)
    second_grad = jnp.zeros((rows, width), f32)
    for source in range(parts_ref.shape[0]):
        dots = dots + parts_ref[source, :, width:].astype(f32)
        second_grad = second_grad + dot_nn(parts_ref[source, :, :width], order_ref[...])
    dots = dots + pltpu.roll(dots, LANES - experts, 1)
    gates = wide_ref[:, width:]
    logit_grad = (gates * (dots - jnp.sum(gates * dots, axis=1, keepdims=True))).astype(bf16)
    second_grad = second_grad + dot_nt(logit_grad, extra)
    gain = gain_rows(extra, experts)[1:2]
    hidden = wide_ref[:, :width]
    scale = rms_scale(hidden)
    scaled = second_grad * gain
    hidden_grad = (
        cot_ref[...].astype(f32)
        + scale * scaled
        - hidden * (scale * scale * scale) * jnp.mean(scaled * hidden, axis=1, keepdims=True)
    )
    hidden_grad_ref[...] = hidden_grad
    branch_grad = hidden_grad.astype(bf16)
    branch_split = dot_nn(branch_grad, split).astype(bf16)
    for place in range(att_ref.shape[0]):
        columns = slice(place * LANES, (place + 1) * LANES)
        mid_ref[place] = dot_nn(branch_grad, out_ref[:, columns]).astype(bf16)
        grad_ref[:, columns] = dot_tn(branch_split, att_ref[place]).astype(bf16)
    second = dot_nn((hidden * scale * gain).astype(bf16), split).astype(bf16)
    sums = second_grad * hidden * scale
    high = sums.astype(bf16)
    low = (sums - high.astype(f32)).astype(bf16)
    place = (lane_iota(rows) == experts + 1).astype(bf16)
    grad_ref[:, width:] = (
        dot_tn(second, logit_grad)
        + dot_tn(dot_nn(high, split).astype(bf16), place)
        + dot_tn(dot_nn(low, split).astype(bf16), place)
    ).astype(bf16)


def heads_back(
    experts,
    x_ref,
    w_ref,
    table_ref,
    allow_ref,
    qkv_ref,
    lse_ref,
    mid_ref,
    grad_ref,
    normed_grad_ref,
    normed_ref,
    proj_ref,
    sums_ref,
):
    f32, bf16 = jnp.float32, jnp.bfloat16
    block = pl.program_id(0)
    rows = x_ref.shape[0]
    width = w_ref.shape[0]
    score_scale = HEAD_DIMENSION ** (-0.5)
    here = pl.ds(pl.multiple_of(block * rows, rows), rows)
    gains = gain_rows(w_ref[:, 2 * LANES :], experts)
    x = x_ref[:, :width].astype(f32)
    scale = rms_scale(x)
    normed_ref[here, :] = (x * scale * gains[0:1]).astype(bf16)
    keys = qkv_ref[:, LANES : LANES + HEAD_DIMENSION]
    values = qkv_ref[:, LANES + HEAD_DIMENSION :]
    allowed = allow_ref[0] > 0.0
    lane = lane_iota(rows)
    logs = lse_ref[...]
    query_grads = []
    key_grad = jnp.zeros((rows, HEAD_DIMENSION), f32)
    value_grad = jnp.zeros((rows, HEAD_DIMENSION), f32)
    for head in range(QUERY_HEADS // KEY_VALUE_HEADS):
        queries = qkv_ref[:, head_block(head)]
        mid = mid_ref[0, :, head_block(head)]
        log_total = jnp.sum(jnp.where(lane == head, logs, 0.0), axis=1, keepdims=True)
        scores = jnp.where(allowed, dot_nt(queries, keys) * score_scale, mask_fill)
        weights = jnp.exp(scores - log_total)
        weight_grad = dot_nt(mid, values)
        delta = jnp.sum(weights * weight_grad, axis=1, keepdims=True)
        score_grad = (weights * (weight_grad - delta)).astype(bf16)
        query_grads.append(dot_nn(score_grad, keys) * score_scale)
        key_grad = key_grad + dot_tn(score_grad, queries)
        value_grad = value_grad + dot_tn(weights.astype(bf16), mid)
    cosine, sine = table_ref[:, :LANES], table_ref[:, LANES:]
    queries = jnp.concatenate(query_grads, axis=1)
    others = jnp.concatenate([key_grad * score_scale, value_grad], axis=1)
    turned = others * cosine - swap_halves(others) * sine
    queries = (queries * cosine - swap_halves(queries) * sine).astype(bf16)
    others = jnp.where(lane < HEAD_DIMENSION, turned, others).astype(bf16)
    proj_ref[here, :] = jnp.concatenate([queries, others], axis=1)
    normed_grad = dot_nt(proj_ref[here, :], w_ref[:, : 2 * LANES])
    normed_grad_ref[0] = normed_grad.astype(bf16)
    sums = normed_grad * x * scale

    @pl.when(block == 0)
    def _():
        sums_ref[...] = sums

    @pl.when(block > 0)
    def _():
        sums_ref[...] += sums

    @pl.when(block == pl.num_programs(0) - 1)
    def _():
        grad_ref[:, : 2 * LANES] = dot_tn(normed_ref[...], proj_ref[...]).astype(bf16)
        grad_ref[:, 2 * LANES :] = column_sums(sums_ref[...], experts).astype(bf16)


def heads_update(places, qkv_parts_ref, out_parts_ref, *refs):
    f32 = jnp.float32
    sources = qkv_parts_ref.shape[0]
    totals = []
    for place in range(places):
        total = qkv_parts_ref[place].astype(f32)
        for source in range(place + places, sources, places):
            total = total + qkv_parts_ref[source].astype(f32)
        totals.append(total)
    out_total = out_parts_ref[0].astype(f32)
    for source in range(1, out_parts_ref.shape[0]):
        out_total = out_total + out_parts_ref[source].astype(f32)
    width = refs[3].shape[1]
    experts = refs[6].shape[0]
    small = out_total[:, width:]
    for total in totals:
        small = small + total[:, 2 * LANES :]
    small = jnp.transpose(small)
    middle = LANES + HEAD_DIMENSION
    qkv_grad = jnp.concatenate(
        [total[:, :LANES] for total in totals]
        + [total[:, LANES:middle] for total in totals]
        + [total[:, middle : 2 * LANES] for total in totals],
        axis=1,
    )
    grads = (qkv_grad, out_total[:, :width], small[:experts], small[experts : experts + 2])
    rates = ((0.15, decay_rate), (0.3, decay_rate), (0.05, decay_rate), (0.8, 0.0))
    for index, (rate, decay) in enumerate(rates):
        weight_ref, mean_ref, square_ref = refs[3 * index : 3 * index + 3]
        values = adamw(weight_ref[...], grads[index], mean_ref[...], square_ref[...], rate, decay)
        for out_ref, value in zip(refs[3 * index + 12 : 3 * index + 15], values):
            out_ref[...] = value


def block_call(kernel, blocks, inputs, outputs, operands, scratch, flops):
    def spec(shape, place):
        rank = len(shape)
        if place is None:
            return pl.BlockSpec(shape, lambda i: (0,) * rank)
        return pl.BlockSpec(shape, lambda i: (place(i),) + (0,) * (rank - 1))

    moved = sum(math.prod(item.shape) * item.dtype.itemsize for item in operands)
    return pl.pallas_call(
        kernel,
        grid=(blocks,),
        out_shape=[item for item, _, _ in outputs],
        in_specs=[spec(shape, place) for shape, place in inputs],
        out_specs=[spec(shape, place) for _, shape, place in outputs],
        scratch_shapes=scratch,
        compiler_params=pltpu.CompilerParams(vmem_limit_bytes=VMEM_BYTES),
        cost_estimate=pl.CostEstimate(flops=flops, bytes_accessed=moved, transcendentals=0),
    )(*operands)


def body_heads(
    tokens,
    cotangent,
    doc_lengths,
    routes,
    qkv_weight,
    qkv_mean,
    qkv_square,
    out_weight,
    out_mean,
    out_square,
    router_weight,
    router_mean,
    router_square,
    norm_gains,
    gains_mean,
    gains_square,
    in_weight,
    in_mean,
    in_square,
    down_weight,
    down_mean,
    down_square,
):
    f32, bf16 = jnp.float32, jnp.bfloat16
    shape = jax.ShapeDtypeStruct
    plane = ("r", "core", "exp")
    n_a, n_r, n_c, n_e = (lax.axis_size(name) for name in MESH_AXES)
    places = n_r * n_c * n_e
    rows, width = tokens.shape
    experts = router_weight.shape[1]
    local_count = in_weight.shape[0]
    local_rows = qkv_weight.shape[0]
    sizes = (n_a, n_r, n_c, n_e, local_rows)
    home, expert, split = (order_of(kind, sizes) for kind in ("home", "expert", "dense"))
    query_width = QUERY_HEADS * HEAD_DIMENSION
    key_width = KEY_VALUE_HEADS * HEAD_DIMENSION
    lines = places * local_rows

    positions, segment = doc_layout(doc_lengths.reshape(-1), rows)
    marks = jnp.stack([positions, segment.astype(f32)], axis=1).astype(bf16)
    marks = jnp.concatenate([marks, jnp.zeros((rows, LANES - 2), bf16)], axis=1)
    x_all = lax.all_gather(jnp.concatenate([tokens, marks], axis=1), plane, axis=0, tiled=True)

    def by_place(values, start, stop):
        return values[:, start:stop].reshape(local_rows, places, (stop - start) // places)

    qkv_low = qkv_weight.astype(bf16)
    extra = jnp.concatenate(
        [
            router_weight.astype(bf16),
            norm_gains.astype(bf16),
            jnp.zeros((local_rows, LANES - experts - 2), bf16),
        ],
        axis=1,
    )
    pack = jnp.concatenate(
        [
            by_place(qkv_low, 0, query_width),
            by_place(qkv_low, query_width, query_width + key_width),
            by_place(qkv_low, query_width + key_width, query_width + 2 * key_width),
            jnp.broadcast_to(extra[:, None], (local_rows, places, LANES)),
        ],
        axis=2,
    )
    pack = exchange(pack.transpose(1, 0, 2), plane).reshape(lines, 3 * LANES)
    pack = jnp.concatenate([pack, out_weight.astype(bf16).reshape(lines, LANES)], axis=1)
    pack = spread(pack, "a")
    out_full = pack[:, 3 * LANES :].reshape(n_a * local_rows, width)
    out_full = spread(spread(out_full, ("r", "exp")), "core")
    out_full = out_full.reshape(n_c, n_r, n_e, n_a, local_rows, width)
    out_full = out_full.transpose(3, 1, 0, 2, 4, 5).reshape(width, width)
    extra_full = pack[:, 2 * LANES : 3 * LANES]
    first_gain = extra_full[:, experts].astype(f32)

    expert_pack = jnp.concatenate([in_weight.astype(bf16), down_weight.astype(bf16)], axis=2)
    expert_pack = exchange_aside(pieces_for(expert_pack, ("core", "a")), ("core", "a"))
    cot_expert = dot_nn(cotangent, reorder_matrix(home, expert)).astype(bf16)
    cot_expert, expert_pack = lax.optimization_barrier((cot_expert, expert_pack))
    cot_group = spread_aside(spread_aside(cot_expert, "a"), "core")
    expert_full = lax.all_gather(expert_pack, ("exp", "r"), axis=0, tiled=True).reshape(
        n_e, width, 3 * FF
    )

    cosine, sine = rope_tables(x_all[:, width].astype(f32), HEAD_DIMENSION)
    repeat = LANES // HEAD_DIMENSION
    tables = jnp.concatenate([cosine, cosine] * repeat + [-sine, sine] * repeat, axis=1)
    segments = x_all[:, width + 1].astype(f32).reshape(places, rows)
    row_index = jnp.arange(rows, dtype=jnp.int32)
    allowed = (
        (segments[:, :, None] == segments[:, None, :])
        & (row_index[None, None, :] <= row_index[None, :, None])
    ).astype(f32)
    used = jnp.any(
        routes[:, :, None] == jnp.arange(LANES, dtype=jnp.int32)[None, None, :], axis=1
    ).astype(f32)

    def same(index):
        return index

    row_inputs = [
        ((rows, width + LANES), same),
        ((width, 3 * LANES), None),
        ((rows, 2 * LANES), same),
        ((1, rows, rows), same),
    ]
    qkv, logs, attended = block_call(
        functools.partial(attend_heads, experts),
        places,
        row_inputs,
        [
            (shape((places * rows, 2 * LANES), bf16), (rows, 2 * LANES), same),
            (shape((places * rows, LANES), f32), (rows, LANES), same),
            (shape((places, rows, LANES), bf16), (1, rows, LANES), same),
        ],
        [x_all, pack, tables, allowed],
        [],
        flops=2 * places * rows * width * 3 * LANES,
    )
    attended = exchange(attended, plane)
    wide, sent = whole_call(
        functools.partial(home_forward, experts, n_a),
        [shape((rows, width + LANES), f32), shape((n_a, rows, width + LANES), bf16)],
        [tokens, attended, out_full, extra_full, used, reorder_matrix(home, expert)],
        flops=4 * rows * width * width,
    )

    arrived = exchange(sent, "a").reshape(n_a * rows, width + LANES)
    arrived = spread(arrived, "core")
    place = (lax.axis_index("core") * n_a + lax.axis_index("a")).astype(jnp.int32).reshape(1)
    out, inner = run_forward(place, arrived, expert_full, experts, local_count)
    back, inner_grad, activation = run_backward(
        place, arrived, cot_group, expert_full, inner, experts, local_count
    )
    out = collect_aside(out, "core").astype(bf16).reshape(n_a, rows, width)
    back = collect(back, "core").astype(bf16)

    factors = (arrived, inner_grad, cot_group, activation)
    expert_grads = list(weight_grads(factors, n_e, n_r))
    back = exchange(back.reshape(n_a, rows, width + LANES), "a")
    received = send_grads(expert_grads, n_e, n_r, width)
    back, out, expert_grads[0] = lax.optimization_barrier((back, out, expert_grads[0]))
    out = exchange(out, "a")

    from_expert = reorder_matrix(expert, home)
    hidden_grad, mid, out_grad = whole_call(
        functools.partial(home_back, experts),
        [
            shape((rows, width), f32),
            shape((places, rows, LANES), bf16),
            shape((width, query_width + LANES), bf16),
        ],
        [
            back,
            from_expert,
            cotangent,
            wide,
            extra_full,
            out_full,
            attended,
            reorder_matrix(home, split),
        ],
        earlier=expert_grads[:1],
        flops=1,
    )
    mid, out = lax.optimization_barrier((mid, out))
    mid = exchange(mid, plane)

    def core_first(index):
        return (index // n_e % n_c * n_r + index // (n_c * n_e)) * n_e + index % n_e

    qkv_grad, normed_grad = block_call(
        functools.partial(heads_back, experts),
        places,
        row_inputs
        + [((rows, 2 * LANES), same), ((rows, LANES), same), ((1, rows, LANES), same)],
        [
            (shape((width, 3 * LANES), bf16), (width, 3 * LANES), None),
            (shape((places, rows, width), bf16), (1, rows, width), core_first),
        ],
        [x_all, pack, tables, allowed, qkv, logs, mid],
        [
            pltpu.VMEM((places * rows, width), bf16),
            pltpu.VMEM((places * rows, 2 * LANES), bf16),
            pltpu.VMEM((rows, width), f32),
        ],
        flops=2 * places * rows * width * 6 * LANES,
    )
    qkv_grad, out_grad = lax.optimization_barrier((qkv_grad, out_grad))
    qkv_grad = exchange(qkv_grad.reshape(n_a * places, local_rows, 3 * LANES), MESH_AXES)
    normed_grad = collect(normed_grad.reshape(places * rows, width), "core").astype(bf16)
    normed_grad = collect(normed_grad, ("r", "exp"))
    out_grad = collect(out_grad, "core").astype(bf16)
    qkv_grad, normed_grad, out_grad, *received = lax.optimization_barrier(
        (qkv_grad, normed_grad, out_grad, *received)
    )
    out_grad = collect(out_grad, ("r", "exp")).astype(bf16)
    out_grad = exchange(out_grad.reshape(n_a, local_rows, query_width + LANES), "a")

    residual = tokens.astype(f32)
    first_scale = rms_scale(residual)
    scaled = normed_grad * first_gain
    input_grad = (
        hidden_grad
        + first_scale * scaled
        - residual * first_scale**3 * jnp.mean(scaled * residual, axis=-1, keepdims=True)
    ).astype(bf16)
    mixed = dot_nn(out[0], from_expert)
    for index in range(1, n_a):
        mixed = mixed + dot_nn(out[index], from_expert)
    block_out = (wide[:, :width] + mixed).astype(bf16)

    expert_grad = received[0].astype(f32)
    for part in received[1:]:
        expert_grad = expert_grad + part.astype(f32)
    expert_grad = expert_grad.astype(bf16).reshape(
        n_c * n_a, width // (n_r * n_c * n_a), 3 * FF
    )
    expert_grad = exchange_aside(
        pieces_for(expert_grad, ("core", "a")), ("core", "a")
    ).astype(f32)
    d_in = expert_grad[:, :, : 2 * FF]
    d_down = expert_grad[:, :, 2 * FF :]

    dense_state = [
        qkv_weight,
        qkv_mean,
        qkv_square,
        out_weight,
        out_mean,
        out_square,
        router_weight.T,
        router_mean.T,
        router_square.T,
        norm_gains.T,
        gains_mean.T,
        gains_square.T,
    ]
    (
        new_qkv,
        new_qkv_mean,
        new_qkv_square,
        new_out,
        new_out_mean,
        new_out_square,
        new_router,
        new_router_mean,
        new_router_square,
        new_gains,
        new_gains_mean,
        new_gains_square,
    ) = whole_call(
        functools.partial(heads_update, places),
        [shape(item.shape, f32) for item in dense_state],
        [qkv_grad, out_grad] + dense_state,
        flops=60 * local_rows * width,
    )
    new_router, new_router_mean, new_router_square = (
        item.T for item in (new_router, new_router_mean, new_router_square)
    )
    new_gains, new_gains_mean, new_gains_square = (
        item.T for item in (new_gains, new_gains_mean, new_gains_square)
    )
    new_in, new_in_mean, new_in_square = adamw(in_weight, d_in, in_mean, in_square, 0.1, decay_rate)
    new_down, new_down_mean, new_down_square = adamw(
        down_weight, d_down, down_mean, down_square, 1.0, decay_rate
    )
    return (
        block_out,
        input_grad,
        new_qkv,
        new_qkv_mean,
        new_qkv_square,
        new_out,
        new_out_mean,
        new_out_square,
        new_router,
        new_router_mean,
        new_router_square,
        new_gains,
        new_gains_mean,
        new_gains_square,
        new_in,
        new_in_mean,
        new_in_square,
        new_down,
        new_down_mean,
        new_down_square,
    )


def solution(mesh):
    n_dp, n_exp = mesh.shape["dp"], mesh.shape["exp"]
    n_a = EXPERTS // n_exp // 2
    mesh = Mesh(
        mesh.devices.reshape(n_a, n_dp // (2 * n_a), 2, n_exp), MESH_AXES
    )
    placed = (
        P(("a", "r", "core", "exp"), None),
        P(("a", "r", "core", "exp"), None),
        P(("a", "r", "core", "exp"), None),
        P(("a", "r", "core", "exp"), None),
        P(("a", "r", "core", "exp"), None),
        P(("a", "r", "core", "exp"), None),
        P(("a", "r", "core", "exp"), None),
        P(("a", "r", "core", "exp"), None),
        P(("a", "r", "core", "exp"), None),
        P(("a", "r", "core", "exp"), None),
        P(("a", "r", "core", "exp"), None),
        P(("a", "r", "core", "exp"), None),
        P(("a", "r", "core", "exp"), None),
        P(("a", "r", "core", "exp"), None),
        P(("a", "r", "core", "exp"), None),
        P(("a", "r", "core", "exp"), None),
        P("exp", ("a", "r", "core"), None),
        P("exp", ("a", "r", "core"), None),
        P("exp", ("a", "r", "core"), None),
        P("exp", ("a", "r", "core"), None),
        P("exp", ("a", "r", "core"), None),
        P("exp", ("a", "r", "core"), None),
    )
    shared = mesh.size // n_a == KEY_VALUE_HEADS
    return jax.shard_map(
        body_heads if shared else body,
        mesh=mesh,
        in_specs=placed,
        out_specs=(
            P(("a", "r", "core", "exp"), None),
            P(("a", "r", "core", "exp"), None),
            P(("a", "r", "core", "exp"), None),
            P(("a", "r", "core", "exp"), None),
            P(("a", "r", "core", "exp"), None),
            P(("a", "r", "core", "exp"), None),
            P(("a", "r", "core", "exp"), None),
            P(("a", "r", "core", "exp"), None),
            P(("a", "r", "core", "exp"), None),
            P(("a", "r", "core", "exp"), None),
            P(("a", "r", "core", "exp"), None),
            P(("a", "r", "core", "exp"), None),
            P(("a", "r", "core", "exp"), None),
            P(("a", "r", "core", "exp"), None),
            P("exp", ("a", "r", "core"), None),
            P("exp", ("a", "r", "core"), None),
            P("exp", ("a", "r", "core"), None),
            P("exp", ("a", "r", "core"), None),
            P("exp", ("a", "r", "core"), None),
            P("exp", ("a", "r", "core"), None),
        ),
        check_vma=False,
    )
```

```python
import functools
import math

import jax
import jax.numpy as jnp
import numpy as np
from jax import lax
from jax.experimental import pallas as pl
from jax.experimental.pallas import tpu as pltpu
from jax.sharding import Mesh
from jax.sharding import PartitionSpec as P

QUERY_HEADS = 16
KEY_VALUE_HEADS = 8
HEAD_DIMENSION = 64
FF = 512
STEP = 10
EXPERTS = 16
LANES = 128
MESH_AXES = ("a", "r", "core", "exp")
VMEM_BYTES = 26 * 1024 * 1024


norm_eps = 1e-06
rope_base = 10000.0
mask_fill = -1e30
beta_one = 0.9
beta_two = 0.95
adam_eps = 1e-08
decay_rate = 0.1


def rms_scale(values):
    return lax.rsqrt(jnp.mean(values * values, axis=-1, keepdims=True) + norm_eps)


def doc_layout(doc_lens, sequence_length):
    row_index = jnp.arange(sequence_length, dtype=jnp.int32)
    doc_ends = jnp.cumsum(doc_lens, dtype=jnp.int32)
    passed = (row_index[:, None] >= doc_ends[None, :]).astype(jnp.int32)
    segment = jnp.sum(passed, axis=1, dtype=jnp.int32)
    starts = jnp.sum(passed * doc_lens[None, :], axis=1, dtype=jnp.int32)
    return ((row_index - starts).astype(jnp.float32), segment)


def rope_tables(positions, head_size):
    half_size = head_size // 2
    freq_index = jnp.arange(half_size, dtype=jnp.float32)
    inverse = jnp.exp(freq_index * (-2.0 * math.log(rope_base) / head_size))
    angles = positions[:, None] * inverse[None, :]
    return (jnp.cos(angles), jnp.sin(angles))


def adamw(weight, gradient, mean_old, square_old, step_rate, weight_decay):
    mean_new = beta_one * mean_old + (1.0 - beta_one) * gradient
    square_new = beta_two * square_old + (1.0 - beta_two) * gradient * gradient
    corrected = (
        mean_new
        / (1.0 - beta_one**STEP)
        / (jnp.sqrt(square_new / (1.0 - beta_two**STEP)) + adam_eps)
    )
    return (weight - step_rate * (corrected + weight_decay * weight), mean_new, square_new)

def dot_nn(left, right):
    return jnp.dot(left, right, preferred_element_type=jnp.float32)


def dot_nt(left, right):
    return lax.dot_general(left, right, (((1,), (1,)), ((), ())), preferred_element_type=jnp.float32)


def dot_tn(left, right):
    return lax.dot_general(left, right, (((0,), (0,)), ((), ())), preferred_element_type=jnp.float32)


def lane_iota(rows):
    return lax.broadcasted_iota(jnp.int32, (rows, LANES), 1)


def gain_rows(extra, experts):
    row = lax.broadcasted_iota(jnp.int32, (8, LANES), 0)
    pick = (lane_iota(8) == row + experts).astype(jnp.bfloat16)
    return dot_nt(jnp.where(row < 2, pick, jnp.zeros_like(pick)), extra)


def swap_halves(values):
    half = HEAD_DIMENSION // 2
    lower = lane_iota(values.shape[0]) % HEAD_DIMENSION < half
    return jnp.where(lower, pltpu.roll(values, LANES - half, 1), pltpu.roll(values, half, 1))


def column_sums(values, lane):
    high = values.astype(jnp.bfloat16)
    low = (values - high.astype(jnp.float32)).astype(jnp.bfloat16)
    place = (lane_iota(values.shape[0]) == lane).astype(jnp.bfloat16)
    return dot_tn(high, place) + dot_tn(low, place)


def head_block(index):
    return slice(index * HEAD_DIMENSION, (index + 1) * HEAD_DIMENSION)


def attention_forward(
    experts,
    copies,
    x_ref,
    w_ref,
    cos_ref,
    sin_ref,
    allow_ref,
    used_ref,
    order_ref,
    wide_ref,
    qkv_ref,
    sent_ref,
):
    f32, bf16 = jnp.float32, jnp.bfloat16
    rows, width = x_ref.shape
    query_width = QUERY_HEADS * HEAD_DIMENSION
    key_width = KEY_VALUE_HEADS * HEAD_DIMENSION
    qkv_width = query_width + 2 * key_width
    extra = w_ref[:, qkv_width + width :]
    gains = gain_rows(extra, experts)
    x = x_ref[...].astype(f32)
    normed = (x * rms_scale(x) * gains[0:1]).astype(bf16)
    cosine, sine = cos_ref[...], sin_ref[...]
    for start in range(0, qkv_width, 512):
        part = dot_nn(normed, w_ref[:, start : start + 512])
        for inner in range(0, 512, LANES):
            piece = part[:, inner : inner + LANES]
            if start + inner < query_width + key_width:
                piece = piece * cosine + swap_halves(piece) * sine
            qkv_ref[:, start + inner : start + inner + LANES] = piece.astype(bf16)
    allowed = allow_ref[...] > 0.0
    lane = lane_iota(rows)
    logs = jnp.zeros((rows, LANES), f32)
    fold = QUERY_HEADS // KEY_VALUE_HEADS
    for group in range(KEY_VALUE_HEADS):
        keys = qkv_ref[:, query_width + group * HEAD_DIMENSION : query_width + (group + 1) * HEAD_DIMENSION]
        values = qkv_ref[
            :,
            query_width + key_width + group * HEAD_DIMENSION : query_width
            + key_width
            + (group + 1) * HEAD_DIMENSION,
        ]
        outs = []
        for head in range(group * fold, (group + 1) * fold):
            scores = dot_nt(qkv_ref[:, head_block(head)], keys) * HEAD_DIMENSION ** (-0.5)
            scores = jnp.where(allowed, scores, mask_fill)
            peak = jnp.max(scores, axis=1, keepdims=True)
            log_total = peak + jnp.log(jnp.sum(jnp.exp(scores - peak), axis=1, keepdims=True))
            logs = jnp.where(lane == head, log_total, logs)
            outs.append(dot_nn(jnp.exp(scores - log_total).astype(bf16), values))
        start = qkv_width + group * LANES
        qkv_ref[:, start : start + LANES] = jnp.concatenate(outs, axis=1).astype(bf16)
    wide_ref[:, width : width + LANES] = logs
    hidden = x + dot_nt(qkv_ref[:, qkv_width:], w_ref[:, qkv_width : qkv_width + width])
    wide_ref[:, :width] = hidden
    second = (hidden * rms_scale(hidden) * gains[1:2]).astype(bf16)
    used = used_ref[...] > 0.0
    logits = jnp.where(used, dot_nn(second, extra), mask_fill)
    powers = jnp.where(used, jnp.exp(logits - jnp.max(logits, axis=1, keepdims=True)), 0.0)
    gates = powers / jnp.sum(powers, axis=1, keepdims=True)
    wide_ref[:, width + LANES :] = gates
    high = gates.astype(bf16).astype(f32)
    lanes = (high + pltpu.roll(gates - high, experts, 1)).astype(bf16)
    moved = dot_nn(second, order_ref[...]).astype(bf16)
    for copy in range(copies):
        sent_ref[copy, :, :width] = moved
        sent_ref[copy, :, width:] = lanes


def own_gate(lanes, number, experts):
    lane = lane_iota(lanes.shape[0])
    chosen = (lane == number) | (lane == number + experts)
    return jnp.sum(jnp.where(chosen, lanes.astype(jnp.float32), 0.0), axis=1, keepdims=True)


def experts_forward(
    experts, local_count, place_ref, rows_ref, w_ref, out_ref, inner_ref, sum_ref
):
    f32, bf16 = jnp.float32, jnp.bfloat16
    index, chunk = pl.program_id(0), pl.program_id(1)
    count, width = out_ref.shape
    gate = own_gate(rows_ref[:, width:], index * local_count + place_ref[0], experts)
    inner = dot_nn(rows_ref[:, :width], w_ref[0, :, : 2 * FF])
    inner_ref[0] = inner
    gate_part = inner[:, :FF]
    activation = (gate_part * jax.nn.sigmoid(gate_part) * inner[:, FF:]).astype(bf16)
    result = dot_nt(activation, w_ref[0, :, 2 * FF :]).astype(bf16).astype(f32)
    here = pl.ds(pl.multiple_of(chunk * count, count), count)

    @pl.when(index == 0)
    def _():
        sum_ref[here, :] = gate * result

    @pl.when(index > 0)
    def _():
        sum_ref[here, :] += gate * result

    out_ref[...] = sum_ref[here, :].astype(bf16)


def experts_backward(
    experts,
    local_count,
    place_ref,
    gates_ref,
    cot_ref,
    w_ref,
    inner_ref,
    back_ref,
    inner_grad_ref,
    act_ref,
    sum_ref,
    dots_sum_ref,
):
    f32, bf16 = jnp.float32, jnp.bfloat16
    index, chunk = pl.program_id(0), pl.program_id(1)
    count, width = cot_ref.shape
    number = index * local_count + place_ref[0]
    gate = own_gate(gates_ref[...], number, experts)
    gate_part = inner_ref[0, :, :FF]
    up_part = inner_ref[0, :, FF:]
    gate_sigmoid = jax.nn.sigmoid(gate_part)
    gate_silu = gate_part * gate_sigmoid
    activation = (gate_silu * up_part).astype(bf16).astype(f32)
    act_ref[0] = (gate * activation).astype(bf16)
    act_grad = dot_nn(cot_ref[...], w_ref[0, :, 2 * FF :])
    dots = jnp.sum(activation * act_grad, axis=1, keepdims=True)
    dots_high = dots.astype(bf16).astype(f32)
    lane = lane_iota(count)
    lanes = jnp.where(lane == number, dots_high, 0.0) + jnp.where(
        lane == number + experts, dots - dots_high, 0.0
    )
    act_grad = gate * act_grad
    inner_grad_ref[0, :, :FF] = (
        act_grad * up_part * gate_sigmoid * (1.0 + gate_part * (1.0 - gate_sigmoid))
    ).astype(bf16)
    inner_grad_ref[0, :, FF:] = (act_grad * gate_silu).astype(bf16)
    copy_grad = dot_nt(inner_grad_ref[0], w_ref[0, :, : 2 * FF])
    here = pl.ds(pl.multiple_of(chunk * count, count), count)

    @pl.when(index == 0)
    def _():
        sum_ref[here, :] = copy_grad
        dots_sum_ref[here, :] = lanes

    @pl.when(index > 0)
    def _():
        sum_ref[here, :] += copy_grad
        dots_sum_ref[here, :] += lanes

    back_ref[:, :width] = sum_ref[here, :].astype(bf16)
    back_ref[:, width:] = dots_sum_ref[here, :].astype(bf16)


def experts_weights(where_ref, rows_ref, inner_grad_ref, cot_ref, act_ref, *grad_refs):
    goal = pl.program_id(0)
    inner = dot_tn(rows_ref[...], inner_grad_ref[0]).astype(jnp.bfloat16)
    down = dot_tn(cot_ref[...], act_ref[0]).astype(jnp.bfloat16)
    for index, grad_ref in enumerate(grad_refs):

        @pl.when(goal == index)
        def _(grad_ref=grad_ref):
            grad_ref[:, : 2 * FF] = inner
            grad_ref[:, 2 * FF :] = down


def home_backward(
    experts,
    parts_ref,
    order_ref,
    cot_ref,
    wide_ref,
    w_ref,
    qkv_ref,
    x_ref,
    cos_ref,
    sin_ref,
    allow_ref,
    grad_ref,
    input_grad_ref,
    mid_ref,
    proj_ref,
):
    f32, bf16 = jnp.float32, jnp.bfloat16
    rows, width = x_ref.shape
    sources = parts_ref.shape[0]
    query_width = QUERY_HEADS * HEAD_DIMENSION
    key_width = KEY_VALUE_HEADS * HEAD_DIMENSION
    qkv_width = query_width + 2 * key_width
    fold = QUERY_HEADS // KEY_VALUE_HEADS
    score_scale = HEAD_DIMENSION ** (-0.5)
    extra = w_ref[:, qkv_width + width :]
    gains = gain_rows(extra, experts)
    dots = jnp.zeros((rows, LANES), f32)
    second_grad = jnp.zeros((rows, width), f32)
    for source in range(sources):
        dots = dots + parts_ref[source, :, width:].astype(f32)
        second_grad = second_grad + dot_nn(parts_ref[source, :, :width], order_ref[...])
    dots = dots + pltpu.roll(dots, LANES - experts, 1)
    gates = wide_ref[:, width + LANES :]
    logit_grad = (gates * (dots - jnp.sum(gates * dots, axis=1, keepdims=True))).astype(bf16)
    second_grad = second_grad + dot_nt(logit_grad, extra)
    hidden = wide_ref[:, :width]
    scale = rms_scale(hidden)
    second = (hidden * scale * gains[1:2]).astype(bf16)
    scaled = second_grad * gains[1:2]
    hidden_grad = (
        cot_ref[...].astype(f32)
        + scale * scaled
        - hidden * (scale * scale * scale) * jnp.mean(scaled * hidden, axis=1, keepdims=True)
    )
    branch_grad = hidden_grad.astype(bf16)
    for start in range(0, width, 512):
        grad_ref[:, qkv_width + start : qkv_width + start + 512] = dot_tn(
            branch_grad, qkv_ref[:, qkv_width + start : qkv_width + start + 512]
        ).astype(bf16)
    small_grad = dot_tn(second, logit_grad) + column_sums(
        second_grad * hidden * scale, experts + 1
    )
    mid_ref[...] = dot_nn(branch_grad, w_ref[:, qkv_width : qkv_width + width]).astype(bf16)
    cosine, sine = cos_ref[...], sin_ref[...]
    allowed = allow_ref[...] > 0.0
    lane = lane_iota(rows)
    logs = wide_ref[:, width : width + LANES]

    def turned_back(values):
        return (values * cosine - swap_halves(values) * sine).astype(bf16)

    key_grads, value_grads = [], []
    for group in range(KEY_VALUE_HEADS):
        keys = qkv_ref[:, query_width + group * HEAD_DIMENSION : query_width + (group + 1) * HEAD_DIMENSION]
        values = qkv_ref[
            :,
            query_width + key_width + group * HEAD_DIMENSION : query_width
            + key_width
            + (group + 1) * HEAD_DIMENSION,
        ]
        query_grads = []
        key_grad = jnp.zeros((rows, HEAD_DIMENSION), f32)
        value_grad = jnp.zeros((rows, HEAD_DIMENSION), f32)
        for head in range(group * fold, (group + 1) * fold):
            queries = qkv_ref[:, head_block(head)]
            mid = mid_ref[:, head_block(head)]
            log_total = jnp.sum(jnp.where(lane == head, logs, 0.0), axis=1, keepdims=True)
            scores = jnp.where(allowed, dot_nt(queries, keys) * score_scale, mask_fill)
            weights = jnp.exp(scores - log_total)
            weight_grad = dot_nt(mid, values)
            delta = jnp.sum(weights * weight_grad, axis=1, keepdims=True)
            score_grad = (weights * (weight_grad - delta)).astype(bf16)
            query_grads.append(dot_nn(score_grad, keys) * score_scale)
            key_grad = key_grad + dot_tn(score_grad, queries)
            value_grad = value_grad + dot_tn(weights.astype(bf16), mid)
        proj_ref[:, group * LANES : (group + 1) * LANES] = turned_back(
            jnp.concatenate(query_grads, axis=1)
        )
        key_grads.append(key_grad * score_scale)
        value_grads.append(value_grad)
        if group % 2 == 1:
            start = query_width + (group // 2) * LANES
            proj_ref[:, start : start + LANES] = turned_back(
                jnp.concatenate(key_grads[-2:], axis=1)
            )
            start = start + key_width
            proj_ref[:, start : start + LANES] = jnp.concatenate(value_grads[-2:], axis=1).astype(
                bf16
            )
    x = x_ref[...].astype(f32)
    scale = rms_scale(x)
    normed = (x * scale * gains[0:1]).astype(bf16)
    for start in range(0, qkv_width, 512):
        grad_ref[:, start : start + 512] = dot_tn(normed, proj_ref[:, start : start + 512]).astype(
            bf16
        )
    normed_grad = dot_nt(proj_ref[...], w_ref[:, :qkv_width])
    scaled = normed_grad * gains[0:1]
    small_grad = small_grad + column_sums(normed_grad * x * scale, experts)
    grad_ref[:, qkv_width + width :] = small_grad.astype(bf16)
    input_grad_ref[...] = (
        hidden_grad
        + scale * scaled
        - x * (scale * scale * scale) * jnp.mean(scaled * x, axis=1, keepdims=True)
    ).astype(bf16)


def dense_update(parts_ref, *refs):
    total = parts_ref[0].astype(jnp.float32)
    for source in range(1, parts_ref.shape[0]):
        total = total + parts_ref[source].astype(jnp.float32)
    start = total.shape[1] - LANES
    small = jnp.transpose(total[:, start:])
    experts = refs[6].shape[0]
    qkv_width = refs[0].shape[1]
    grads = (
        total[:, :qkv_width],
        total[:, qkv_width:start],
        small[:experts],
        small[experts : experts + 2],
    )
    rates = ((0.15, decay_rate), (0.3, decay_rate), (0.05, decay_rate), (0.8, 0.0))
    for index, (rate, decay) in enumerate(rates):
        weight_ref, mean_ref, square_ref = refs[3 * index : 3 * index + 3]
        values = adamw(weight_ref[...], grads[index], mean_ref[...], square_ref[...], rate, decay)
        for out_ref, value in zip(refs[3 * index + 12 : 3 * index + 15], values):
            out_ref[...] = value


def whole_call(kernel, outputs, operands, flops, scratch=(), earlier=()):
    operands_read = len(operands)

    def run(*refs):
        kernel(*refs[:operands_read], *refs[operands_read + len(earlier) :])

    moved = sum(math.prod(item.shape) * item.dtype.itemsize for item in list(outputs) + list(operands))
    moved = moved if flops > 1 else 1
    return pl.pallas_call(
        run,
        out_shape=outputs,
        in_specs=[pl.BlockSpec(memory_space=pltpu.VMEM)] * len(operands)
        + [pl.BlockSpec(memory_space=pl.ANY)] * len(earlier),
        out_specs=[pl.BlockSpec(memory_space=pltpu.VMEM)] * len(outputs),
        scratch_shapes=list(scratch),
        compiler_params=pltpu.CompilerParams(vmem_limit_bytes=VMEM_BYTES),
        cost_estimate=pl.CostEstimate(flops=flops, bytes_accessed=moved, transcendentals=0),
    )(*operands, *earlier)


def order_of(kind, sizes):
    axes = {"home": (0, 1, 2, 3, 4), "dense": (2, 1, 3, 0, 4), "expert": (1, 2, 0, 3, 4)}[kind]
    return np.arange(math.prod(sizes), dtype=np.int32).reshape(sizes).transpose(axes).reshape(-1)


def reorder_matrix(before, after):
    return (jnp.asarray(before)[:, None] == jnp.asarray(after)[None, :]).astype(jnp.bfloat16)


def exchange(values, axes):
    return lax.all_to_all(values, axes, split_axis=0, concat_axis=0, tiled=True)


def spread(values, axes):
    count = lax.axis_size(axes)
    copies = exchange(jnp.broadcast_to(values[None], (count,) + values.shape), axes)
    return copies.reshape((count * values.shape[0],) + values.shape[1:])


def collect(values, axes):
    count = lax.axis_size(axes)
    parts = exchange(values.reshape((count, values.shape[0] // count) + values.shape[1:]), axes)
    total = parts[0].astype(jnp.float32)
    for index in range(1, count):
        total = total + parts[index].astype(jnp.float32)
    return total


def partner(values, axes, step):
    names = (axes,) if isinstance(axes, str) else axes
    steps = {}
    for name in reversed(names):
        step, steps[name] = divmod(step, lax.axis_size(name))
    names = tuple(name for name in MESH_AXES if name in names)
    flat = 0
    for name in names:
        flat = flat * lax.axis_size(name) + steps[name]
    pairs = [(index, index ^ flat) for index in range(lax.axis_size(names))]
    return lax.ppermute(values, names, pairs)


def piece_of(values, index):
    return lax.dynamic_index_in_dim(values, index, 0, keepdims=False)


def in_order(own, received, me):
    result = jnp.zeros((len(received) + 1,) + own.shape, own.dtype)
    for step, part in enumerate([own] + received):
        result = lax.dynamic_update_index_in_dim(result, part, me ^ step, 0)
    return result


def spread_aside(values, axes):
    count = lax.axis_size(axes)
    received = [partner(values, axes, step) for step in range(1, count)]
    result = in_order(values, received, lax.axis_index(axes))
    return result.reshape((count * values.shape[0],) + values.shape[1:])


def pieces_for(values, axes):
    me = lax.axis_index(axes)
    return [piece_of(values, me ^ step) for step in range(values.shape[0])]


def exchange_aside(pieces, axes):
    received = [partner(piece, axes, step) for step, piece in enumerate(pieces) if step > 0]
    return in_order(pieces[0], received, lax.axis_index(axes))


def collect_aside(values, axes):
    count = lax.axis_size(axes)
    pieces = pieces_for(values.reshape((count, values.shape[0] // count) + values.shape[1:]), axes)
    total = pieces[0].astype(jnp.float32)
    for step in range(1, count):
        total = total + partner(pieces[step], axes, step).astype(jnp.float32)
    return total


def expert_specs(n_e, group_rows, width):
    count = min(256, group_rows)
    return dict(
        grid=(n_e, group_rows // count),
        scalar=pl.BlockSpec(memory_space=pltpu.SMEM),
        wide=pl.BlockSpec((count, width), lambda k, i: (i, 0)),
        wider=pl.BlockSpec((count, width + LANES), lambda k, i: (i, 0)),
        lanes=pl.BlockSpec((count, LANES), lambda k, i: (i, width // LANES)),
        weight=pl.BlockSpec((1, width, 3 * FF), lambda k, i: (k, 0, 0)),
        inner=pl.BlockSpec((1, count, 2 * FF), lambda k, i: (k, i, 0)),
        act=pl.BlockSpec((1, count, FF), lambda k, i: (k, i, 0)),
    )


def run_forward(place, arrived, expert_full, experts, local_count):
    n_e, width, _ = expert_full.shape
    group_rows = arrived.shape[0]
    specs = expert_specs(n_e, group_rows, width)
    return pl.pallas_call(
        functools.partial(experts_forward, experts, local_count),
        grid=specs["grid"],
        out_shape=[
            jax.ShapeDtypeStruct((group_rows, width), jnp.bfloat16),
            jax.ShapeDtypeStruct((n_e, group_rows, 2 * FF), jnp.float32),
        ],
        in_specs=[specs["scalar"], specs["wider"], specs["weight"]],
        out_specs=[specs["wide"], specs["inner"]],
        scratch_shapes=[pltpu.VMEM((group_rows, width), jnp.float32)],
        compiler_params=pltpu.CompilerParams(vmem_limit_bytes=VMEM_BYTES),
        cost_estimate=pl.CostEstimate(
            flops=2 * n_e * group_rows * width * 3 * FF,
            bytes_accessed=n_e * width * (3 * FF * 2 + group_rows * 8),
            transcendentals=n_e * group_rows * FF,
        ),
    )(place, arrived, expert_full)


def run_backward(place, arrived, cot_group, expert_full, inner, experts, local_count):
    bf16 = jnp.bfloat16
    n_e, width, _ = expert_full.shape
    group_rows = arrived.shape[0]
    specs = expert_specs(n_e, group_rows, width)
    return pl.pallas_call(
        functools.partial(experts_backward, experts, local_count),
        grid=specs["grid"],
        out_shape=[
            jax.ShapeDtypeStruct((group_rows, width + LANES), bf16),
            jax.ShapeDtypeStruct((n_e, group_rows, 2 * FF), bf16),
            jax.ShapeDtypeStruct((n_e, group_rows, FF), bf16),
        ],
        in_specs=[
            specs["scalar"],
            specs["lanes"],
            specs["wide"],
            specs["weight"],
            specs["inner"],
        ],
        out_specs=[specs["wider"], specs["inner"], specs["act"]],
        scratch_shapes=[
            pltpu.VMEM((group_rows, width), jnp.float32),
            pltpu.VMEM((group_rows, LANES), jnp.float32),
        ],
        compiler_params=pltpu.CompilerParams(vmem_limit_bytes=VMEM_BYTES),
        cost_estimate=pl.CostEstimate(
            flops=2 * n_e * group_rows * width * 3 * FF,
            bytes_accessed=n_e * width * (3 * FF * 2 + group_rows * 10),
            transcendentals=n_e * group_rows * FF,
        ),
    )(place, arrived, cot_group, expert_full, inner)


def run_weights(arrived, inner_grad, cot_group, act, slots, firsts, blocks, part):
    group_rows = arrived.shape[0]
    goals = len(slots)
    where = jnp.stack(slots + firsts).astype(jnp.int32)

    def block_of(index):
        return lambda g, j, at: (jnp.where(g == index, j, jnp.where(g < index, 0, blocks - 1)), 0)

    return pl.pallas_call(
        experts_weights,
        grid_spec=pltpu.PrefetchScalarGridSpec(
            num_scalar_prefetch=1,
            grid=(goals, blocks),
            in_specs=[
                pl.BlockSpec((group_rows, part), lambda g, j, at: (0, at[goals + g] + j)),
                pl.BlockSpec((1, group_rows, 2 * FF), lambda g, j, at: (at[g], 0, 0)),
                pl.BlockSpec((group_rows, part), lambda g, j, at: (0, at[goals + g] + j)),
                pl.BlockSpec((1, group_rows, FF), lambda g, j, at: (at[g], 0, 0)),
            ],
            out_specs=[pl.BlockSpec((part, 3 * FF), block_of(index)) for index in range(goals)],
        ),
        out_shape=[jax.ShapeDtypeStruct((blocks * part, 3 * FF), jnp.bfloat16)] * goals,
        compiler_params=pltpu.CompilerParams(vmem_limit_bytes=VMEM_BYTES),
        cost_estimate=pl.CostEstimate(
            flops=2 * goals * blocks * part * group_rows * 3 * FF,
            bytes_accessed=goals * (group_rows * 6 * FF + blocks * part * (group_rows * 4 + 6 * FF)),
            transcendentals=0,
        ),
    )(where, arrived, inner_grad, cot_group, act)


def in_pieces(n_e, n_r, width):
    return n_e * n_r <= 8 and width // n_r % min(256, width) == 0


def weight_grads(factors, n_e, n_r):
    width = factors[2].shape[1]
    part = min(256, width)
    if in_pieces(n_e, n_r, width):
        me = lax.axis_index(("exp", "r"))
        blocks = width // n_r // part
        goals = [me ^ step for step in range(n_e * n_r)]
        slots = [goal // n_r for goal in goals]
        firsts = [goal % n_r * blocks for goal in goals]
        return run_weights(*factors, slots, firsts, blocks, part)
    grads = []
    for slot in range(n_e):
        grads += run_weights(*factors, [jnp.int32(slot)], [jnp.int32(0)], width // part, part)
    return grads


def send_grads(grads, n_e, n_r, width):
    axes = ("exp", "r")
    if not in_pieces(n_e, n_r, width):
        grads = jnp.concatenate(grads, axis=0)
        return list(exchange(grads.reshape((n_e * n_r, -1) + grads.shape[1:]), axes))
    return [grads[0]] + [
        partner(grads[step], axes, step) for step in reversed(range(1, len(grads)))
    ]


def body(
    tokens,
    cotangent,
    doc_lengths,
    routes,
    qkv_weight,
    qkv_mean,
    qkv_square,
    out_weight,
    out_mean,
    out_square,
    router_weight,
    router_mean,
    router_square,
    norm_gains,
    gains_mean,
    gains_square,
    in_weight,
    in_mean,
    in_square,
    down_weight,
    down_mean,
    down_square,
):
    f32, bf16 = jnp.float32, jnp.bfloat16
    shape = jax.ShapeDtypeStruct
    n_a, n_r, n_c, n_e = (lax.axis_size(name) for name in ("a", "r", "core", "exp"))
    rows, width = tokens.shape
    experts = router_weight.shape[1]
    local_count = in_weight.shape[0]
    sizes = (n_a, n_r, n_c, n_e, width // (n_a * n_r * n_c * n_e))
    home, dense, expert = (order_of(kind, sizes) for kind in ("home", "dense", "expert"))
    query_width = QUERY_HEADS * HEAD_DIMENSION
    qkv_width = query_width + 2 * KEY_VALUE_HEADS * HEAD_DIMENSION

    local_rows = qkv_weight.shape[0]
    extra = jnp.zeros((local_rows, LANES - experts - 2), bf16)
    pack = jnp.concatenate(
        [
            qkv_weight.astype(bf16),
            out_weight.astype(bf16),
            router_weight.astype(bf16),
            norm_gains.astype(bf16),
            extra,
        ],
        axis=1,
    )
    pack = spread(pack, "a")

    to_dense = reorder_matrix(home, dense)
    x_dense = dot_nn(tokens, to_dense).astype(bf16)
    cot_dense = dot_nn(cotangent, to_dense).astype(bf16)
    positions, segment = doc_layout(doc_lengths.reshape(-1), rows)
    cosine, sine = rope_tables(positions, HEAD_DIMENSION)
    repeat = LANES // HEAD_DIMENSION
    cosine = jnp.concatenate([cosine, cosine] * repeat, axis=1)
    sine = jnp.concatenate([-sine, sine] * repeat, axis=1)
    row_index = jnp.arange(rows, dtype=jnp.int32)
    allowed = (segment[:, None] == segment[None, :]) & (row_index[None, :] <= row_index[:, None])
    allowed = allowed.astype(f32)
    used = jnp.any(
        routes[:, :, None] == jnp.arange(LANES, dtype=jnp.int32)[None, None, :], axis=1
    ).astype(f32)

    cot_expert = dot_nn(cotangent, reorder_matrix(home, expert)).astype(bf16)
    expert_pack = jnp.concatenate([in_weight.astype(bf16), down_weight.astype(bf16)], axis=2)
    to_expert = reorder_matrix(dense, expert)
    pieces = pieces_for(expert_pack, ("core", "a"))
    pack, x_dense, cot_dense, cosine, sine, allowed, used, to_expert, *pieces = (
        lax.optimization_barrier(
            (pack, x_dense, cot_dense, cosine, sine, allowed, used, to_expert, *pieces)
        )
    )
    pack = spread(pack, ("r", "exp"))
    expert_pack = exchange_aside(pieces, ("core", "a"))
    pack, expert_pack = lax.optimization_barrier((pack, expert_pack))
    cot_expert, expert_pack = lax.optimization_barrier((cot_expert, expert_pack))
    cot_group = spread_aside(spread_aside(cot_expert, "a"), "core")
    expert_full = lax.all_gather(expert_pack, ("exp", "r"), axis=0, tiled=True).reshape(
        n_e, width, 3 * FF
    )
    dense_full = spread(pack, "core")

    wide, qkv, sent = whole_call(
        functools.partial(attention_forward, experts, n_a),
        [
            shape((rows, width + 2 * LANES), f32),
            shape((rows, qkv_width + query_width), bf16),
            shape((n_a, rows, width + LANES), bf16),
        ],
        [x_dense, dense_full, cosine, sine, allowed, used, to_expert],
        flops=2 * rows * width * (qkv_width + 2 * width + 2 * rows),
    )

    arrived = exchange(sent, "a").reshape(n_a * rows, width + LANES)
    arrived = spread(arrived, "core")
    place = (lax.axis_index("core") * n_a + lax.axis_index("a")).astype(jnp.int32).reshape(1)
    out, inner = run_forward(place, arrived, expert_full, experts, local_count)
    back, inner_grad, activation = run_backward(
        place, arrived, cot_group, expert_full, inner, experts, local_count
    )
    out = collect_aside(out, "core").astype(bf16).reshape(n_a, rows, width)
    back = collect(back, "core").astype(bf16)

    factors = (arrived, inner_grad, cot_group, activation)
    expert_grads = list(weight_grads(factors, n_e, n_r))
    back = exchange(back.reshape(n_a, rows, width + LANES), "a")
    received = send_grads(expert_grads, n_e, n_r, width)
    back, out, expert_grads[0] = lax.optimization_barrier((back, out, expert_grads[0]))
    out = exchange(out, "a")

    from_expert = reorder_matrix(expert, dense)
    dense_grad, input_grad = whole_call(
        functools.partial(home_backward, experts),
        [shape((width, qkv_width + width + LANES), bf16), shape((rows, width), bf16)],
        [
            back,
            from_expert,
            cot_dense,
            wide,
            dense_full,
            qkv,
            x_dense,
            cosine,
            sine,
            allowed,
        ],
        earlier=expert_grads[:1],
        flops=1,
        scratch=[pltpu.VMEM((rows, query_width), bf16), pltpu.VMEM((rows, qkv_width), bf16)],
    )
    dense_grad, out = lax.optimization_barrier((dense_grad, out))
    dense_grad = collect(dense_grad, "core").astype(bf16)
    dense_grad, *received = lax.optimization_barrier((dense_grad, *received))
    expert_grad = received[0].astype(f32)
    for part in received[1:]:
        expert_grad = expert_grad + part.astype(f32)
    expert_grad = expert_grad.astype(bf16).reshape(
        n_c * n_a, width // (n_r * n_c * n_a), 3 * FF
    )
    expert_grad = exchange_aside(
        pieces_for(expert_grad, ("core", "a")), ("core", "a")
    ).astype(f32)
    d_in = expert_grad[:, :, : 2 * FF]
    d_down = expert_grad[:, :, 2 * FF :]
    dense_grad = collect(dense_grad, ("r", "exp")).astype(bf16)
    from_dense = reorder_matrix(dense, home)
    mixed = dot_nn(out[0], from_expert)
    for index in range(1, n_a):
        mixed = mixed + dot_nn(out[index], from_expert)
    block_out = dot_nn((wide[:, :width] + mixed).astype(bf16), from_dense).astype(bf16)
    input_grad = dot_nn(input_grad, from_dense).astype(bf16)
    dense_grad, block_out, input_grad = lax.optimization_barrier(
        (dense_grad, block_out, input_grad)
    )
    dense_grad = exchange(dense_grad.reshape((n_a, local_rows) + dense_grad.shape[1:]), "a")

    dense_state = [
        qkv_weight,
        qkv_mean,
        qkv_square,
        out_weight,
        out_mean,
        out_square,
        router_weight.T,
        router_mean.T,
        router_square.T,
        norm_gains.T,
        gains_mean.T,
        gains_square.T,
    ]
    (
        new_qkv,
        new_qkv_mean,
        new_qkv_square,
        new_out,
        new_out_mean,
        new_out_square,
        new_router,
        new_router_mean,
        new_router_square,
        new_gains,
        new_gains_mean,
        new_gains_square,
    ) = whole_call(
        dense_update,
        [shape(item.shape, f32) for item in dense_state],
        [dense_grad] + dense_state,
        flops=20 * local_rows * (qkv_width + width),
    )
    new_router, new_router_mean, new_router_square = (
        item.T for item in (new_router, new_router_mean, new_router_square)
    )
    new_gains, new_gains_mean, new_gains_square = (
        item.T for item in (new_gains, new_gains_mean, new_gains_square)
    )
    new_in, new_in_mean, new_in_square = adamw(in_weight, d_in, in_mean, in_square, 0.1, decay_rate)
    new_down, new_down_mean, new_down_square = adamw(
        down_weight, d_down, down_mean, down_square, 1.0, decay_rate
    )
    return (
        block_out,
        input_grad,
        new_qkv,
        new_qkv_mean,
        new_qkv_square,
        new_out,
        new_out_mean,
        new_out_square,
        new_router,
        new_router_mean,
        new_router_square,
        new_gains,
        new_gains_mean,
        new_gains_square,
        new_in,
        new_in_mean,
        new_in_square,
        new_down,
        new_down_mean,
        new_down_square,
    )


def attend_heads(experts, x_ref, w_ref, table_ref, allow_ref, qkv_ref, lse_ref, att_ref):
    f32, bf16 = jnp.float32, jnp.bfloat16
    rows = x_ref.shape[0]
    width = w_ref.shape[0]
    gains = gain_rows(w_ref[:, 2 * LANES :], experts)
    x = x_ref[:, :width].astype(f32)
    normed = (x * rms_scale(x) * gains[0:1]).astype(bf16)
    projected = dot_nn(normed, w_ref[:, : 2 * LANES])
    lane = lane_iota(rows)
    cosine, sine = table_ref[:, :LANES], table_ref[:, LANES:]
    queries, others = projected[:, :LANES], projected[:, LANES:]
    turned = others * cosine + swap_halves(others) * sine
    qkv_ref[:, :LANES] = (queries * cosine + swap_halves(queries) * sine).astype(bf16)
    qkv_ref[:, LANES:] = jnp.where(lane < HEAD_DIMENSION, turned, others).astype(bf16)
    keys = qkv_ref[:, LANES : LANES + HEAD_DIMENSION]
    values = qkv_ref[:, LANES + HEAD_DIMENSION :]
    allowed = allow_ref[0] > 0.0
    logs = jnp.zeros((rows, LANES), f32)
    outs = []
    for head in range(QUERY_HEADS // KEY_VALUE_HEADS):
        scores = dot_nt(qkv_ref[:, head_block(head)], keys) * HEAD_DIMENSION ** (-0.5)
        scores = jnp.where(allowed, scores, mask_fill)
        peak = jnp.max(scores, axis=1, keepdims=True)
        log_total = peak + jnp.log(jnp.sum(jnp.exp(scores - peak), axis=1, keepdims=True))
        logs = jnp.where(lane == head, log_total, logs)
        outs.append(dot_nn(jnp.exp(scores - log_total).astype(bf16), values))
    lse_ref[...] = logs
    att_ref[0] = jnp.concatenate(outs, axis=1).astype(bf16)


def home_forward(
    experts, copies, x_ref, att_ref, out_ref, extra_ref, used_ref, order_ref, wide_ref, sent_ref
):
    f32, bf16 = jnp.float32, jnp.bfloat16
    width = x_ref.shape[1]
    extra = extra_ref[...]
    hidden = x_ref[...].astype(f32)
    for place in range(att_ref.shape[0]):
        hidden = hidden + dot_nt(att_ref[place], out_ref[:, place * LANES : (place + 1) * LANES])
    wide_ref[:, :width] = hidden
    second = (hidden * rms_scale(hidden) * gain_rows(extra, experts)[1:2]).astype(bf16)
    used = used_ref[...] > 0.0
    logits = jnp.where(used, dot_nn(second, extra), mask_fill)
    powers = jnp.where(used, jnp.exp(logits - jnp.max(logits, axis=1, keepdims=True)), 0.0)
    gates = powers / jnp.sum(powers, axis=1, keepdims=True)
    wide_ref[:, width:] = gates
    high = gates.astype(bf16).astype(f32)
    lanes = (high + pltpu.roll(gates - high, experts, 1)).astype(bf16)
    moved = dot_nn(second, order_ref[...]).astype(bf16)
    for copy in range(copies):
        sent_ref[copy, :, :width] = moved
        sent_ref[copy, :, width:] = lanes


def home_back(
    experts,
    parts_ref,
    order_ref,
    cot_ref,
    wide_ref,
    extra_ref,
    out_ref,
    att_ref,
    split_ref,
    hidden_grad_ref,
    mid_ref,
    grad_ref,
):
    f32, bf16 = jnp.float32, jnp.bfloat16
    rows, width = cot_ref.shape
    extra = extra_ref[...]
    split = split_ref[...]
    dots = jnp.zeros((rows, LANES), f32)
    second_grad = jnp.zeros((rows, width), f32)
    for source in range(parts_ref.shape[0]):
        dots = dots + parts_ref[source, :, width:].astype(f32)
        second_grad = second_grad + dot_nn(parts_ref[source, :, :width], order_ref[...])
    dots = dots + pltpu.roll(dots, LANES - experts, 1)
    gates = wide_ref[:, width:]
    logit_grad = (gates * (dots - jnp.sum(gates * dots, axis=1, keepdims=True))).astype(bf16)
    second_grad = second_grad + dot_nt(logit_grad, extra)
    gain = gain_rows(extra, experts)[1:2]
    hidden = wide_ref[:, :width]
    scale = rms_scale(hidden)
    scaled = second_grad * gain
    hidden_grad = (
        cot_ref[...].astype(f32)
        + scale * scaled
        - hidden * (scale * scale * scale) * jnp.mean(scaled * hidden, axis=1, keepdims=True)
    )
    hidden_grad_ref[...] = hidden_grad
    branch_grad = hidden_grad.astype(bf16)
    branch_split = dot_nn(branch_grad, split).astype(bf16)
    for place in range(att_ref.shape[0]):
        columns = slice(place * LANES, (place + 1) * LANES)
        mid_ref[place] = dot_nn(branch_grad, out_ref[:, columns]).astype(bf16)
        grad_ref[:, columns] = dot_tn(branch_split, att_ref[place]).astype(bf16)
    second = dot_nn((hidden * scale * gain).astype(bf16), split).astype(bf16)
    sums = second_grad * hidden * scale
    high = sums.astype(bf16)
    low = (sums - high.astype(f32)).astype(bf16)
    place = (lane_iota(rows) == experts + 1).astype(bf16)
    grad_ref[:, width:] = (
        dot_tn(second, logit_grad)
        + dot_tn(dot_nn(high, split).astype(bf16), place)
        + dot_tn(dot_nn(low, split).astype(bf16), place)
    ).astype(bf16)


def heads_back(
    experts,
    x_ref,
    w_ref,
    table_ref,
    allow_ref,
    qkv_ref,
    lse_ref,
    mid_ref,
    grad_ref,
    normed_grad_ref,
    normed_ref,
    proj_ref,
    sums_ref,
):
    f32, bf16 = jnp.float32, jnp.bfloat16
    block = pl.program_id(0)
    rows = x_ref.shape[0]
    width = w_ref.shape[0]
    score_scale = HEAD_DIMENSION ** (-0.5)
    here = pl.ds(pl.multiple_of(block * rows, rows), rows)
    gains = gain_rows(w_ref[:, 2 * LANES :], experts)
    x = x_ref[:, :width].astype(f32)
    scale = rms_scale(x)
    normed_ref[here, :] = (x * scale * gains[0:1]).astype(bf16)
    keys = qkv_ref[:, LANES : LANES + HEAD_DIMENSION]
    values = qkv_ref[:, LANES + HEAD_DIMENSION :]
    allowed = allow_ref[0] > 0.0
    lane = lane_iota(rows)
    logs = lse_ref[...]
    query_grads = []
    key_grad = jnp.zeros((rows, HEAD_DIMENSION), f32)
    value_grad = jnp.zeros((rows, HEAD_DIMENSION), f32)
    for head in range(QUERY_HEADS // KEY_VALUE_HEADS):
        queries = qkv_ref[:, head_block(head)]
        mid = mid_ref[0, :, head_block(head)]
        log_total = jnp.sum(jnp.where(lane == head, logs, 0.0), axis=1, keepdims=True)
        scores = jnp.where(allowed, dot_nt(queries, keys) * score_scale, mask_fill)
        weights = jnp.exp(scores - log_total)
        weight_grad = dot_nt(mid, values)
        delta = jnp.sum(weights * weight_grad, axis=1, keepdims=True)
        score_grad = (weights * (weight_grad - delta)).astype(bf16)
        query_grads.append(dot_nn(score_grad, keys) * score_scale)
        key_grad = key_grad + dot_tn(score_grad, queries)
        value_grad = value_grad + dot_tn(weights.astype(bf16), mid)
    cosine, sine = table_ref[:, :LANES], table_ref[:, LANES:]
    queries = jnp.concatenate(query_grads, axis=1)
    others = jnp.concatenate([key_grad * score_scale, value_grad], axis=1)
    turned = others * cosine - swap_halves(others) * sine
    queries = (queries * cosine - swap_halves(queries) * sine).astype(bf16)
    others = jnp.where(lane < HEAD_DIMENSION, turned, others).astype(bf16)
    proj_ref[here, :] = jnp.concatenate([queries, others], axis=1)
    normed_grad = dot_nt(proj_ref[here, :], w_ref[:, : 2 * LANES])
    normed_grad_ref[0] = normed_grad.astype(bf16)
    sums = normed_grad * x * scale

    @pl.when(block == 0)
    def _():
        sums_ref[...] = sums

    @pl.when(block > 0)
    def _():
        sums_ref[...] += sums

    @pl.when(block == pl.num_programs(0) - 1)
    def _():
        grad_ref[:, : 2 * LANES] = dot_tn(normed_ref[...], proj_ref[...]).astype(bf16)
        grad_ref[:, 2 * LANES :] = column_sums(sums_ref[...], experts).astype(bf16)


def heads_update(places, qkv_parts_ref, out_parts_ref, *refs):
    f32 = jnp.float32
    sources = qkv_parts_ref.shape[0]
    totals = []
    for place in range(places):
        total = qkv_parts_ref[place].astype(f32)
        for source in range(place + places, sources, places):
            total = total + qkv_parts_ref[source].astype(f32)
        totals.append(total)
    out_total = out_parts_ref[0].astype(f32)
    for source in range(1, out_parts_ref.shape[0]):
        out_total = out_total + out_parts_ref[source].astype(f32)
    width = refs[3].shape[1]
    experts = refs[6].shape[0]
    small = out_total[:, width:]
    for total in totals:
        small = small + total[:, 2 * LANES :]
    small = jnp.transpose(small)
    middle = LANES + HEAD_DIMENSION
    qkv_grad = jnp.concatenate(
        [total[:, :LANES] for total in totals]
        + [total[:, LANES:middle] for total in totals]
        + [total[:, middle : 2 * LANES] for total in totals],
        axis=1,
    )
    grads = (qkv_grad, out_total[:, :width], small[:experts], small[experts : experts + 2])
    rates = ((0.15, decay_rate), (0.3, decay_rate), (0.05, decay_rate), (0.8, 0.0))
    for index, (rate, decay) in enumerate(rates):
        weight_ref, mean_ref, square_ref = refs[3 * index : 3 * index + 3]
        values = adamw(weight_ref[...], grads[index], mean_ref[...], square_ref[...], rate, decay)
        for out_ref, value in zip(refs[3 * index + 12 : 3 * index + 15], values):
            out_ref[...] = value


def block_call(kernel, blocks, inputs, outputs, operands, scratch, flops):
    def spec(shape, place):
        rank = len(shape)
        if place is None:
            return pl.BlockSpec(shape, lambda i: (0,) * rank)
        return pl.BlockSpec(shape, lambda i: (place(i),) + (0,) * (rank - 1))

    moved = sum(math.prod(item.shape) * item.dtype.itemsize for item in operands)
    return pl.pallas_call(
        kernel,
        grid=(blocks,),
        out_shape=[item for item, _, _ in outputs],
        in_specs=[spec(shape, place) for shape, place in inputs],
        out_specs=[spec(shape, place) for _, shape, place in outputs],
        scratch_shapes=scratch,
        compiler_params=pltpu.CompilerParams(vmem_limit_bytes=VMEM_BYTES),
        cost_estimate=pl.CostEstimate(flops=flops, bytes_accessed=moved, transcendentals=0),
    )(*operands)


def body_heads(
    tokens,
    cotangent,
    doc_lengths,
    routes,
    qkv_weight,
    qkv_mean,
    qkv_square,
    out_weight,
    out_mean,
    out_square,
    router_weight,
    router_mean,
    router_square,
    norm_gains,
    gains_mean,
    gains_square,
    in_weight,
    in_mean,
    in_square,
    down_weight,
    down_mean,
    down_square,
):
    f32, bf16 = jnp.float32, jnp.bfloat16
    shape = jax.ShapeDtypeStruct
    plane = ("r", "core", "exp")
    n_a, n_r, n_c, n_e = (lax.axis_size(name) for name in MESH_AXES)
    places = n_r * n_c * n_e
    rows, width = tokens.shape
    experts = router_weight.shape[1]
    local_count = in_weight.shape[0]
    local_rows = qkv_weight.shape[0]
    sizes = (n_a, n_r, n_c, n_e, local_rows)
    home, expert, split = (order_of(kind, sizes) for kind in ("home", "expert", "dense"))
    query_width = QUERY_HEADS * HEAD_DIMENSION
    key_width = KEY_VALUE_HEADS * HEAD_DIMENSION
    lines = places * local_rows

    positions, segment = doc_layout(doc_lengths.reshape(-1), rows)
    marks = jnp.stack([positions, segment.astype(f32)], axis=1).astype(bf16)
    marks = jnp.concatenate([marks, jnp.zeros((rows, LANES - 2), bf16)], axis=1)
    x_all = lax.all_gather(jnp.concatenate([tokens, marks], axis=1), plane, axis=0, tiled=True)

    def by_place(values, start, stop):
        return values[:, start:stop].reshape(local_rows, places, (stop - start) // places)

    qkv_low = qkv_weight.astype(bf16)
    extra = jnp.concatenate(
        [
            router_weight.astype(bf16),
            norm_gains.astype(bf16),
            jnp.zeros((local_rows, LANES - experts - 2), bf16),
        ],
        axis=1,
    )
    pack = jnp.concatenate(
        [
            by_place(qkv_low, 0, query_width),
            by_place(qkv_low, query_width, query_width + key_width),
            by_place(qkv_low, query_width + key_width, query_width + 2 * key_width),
            jnp.broadcast_to(extra[:, None], (local_rows, places, LANES)),
        ],
        axis=2,
    )
    pack = exchange(pack.transpose(1, 0, 2), plane).reshape(lines, 3 * LANES)
    expert_pack = jnp.concatenate([in_weight.astype(bf16), down_weight.astype(bf16)], axis=2)
    pieces = pieces_for(expert_pack, ("core", "a"))
    pack, *pieces = lax.optimization_barrier((pack, *pieces))
    pack = jnp.concatenate([pack, out_weight.astype(bf16).reshape(lines, LANES)], axis=1)
    pack = spread(pack, "a")
    expert_pack = exchange_aside(pieces, ("core", "a"))

    cosine, sine = rope_tables(x_all[:, width].astype(f32), HEAD_DIMENSION)
    repeat = LANES // HEAD_DIMENSION
    tables = jnp.concatenate([cosine, cosine] * repeat + [-sine, sine] * repeat, axis=1)
    segments = x_all[:, width + 1].astype(f32).reshape(places, rows)
    row_index = jnp.arange(rows, dtype=jnp.int32)
    allowed = (
        (segments[:, :, None] == segments[:, None, :])
        & (row_index[None, None, :] <= row_index[None, :, None])
    ).astype(f32)
    used = jnp.any(
        routes[:, :, None] == jnp.arange(LANES, dtype=jnp.int32)[None, None, :], axis=1
    ).astype(f32)

    cot_expert = dot_nn(cotangent, reorder_matrix(home, expert)).astype(bf16)
    to_expert = reorder_matrix(home, expert)
    pack, expert_pack, tables, allowed, used, cot_expert, to_expert = lax.optimization_barrier(
        (pack, expert_pack, tables, allowed, used, cot_expert, to_expert)
    )
    out_rows = pack[:, 3 * LANES :].reshape(n_a * local_rows, width)
    out_rows = spread(out_rows, ("r", "exp"))
    extra_full = pack[:, 2 * LANES : 3 * LANES]
    first_gain = extra_full[:, experts].astype(f32)
    cot_group = spread_aside(spread_aside(cot_expert, "a"), "core")
    expert_full = lax.all_gather(expert_pack, ("exp", "r"), axis=0, tiled=True).reshape(
        n_e, width, 3 * FF
    )

    def same(index):
        return index

    row_inputs = [
        ((rows, width + LANES), same),
        ((width, 3 * LANES), None),
        ((rows, 2 * LANES), same),
        ((1, rows, rows), same),
    ]
    qkv, logs, attended = block_call(
        functools.partial(attend_heads, experts),
        places,
        row_inputs,
        [
            (shape((places * rows, 2 * LANES), bf16), (rows, 2 * LANES), same),
            (shape((places * rows, LANES), f32), (rows, LANES), same),
            (shape((places, rows, LANES), bf16), (1, rows, LANES), same),
        ],
        [x_all, pack, tables, allowed],
        [],
        flops=2 * places * rows * width * 3 * LANES,
    )
    attended, out_rows = lax.optimization_barrier((attended, out_rows))
    attended = exchange(attended, plane)
    attended, out_rows = lax.optimization_barrier((attended, out_rows))
    out_full = spread(out_rows, "core").reshape(n_c, n_r, n_e, n_a, local_rows, width)
    out_full = out_full.transpose(3, 1, 0, 2, 4, 5).reshape(width, width)
    wide, sent = whole_call(
        functools.partial(home_forward, experts, n_a),
        [shape((rows, width + LANES), f32), shape((n_a, rows, width + LANES), bf16)],
        [tokens, attended, out_full, extra_full, used, to_expert],
        flops=4 * rows * width * width,
    )

    arrived = exchange(sent, "a").reshape(n_a * rows, width + LANES)
    arrived = spread(arrived, "core")
    place = (lax.axis_index("core") * n_a + lax.axis_index("a")).astype(jnp.int32).reshape(1)
    out, inner = run_forward(place, arrived, expert_full, experts, local_count)
    back, inner_grad, activation = run_backward(
        place, arrived, cot_group, expert_full, inner, experts, local_count
    )
    out = collect_aside(out, "core").astype(bf16).reshape(n_a, rows, width)
    back = collect(back, "core").astype(bf16)

    factors = (arrived, inner_grad, cot_group, activation)
    expert_grads = list(weight_grads(factors, n_e, n_r))
    back = exchange(back.reshape(n_a, rows, width + LANES), "a")
    received = send_grads(expert_grads, n_e, n_r, width)
    back, out, expert_grads[0] = lax.optimization_barrier((back, out, expert_grads[0]))
    out = exchange(out, "a")

    from_expert = reorder_matrix(expert, home)
    hidden_grad, mid, out_grad = whole_call(
        functools.partial(home_back, experts),
        [
            shape((rows, width), f32),
            shape((places, rows, LANES), bf16),
            shape((width, query_width + LANES), bf16),
        ],
        [
            back,
            from_expert,
            cotangent,
            wide,
            extra_full,
            out_full,
            attended,
            reorder_matrix(home, split),
        ],
        earlier=expert_grads[:1],
        flops=1,
    )
    mid, out = lax.optimization_barrier((mid, out))
    mid = exchange(mid, plane)
    mid, out_grad = lax.optimization_barrier((mid, out_grad))
    out_grad = collect(out_grad, "core").astype(bf16)
    out_grad = collect(out_grad, ("r", "exp")).astype(bf16)
    out_grad = exchange(out_grad.reshape(n_a, local_rows, query_width + LANES), "a")
    mid, out_grad, *received = lax.optimization_barrier((mid, out_grad, *received))

    def core_first(index):
        return (index // n_e % n_c * n_r + index // (n_c * n_e)) * n_e + index % n_e

    qkv_grad, normed_grad = block_call(
        functools.partial(heads_back, experts),
        places,
        row_inputs
        + [((rows, 2 * LANES), same), ((rows, LANES), same), ((1, rows, LANES), same)],
        [
            (shape((width, 3 * LANES), bf16), (width, 3 * LANES), None),
            (shape((places, rows, width), bf16), (1, rows, width), core_first),
        ],
        [x_all, pack, tables, allowed, qkv, logs, mid],
        [
            pltpu.VMEM((places * rows, width), bf16),
            pltpu.VMEM((places * rows, 2 * LANES), bf16),
            pltpu.VMEM((rows, width), f32),
        ],
        flops=2 * places * rows * width * 6 * LANES,
    )
    qkv_grad = exchange(qkv_grad.reshape(n_a * places, local_rows, 3 * LANES), MESH_AXES)
    normed_grad = collect(normed_grad.reshape(places * rows, width), "core").astype(bf16)
    expert_grad = received[0].astype(f32)
    for part in received[1:]:
        expert_grad = expert_grad + part.astype(f32)
    expert_grad = expert_grad.astype(bf16).reshape(
        n_c * n_a, width // (n_r * n_c * n_a), 3 * FF
    )
    expert_grad = exchange_aside(
        pieces_for(expert_grad, ("core", "a")), ("core", "a")
    ).astype(f32)
    normed_grad, expert_grad = lax.optimization_barrier((normed_grad, expert_grad))
    normed_grad = collect(normed_grad, ("r", "exp"))

    residual = tokens.astype(f32)
    first_scale = rms_scale(residual)
    scaled = normed_grad * first_gain
    input_grad = (
        hidden_grad
        + first_scale * scaled
        - residual * first_scale**3 * jnp.mean(scaled * residual, axis=-1, keepdims=True)
    ).astype(bf16)
    mixed = dot_nn(out[0], from_expert)
    for index in range(1, n_a):
        mixed = mixed + dot_nn(out[index], from_expert)
    block_out = (wide[:, :width] + mixed).astype(bf16)

    d_in = expert_grad[:, :, : 2 * FF]
    d_down = expert_grad[:, :, 2 * FF :]

    dense_state = [
        qkv_weight,
        qkv_mean,
        qkv_square,
        out_weight,
        out_mean,
        out_square,
        router_weight.T,
        router_mean.T,
        router_square.T,
        norm_gains.T,
        gains_mean.T,
        gains_square.T,
    ]
    (
        new_qkv,
        new_qkv_mean,
        new_qkv_square,
        new_out,
        new_out_mean,
        new_out_square,
        new_router,
        new_router_mean,
        new_router_square,
        new_gains,
        new_gains_mean,
        new_gains_square,
    ) = whole_call(
        functools.partial(heads_update, places),
        [shape(item.shape, f32) for item in dense_state],
        [qkv_grad, out_grad] + dense_state,
        flops=60 * local_rows * width,
    )
    new_router, new_router_mean, new_router_square = (
        item.T for item in (new_router, new_router_mean, new_router_square)
    )
    new_gains, new_gains_mean, new_gains_square = (
        item.T for item in (new_gains, new_gains_mean, new_gains_square)
    )
    new_in, new_in_mean, new_in_square = adamw(in_weight, d_in, in_mean, in_square, 0.1, decay_rate)
    new_down, new_down_mean, new_down_square = adamw(
        down_weight, d_down, down_mean, down_square, 1.0, decay_rate
    )
    return (
        block_out,
        input_grad,
        new_qkv,
        new_qkv_mean,
        new_qkv_square,
        new_out,
        new_out_mean,
        new_out_square,
        new_router,
        new_router_mean,
        new_router_square,
        new_gains,
        new_gains_mean,
        new_gains_square,
        new_in,
        new_in_mean,
        new_in_square,
        new_down,
        new_down_mean,
        new_down_square,
    )


def solution(mesh):
    n_dp, n_exp = mesh.shape["dp"], mesh.shape["exp"]
    n_a = EXPERTS // n_exp // 2
    mesh = Mesh(
        mesh.devices.reshape(n_a, n_dp // (2 * n_a), 2, n_exp), MESH_AXES
    )
    placed = (
        P(("a", "r", "core", "exp"), None),
        P(("a", "r", "core", "exp"), None),
        P(("a", "r", "core", "exp"), None),
        P(("a", "r", "core", "exp"), None),
        P(("a", "r", "core", "exp"), None),
        P(("a", "r", "core", "exp"), None),
        P(("a", "r", "core", "exp"), None),
        P(("a", "r", "core", "exp"), None),
        P(("a", "r", "core", "exp"), None),
        P(("a", "r", "core", "exp"), None),
        P(("a", "r", "core", "exp"), None),
        P(("a", "r", "core", "exp"), None),
        P(("a", "r", "core", "exp"), None),
        P(("a", "r", "core", "exp"), None),
        P(("a", "r", "core", "exp"), None),
        P(("a", "r", "core", "exp"), None),
        P("exp", ("a", "r", "core"), None),
        P("exp", ("a", "r", "core"), None),
        P("exp", ("a", "r", "core"), None),
        P("exp", ("a", "r", "core"), None),
        P("exp", ("a", "r", "core"), None),
        P("exp", ("a", "r", "core"), None),
    )
    shared = mesh.size // n_a == KEY_VALUE_HEADS
    return jax.shard_map(
        body_heads if shared else body,
        mesh=mesh,
        in_specs=placed,
        out_specs=(
            P(("a", "r", "core", "exp"), None),
            P(("a", "r", "core", "exp"), None),
            P(("a", "r", "core", "exp"), None),
            P(("a", "r", "core", "exp"), None),
            P(("a", "r", "core", "exp"), None),
            P(("a", "r", "core", "exp"), None),
            P(("a", "r", "core", "exp"), None),
            P(("a", "r", "core", "exp"), None),
            P(("a", "r", "core", "exp"), None),
            P(("a", "r", "core", "exp"), None),
            P(("a", "r", "core", "exp"), None),
            P(("a", "r", "core", "exp"), None),
            P(("a", "r", "core", "exp"), None),
            P(("a", "r", "core", "exp"), None),
            P("exp", ("a", "r", "core"), None),
            P("exp", ("a", "r", "core"), None),
            P("exp", ("a", "r", "core"), None),
            P("exp", ("a", "r", "core"), None),
            P("exp", ("a", "r", "core"), None),
            P("exp", ("a", "r", "core"), None),
        ),
        check_vma=False,
    )
```

```python
import functools
import math

import jax
import jax.numpy as jnp
import numpy as np
from jax import lax
from jax.experimental import pallas as pl
from jax.experimental.pallas import tpu as pltpu
from jax.sharding import Mesh
from jax.sharding import PartitionSpec as P

QUERY_HEADS = 16
KEY_VALUE_HEADS = 8
HEAD_DIMENSION = 64
FF = 512
STEP = 10
EXPERTS = 16
LANES = 128
MESH_AXES = ("a", "r", "core", "exp")
VMEM_BYTES = 26 * 1024 * 1024


norm_eps = 1e-06
rope_base = 10000.0
mask_fill = -1e30
beta_one = 0.9
beta_two = 0.95
adam_eps = 1e-08
decay_rate = 0.1


def rms_scale(values):
    return lax.rsqrt(jnp.mean(values * values, axis=-1, keepdims=True) + norm_eps)


def doc_layout(doc_lens, sequence_length):
    row_index = jnp.arange(sequence_length, dtype=jnp.int32)
    doc_ends = jnp.cumsum(doc_lens, dtype=jnp.int32)
    passed = (row_index[:, None] >= doc_ends[None, :]).astype(jnp.int32)
    segment = jnp.sum(passed, axis=1, dtype=jnp.int32)
    starts = jnp.sum(passed * doc_lens[None, :], axis=1, dtype=jnp.int32)
    return ((row_index - starts).astype(jnp.float32), segment)


def rope_tables(positions, head_size):
    half_size = head_size // 2
    freq_index = jnp.arange(half_size, dtype=jnp.float32)
    inverse = jnp.exp(freq_index * (-2.0 * math.log(rope_base) / head_size))
    angles = positions[:, None] * inverse[None, :]
    return (jnp.cos(angles), jnp.sin(angles))


def adamw(weight, gradient, mean_old, square_old, step_rate, weight_decay):
    mean_new = beta_one * mean_old + (1.0 - beta_one) * gradient
    square_new = beta_two * square_old + (1.0 - beta_two) * gradient * gradient
    corrected = (
        mean_new
        / (1.0 - beta_one**STEP)
        / (jnp.sqrt(square_new / (1.0 - beta_two**STEP)) + adam_eps)
    )
    return (weight - step_rate * (corrected + weight_decay * weight), mean_new, square_new)

def dot_nn(left, right):
    return jnp.dot(left, right, preferred_element_type=jnp.float32)


def dot_nt(left, right):
    return lax.dot_general(left, right, (((1,), (1,)), ((), ())), preferred_element_type=jnp.float32)


def dot_tn(left, right):
    return lax.dot_general(left, right, (((0,), (0,)), ((), ())), preferred_element_type=jnp.float32)


def lane_iota(rows):
    return lax.broadcasted_iota(jnp.int32, (rows, LANES), 1)


def gain_rows(extra, experts):
    row = lax.broadcasted_iota(jnp.int32, (8, LANES), 0)
    pick = (lane_iota(8) == row + experts).astype(jnp.bfloat16)
    return dot_nt(jnp.where(row < 2, pick, jnp.zeros_like(pick)), extra)


def swap_halves(values):
    half = HEAD_DIMENSION // 2
    lower = lane_iota(values.shape[0]) % HEAD_DIMENSION < half
    return jnp.where(lower, pltpu.roll(values, LANES - half, 1), pltpu.roll(values, half, 1))


def column_sums(values, lane):
    high = values.astype(jnp.bfloat16)
    low = (values - high.astype(jnp.float32)).astype(jnp.bfloat16)
    place = (lane_iota(values.shape[0]) == lane).astype(jnp.bfloat16)
    return dot_tn(high, place) + dot_tn(low, place)


def head_block(index):
    return slice(index * HEAD_DIMENSION, (index + 1) * HEAD_DIMENSION)


def attention_forward(
    experts,
    copies,
    x_ref,
    w_ref,
    cos_ref,
    sin_ref,
    allow_ref,
    used_ref,
    order_ref,
    wide_ref,
    qkv_ref,
    sent_ref,
):
    f32, bf16 = jnp.float32, jnp.bfloat16
    rows, width = x_ref.shape
    query_width = QUERY_HEADS * HEAD_DIMENSION
    key_width = KEY_VALUE_HEADS * HEAD_DIMENSION
    qkv_width = query_width + 2 * key_width
    extra = w_ref[:, qkv_width + width :]
    gains = gain_rows(extra, experts)
    x = x_ref[...].astype(f32)
    normed = (x * rms_scale(x) * gains[0:1]).astype(bf16)
    cosine, sine = cos_ref[...], sin_ref[...]
    for start in range(0, qkv_width, 512):
        part = dot_nn(normed, w_ref[:, start : start + 512])
        for inner in range(0, 512, LANES):
            piece = part[:, inner : inner + LANES]
            if start + inner < query_width + key_width:
                piece = piece * cosine + swap_halves(piece) * sine
            qkv_ref[:, start + inner : start + inner + LANES] = piece.astype(bf16)
    allowed = allow_ref[...] > 0.0
    lane = lane_iota(rows)
    logs = jnp.zeros((rows, LANES), f32)
    fold = QUERY_HEADS // KEY_VALUE_HEADS
    for group in range(KEY_VALUE_HEADS):
        keys = qkv_ref[:, query_width + group * HEAD_DIMENSION : query_width + (group + 1) * HEAD_DIMENSION]
        values = qkv_ref[
            :,
            query_width + key_width + group * HEAD_DIMENSION : query_width
            + key_width
            + (group + 1) * HEAD_DIMENSION,
        ]
        outs = []
        for head in range(group * fold, (group + 1) * fold):
            scores = dot_nt(qkv_ref[:, head_block(head)], keys) * HEAD_DIMENSION ** (-0.5)
            scores = jnp.where(allowed, scores, mask_fill)
            peak = jnp.max(scores, axis=1, keepdims=True)
            log_total = peak + jnp.log(jnp.sum(jnp.exp(scores - peak), axis=1, keepdims=True))
            logs = jnp.where(lane == head, log_total, logs)
            outs.append(dot_nn(jnp.exp(scores - log_total).astype(bf16), values))
        start = qkv_width + group * LANES
        qkv_ref[:, start : start + LANES] = jnp.concatenate(outs, axis=1).astype(bf16)
    wide_ref[:, width : width + LANES] = logs
    hidden = x + dot_nt(qkv_ref[:, qkv_width:], w_ref[:, qkv_width : qkv_width + width])
    wide_ref[:, :width] = hidden
    second = (hidden * rms_scale(hidden) * gains[1:2]).astype(bf16)
    used = used_ref[...] > 0.0
    logits = jnp.where(used, dot_nn(second, extra), mask_fill)
    powers = jnp.where(used, jnp.exp(logits - jnp.max(logits, axis=1, keepdims=True)), 0.0)
    gates = powers / jnp.sum(powers, axis=1, keepdims=True)
    wide_ref[:, width + LANES :] = gates
    high = gates.astype(bf16).astype(f32)
    lanes = (high + pltpu.roll(gates - high, experts, 1)).astype(bf16)
    moved = dot_nn(second, order_ref[...]).astype(bf16)
    for copy in range(copies):
        sent_ref[copy, :, :width] = moved
        sent_ref[copy, :, width:] = lanes


def own_gate(lanes, number, experts):
    lane = lane_iota(lanes.shape[0])
    chosen = (lane == number) | (lane == number + experts)
    return jnp.sum(jnp.where(chosen, lanes.astype(jnp.float32), 0.0), axis=1, keepdims=True)


def experts_forward(
    experts, local_count, place_ref, rows_ref, w_ref, out_ref, inner_ref, sum_ref
):
    f32, bf16 = jnp.float32, jnp.bfloat16
    index, chunk = pl.program_id(0), pl.program_id(1)
    count, width = out_ref.shape
    gate = own_gate(rows_ref[:, width:], index * local_count + place_ref[0], experts)
    inner = dot_nn(rows_ref[:, :width], w_ref[0, :, : 2 * FF])
    inner_ref[0] = inner
    gate_part = inner[:, :FF]
    activation = (gate_part * jax.nn.sigmoid(gate_part) * inner[:, FF:]).astype(bf16)
    result = dot_nt(activation, w_ref[0, :, 2 * FF :]).astype(bf16).astype(f32)
    here = pl.ds(pl.multiple_of(chunk * count, count), count)

    @pl.when(index == 0)
    def _():
        sum_ref[here, :] = gate * result

    @pl.when(index > 0)
    def _():
        sum_ref[here, :] += gate * result

    out_ref[...] = sum_ref[here, :].astype(bf16)


def experts_backward(
    experts,
    local_count,
    place_ref,
    gates_ref,
    cot_ref,
    w_ref,
    inner_ref,
    back_ref,
    inner_grad_ref,
    act_ref,
    sum_ref,
    dots_sum_ref,
):
    f32, bf16 = jnp.float32, jnp.bfloat16
    index, chunk = pl.program_id(0), pl.program_id(1)
    count, width = cot_ref.shape
    number = index * local_count + place_ref[0]
    gate = own_gate(gates_ref[...], number, experts)
    gate_part = inner_ref[0, :, :FF]
    up_part = inner_ref[0, :, FF:]
    gate_sigmoid = jax.nn.sigmoid(gate_part)
    gate_silu = gate_part * gate_sigmoid
    activation = (gate_silu * up_part).astype(bf16).astype(f32)
    act_ref[0] = (gate * activation).astype(bf16)
    act_grad = dot_nn(cot_ref[...], w_ref[0, :, 2 * FF :])
    dots = jnp.sum(activation * act_grad, axis=1, keepdims=True)
    dots_high = dots.astype(bf16).astype(f32)
    lane = lane_iota(count)
    lanes = jnp.where(lane == number, dots_high, 0.0) + jnp.where(
        lane == number + experts, dots - dots_high, 0.0
    )
    act_grad = gate * act_grad
    inner_grad_ref[0, :, :FF] = (
        act_grad * up_part * gate_sigmoid * (1.0 + gate_part * (1.0 - gate_sigmoid))
    ).astype(bf16)
    inner_grad_ref[0, :, FF:] = (act_grad * gate_silu).astype(bf16)
    copy_grad = dot_nt(inner_grad_ref[0], w_ref[0, :, : 2 * FF])
    here = pl.ds(pl.multiple_of(chunk * count, count), count)

    @pl.when(index == 0)
    def _():
        sum_ref[here, :] = copy_grad
        dots_sum_ref[here, :] = lanes

    @pl.when(index > 0)
    def _():
        sum_ref[here, :] += copy_grad
        dots_sum_ref[here, :] += lanes

    back_ref[:, :width] = sum_ref[here, :].astype(bf16)
    back_ref[:, width:] = dots_sum_ref[here, :].astype(bf16)


def experts_weights(where_ref, rows_ref, inner_grad_ref, cot_ref, act_ref, *grad_refs):
    goal = pl.program_id(0)
    inner = dot_tn(rows_ref[...], inner_grad_ref[0]).astype(jnp.bfloat16)
    down = dot_tn(cot_ref[...], act_ref[0]).astype(jnp.bfloat16)
    for index, grad_ref in enumerate(grad_refs):

        @pl.when(goal == index)
        def _(grad_ref=grad_ref):
            grad_ref[:, : 2 * FF] = inner
            grad_ref[:, 2 * FF :] = down


def home_backward(
    experts,
    parts_ref,
    order_ref,
    cot_ref,
    wide_ref,
    w_ref,
    qkv_ref,
    x_ref,
    cos_ref,
    sin_ref,
    allow_ref,
    grad_ref,
    input_grad_ref,
    mid_ref,
    proj_ref,
):
    f32, bf16 = jnp.float32, jnp.bfloat16
    rows, width = x_ref.shape
    sources = parts_ref.shape[0]
    query_width = QUERY_HEADS * HEAD_DIMENSION
    key_width = KEY_VALUE_HEADS * HEAD_DIMENSION
    qkv_width = query_width + 2 * key_width
    fold = QUERY_HEADS // KEY_VALUE_HEADS
    score_scale = HEAD_DIMENSION ** (-0.5)
    extra = w_ref[:, qkv_width + width :]
    gains = gain_rows(extra, experts)
    dots = jnp.zeros((rows, LANES), f32)
    second_grad = jnp.zeros((rows, width), f32)
    for source in range(sources):
        dots = dots + parts_ref[source, :, width:].astype(f32)
        second_grad = second_grad + dot_nn(parts_ref[source, :, :width], order_ref[...])
    dots = dots + pltpu.roll(dots, LANES - experts, 1)
    gates = wide_ref[:, width + LANES :]
    logit_grad = (gates * (dots - jnp.sum(gates * dots, axis=1, keepdims=True))).astype(bf16)
    second_grad = second_grad + dot_nt(logit_grad, extra)
    hidden = wide_ref[:, :width]
    scale = rms_scale(hidden)
    second = (hidden * scale * gains[1:2]).astype(bf16)
    scaled = second_grad * gains[1:2]
    hidden_grad = (
        cot_ref[...].astype(f32)
        + scale * scaled
        - hidden * (scale * scale * scale) * jnp.mean(scaled * hidden, axis=1, keepdims=True)
    )
    branch_grad = hidden_grad.astype(bf16)
    for start in range(0, width, 512):
        grad_ref[:, qkv_width + start : qkv_width + start + 512] = dot_tn(
            branch_grad, qkv_ref[:, qkv_width + start : qkv_width + start + 512]
        ).astype(bf16)
    small_grad = dot_tn(second, logit_grad) + column_sums(
        second_grad * hidden * scale, experts + 1
    )
    mid_ref[...] = dot_nn(branch_grad, w_ref[:, qkv_width : qkv_width + width]).astype(bf16)
    cosine, sine = cos_ref[...], sin_ref[...]
    allowed = allow_ref[...] > 0.0
    lane = lane_iota(rows)
    logs = wide_ref[:, width : width + LANES]

    def turned_back(values):
        return (values * cosine - swap_halves(values) * sine).astype(bf16)

    key_grads, value_grads = [], []
    for group in range(KEY_VALUE_HEADS):
        keys = qkv_ref[:, query_width + group * HEAD_DIMENSION : query_width + (group + 1) * HEAD_DIMENSION]
        values = qkv_ref[
            :,
            query_width + key_width + group * HEAD_DIMENSION : query_width
            + key_width
            + (group + 1) * HEAD_DIMENSION,
        ]
        query_grads = []
        key_grad = jnp.zeros((rows, HEAD_DIMENSION), f32)
        value_grad = jnp.zeros((rows, HEAD_DIMENSION), f32)
        for head in range(group * fold, (group + 1) * fold):
            queries = qkv_ref[:, head_block(head)]
            mid = mid_ref[:, head_block(head)]
            log_total = jnp.sum(jnp.where(lane == head, logs, 0.0), axis=1, keepdims=True)
            scores = jnp.where(allowed, dot_nt(queries, keys) * score_scale, mask_fill)
            weights = jnp.exp(scores - log_total)
            weight_grad = dot_nt(mid, values)
            delta = jnp.sum(weights * weight_grad, axis=1, keepdims=True)
            score_grad = (weights * (weight_grad - delta)).astype(bf16)
            query_grads.append(dot_nn(score_grad, keys) * score_scale)
            key_grad = key_grad + dot_tn(score_grad, queries)
            value_grad = value_grad + dot_tn(weights.astype(bf16), mid)
        proj_ref[:, group * LANES : (group + 1) * LANES] = turned_back(
            jnp.concatenate(query_grads, axis=1)
        )
        key_grads.append(key_grad * score_scale)
        value_grads.append(value_grad)
        if group % 2 == 1:
            start = query_width + (group // 2) * LANES
            proj_ref[:, start : start + LANES] = turned_back(
                jnp.concatenate(key_grads[-2:], axis=1)
            )
            start = start + key_width
            proj_ref[:, start : start + LANES] = jnp.concatenate(value_grads[-2:], axis=1).astype(
                bf16
            )
    x = x_ref[...].astype(f32)
    scale = rms_scale(x)
    normed = (x * scale * gains[0:1]).astype(bf16)
    for start in range(0, qkv_width, 512):
        grad_ref[:, start : start + 512] = dot_tn(normed, proj_ref[:, start : start + 512]).astype(
            bf16
        )
    normed_grad = dot_nt(proj_ref[...], w_ref[:, :qkv_width])
    scaled = normed_grad * gains[0:1]
    small_grad = small_grad + column_sums(normed_grad * x * scale, experts)
    grad_ref[:, qkv_width + width :] = small_grad.astype(bf16)
    input_grad_ref[...] = (
        hidden_grad
        + scale * scaled
        - x * (scale * scale * scale) * jnp.mean(scaled * x, axis=1, keepdims=True)
    ).astype(bf16)


def dense_update(parts_ref, *refs):
    total = parts_ref[0].astype(jnp.float32)
    for source in range(1, parts_ref.shape[0]):
        total = total + parts_ref[source].astype(jnp.float32)
    start = total.shape[1] - LANES
    small = jnp.transpose(total[:, start:])
    experts = refs[6].shape[0]
    qkv_width = refs[0].shape[1]
    grads = (
        total[:, :qkv_width],
        total[:, qkv_width:start],
        small[:experts],
        small[experts : experts + 2],
    )
    rates = ((0.15, decay_rate), (0.3, decay_rate), (0.05, decay_rate), (0.8, 0.0))
    for index, (rate, decay) in enumerate(rates):
        weight_ref, mean_ref, square_ref = refs[3 * index : 3 * index + 3]
        values = adamw(weight_ref[...], grads[index], mean_ref[...], square_ref[...], rate, decay)
        for out_ref, value in zip(refs[3 * index + 12 : 3 * index + 15], values):
            out_ref[...] = value


def whole_call(kernel, outputs, operands, flops, scratch=(), earlier=()):
    operands_read = len(operands)

    def run(*refs):
        kernel(*refs[:operands_read], *refs[operands_read + len(earlier) :])

    moved = sum(math.prod(item.shape) * item.dtype.itemsize for item in list(outputs) + list(operands))
    moved = moved if flops > 1 else 1
    return pl.pallas_call(
        run,
        out_shape=outputs,
        in_specs=[pl.BlockSpec(memory_space=pltpu.VMEM)] * len(operands)
        + [pl.BlockSpec(memory_space=pl.ANY)] * len(earlier),
        out_specs=[pl.BlockSpec(memory_space=pltpu.VMEM)] * len(outputs),
        scratch_shapes=list(scratch),
        compiler_params=pltpu.CompilerParams(vmem_limit_bytes=VMEM_BYTES),
        cost_estimate=pl.CostEstimate(flops=flops, bytes_accessed=moved, transcendentals=0),
    )(*operands, *earlier)


def order_of(kind, sizes):
    axes = {"home": (0, 1, 2, 3, 4), "dense": (2, 1, 3, 0, 4), "expert": (1, 2, 0, 3, 4)}[kind]
    return np.arange(math.prod(sizes), dtype=np.int32).reshape(sizes).transpose(axes).reshape(-1)


def reorder_matrix(before, after):
    return (jnp.asarray(before)[:, None] == jnp.asarray(after)[None, :]).astype(jnp.bfloat16)


def exchange(values, axes):
    return lax.all_to_all(values, axes, split_axis=0, concat_axis=0, tiled=True)


def spread(values, axes):
    count = lax.axis_size(axes)
    copies = exchange(jnp.broadcast_to(values[None], (count,) + values.shape), axes)
    return copies.reshape((count * values.shape[0],) + values.shape[1:])


def collect(values, axes):
    count = lax.axis_size(axes)
    parts = exchange(values.reshape((count, values.shape[0] // count) + values.shape[1:]), axes)
    total = parts[0].astype(jnp.float32)
    for index in range(1, count):
        total = total + parts[index].astype(jnp.float32)
    return total


def partner(values, axes, step):
    names = (axes,) if isinstance(axes, str) else axes
    steps = {}
    for name in reversed(names):
        step, steps[name] = divmod(step, lax.axis_size(name))
    names = tuple(name for name in MESH_AXES if name in names)
    flat = 0
    for name in names:
        flat = flat * lax.axis_size(name) + steps[name]
    pairs = [(index, index ^ flat) for index in range(lax.axis_size(names))]
    return lax.ppermute(values, names, pairs)


def piece_of(values, index):
    return lax.dynamic_index_in_dim(values, index, 0, keepdims=False)


def in_order(own, received, me):
    result = jnp.zeros((len(received) + 1,) + own.shape, own.dtype)
    for step, part in enumerate([own] + received):
        result = lax.dynamic_update_index_in_dim(result, part, me ^ step, 0)
    return result


def spread_aside(values, axes):
    count = lax.axis_size(axes)
    received = [partner(values, axes, step) for step in range(1, count)]
    result = in_order(values, received, lax.axis_index(axes))
    return result.reshape((count * values.shape[0],) + values.shape[1:])


def pieces_for(values, axes):
    me = lax.axis_index(axes)
    return [piece_of(values, me ^ step) for step in range(values.shape[0])]


def exchange_aside(pieces, axes):
    received = [partner(piece, axes, step) for step, piece in enumerate(pieces) if step > 0]
    return in_order(pieces[0], received, lax.axis_index(axes))


def collect_aside(values, axes):
    count = lax.axis_size(axes)
    pieces = pieces_for(values.reshape((count, values.shape[0] // count) + values.shape[1:]), axes)
    total = pieces[0].astype(jnp.float32)
    for step in range(1, count):
        total = total + partner(pieces[step], axes, step).astype(jnp.float32)
    return total


def expert_specs(n_e, group_rows, width):
    count = min(256, group_rows)
    return dict(
        grid=(n_e, group_rows // count),
        scalar=pl.BlockSpec(memory_space=pltpu.SMEM),
        wide=pl.BlockSpec((count, width), lambda k, i: (i, 0)),
        wider=pl.BlockSpec((count, width + LANES), lambda k, i: (i, 0)),
        lanes=pl.BlockSpec((count, LANES), lambda k, i: (i, width // LANES)),
        weight=pl.BlockSpec((1, width, 3 * FF), lambda k, i: (k, 0, 0)),
        inner=pl.BlockSpec((1, count, 2 * FF), lambda k, i: (k, i, 0)),
        act=pl.BlockSpec((1, count, FF), lambda k, i: (k, i, 0)),
    )


def run_forward(place, arrived, expert_full, experts, local_count):
    n_e, width, _ = expert_full.shape
    group_rows = arrived.shape[0]
    specs = expert_specs(n_e, group_rows, width)
    return pl.pallas_call(
        functools.partial(experts_forward, experts, local_count),
        grid=specs["grid"],
        out_shape=[
            jax.ShapeDtypeStruct((group_rows, width), jnp.bfloat16),
            jax.ShapeDtypeStruct((n_e, group_rows, 2 * FF), jnp.float32),
        ],
        in_specs=[specs["scalar"], specs["wider"], specs["weight"]],
        out_specs=[specs["wide"], specs["inner"]],
        scratch_shapes=[pltpu.VMEM((group_rows, width), jnp.float32)],
        compiler_params=pltpu.CompilerParams(vmem_limit_bytes=VMEM_BYTES),
        cost_estimate=pl.CostEstimate(
            flops=2 * n_e * group_rows * width * 3 * FF,
            bytes_accessed=n_e * width * (3 * FF * 2 + group_rows * 8),
            transcendentals=n_e * group_rows * FF,
        ),
    )(place, arrived, expert_full)


def run_backward(place, arrived, cot_group, expert_full, inner, experts, local_count):
    bf16 = jnp.bfloat16
    n_e, width, _ = expert_full.shape
    group_rows = arrived.shape[0]
    specs = expert_specs(n_e, group_rows, width)
    return pl.pallas_call(
        functools.partial(experts_backward, experts, local_count),
        grid=specs["grid"],
        out_shape=[
            jax.ShapeDtypeStruct((group_rows, width + LANES), bf16),
            jax.ShapeDtypeStruct((n_e, group_rows, 2 * FF), bf16),
            jax.ShapeDtypeStruct((n_e, group_rows, FF), bf16),
        ],
        in_specs=[
            specs["scalar"],
            specs["lanes"],
            specs["wide"],
            specs["weight"],
            specs["inner"],
        ],
        out_specs=[specs["wider"], specs["inner"], specs["act"]],
        scratch_shapes=[
            pltpu.VMEM((group_rows, width), jnp.float32),
            pltpu.VMEM((group_rows, LANES), jnp.float32),
        ],
        compiler_params=pltpu.CompilerParams(vmem_limit_bytes=VMEM_BYTES),
        cost_estimate=pl.CostEstimate(
            flops=2 * n_e * group_rows * width * 3 * FF,
            bytes_accessed=n_e * width * (3 * FF * 2 + group_rows * 10),
            transcendentals=n_e * group_rows * FF,
        ),
    )(place, arrived, cot_group, expert_full, inner)


def run_weights(arrived, inner_grad, cot_group, act, slots, firsts, blocks, part):
    group_rows = arrived.shape[0]
    goals = len(slots) // blocks
    where = jnp.stack(slots + firsts).astype(jnp.int32)

    def block_of(index):
        return lambda g, j, at: (jnp.where(g == index, j, jnp.where(g < index, 0, blocks - 1)), 0)

    return pl.pallas_call(
        experts_weights,
        grid_spec=pltpu.PrefetchScalarGridSpec(
            num_scalar_prefetch=1,
            grid=(goals, blocks),
            in_specs=[
                pl.BlockSpec((group_rows, part), lambda g, j, at: (0, at[(goals + g) * blocks + j])),
                pl.BlockSpec((1, group_rows, 2 * FF), lambda g, j, at: (at[g * blocks + j], 0, 0)),
                pl.BlockSpec((group_rows, part), lambda g, j, at: (0, at[(goals + g) * blocks + j])),
                pl.BlockSpec((1, group_rows, FF), lambda g, j, at: (at[g * blocks + j], 0, 0)),
            ],
            out_specs=[pl.BlockSpec((part, 3 * FF), block_of(index)) for index in range(goals)],
        ),
        out_shape=[jax.ShapeDtypeStruct((blocks * part, 3 * FF), jnp.bfloat16)] * goals,
        compiler_params=pltpu.CompilerParams(vmem_limit_bytes=VMEM_BYTES),
        cost_estimate=pl.CostEstimate(
            flops=2 * goals * blocks * part * group_rows * 3 * FF,
            bytes_accessed=goals * (group_rows * 6 * FF + blocks * part * (group_rows * 4 + 6 * FF)),
            transcendentals=0,
        ),
    )(where, arrived, inner_grad, cot_group, act)


def in_pieces(n_e, n_r, width):
    return n_e == 2 and n_r == 2 and width // n_r == 2 * min(256, width)


def weight_grads(factors, n_e, n_r):
    width = factors[2].shape[1]
    part = min(256, width)
    if in_pieces(n_e, n_r, width):
        me = lax.axis_index(("exp", "r"))
        own, beside, across, both = (me ^ step for step in range(4))
        goals = [both, across, both, beside, beside, own, across, own]
        later = [0, 0, 1, 1, 0, 0, 1, 1]
        slots = [goal // n_r for goal in goals]
        firsts = [goal % n_r * 2 + half for goal, half in zip(goals, later)]
        return run_weights(*factors, slots, firsts, 2, part)
    grads = []
    blocks = width // part
    for slot in range(n_e):
        firsts = [jnp.int32(first) for first in range(blocks)]
        grads += run_weights(*factors, [jnp.int32(slot)] * blocks, firsts, blocks, part)
    return grads


def send_grads(grads, n_e, n_r, width):
    if not in_pieces(n_e, n_r, width):
        grads = jnp.concatenate(grads, axis=0)
        parts = exchange(grads.reshape((n_e * n_r, -1) + grads.shape[1:]), ("exp", "r"))
        return [list(parts)], []
    results = []
    halfway = []
    for away, kept, ways in ((0, 2, ("exp", "r")), (1, 3, ("r", "exp"))):
        arrived = partner(grads[away], ways[0], 1)
        part = arrived.shape[0] // 2
        onward = grads[kept][:part].astype(jnp.float32) + arrived[:part].astype(jnp.float32)
        halfway.append(onward.astype(jnp.bfloat16))
        onward = partner(halfway[-1], ways[1], 1)
        results.append([grads[kept][part:], arrived[part:], onward])
    return results, halfway


def body(
    tokens,
    cotangent,
    doc_lengths,
    routes,
    qkv_weight,
    qkv_mean,
    qkv_square,
    out_weight,
    out_mean,
    out_square,
    router_weight,
    router_mean,
    router_square,
    norm_gains,
    gains_mean,
    gains_square,
    in_weight,
    in_mean,
    in_square,
    down_weight,
    down_mean,
    down_square,
):
    f32, bf16 = jnp.float32, jnp.bfloat16
    shape = jax.ShapeDtypeStruct
    n_a, n_r, n_c, n_e = (lax.axis_size(name) for name in ("a", "r", "core", "exp"))
    rows, width = tokens.shape
    experts = router_weight.shape[1]
    local_count = in_weight.shape[0]
    sizes = (n_a, n_r, n_c, n_e, width // (n_a * n_r * n_c * n_e))
    home, dense, expert = (order_of(kind, sizes) for kind in ("home", "dense", "expert"))
    query_width = QUERY_HEADS * HEAD_DIMENSION
    qkv_width = query_width + 2 * KEY_VALUE_HEADS * HEAD_DIMENSION

    local_rows = qkv_weight.shape[0]
    extra = jnp.zeros((local_rows, LANES - experts - 2), bf16)
    pack = jnp.concatenate(
        [
            qkv_weight.astype(bf16),
            out_weight.astype(bf16),
            router_weight.astype(bf16),
            norm_gains.astype(bf16),
            extra,
        ],
        axis=1,
    )
    pack = spread(pack, "a")

    to_dense = reorder_matrix(home, dense)
    x_dense = dot_nn(tokens, to_dense).astype(bf16)
    cot_dense = dot_nn(cotangent, to_dense).astype(bf16)
    positions, segment = doc_layout(doc_lengths.reshape(-1), rows)
    cosine, sine = rope_tables(positions, HEAD_DIMENSION)
    repeat = LANES // HEAD_DIMENSION
    cosine = jnp.concatenate([cosine, cosine] * repeat, axis=1)
    sine = jnp.concatenate([-sine, sine] * repeat, axis=1)
    row_index = jnp.arange(rows, dtype=jnp.int32)
    allowed = (segment[:, None] == segment[None, :]) & (row_index[None, :] <= row_index[:, None])
    allowed = allowed.astype(f32)
    used = jnp.any(
        routes[:, :, None] == jnp.arange(LANES, dtype=jnp.int32)[None, None, :], axis=1
    ).astype(f32)

    cot_expert = dot_nn(cotangent, reorder_matrix(home, expert)).astype(bf16)
    expert_pack = jnp.concatenate([in_weight.astype(bf16), down_weight.astype(bf16)], axis=2)
    to_expert = reorder_matrix(dense, expert)
    pieces = pieces_for(expert_pack, ("core", "a"))
    pack, x_dense, cot_dense, cosine, sine, allowed, used, to_expert, *pieces = (
        lax.optimization_barrier(
            (pack, x_dense, cot_dense, cosine, sine, allowed, used, to_expert, *pieces)
        )
    )
    pack = spread(pack, ("r", "exp"))
    expert_pack = exchange_aside(pieces, ("core", "a"))
    pack, expert_pack = lax.optimization_barrier((pack, expert_pack))
    cot_expert, expert_pack = lax.optimization_barrier((cot_expert, expert_pack))
    cot_group = spread_aside(spread_aside(cot_expert, "a"), "core")
    expert_full = lax.all_gather(expert_pack, ("exp", "r"), axis=0, tiled=True).reshape(
        n_e, width, 3 * FF
    )
    dense_full = spread(pack, "core")

    wide, qkv, sent = whole_call(
        functools.partial(attention_forward, experts, n_a),
        [
            shape((rows, width + 2 * LANES), f32),
            shape((rows, qkv_width + query_width), bf16),
            shape((n_a, rows, width + LANES), bf16),
        ],
        [x_dense, dense_full, cosine, sine, allowed, used, to_expert],
        flops=2 * rows * width * (qkv_width + 2 * width + 2 * rows),
    )

    arrived = exchange(sent, "a").reshape(n_a * rows, width + LANES)
    arrived = spread(arrived, "core")
    place = (lax.axis_index("core") * n_a + lax.axis_index("a")).astype(jnp.int32).reshape(1)
    out, inner = run_forward(place, arrived, expert_full, experts, local_count)
    back, inner_grad, activation = run_backward(
        place, arrived, cot_group, expert_full, inner, experts, local_count
    )
    out = collect_aside(out, "core").astype(bf16).reshape(n_a, rows, width)
    back = collect(back, "core").astype(bf16)

    factors = (arrived, inner_grad, cot_group, activation)
    expert_grads = list(weight_grads(factors, n_e, n_r))
    back = exchange(back.reshape(n_a, rows, width + LANES), "a")
    received, halfway = send_grads(expert_grads, n_e, n_r, width)
    back, out, expert_grads[-1] = lax.optimization_barrier((back, out, expert_grads[-1]))
    out = exchange(out, "a")

    from_expert = reorder_matrix(expert, dense)
    dense_grad, input_grad = whole_call(
        functools.partial(home_backward, experts),
        [shape((width, qkv_width + width + LANES), bf16), shape((rows, width), bf16)],
        [
            back,
            from_expert,
            cot_dense,
            wide,
            dense_full,
            qkv,
            x_dense,
            cosine,
            sine,
            allowed,
        ],
        earlier=expert_grads[-1:] + halfway,
        flops=1,
        scratch=[pltpu.VMEM((rows, query_width), bf16), pltpu.VMEM((rows, qkv_width), bf16)],
    )
    dense_grad, out = lax.optimization_barrier((dense_grad, out))
    dense_grad = collect(dense_grad, "core").astype(bf16)
    dense_grad, received = lax.optimization_barrier((dense_grad, received))
    expert_grad = []
    for parts in received:
        total = parts[0].astype(f32)
        for part in parts[1:]:
            total = total + part.astype(f32)
        expert_grad.append(total.astype(bf16))
    expert_grad = jnp.concatenate(expert_grad, axis=0)
    expert_grad = expert_grad.reshape(
        n_c * n_a, width // (n_r * n_c * n_a), 3 * FF
    )
    expert_grad = exchange_aside(
        pieces_for(expert_grad, ("core", "a")), ("core", "a")
    ).astype(f32)
    d_in = expert_grad[:, :, : 2 * FF]
    d_down = expert_grad[:, :, 2 * FF :]
    dense_grad = collect(dense_grad, ("r", "exp")).astype(bf16)
    dense_grad, out, input_grad = lax.optimization_barrier((dense_grad, out, input_grad))
    dense_grad = exchange(dense_grad.reshape((n_a, local_rows) + dense_grad.shape[1:]), "a")

    from_dense = reorder_matrix(dense, home)
    mixed = dot_nn(out[0], from_expert)
    for index in range(1, n_a):
        mixed = mixed + dot_nn(out[index], from_expert)
    block_out = dot_nn((wide[:, :width] + mixed).astype(bf16), from_dense).astype(bf16)
    input_grad = dot_nn(input_grad, from_dense).astype(bf16)
    dense_state = [
        qkv_weight,
        qkv_mean,
        qkv_square,
        out_weight,
        out_mean,
        out_square,
        router_weight.T,
        router_mean.T,
        router_square.T,
        norm_gains.T,
        gains_mean.T,
        gains_square.T,
    ]
    (
        new_qkv,
        new_qkv_mean,
        new_qkv_square,
        new_out,
        new_out_mean,
        new_out_square,
        new_router,
        new_router_mean,
        new_router_square,
        new_gains,
        new_gains_mean,
        new_gains_square,
    ) = whole_call(
        dense_update,
        [shape(item.shape, f32) for item in dense_state],
        [dense_grad] + dense_state,
        flops=20 * local_rows * (qkv_width + width),
    )
    new_router, new_router_mean, new_router_square = (
        item.T for item in (new_router, new_router_mean, new_router_square)
    )
    new_gains, new_gains_mean, new_gains_square = (
        item.T for item in (new_gains, new_gains_mean, new_gains_square)
    )
    new_in, new_in_mean, new_in_square = adamw(in_weight, d_in, in_mean, in_square, 0.1, decay_rate)
    new_down, new_down_mean, new_down_square = adamw(
        down_weight, d_down, down_mean, down_square, 1.0, decay_rate
    )
    return (
        block_out,
        input_grad,
        new_qkv,
        new_qkv_mean,
        new_qkv_square,
        new_out,
        new_out_mean,
        new_out_square,
        new_router,
        new_router_mean,
        new_router_square,
        new_gains,
        new_gains_mean,
        new_gains_square,
        new_in,
        new_in_mean,
        new_in_square,
        new_down,
        new_down_mean,
        new_down_square,
    )


def solution(mesh):
    n_dp, n_exp = mesh.shape["dp"], mesh.shape["exp"]
    n_a = EXPERTS // n_exp // 2
    mesh = Mesh(
        mesh.devices.reshape(n_a, n_dp // (2 * n_a), 2, n_exp), MESH_AXES
    )
    placed = (
        P(("a", "r", "core", "exp"), None),
        P(("a", "r", "core", "exp"), None),
        P(("a", "r", "core", "exp"), None),
        P(("a", "r", "core", "exp"), None),
        P(("a", "r", "core", "exp"), None),
        P(("a", "r", "core", "exp"), None),
        P(("a", "r", "core", "exp"), None),
        P(("a", "r", "core", "exp"), None),
        P(("a", "r", "core", "exp"), None),
        P(("a", "r", "core", "exp"), None),
        P(("a", "r", "core", "exp"), None),
        P(("a", "r", "core", "exp"), None),
        P(("a", "r", "core", "exp"), None),
        P(("a", "r", "core", "exp"), None),
        P(("a", "r", "core", "exp"), None),
        P(("a", "r", "core", "exp"), None),
        P("exp", ("a", "r", "core"), None),
        P("exp", ("a", "r", "core"), None),
        P("exp", ("a", "r", "core"), None),
        P("exp", ("a", "r", "core"), None),
        P("exp", ("a", "r", "core"), None),
        P("exp", ("a", "r", "core"), None),
    )
    return jax.shard_map(
        body,
        mesh=mesh,
        in_specs=placed,
        out_specs=(
            P(("a", "r", "core", "exp"), None),
            P(("a", "r", "core", "exp"), None),
            P(("a", "r", "core", "exp"), None),
            P(("a", "r", "core", "exp"), None),
            P(("a", "r", "core", "exp"), None),
            P(("a", "r", "core", "exp"), None),
            P(("a", "r", "core", "exp"), None),
            P(("a", "r", "core", "exp"), None),
            P(("a", "r", "core", "exp"), None),
            P(("a", "r", "core", "exp"), None),
            P(("a", "r", "core", "exp"), None),
            P(("a", "r", "core", "exp"), None),
            P(("a", "r", "core", "exp"), None),
            P(("a", "r", "core", "exp"), None),
            P("exp", ("a", "r", "core"), None),
            P("exp", ("a", "r", "core"), None),
            P("exp", ("a", "r", "core"), None),
            P("exp", ("a", "r", "core"), None),
            P("exp", ("a", "r", "core"), None),
            P("exp", ("a", "r", "core"), None),
        ),
        check_vma=False,
    )
```

```python
import functools
import math

import jax
import jax.numpy as jnp
import numpy as np
from jax import lax
from jax.experimental import pallas as pl
from jax.experimental.pallas import tpu as pltpu
from jax.sharding import Mesh
from jax.sharding import PartitionSpec as P

QUERY_HEADS = 16
KEY_VALUE_HEADS = 8
HEAD_DIMENSION = 64
FF = 512
STEP = 10
EXPERTS = 16
LANES = 128
MESH_AXES = ("a", "r", "core", "exp")
VMEM_BYTES = 26 * 1024 * 1024


norm_eps = 1e-06
rope_base = 10000.0
mask_fill = -1e30
beta_one = 0.9
beta_two = 0.95
adam_eps = 1e-08
decay_rate = 0.1


def rms_scale(values):
    return lax.rsqrt(jnp.mean(values * values, axis=-1, keepdims=True) + norm_eps)


def doc_layout(doc_lens, sequence_length):
    row_index = jnp.arange(sequence_length, dtype=jnp.int32)
    doc_ends = jnp.cumsum(doc_lens, dtype=jnp.int32)
    passed = (row_index[:, None] >= doc_ends[None, :]).astype(jnp.int32)
    segment = jnp.sum(passed, axis=1, dtype=jnp.int32)
    starts = jnp.sum(passed * doc_lens[None, :], axis=1, dtype=jnp.int32)
    return ((row_index - starts).astype(jnp.float32), segment)


def rope_tables(positions, head_size):
    half_size = head_size // 2
    freq_index = jnp.arange(half_size, dtype=jnp.float32)
    inverse = jnp.exp(freq_index * (-2.0 * math.log(rope_base) / head_size))
    angles = positions[:, None] * inverse[None, :]
    return (jnp.cos(angles), jnp.sin(angles))


def adamw(weight, gradient, mean_old, square_old, step_rate, weight_decay):
    mean_new = beta_one * mean_old + (1.0 - beta_one) * gradient
    square_new = beta_two * square_old + (1.0 - beta_two) * gradient * gradient
    corrected = (
        mean_new
        / (1.0 - beta_one**STEP)
        / (jnp.sqrt(square_new / (1.0 - beta_two**STEP)) + adam_eps)
    )
    return (weight - step_rate * (corrected + weight_decay * weight), mean_new, square_new)

def dot_nn(left, right):
    return jnp.dot(left, right, preferred_element_type=jnp.float32)


def dot_nt(left, right):
    return lax.dot_general(left, right, (((1,), (1,)), ((), ())), preferred_element_type=jnp.float32)


def dot_tn(left, right):
    return lax.dot_general(left, right, (((0,), (0,)), ((), ())), preferred_element_type=jnp.float32)


def lane_iota(rows):
    return lax.broadcasted_iota(jnp.int32, (rows, LANES), 1)


def gain_rows(extra, experts):
    row = lax.broadcasted_iota(jnp.int32, (8, LANES), 0)
    pick = (lane_iota(8) == row + experts).astype(jnp.bfloat16)
    return dot_nt(jnp.where(row < 2, pick, jnp.zeros_like(pick)), extra)


def swap_halves(values):
    half = HEAD_DIMENSION // 2
    lower = lane_iota(values.shape[0]) % HEAD_DIMENSION < half
    return jnp.where(lower, pltpu.roll(values, LANES - half, 1), pltpu.roll(values, half, 1))


def column_sums(values, lane):
    high = values.astype(jnp.bfloat16)
    low = (values - high.astype(jnp.float32)).astype(jnp.bfloat16)
    place = (lane_iota(values.shape[0]) == lane).astype(jnp.bfloat16)
    return dot_tn(high, place) + dot_tn(low, place)


def head_block(index):
    return slice(index * HEAD_DIMENSION, (index + 1) * HEAD_DIMENSION)


def attention_forward(
    experts,
    copies,
    x_ref,
    w_ref,
    cos_ref,
    sin_ref,
    allow_ref,
    used_ref,
    order_ref,
    wide_ref,
    qkv_ref,
    sent_ref,
):
    f32, bf16 = jnp.float32, jnp.bfloat16
    rows, width = x_ref.shape
    query_width = QUERY_HEADS * HEAD_DIMENSION
    key_width = KEY_VALUE_HEADS * HEAD_DIMENSION
    qkv_width = query_width + 2 * key_width
    extra = w_ref[:, qkv_width + width :]
    gains = gain_rows(extra, experts)
    x = x_ref[...].astype(f32)
    normed = (x * rms_scale(x) * gains[0:1]).astype(bf16)
    cosine, sine = cos_ref[...], sin_ref[...]
    for start in range(0, qkv_width, 512):
        part = dot_nn(normed, w_ref[:, start : start + 512])
        for inner in range(0, 512, LANES):
            piece = part[:, inner : inner + LANES]
            if start + inner < query_width + key_width:
                piece = piece * cosine + swap_halves(piece) * sine
            qkv_ref[:, start + inner : start + inner + LANES] = piece.astype(bf16)
    allowed = allow_ref[...] > 0.0
    lane = lane_iota(rows)
    logs = jnp.zeros((rows, LANES), f32)
    fold = QUERY_HEADS // KEY_VALUE_HEADS
    for group in range(KEY_VALUE_HEADS):
        keys = qkv_ref[:, query_width + group * HEAD_DIMENSION : query_width + (group + 1) * HEAD_DIMENSION]
        values = qkv_ref[
            :,
            query_width + key_width + group * HEAD_DIMENSION : query_width
            + key_width
            + (group + 1) * HEAD_DIMENSION,
        ]
        outs = []
        for head in range(group * fold, (group + 1) * fold):
            scores = dot_nt(qkv_ref[:, head_block(head)], keys) * HEAD_DIMENSION ** (-0.5)
            scores = jnp.where(allowed, scores, mask_fill)
            peak = jnp.max(scores, axis=1, keepdims=True)
            log_total = peak + jnp.log(jnp.sum(jnp.exp(scores - peak), axis=1, keepdims=True))
            logs = jnp.where(lane == head, log_total, logs)
            outs.append(dot_nn(jnp.exp(scores - log_total).astype(bf16), values))
        start = qkv_width + group * LANES
        qkv_ref[:, start : start + LANES] = jnp.concatenate(outs, axis=1).astype(bf16)
    wide_ref[:, width : width + LANES] = logs
    hidden = x + dot_nt(qkv_ref[:, qkv_width:], w_ref[:, qkv_width : qkv_width + width])
    wide_ref[:, :width] = hidden
    second = (hidden * rms_scale(hidden) * gains[1:2]).astype(bf16)
    used = used_ref[...] > 0.0
    logits = jnp.where(used, dot_nn(second, extra), mask_fill)
    powers = jnp.where(used, jnp.exp(logits - jnp.max(logits, axis=1, keepdims=True)), 0.0)
    gates = powers / jnp.sum(powers, axis=1, keepdims=True)
    wide_ref[:, width + LANES :] = gates
    high = gates.astype(bf16).astype(f32)
    lanes = (high + pltpu.roll(gates - high, experts, 1)).astype(bf16)
    moved = dot_nn(second, order_ref[...]).astype(bf16)
    for copy in range(copies):
        sent_ref[copy, :, :width] = moved
        sent_ref[copy, :, width:] = lanes


def own_gate(lanes, number, experts):
    lane = lane_iota(lanes.shape[0])
    chosen = (lane == number) | (lane == number + experts)
    return jnp.sum(jnp.where(chosen, lanes.astype(jnp.float32), 0.0), axis=1, keepdims=True)


def experts_forward(
    experts, local_count, place_ref, rows_ref, w_ref, out_ref, inner_ref, sum_ref
):
    f32, bf16 = jnp.float32, jnp.bfloat16
    index, chunk = pl.program_id(0), pl.program_id(1)
    count, width = out_ref.shape
    gate = own_gate(rows_ref[:, width:], index * local_count + place_ref[0], experts)
    inner = dot_nn(rows_ref[:, :width], w_ref[0, :, : 2 * FF])
    inner_ref[0] = inner
    gate_part = inner[:, :FF]
    activation = (gate_part * jax.nn.sigmoid(gate_part) * inner[:, FF:]).astype(bf16)
    result = dot_nt(activation, w_ref[0, :, 2 * FF :]).astype(bf16).astype(f32)
    here = pl.ds(pl.multiple_of(chunk * count, count), count)

    @pl.when(index == 0)
    def _():
        sum_ref[here, :] = gate * result

    @pl.when(index > 0)
    def _():
        sum_ref[here, :] += gate * result

    out_ref[...] = sum_ref[here, :].astype(bf16)


def experts_backward(
    experts,
    local_count,
    place_ref,
    gates_ref,
    cot_ref,
    w_ref,
    inner_ref,
    back_ref,
    inner_grad_ref,
    act_ref,
    sum_ref,
    dots_sum_ref,
):
    f32, bf16 = jnp.float32, jnp.bfloat16
    index, chunk = pl.program_id(0), pl.program_id(1)
    count, width = cot_ref.shape
    number = index * local_count + place_ref[0]
    gate = own_gate(gates_ref[...], number, experts)
    gate_part = inner_ref[0, :, :FF]
    up_part = inner_ref[0, :, FF:]
    gate_sigmoid = jax.nn.sigmoid(gate_part)
    gate_silu = gate_part * gate_sigmoid
    activation = (gate_silu * up_part).astype(bf16).astype(f32)
    act_ref[0] = (gate * activation).astype(bf16)
    act_grad = dot_nn(cot_ref[...], w_ref[0, :, 2 * FF :])
    dots = jnp.sum(activation * act_grad, axis=1, keepdims=True)
    dots_high = dots.astype(bf16).astype(f32)
    lane = lane_iota(count)
    lanes = jnp.where(lane == number, dots_high, 0.0) + jnp.where(
        lane == number + experts, dots - dots_high, 0.0
    )
    act_grad = gate * act_grad
    inner_grad_ref[0, :, :FF] = (
        act_grad * up_part * gate_sigmoid * (1.0 + gate_part * (1.0 - gate_sigmoid))
    ).astype(bf16)
    inner_grad_ref[0, :, FF:] = (act_grad * gate_silu).astype(bf16)
    copy_grad = dot_nt(inner_grad_ref[0], w_ref[0, :, : 2 * FF])
    here = pl.ds(pl.multiple_of(chunk * count, count), count)

    @pl.when(index == 0)
    def _():
        sum_ref[here, :] = copy_grad
        dots_sum_ref[here, :] = lanes

    @pl.when(index > 0)
    def _():
        sum_ref[here, :] += copy_grad
        dots_sum_ref[here, :] += lanes

    back_ref[:, :width] = sum_ref[here, :].astype(bf16)
    back_ref[:, width:] = dots_sum_ref[here, :].astype(bf16)


def experts_weights(where_ref, rows_ref, inner_grad_ref, cot_ref, act_ref, *grad_refs):
    goal = pl.program_id(0)
    inner = dot_tn(rows_ref[...], inner_grad_ref[0]).astype(jnp.bfloat16)
    down = dot_tn(cot_ref[...], act_ref[0]).astype(jnp.bfloat16)
    for index, grad_ref in enumerate(grad_refs):

        @pl.when(goal == index)
        def _(grad_ref=grad_ref):
            grad_ref[:, : 2 * FF] = inner
            grad_ref[:, 2 * FF :] = down


def home_backward(
    experts,
    parts_ref,
    order_ref,
    cot_ref,
    wide_ref,
    w_ref,
    qkv_ref,
    x_ref,
    cos_ref,
    sin_ref,
    allow_ref,
    grad_ref,
    input_grad_ref,
    mid_ref,
    proj_ref,
):
    f32, bf16 = jnp.float32, jnp.bfloat16
    rows, width = x_ref.shape
    sources = parts_ref.shape[0]
    query_width = QUERY_HEADS * HEAD_DIMENSION
    key_width = KEY_VALUE_HEADS * HEAD_DIMENSION
    qkv_width = query_width + 2 * key_width
    fold = QUERY_HEADS // KEY_VALUE_HEADS
    score_scale = HEAD_DIMENSION ** (-0.5)
    extra = w_ref[:, qkv_width + width :]
    gains = gain_rows(extra, experts)
    dots = jnp.zeros((rows, LANES), f32)
    second_grad = jnp.zeros((rows, width), f32)
    for source in range(sources):
        dots = dots + parts_ref[source, :, width:].astype(f32)
        second_grad = second_grad + dot_nn(parts_ref[source, :, :width], order_ref[...])
    dots = dots + pltpu.roll(dots, LANES - experts, 1)
    gates = wide_ref[:, width + LANES :]
    logit_grad = (gates * (dots - jnp.sum(gates * dots, axis=1, keepdims=True))).astype(bf16)
    second_grad = second_grad + dot_nt(logit_grad, extra)
    hidden = wide_ref[:, :width]
    scale = rms_scale(hidden)
    second = (hidden * scale * gains[1:2]).astype(bf16)
    scaled = second_grad * gains[1:2]
    hidden_grad = (
        cot_ref[...].astype(f32)
        + scale * scaled
        - hidden * (scale * scale * scale) * jnp.mean(scaled * hidden, axis=1, keepdims=True)
    )
    branch_grad = hidden_grad.astype(bf16)
    for start in range(0, width, 512):
        grad_ref[:, qkv_width + start : qkv_width + start + 512] = dot_tn(
            branch_grad, qkv_ref[:, qkv_width + start : qkv_width + start + 512]
        ).astype(bf16)
    small_grad = dot_tn(second, logit_grad) + column_sums(
        second_grad * hidden * scale, experts + 1
    )
    mid_ref[...] = dot_nn(branch_grad, w_ref[:, qkv_width : qkv_width + width]).astype(bf16)
    cosine, sine = cos_ref[...], sin_ref[...]
    allowed = allow_ref[...] > 0.0
    lane = lane_iota(rows)
    logs = wide_ref[:, width : width + LANES]

    def turned_back(values):
        return (values * cosine - swap_halves(values) * sine).astype(bf16)

    key_grads, value_grads = [], []
    for group in range(KEY_VALUE_HEADS):
        keys = qkv_ref[:, query_width + group * HEAD_DIMENSION : query_width + (group + 1) * HEAD_DIMENSION]
        values = qkv_ref[
            :,
            query_width + key_width + group * HEAD_DIMENSION : query_width
            + key_width
            + (group + 1) * HEAD_DIMENSION,
        ]
        query_grads = []
        key_grad = jnp.zeros((rows, HEAD_DIMENSION), f32)
        value_grad = jnp.zeros((rows, HEAD_DIMENSION), f32)
        for head in range(group * fold, (group + 1) * fold):
            queries = qkv_ref[:, head_block(head)]
            mid = mid_ref[:, head_block(head)]
            log_total = jnp.sum(jnp.where(lane == head, logs, 0.0), axis=1, keepdims=True)
            scores = jnp.where(allowed, dot_nt(queries, keys) * score_scale, mask_fill)
            weights = jnp.exp(scores - log_total)
            weight_grad = dot_nt(mid, values)
            delta = jnp.sum(weights * weight_grad, axis=1, keepdims=True)
            score_grad = (weights * (weight_grad - delta)).astype(bf16)
            query_grads.append(dot_nn(score_grad, keys) * score_scale)
            key_grad = key_grad + dot_tn(score_grad, queries)
            value_grad = value_grad + dot_tn(weights.astype(bf16), mid)
        proj_ref[:, group * LANES : (group + 1) * LANES] = turned_back(
            jnp.concatenate(query_grads, axis=1)
        )
        key_grads.append(key_grad * score_scale)
        value_grads.append(value_grad)
        if group % 2 == 1:
            start = query_width + (group // 2) * LANES
            proj_ref[:, start : start + LANES] = turned_back(
                jnp.concatenate(key_grads[-2:], axis=1)
            )
            start = start + key_width
            proj_ref[:, start : start + LANES] = jnp.concatenate(value_grads[-2:], axis=1).astype(
                bf16
            )
    x = x_ref[...].astype(f32)
    scale = rms_scale(x)
    normed = (x * scale * gains[0:1]).astype(bf16)
    for start in range(0, qkv_width, 512):
        grad_ref[:, start : start + 512] = dot_tn(normed, proj_ref[:, start : start + 512]).astype(
            bf16
        )
    normed_grad = dot_nt(proj_ref[...], w_ref[:, :qkv_width])
    scaled = normed_grad * gains[0:1]
    small_grad = small_grad + column_sums(normed_grad * x * scale, experts)
    grad_ref[:, qkv_width + width :] = small_grad.astype(bf16)
    input_grad_ref[...] = (
        hidden_grad
        + scale * scaled
        - x * (scale * scale * scale) * jnp.mean(scaled * x, axis=1, keepdims=True)
    ).astype(bf16)


def dense_update(parts_ref, *refs):
    total = parts_ref[0].astype(jnp.float32)
    for source in range(1, parts_ref.shape[0]):
        total = total + parts_ref[source].astype(jnp.float32)
    start = total.shape[1] - LANES
    small = jnp.transpose(total[:, start:])
    experts = refs[6].shape[0]
    qkv_width = refs[0].shape[1]
    grads = (
        total[:, :qkv_width],
        total[:, qkv_width:start],
        small[:experts],
        small[experts : experts + 2],
    )
    rates = ((0.15, decay_rate), (0.3, decay_rate), (0.05, decay_rate), (0.8, 0.0))
    for index, (rate, decay) in enumerate(rates):
        weight_ref, mean_ref, square_ref = refs[3 * index : 3 * index + 3]
        values = adamw(weight_ref[...], grads[index], mean_ref[...], square_ref[...], rate, decay)
        for out_ref, value in zip(refs[3 * index + 12 : 3 * index + 15], values):
            out_ref[...] = value


def whole_call(kernel, outputs, operands, flops, scratch=(), earlier=()):
    operands_read = len(operands)

    def run(*refs):
        kernel(*refs[:operands_read], *refs[operands_read + len(earlier) :])

    moved = sum(math.prod(item.shape) * item.dtype.itemsize for item in list(outputs) + list(operands))
    moved = moved if flops > 1 else 1
    return pl.pallas_call(
        run,
        out_shape=outputs,
        in_specs=[pl.BlockSpec(memory_space=pltpu.VMEM)] * len(operands)
        + [pl.BlockSpec(memory_space=pl.ANY)] * len(earlier),
        out_specs=[pl.BlockSpec(memory_space=pltpu.VMEM)] * len(outputs),
        scratch_shapes=list(scratch),
        compiler_params=pltpu.CompilerParams(vmem_limit_bytes=VMEM_BYTES),
        cost_estimate=pl.CostEstimate(flops=flops, bytes_accessed=moved, transcendentals=0),
    )(*operands, *earlier)


def order_of(kind, sizes):
    axes = {"home": (0, 1, 2, 3, 4), "dense": (2, 1, 3, 0, 4), "expert": (1, 2, 0, 3, 4)}[kind]
    return np.arange(math.prod(sizes), dtype=np.int32).reshape(sizes).transpose(axes).reshape(-1)


def reorder_matrix(before, after):
    return (jnp.asarray(before)[:, None] == jnp.asarray(after)[None, :]).astype(jnp.bfloat16)


def exchange(values, axes):
    return lax.all_to_all(values, axes, split_axis=0, concat_axis=0, tiled=True)


def spread(values, axes):
    count = lax.axis_size(axes)
    copies = exchange(jnp.broadcast_to(values[None], (count,) + values.shape), axes)
    return copies.reshape((count * values.shape[0],) + values.shape[1:])


def collect(values, axes):
    count = lax.axis_size(axes)
    parts = exchange(values.reshape((count, values.shape[0] // count) + values.shape[1:]), axes)
    total = parts[0].astype(jnp.float32)
    for index in range(1, count):
        total = total + parts[index].astype(jnp.float32)
    return total


def partner(values, axes, step):
    names = (axes,) if isinstance(axes, str) else axes
    steps = {}
    for name in reversed(names):
        step, steps[name] = divmod(step, lax.axis_size(name))
    names = tuple(name for name in MESH_AXES if name in names)
    flat = 0
    for name in names:
        flat = flat * lax.axis_size(name) + steps[name]
    pairs = [(index, index ^ flat) for index in range(lax.axis_size(names))]
    return lax.ppermute(values, names, pairs)


def piece_of(values, index):
    return lax.dynamic_index_in_dim(values, index, 0, keepdims=False)


def in_order(own, received, me):
    result = jnp.zeros((len(received) + 1,) + own.shape, own.dtype)
    for step, part in enumerate([own] + received):
        result = lax.dynamic_update_index_in_dim(result, part, me ^ step, 0)
    return result


def spread_aside(values, axes):
    count = lax.axis_size(axes)
    received = [partner(values, axes, step) for step in range(1, count)]
    result = in_order(values, received, lax.axis_index(axes))
    return result.reshape((count * values.shape[0],) + values.shape[1:])


def pieces_for(values, axes):
    me = lax.axis_index(axes)
    return [piece_of(values, me ^ step) for step in range(values.shape[0])]


def exchange_aside(pieces, axes):
    received = [partner(piece, axes, step) for step, piece in enumerate(pieces) if step > 0]
    return in_order(pieces[0], received, lax.axis_index(axes))


def collect_aside(values, axes):
    count = lax.axis_size(axes)
    pieces = pieces_for(values.reshape((count, values.shape[0] // count) + values.shape[1:]), axes)
    total = pieces[0].astype(jnp.float32)
    for step in range(1, count):
        total = total + partner(pieces[step], axes, step).astype(jnp.float32)
    return total


def expert_specs(n_e, group_rows, width):
    count = min(256, group_rows)
    return dict(
        grid=(n_e, group_rows // count),
        scalar=pl.BlockSpec(memory_space=pltpu.SMEM),
        wide=pl.BlockSpec((count, width), lambda k, i: (i, 0)),
        wider=pl.BlockSpec((count, width + LANES), lambda k, i: (i, 0)),
        lanes=pl.BlockSpec((count, LANES), lambda k, i: (i, width // LANES)),
        weight=pl.BlockSpec((1, width, 3 * FF), lambda k, i: (k, 0, 0)),
        inner=pl.BlockSpec((1, count, 2 * FF), lambda k, i: (k, i, 0)),
        act=pl.BlockSpec((1, count, FF), lambda k, i: (k, i, 0)),
    )


def run_forward(place, arrived, expert_full, experts, local_count):
    n_e, width, _ = expert_full.shape
    group_rows = arrived.shape[0]
    specs = expert_specs(n_e, group_rows, width)
    return pl.pallas_call(
        functools.partial(experts_forward, experts, local_count),
        grid=specs["grid"],
        out_shape=[
            jax.ShapeDtypeStruct((group_rows, width), jnp.bfloat16),
            jax.ShapeDtypeStruct((n_e, group_rows, 2 * FF), jnp.float32),
        ],
        in_specs=[specs["scalar"], specs["wider"], specs["weight"]],
        out_specs=[specs["wide"], specs["inner"]],
        scratch_shapes=[pltpu.VMEM((group_rows, width), jnp.float32)],
        compiler_params=pltpu.CompilerParams(vmem_limit_bytes=VMEM_BYTES),
        cost_estimate=pl.CostEstimate(
            flops=2 * n_e * group_rows * width * 3 * FF,
            bytes_accessed=n_e * width * (3 * FF * 2 + group_rows * 8),
            transcendentals=n_e * group_rows * FF,
        ),
    )(place, arrived, expert_full)


def run_backward(place, arrived, cot_group, expert_full, inner, experts, local_count):
    bf16 = jnp.bfloat16
    n_e, width, _ = expert_full.shape
    group_rows = arrived.shape[0]
    specs = expert_specs(n_e, group_rows, width)
    return pl.pallas_call(
        functools.partial(experts_backward, experts, local_count),
        grid=specs["grid"],
        out_shape=[
            jax.ShapeDtypeStruct((group_rows, width + LANES), bf16),
            jax.ShapeDtypeStruct((n_e, group_rows, 2 * FF), bf16),
            jax.ShapeDtypeStruct((n_e, group_rows, FF), bf16),
        ],
        in_specs=[
            specs["scalar"],
            specs["lanes"],
            specs["wide"],
            specs["weight"],
            specs["inner"],
        ],
        out_specs=[specs["wider"], specs["inner"], specs["act"]],
        scratch_shapes=[
            pltpu.VMEM((group_rows, width), jnp.float32),
            pltpu.VMEM((group_rows, LANES), jnp.float32),
        ],
        compiler_params=pltpu.CompilerParams(vmem_limit_bytes=VMEM_BYTES),
        cost_estimate=pl.CostEstimate(
            flops=2 * n_e * group_rows * width * 3 * FF,
            bytes_accessed=n_e * width * (3 * FF * 2 + group_rows * 10),
            transcendentals=n_e * group_rows * FF,
        ),
    )(place, arrived, cot_group, expert_full, inner)


def run_weights(arrived, inner_grad, cot_group, act, slots, firsts, blocks, part):
    group_rows = arrived.shape[0]
    goals = len(slots) // blocks
    where = jnp.stack(slots + firsts).astype(jnp.int32)

    def block_of(index):
        return lambda g, j, at: (jnp.where(g == index, j, jnp.where(g < index, 0, blocks - 1)), 0)

    return pl.pallas_call(
        experts_weights,
        grid_spec=pltpu.PrefetchScalarGridSpec(
            num_scalar_prefetch=1,
            grid=(goals, blocks),
            in_specs=[
                pl.BlockSpec((group_rows, part), lambda g, j, at: (0, at[(goals + g) * blocks + j])),
                pl.BlockSpec((1, group_rows, 2 * FF), lambda g, j, at: (at[g * blocks + j], 0, 0)),
                pl.BlockSpec((group_rows, part), lambda g, j, at: (0, at[(goals + g) * blocks + j])),
                pl.BlockSpec((1, group_rows, FF), lambda g, j, at: (at[g * blocks + j], 0, 0)),
            ],
            out_specs=[pl.BlockSpec((part, 3 * FF), block_of(index)) for index in range(goals)],
        ),
        out_shape=[jax.ShapeDtypeStruct((blocks * part, 3 * FF), jnp.bfloat16)] * goals,
        compiler_params=pltpu.CompilerParams(vmem_limit_bytes=VMEM_BYTES),
        cost_estimate=pl.CostEstimate(
            flops=2 * goals * blocks * part * group_rows * 3 * FF,
            bytes_accessed=goals * (group_rows * 6 * FF + blocks * part * (group_rows * 4 + 6 * FF)),
            transcendentals=0,
        ),
    )(where, arrived, inner_grad, cot_group, act)


def in_pieces(n_e, n_r, width):
    return n_e == 2 and n_r == 2 and width // n_r == 2 * min(256, width)


def weight_grads(factors, n_e, n_r):
    width = factors[2].shape[1]
    part = min(256, width)
    if in_pieces(n_e, n_r, width):
        me = lax.axis_index(("exp", "r"))
        own, beside, across, both = (me ^ step for step in range(4))
        goals = [both, across, both, beside, beside, own, across, own]
        later = [0, 0, 1, 1, 0, 0, 1, 1]
        slots = [goal // n_r for goal in goals]
        firsts = [goal % n_r * 2 + half for goal, half in zip(goals, later)]
        return run_weights(*factors, slots, firsts, 2, part)
    grads = []
    blocks = width // part
    for slot in range(n_e):
        firsts = [jnp.int32(first) for first in range(blocks)]
        grads += run_weights(*factors, [jnp.int32(slot)] * blocks, firsts, blocks, part)
    return grads


def send_grads(grads, n_e, n_r, width):
    if not in_pieces(n_e, n_r, width):
        grads = jnp.concatenate(grads, axis=0)
        return [list(exchange(grads.reshape((n_e * n_r, -1) + grads.shape[1:]), ("exp", "r")))]
    return [[grads[2], partner(grads[0], "exp", 1)], [grads[3], partner(grads[1], "r", 1)]]


def send_onward(parts, ways):
    if len(parts) != 2:
        return parts
    count = parts[0].shape[0] // 2
    onward = parts[0][:count].astype(jnp.float32) + parts[1][:count].astype(jnp.float32)
    return parts + [partner(onward.astype(jnp.bfloat16), ways, 1)]


def add_parts(parts):
    count = parts[-1].shape[0]
    total = parts[-1].astype(jnp.float32)
    for part in parts[:-1]:
        total = total + part[part.shape[0] - count :].astype(jnp.float32)
    return total.astype(jnp.bfloat16)


def body(
    tokens,
    cotangent,
    doc_lengths,
    routes,
    qkv_weight,
    qkv_mean,
    qkv_square,
    out_weight,
    out_mean,
    out_square,
    router_weight,
    router_mean,
    router_square,
    norm_gains,
    gains_mean,
    gains_square,
    in_weight,
    in_mean,
    in_square,
    down_weight,
    down_mean,
    down_square,
):
    f32, bf16 = jnp.float32, jnp.bfloat16
    shape = jax.ShapeDtypeStruct
    n_a, n_r, n_c, n_e = (lax.axis_size(name) for name in ("a", "r", "core", "exp"))
    rows, width = tokens.shape
    experts = router_weight.shape[1]
    local_count = in_weight.shape[0]
    sizes = (n_a, n_r, n_c, n_e, width // (n_a * n_r * n_c * n_e))
    home, dense, expert = (order_of(kind, sizes) for kind in ("home", "dense", "expert"))
    query_width = QUERY_HEADS * HEAD_DIMENSION
    qkv_width = query_width + 2 * KEY_VALUE_HEADS * HEAD_DIMENSION

    local_rows = qkv_weight.shape[0]
    extra = jnp.zeros((local_rows, LANES - experts - 2), bf16)
    pack = jnp.concatenate(
        [
            qkv_weight.astype(bf16),
            out_weight.astype(bf16),
            router_weight.astype(bf16),
            norm_gains.astype(bf16),
            extra,
        ],
        axis=1,
    )
    pack = spread(pack, "a")

    to_dense = reorder_matrix(home, dense)
    x_dense = dot_nn(tokens, to_dense).astype(bf16)
    cot_dense = dot_nn(cotangent, to_dense).astype(bf16)
    positions, segment = doc_layout(doc_lengths.reshape(-1), rows)
    cosine, sine = rope_tables(positions, HEAD_DIMENSION)
    repeat = LANES // HEAD_DIMENSION
    cosine = jnp.concatenate([cosine, cosine] * repeat, axis=1)
    sine = jnp.concatenate([-sine, sine] * repeat, axis=1)
    row_index = jnp.arange(rows, dtype=jnp.int32)
    allowed = (segment[:, None] == segment[None, :]) & (row_index[None, :] <= row_index[:, None])
    allowed = allowed.astype(f32)
    used = jnp.any(
        routes[:, :, None] == jnp.arange(LANES, dtype=jnp.int32)[None, None, :], axis=1
    ).astype(f32)

    cot_expert = dot_nn(cotangent, reorder_matrix(home, expert)).astype(bf16)
    expert_pack = jnp.concatenate([in_weight.astype(bf16), down_weight.astype(bf16)], axis=2)
    to_expert = reorder_matrix(dense, expert)
    pieces = pieces_for(expert_pack, ("core", "a"))
    pack, x_dense, cot_dense, cosine, sine, allowed, used, to_expert, *pieces = (
        lax.optimization_barrier(
            (pack, x_dense, cot_dense, cosine, sine, allowed, used, to_expert, *pieces)
        )
    )
    pack = spread(pack, ("r", "exp"))
    expert_pack = exchange_aside(pieces, ("core", "a"))
    pack, expert_pack = lax.optimization_barrier((pack, expert_pack))
    cot_expert, expert_pack = lax.optimization_barrier((cot_expert, expert_pack))
    cot_group = spread_aside(spread_aside(cot_expert, "a"), "core")
    expert_full = lax.all_gather(expert_pack, ("exp", "r"), axis=0, tiled=True).reshape(
        n_e, width, 3 * FF
    )
    dense_full = spread(pack, "core")

    wide, qkv, sent = whole_call(
        functools.partial(attention_forward, experts, n_a),
        [
            shape((rows, width + 2 * LANES), f32),
            shape((rows, qkv_width + query_width), bf16),
            shape((n_a, rows, width + LANES), bf16),
        ],
        [x_dense, dense_full, cosine, sine, allowed, used, to_expert],
        flops=2 * rows * width * (qkv_width + 2 * width + 2 * rows),
    )

    arrived = exchange(sent, "a").reshape(n_a * rows, width + LANES)
    arrived = spread(arrived, "core")
    place = (lax.axis_index("core") * n_a + lax.axis_index("a")).astype(jnp.int32).reshape(1)
    out, inner = run_forward(place, arrived, expert_full, experts, local_count)
    back, inner_grad, activation = run_backward(
        place, arrived, cot_group, expert_full, inner, experts, local_count
    )
    out = collect_aside(out, "core").astype(bf16).reshape(n_a, rows, width)
    back = collect(back, "core").astype(bf16)

    factors = (arrived, inner_grad, cot_group, activation)
    expert_grads = list(weight_grads(factors, n_e, n_r))
    back = exchange(back.reshape(n_a, rows, width + LANES), "a")
    received = send_grads(expert_grads, n_e, n_r, width)
    back, out, expert_grads[-1] = lax.optimization_barrier((back, out, expert_grads[-1]))
    out = exchange(out, "a")

    from_expert = reorder_matrix(expert, dense)
    dense_grad, input_grad = whole_call(
        functools.partial(home_backward, experts),
        [shape((width, qkv_width + width + LANES), bf16), shape((rows, width), bf16)],
        [
            back,
            from_expert,
            cot_dense,
            wide,
            dense_full,
            qkv,
            x_dense,
            cosine,
            sine,
            allowed,
        ],
        earlier=expert_grads[-1:],
        flops=1,
        scratch=[pltpu.VMEM((rows, query_width), bf16), pltpu.VMEM((rows, qkv_width), bf16)],
    )
    dense_grad, out, received = lax.optimization_barrier((dense_grad, out, received))
    received = [send_onward(parts, way) for parts, way in zip(received, ("r", "exp"))]
    dense_grad = collect(dense_grad, "core").astype(bf16)
    dense_grad, received = lax.optimization_barrier((dense_grad, received))
    expert_grad = jnp.concatenate([add_parts(parts) for parts in received], axis=0)
    expert_grad = expert_grad.reshape(
        n_c * n_a, width // (n_r * n_c * n_a), 3 * FF
    )
    expert_grad = exchange_aside(
        pieces_for(expert_grad, ("core", "a")), ("core", "a")
    ).astype(f32)
    d_in = expert_grad[:, :, : 2 * FF]
    d_down = expert_grad[:, :, 2 * FF :]
    dense_grad = collect(dense_grad, ("r", "exp")).astype(bf16)
    dense_grad, out, input_grad = lax.optimization_barrier((dense_grad, out, input_grad))
    dense_grad = exchange(dense_grad.reshape((n_a, local_rows) + dense_grad.shape[1:]), "a")

    from_dense = reorder_matrix(dense, home)
    mixed = dot_nn(out[0], from_expert)
    for index in range(1, n_a):
        mixed = mixed + dot_nn(out[index], from_expert)
    block_out = dot_nn((wide[:, :width] + mixed).astype(bf16), from_dense).astype(bf16)
    input_grad = dot_nn(input_grad, from_dense).astype(bf16)
    dense_state = [
        qkv_weight,
        qkv_mean,
        qkv_square,
        out_weight,
        out_mean,
        out_square,
        router_weight.T,
        router_mean.T,
        router_square.T,
        norm_gains.T,
        gains_mean.T,
        gains_square.T,
    ]
    (
        new_qkv,
        new_qkv_mean,
        new_qkv_square,
        new_out,
        new_out_mean,
        new_out_square,
        new_router,
        new_router_mean,
        new_router_square,
        new_gains,
        new_gains_mean,
        new_gains_square,
    ) = whole_call(
        dense_update,
        [shape(item.shape, f32) for item in dense_state],
        [dense_grad] + dense_state,
        flops=20 * local_rows * (qkv_width + width),
    )
    new_router, new_router_mean, new_router_square = (
        item.T for item in (new_router, new_router_mean, new_router_square)
    )
    new_gains, new_gains_mean, new_gains_square = (
        item.T for item in (new_gains, new_gains_mean, new_gains_square)
    )
    new_in, new_in_mean, new_in_square = adamw(in_weight, d_in, in_mean, in_square, 0.1, decay_rate)
    new_down, new_down_mean, new_down_square = adamw(
        down_weight, d_down, down_mean, down_square, 1.0, decay_rate
    )
    return (
        block_out,
        input_grad,
        new_qkv,
        new_qkv_mean,
        new_qkv_square,
        new_out,
        new_out_mean,
        new_out_square,
        new_router,
        new_router_mean,
        new_router_square,
        new_gains,
        new_gains_mean,
        new_gains_square,
        new_in,
        new_in_mean,
        new_in_square,
        new_down,
        new_down_mean,
        new_down_square,
    )


def solution(mesh):
    n_dp, n_exp = mesh.shape["dp"], mesh.shape["exp"]
    n_a = EXPERTS // n_exp // 2
    mesh = Mesh(
        mesh.devices.reshape(n_a, n_dp // (2 * n_a), 2, n_exp), MESH_AXES
    )
    placed = (
        P(("a", "r", "core", "exp"), None),
        P(("a", "r", "core", "exp"), None),
        P(("a", "r", "core", "exp"), None),
        P(("a", "r", "core", "exp"), None),
        P(("a", "r", "core", "exp"), None),
        P(("a", "r", "core", "exp"), None),
        P(("a", "r", "core", "exp"), None),
        P(("a", "r", "core", "exp"), None),
        P(("a", "r", "core", "exp"), None),
        P(("a", "r", "core", "exp"), None),
        P(("a", "r", "core", "exp"), None),
        P(("a", "r", "core", "exp"), None),
        P(("a", "r", "core", "exp"), None),
        P(("a", "r", "core", "exp"), None),
        P(("a", "r", "core", "exp"), None),
        P(("a", "r", "core", "exp"), None),
        P("exp", ("a", "r", "core"), None),
        P("exp", ("a", "r", "core"), None),
        P("exp", ("a", "r", "core"), None),
        P("exp", ("a", "r", "core"), None),
        P("exp", ("a", "r", "core"), None),
        P("exp", ("a", "r", "core"), None),
    )
    return jax.shard_map(
        body,
        mesh=mesh,
        in_specs=placed,
        out_specs=(
            P(("a", "r", "core", "exp"), None),
            P(("a", "r", "core", "exp"), None),
            P(("a", "r", "core", "exp"), None),
            P(("a", "r", "core", "exp"), None),
            P(("a", "r", "core", "exp"), None),
            P(("a", "r", "core", "exp"), None),
            P(("a", "r", "core", "exp"), None),
            P(("a", "r", "core", "exp"), None),
            P(("a", "r", "core", "exp"), None),
            P(("a", "r", "core", "exp"), None),
            P(("a", "r", "core", "exp"), None),
            P(("a", "r", "core", "exp"), None),
            P(("a", "r", "core", "exp"), None),
            P(("a", "r", "core", "exp"), None),
            P("exp", ("a", "r", "core"), None),
            P("exp", ("a", "r", "core"), None),
            P("exp", ("a", "r", "core"), None),
            P("exp", ("a", "r", "core"), None),
            P("exp", ("a", "r", "core"), None),
            P("exp", ("a", "r", "core"), None),
        ),
        check_vma=False,
    )
```

```python
import functools
import math

import jax
import jax.numpy as jnp
import numpy as np
from jax import lax
from jax.experimental import pallas as pl
from jax.experimental.pallas import tpu as pltpu
from jax.sharding import Mesh
from jax.sharding import PartitionSpec as P

QUERY_HEADS = 16
KEY_VALUE_HEADS = 8
HEAD_DIMENSION = 64
FF = 512
STEP = 10
EXPERTS = 16
LANES = 128
MESH_AXES = ("a", "r", "core", "exp")
VMEM_BYTES = 30 * 1024 * 1024


norm_eps = 1e-06
rope_base = 10000.0
mask_fill = -1e30
beta_one = 0.9
beta_two = 0.95
adam_eps = 1e-08
decay_rate = 0.1


def rms_scale(values):
    return lax.rsqrt(jnp.mean(values * values, axis=-1, keepdims=True) + norm_eps)


def doc_layout(doc_lens, sequence_length):
    row_index = jnp.arange(sequence_length, dtype=jnp.int32)
    doc_ends = jnp.cumsum(doc_lens, dtype=jnp.int32)
    passed = (row_index[:, None] >= doc_ends[None, :]).astype(jnp.int32)
    segment = jnp.sum(passed, axis=1, dtype=jnp.int32)
    starts = jnp.sum(passed * doc_lens[None, :], axis=1, dtype=jnp.int32)
    return ((row_index - starts).astype(jnp.float32), segment)


def rope_tables(positions, head_size):
    half_size = head_size // 2
    freq_index = jnp.arange(half_size, dtype=jnp.float32)
    inverse = jnp.exp(freq_index * (-2.0 * math.log(rope_base) / head_size))
    angles = positions[:, None] * inverse[None, :]
    return (jnp.cos(angles), jnp.sin(angles))


def adamw(weight, gradient, mean_old, square_old, step_rate, weight_decay):
    mean_new = beta_one * mean_old + (1.0 - beta_one) * gradient
    square_new = beta_two * square_old + (1.0 - beta_two) * gradient * gradient
    corrected = (
        mean_new
        / (1.0 - beta_one**STEP)
        / (jnp.sqrt(square_new / (1.0 - beta_two**STEP)) + adam_eps)
    )
    return (weight - step_rate * (corrected + weight_decay * weight), mean_new, square_new)

def dot_nn(left, right):
    return jnp.dot(left, right, preferred_element_type=jnp.float32)


def dot_nt(left, right):
    return lax.dot_general(left, right, (((1,), (1,)), ((), ())), preferred_element_type=jnp.float32)


def dot_tn(left, right):
    return lax.dot_general(left, right, (((0,), (0,)), ((), ())), preferred_element_type=jnp.float32)


def lane_iota(rows):
    return lax.broadcasted_iota(jnp.int32, (rows, LANES), 1)


def gain_rows(extra, experts):
    row = lax.broadcasted_iota(jnp.int32, (8, LANES), 0)
    pick = (lane_iota(8) == row + experts).astype(jnp.bfloat16)
    return dot_nt(jnp.where(row < 2, pick, jnp.zeros_like(pick)), extra)


def swap_halves(values):
    half = HEAD_DIMENSION // 2
    lower = lane_iota(values.shape[0]) % HEAD_DIMENSION < half
    return jnp.where(lower, pltpu.roll(values, LANES - half, 1), pltpu.roll(values, half, 1))


def column_sums(values, lane):
    high = values.astype(jnp.bfloat16)
    low = (values - high.astype(jnp.float32)).astype(jnp.bfloat16)
    place = (lane_iota(values.shape[0]) == lane).astype(jnp.bfloat16)
    return dot_tn(high, place) + dot_tn(low, place)


def head_block(index):
    return slice(index * HEAD_DIMENSION, (index + 1) * HEAD_DIMENSION)


def attention_forward(
    experts,
    copies,
    x_ref,
    w_ref,
    cos_ref,
    sin_ref,
    allow_ref,
    used_ref,
    order_ref,
    wide_ref,
    qkv_ref,
    sent_ref,
):
    f32, bf16 = jnp.float32, jnp.bfloat16
    rows, width = x_ref.shape
    query_width = QUERY_HEADS * HEAD_DIMENSION
    key_width = KEY_VALUE_HEADS * HEAD_DIMENSION
    qkv_width = query_width + 2 * key_width
    extra = w_ref[:, qkv_width + width :]
    gains = gain_rows(extra, experts)
    x = x_ref[...].astype(f32)
    normed = (x * rms_scale(x) * gains[0:1]).astype(bf16)
    cosine, sine = cos_ref[...], sin_ref[...]
    for start in range(0, qkv_width, 512):
        part = dot_nn(normed, w_ref[:, start : start + 512])
        for inner in range(0, 512, LANES):
            piece = part[:, inner : inner + LANES]
            if start + inner < query_width + key_width:
                piece = piece * cosine + swap_halves(piece) * sine
            qkv_ref[:, start + inner : start + inner + LANES] = piece.astype(bf16)
    allowed = allow_ref[...] > 0.0
    lane = lane_iota(rows)
    logs = jnp.zeros((rows, LANES), f32)
    fold = QUERY_HEADS // KEY_VALUE_HEADS
    for group in range(KEY_VALUE_HEADS):
        keys = qkv_ref[:, query_width + group * HEAD_DIMENSION : query_width + (group + 1) * HEAD_DIMENSION]
        values = qkv_ref[
            :,
            query_width + key_width + group * HEAD_DIMENSION : query_width
            + key_width
            + (group + 1) * HEAD_DIMENSION,
        ]
        outs = []
        for head in range(group * fold, (group + 1) * fold):
            scores = dot_nt(qkv_ref[:, head_block(head)], keys) * HEAD_DIMENSION ** (-0.5)
            scores = jnp.where(allowed, scores, mask_fill)
            peak = jnp.max(scores, axis=1, keepdims=True)
            log_total = peak + jnp.log(jnp.sum(jnp.exp(scores - peak), axis=1, keepdims=True))
            logs = jnp.where(lane == head, log_total, logs)
            outs.append(dot_nn(jnp.exp(scores - log_total).astype(bf16), values))
        start = qkv_width + group * LANES
        qkv_ref[:, start : start + LANES] = jnp.concatenate(outs, axis=1).astype(bf16)
    wide_ref[:, width : width + LANES] = logs
    hidden = x + dot_nt(qkv_ref[:, qkv_width:], w_ref[:, qkv_width : qkv_width + width])
    wide_ref[:, :width] = hidden
    second = (hidden * rms_scale(hidden) * gains[1:2]).astype(bf16)
    used = used_ref[...] > 0.0
    logits = jnp.where(used, dot_nn(second, extra), mask_fill)
    powers = jnp.where(used, jnp.exp(logits - jnp.max(logits, axis=1, keepdims=True)), 0.0)
    gates = powers / jnp.sum(powers, axis=1, keepdims=True)
    wide_ref[:, width + LANES :] = gates
    high = gates.astype(bf16).astype(f32)
    lanes = (high + pltpu.roll(gates - high, experts, 1)).astype(bf16)
    moved = dot_nn(second, order_ref[...]).astype(bf16)
    for copy in range(copies):
        sent_ref[copy, :, :width] = moved
        sent_ref[copy, :, width:] = lanes


def own_gate(lanes, number, experts):
    lane = lane_iota(lanes.shape[0])
    chosen = (lane == number) | (lane == number + experts)
    return jnp.sum(jnp.where(chosen, lanes.astype(jnp.float32), 0.0), axis=1, keepdims=True)


def experts_forward(
    experts, local_count, place_ref, rows_ref, w_ref, out_ref, inner_ref, sum_ref
):
    f32, bf16 = jnp.float32, jnp.bfloat16
    index, chunk = pl.program_id(0), pl.program_id(1)
    count, width = out_ref.shape
    gate = own_gate(rows_ref[:, width:], index * local_count + place_ref[0], experts)
    inner = dot_nn(rows_ref[:, :width], w_ref[0, :, : 2 * FF])
    inner_ref[0] = inner
    gate_part = inner[:, :FF]
    activation = (gate_part * jax.nn.sigmoid(gate_part) * inner[:, FF:]).astype(bf16)
    result = dot_nt(activation, w_ref[0, :, 2 * FF :]).astype(bf16).astype(f32)
    here = pl.ds(pl.multiple_of(chunk * count, count), count)

    @pl.when(index == 0)
    def _():
        sum_ref[here, :] = gate * result

    @pl.when(index > 0)
    def _():
        sum_ref[here, :] += gate * result

    out_ref[...] = sum_ref[here, :].astype(bf16)


def experts_backward(
    experts,
    local_count,
    place_ref,
    gates_ref,
    cot_ref,
    w_ref,
    inner_ref,
    back_ref,
    inner_grad_ref,
    act_ref,
    sum_ref,
    dots_sum_ref,
):
    f32, bf16 = jnp.float32, jnp.bfloat16
    index, chunk = pl.program_id(0), pl.program_id(1)
    count, width = cot_ref.shape
    number = index * local_count + place_ref[0]
    gate = own_gate(gates_ref[...], number, experts)
    gate_part = inner_ref[0, :, :FF]
    up_part = inner_ref[0, :, FF:]
    gate_sigmoid = jax.nn.sigmoid(gate_part)
    gate_silu = gate_part * gate_sigmoid
    activation = (gate_silu * up_part).astype(bf16).astype(f32)
    act_ref[0] = (gate * activation).astype(bf16)
    act_grad = dot_nn(cot_ref[...], w_ref[0, :, 2 * FF :])
    dots = jnp.sum(activation * act_grad, axis=1, keepdims=True)
    dots_high = dots.astype(bf16).astype(f32)
    lane = lane_iota(count)
    lanes = jnp.where(lane == number, dots_high, 0.0) + jnp.where(
        lane == number + experts, dots - dots_high, 0.0
    )
    act_grad = gate * act_grad
    inner_grad_ref[0, :, :FF] = (
        act_grad * up_part * gate_sigmoid * (1.0 + gate_part * (1.0 - gate_sigmoid))
    ).astype(bf16)
    inner_grad_ref[0, :, FF:] = (act_grad * gate_silu).astype(bf16)
    copy_grad = dot_nt(inner_grad_ref[0], w_ref[0, :, : 2 * FF])
    here = pl.ds(pl.multiple_of(chunk * count, count), count)

    @pl.when(index == 0)
    def _():
        sum_ref[here, :] = copy_grad
        dots_sum_ref[here, :] = lanes

    @pl.when(index > 0)
    def _():
        sum_ref[here, :] += copy_grad
        dots_sum_ref[here, :] += lanes

    back_ref[:, :width] = sum_ref[here, :].astype(bf16)
    back_ref[:, width:] = dots_sum_ref[here, :].astype(bf16)


def experts_weights(where_ref, rows_ref, inner_grad_ref, cot_ref, act_ref, *grad_refs):
    goal = pl.program_id(0)
    inner = dot_tn(rows_ref[...], inner_grad_ref[0]).astype(jnp.bfloat16)
    down = dot_tn(cot_ref[...], act_ref[0]).astype(jnp.bfloat16)
    for index, grad_ref in enumerate(grad_refs):

        @pl.when(goal == index)
        def _(grad_ref=grad_ref):
            grad_ref[:, : 2 * FF] = inner
            grad_ref[:, 2 * FF :] = down


def home_backward(
    experts,
    parts_ref,
    order_ref,
    cot_ref,
    wide_ref,
    w_ref,
    qkv_ref,
    x_ref,
    cos_ref,
    sin_ref,
    allow_ref,
    grad_ref,
    input_grad_ref,
    mid_ref,
    proj_ref,
):
    f32, bf16 = jnp.float32, jnp.bfloat16
    rows, width = x_ref.shape
    sources = parts_ref.shape[0]
    query_width = QUERY_HEADS * HEAD_DIMENSION
    key_width = KEY_VALUE_HEADS * HEAD_DIMENSION
    qkv_width = query_width + 2 * key_width
    fold = QUERY_HEADS // KEY_VALUE_HEADS
    score_scale = HEAD_DIMENSION ** (-0.5)
    extra = w_ref[:, qkv_width + width :]
    gains = gain_rows(extra, experts)
    dots = jnp.zeros((rows, LANES), f32)
    second_grad = jnp.zeros((rows, width), f32)
    for source in range(sources):
        dots = dots + parts_ref[source, :, width:].astype(f32)
        second_grad = second_grad + dot_nn(parts_ref[source, :, :width], order_ref[...])
    dots = dots + pltpu.roll(dots, LANES - experts, 1)
    gates = wide_ref[:, width + LANES :]
    logit_grad = (gates * (dots - jnp.sum(gates * dots, axis=1, keepdims=True))).astype(bf16)
    second_grad = second_grad + dot_nt(logit_grad, extra)
    hidden = wide_ref[:, :width]
    scale = rms_scale(hidden)
    second = (hidden * scale * gains[1:2]).astype(bf16)
    scaled = second_grad * gains[1:2]
    hidden_grad = (
        cot_ref[...].astype(f32)
        + scale * scaled
        - hidden * (scale * scale * scale) * jnp.mean(scaled * hidden, axis=1, keepdims=True)
    )
    branch_grad = hidden_grad.astype(bf16)
    for start in range(0, width, 512):
        grad_ref[:, qkv_width + start : qkv_width + start + 512] = dot_tn(
            branch_grad, qkv_ref[:, qkv_width + start : qkv_width + start + 512]
        ).astype(bf16)
    small_grad = dot_tn(second, logit_grad) + column_sums(
        second_grad * hidden * scale, experts + 1
    )
    mid_ref[...] = dot_nn(branch_grad, w_ref[:, qkv_width : qkv_width + width]).astype(bf16)
    cosine, sine = cos_ref[...], sin_ref[...]
    allowed = allow_ref[...] > 0.0
    lane = lane_iota(rows)
    logs = wide_ref[:, width : width + LANES]

    def turned_back(values):
        return (values * cosine - swap_halves(values) * sine).astype(bf16)

    key_grads, value_grads = [], []
    for group in range(KEY_VALUE_HEADS):
        keys = qkv_ref[:, query_width + group * HEAD_DIMENSION : query_width + (group + 1) * HEAD_DIMENSION]
        values = qkv_ref[
            :,
            query_width + key_width + group * HEAD_DIMENSION : query_width
            + key_width
            + (group + 1) * HEAD_DIMENSION,
        ]
        query_grads = []
        key_grad = jnp.zeros((rows, HEAD_DIMENSION), f32)
        value_grad = jnp.zeros((rows, HEAD_DIMENSION), f32)
        for head in range(group * fold, (group + 1) * fold):
            queries = qkv_ref[:, head_block(head)]
            mid = mid_ref[:, head_block(head)]
            log_total = jnp.sum(jnp.where(lane == head, logs, 0.0), axis=1, keepdims=True)
            scores = jnp.where(allowed, dot_nt(queries, keys) * score_scale, mask_fill)
            weights = jnp.exp(scores - log_total)
            weight_grad = dot_nt(mid, values)
            delta = jnp.sum(weights * weight_grad, axis=1, keepdims=True)
            score_grad = (weights * (weight_grad - delta)).astype(bf16)
            query_grads.append(dot_nn(score_grad, keys) * score_scale)
            key_grad = key_grad + dot_tn(score_grad, queries)
            value_grad = value_grad + dot_tn(weights.astype(bf16), mid)
        proj_ref[:, group * LANES : (group + 1) * LANES] = turned_back(
            jnp.concatenate(query_grads, axis=1)
        )
        key_grads.append(key_grad * score_scale)
        value_grads.append(value_grad)
        if group % 2 == 1:
            start = query_width + (group // 2) * LANES
            proj_ref[:, start : start + LANES] = turned_back(
                jnp.concatenate(key_grads[-2:], axis=1)
            )
            start = start + key_width
            proj_ref[:, start : start + LANES] = jnp.concatenate(value_grads[-2:], axis=1).astype(
                bf16
            )
    x = x_ref[...].astype(f32)
    scale = rms_scale(x)
    normed = (x * scale * gains[0:1]).astype(bf16)
    for start in range(0, qkv_width, 512):
        grad_ref[:, start : start + 512] = dot_tn(normed, proj_ref[:, start : start + 512]).astype(
            bf16
        )
    normed_grad = dot_nt(proj_ref[...], w_ref[:, :qkv_width])
    scaled = normed_grad * gains[0:1]
    small_grad = small_grad + column_sums(normed_grad * x * scale, experts)
    grad_ref[:, qkv_width + width :] = small_grad.astype(bf16)
    input_grad_ref[...] = (
        hidden_grad
        + scale * scaled
        - x * (scale * scale * scale) * jnp.mean(scaled * x, axis=1, keepdims=True)
    ).astype(bf16)


def dense_update(parts_ref, *refs):
    total = parts_ref[0].astype(jnp.float32)
    for source in range(1, parts_ref.shape[0]):
        total = total + parts_ref[source].astype(jnp.float32)
    start = total.shape[1] - LANES
    small = jnp.transpose(total[:, start:])
    experts = refs[6].shape[0]
    qkv_width = refs[0].shape[1]
    grads = (
        total[:, :qkv_width],
        total[:, qkv_width:start],
        small[:experts],
        small[experts : experts + 2],
    )
    rates = ((0.15, decay_rate), (0.3, decay_rate), (0.05, decay_rate), (0.8, 0.0))
    for index, (rate, decay) in enumerate(rates):
        weight_ref, mean_ref, square_ref = refs[3 * index : 3 * index + 3]
        values = adamw(weight_ref[...], grads[index], mean_ref[...], square_ref[...], rate, decay)
        for out_ref, value in zip(refs[3 * index + 12 : 3 * index + 15], values):
            out_ref[...] = value


def whole_call(kernel, outputs, operands, flops, scratch=(), earlier=()):
    operands_read = len(operands)

    def run(*refs):
        kernel(*refs[:operands_read], *refs[operands_read + len(earlier) :])

    moved = sum(math.prod(item.shape) * item.dtype.itemsize for item in list(outputs) + list(operands))
    moved = moved if flops > 1 else 1
    return pl.pallas_call(
        run,
        out_shape=outputs,
        in_specs=[pl.BlockSpec()] * len(operands)
        + [pl.BlockSpec(memory_space=pl.ANY)] * len(earlier),
        out_specs=[pl.BlockSpec()] * len(outputs),
        scratch_shapes=list(scratch),
        compiler_params=pltpu.CompilerParams(vmem_limit_bytes=VMEM_BYTES),
        cost_estimate=pl.CostEstimate(flops=flops, bytes_accessed=moved, transcendentals=0),
    )(*operands, *earlier)


def order_of(kind, sizes):
    axes = {"home": (0, 1, 2, 3, 4), "dense": (2, 1, 3, 0, 4), "expert": (1, 2, 0, 3, 4)}[kind]
    return np.arange(math.prod(sizes), dtype=np.int32).reshape(sizes).transpose(axes).reshape(-1)


def reorder_matrix(before, after):
    return (jnp.asarray(before)[:, None] == jnp.asarray(after)[None, :]).astype(jnp.bfloat16)


def exchange(values, axes):
    return lax.all_to_all(values, axes, split_axis=0, concat_axis=0, tiled=True)


def spread(values, axes):
    count = lax.axis_size(axes)
    copies = exchange(jnp.broadcast_to(values[None], (count,) + values.shape), axes)
    return copies.reshape((count * values.shape[0],) + values.shape[1:])


def collect(values, axes):
    count = lax.axis_size(axes)
    parts = exchange(values.reshape((count, values.shape[0] // count) + values.shape[1:]), axes)
    total = parts[0].astype(jnp.float32)
    for index in range(1, count):
        total = total + parts[index].astype(jnp.float32)
    return total


def partner(values, axes, step):
    names = (axes,) if isinstance(axes, str) else axes
    steps = {}
    for name in reversed(names):
        step, steps[name] = divmod(step, lax.axis_size(name))
    names = tuple(name for name in MESH_AXES if name in names)
    flat = 0
    for name in names:
        flat = flat * lax.axis_size(name) + steps[name]
    pairs = [(index, index ^ flat) for index in range(lax.axis_size(names))]
    return lax.ppermute(values, names, pairs)


def piece_of(values, index):
    return lax.dynamic_index_in_dim(values, index, 0, keepdims=False)


def in_order(own, received, me):
    result = jnp.zeros((len(received) + 1,) + own.shape, own.dtype)
    for step, part in enumerate([own] + received):
        result = lax.dynamic_update_index_in_dim(result, part, me ^ step, 0)
    return result


def spread_aside(values, axes):
    count = lax.axis_size(axes)
    received = [partner(values, axes, step) for step in range(1, count)]
    result = in_order(values, received, lax.axis_index(axes))
    return result.reshape((count * values.shape[0],) + values.shape[1:])


def pieces_for(values, axes):
    me = lax.axis_index(axes)
    return [piece_of(values, me ^ step) for step in range(values.shape[0])]


def exchange_aside(pieces, axes):
    received = [partner(piece, axes, step) for step, piece in enumerate(pieces) if step > 0]
    return in_order(pieces[0], received, lax.axis_index(axes))


def collect_aside(values, axes):
    count = lax.axis_size(axes)
    pieces = pieces_for(values.reshape((count, values.shape[0] // count) + values.shape[1:]), axes)
    total = pieces[0].astype(jnp.float32)
    for step in range(1, count):
        total = total + partner(pieces[step], axes, step).astype(jnp.float32)
    return total


def expert_specs(n_e, group_rows, width):
    count = min(256, group_rows)
    return dict(
        grid=(n_e, group_rows // count),
        scalar=pl.BlockSpec(memory_space=pltpu.SMEM),
        wide=pl.BlockSpec((count, width), lambda k, i: (i, 0)),
        wider=pl.BlockSpec((count, width + LANES), lambda k, i: (i, 0)),
        lanes=pl.BlockSpec((count, LANES), lambda k, i: (i, width // LANES)),
        weight=pl.BlockSpec((1, width, 3 * FF), lambda k, i: (k, 0, 0)),
        inner=pl.BlockSpec((1, count, 2 * FF), lambda k, i: (k, i, 0)),
        act=pl.BlockSpec((1, count, FF), lambda k, i: (k, i, 0)),
    )


def run_forward(place, arrived, expert_full, experts, local_count):
    n_e, width, _ = expert_full.shape
    group_rows = arrived.shape[0]
    specs = expert_specs(n_e, group_rows, width)
    return pl.pallas_call(
        functools.partial(experts_forward, experts, local_count),
        grid=specs["grid"],
        out_shape=[
            jax.ShapeDtypeStruct((group_rows, width), jnp.bfloat16),
            jax.ShapeDtypeStruct((n_e, group_rows, 2 * FF), jnp.float32),
        ],
        in_specs=[specs["scalar"], specs["wider"], specs["weight"]],
        out_specs=[specs["wide"], specs["inner"]],
        scratch_shapes=[pltpu.VMEM((group_rows, width), jnp.float32)],
        compiler_params=pltpu.CompilerParams(vmem_limit_bytes=VMEM_BYTES),
        cost_estimate=pl.CostEstimate(
            flops=2 * n_e * group_rows * width * 3 * FF,
            bytes_accessed=n_e * width * (3 * FF * 2 + group_rows * 8),
            transcendentals=n_e * group_rows * FF,
        ),
    )(place, arrived, expert_full)


def run_backward(place, arrived, cot_group, expert_full, inner, experts, local_count):
    bf16 = jnp.bfloat16
    n_e, width, _ = expert_full.shape
    group_rows = arrived.shape[0]
    specs = expert_specs(n_e, group_rows, width)
    return pl.pallas_call(
        functools.partial(experts_backward, experts, local_count),
        grid=specs["grid"],
        out_shape=[
            jax.ShapeDtypeStruct((group_rows, width + LANES), bf16),
            jax.ShapeDtypeStruct((n_e, group_rows, 2 * FF), bf16),
            jax.ShapeDtypeStruct((n_e, group_rows, FF), bf16),
        ],
        in_specs=[
            specs["scalar"],
            specs["lanes"],
            specs["wide"],
            specs["weight"],
            specs["inner"],
        ],
        out_specs=[specs["wider"], specs["inner"], specs["act"]],
        scratch_shapes=[
            pltpu.VMEM((group_rows, width), jnp.float32),
            pltpu.VMEM((group_rows, LANES), jnp.float32),
        ],
        compiler_params=pltpu.CompilerParams(vmem_limit_bytes=VMEM_BYTES),
        cost_estimate=pl.CostEstimate(
            flops=2 * n_e * group_rows * width * 3 * FF,
            bytes_accessed=n_e * width * (3 * FF * 2 + group_rows * 10),
            transcendentals=n_e * group_rows * FF,
        ),
    )(place, arrived, cot_group, expert_full, inner)


def run_weights(arrived, inner_grad, cot_group, act, slots, firsts, blocks, part):
    group_rows = arrived.shape[0]
    goals = len(slots) // blocks
    where = jnp.stack(slots + firsts).astype(jnp.int32)

    def block_of(index):
        return lambda g, j, at: (jnp.where(g == index, j, jnp.where(g < index, 0, blocks - 1)), 0)

    return pl.pallas_call(
        experts_weights,
        grid_spec=pltpu.PrefetchScalarGridSpec(
            num_scalar_prefetch=1,
            grid=(goals, blocks),
            in_specs=[
                pl.BlockSpec((group_rows, part), lambda g, j, at: (0, at[(goals + g) * blocks + j])),
                pl.BlockSpec((1, group_rows, 2 * FF), lambda g, j, at: (at[g * blocks + j], 0, 0)),
                pl.BlockSpec((group_rows, part), lambda g, j, at: (0, at[(goals + g) * blocks + j])),
                pl.BlockSpec((1, group_rows, FF), lambda g, j, at: (at[g * blocks + j], 0, 0)),
            ],
            out_specs=[pl.BlockSpec((part, 3 * FF), block_of(index)) for index in range(goals)],
        ),
        out_shape=[jax.ShapeDtypeStruct((blocks * part, 3 * FF), jnp.bfloat16)] * goals,
        compiler_params=pltpu.CompilerParams(vmem_limit_bytes=VMEM_BYTES),
        cost_estimate=pl.CostEstimate(
            flops=2 * goals * blocks * part * group_rows * 3 * FF,
            bytes_accessed=goals * (group_rows * 6 * FF + blocks * part * (group_rows * 4 + 6 * FF)),
            transcendentals=0,
        ),
    )(where, arrived, inner_grad, cot_group, act)


def in_pieces(n_e, n_r, width):
    return n_e == 2 and n_r == 2 and width // n_r == 2 * min(256, width)


def weight_grads(factors, n_e, n_r):
    width = factors[2].shape[1]
    part = min(256, width)
    if in_pieces(n_e, n_r, width):
        me = lax.axis_index(("exp", "r"))
        own, beside, across, both = (me ^ step for step in range(4))
        goals = [both, across, both, beside, beside, own, across, own]
        later = [0, 0, 1, 1, 0, 0, 1, 1]
        slots = [goal // n_r for goal in goals]
        firsts = [goal % n_r * 2 + half for goal, half in zip(goals, later)]
        return run_weights(*factors, slots, firsts, 2, part)
    grads = []
    blocks = width // part
    for slot in range(n_e):
        firsts = [jnp.int32(first) for first in range(blocks)]
        grads += run_weights(*factors, [jnp.int32(slot)] * blocks, firsts, blocks, part)
    return grads


def send_grads(grads, n_e, n_r, width):
    if not in_pieces(n_e, n_r, width):
        grads = jnp.concatenate(grads, axis=0)
        return [list(exchange(grads.reshape((n_e * n_r, -1) + grads.shape[1:]), ("exp", "r")))]
    return [[grads[2], partner(grads[0], "exp", 1)], [grads[3], partner(grads[1], "r", 1)]]


def send_onward(parts, ways):
    if len(parts) != 2:
        return parts
    count = parts[0].shape[0] // 2
    onward = parts[0][:count].astype(jnp.float32) + parts[1][:count].astype(jnp.float32)
    return parts + [partner(onward.astype(jnp.bfloat16), ways, 1)]


def add_parts(parts):
    count = parts[-1].shape[0]
    total = parts[-1].astype(jnp.float32)
    for part in parts[:-1]:
        total = total + part[part.shape[0] - count :].astype(jnp.float32)
    return total.astype(jnp.bfloat16)


def body(
    tokens,
    cotangent,
    doc_lengths,
    routes,
    qkv_weight,
    qkv_mean,
    qkv_square,
    out_weight,
    out_mean,
    out_square,
    router_weight,
    router_mean,
    router_square,
    norm_gains,
    gains_mean,
    gains_square,
    in_weight,
    in_mean,
    in_square,
    down_weight,
    down_mean,
    down_square,
):
    f32, bf16 = jnp.float32, jnp.bfloat16
    shape = jax.ShapeDtypeStruct
    n_a, n_r, n_c, n_e = (lax.axis_size(name) for name in ("a", "r", "core", "exp"))
    rows, width = tokens.shape
    experts = router_weight.shape[1]
    local_count = in_weight.shape[0]
    sizes = (n_a, n_r, n_c, n_e, width // (n_a * n_r * n_c * n_e))
    home, dense, expert = (order_of(kind, sizes) for kind in ("home", "dense", "expert"))
    query_width = QUERY_HEADS * HEAD_DIMENSION
    qkv_width = query_width + 2 * KEY_VALUE_HEADS * HEAD_DIMENSION

    local_rows = qkv_weight.shape[0]
    extra = jnp.zeros((local_rows, LANES - experts - 2), bf16)
    pack = jnp.concatenate(
        [
            qkv_weight.astype(bf16),
            out_weight.astype(bf16),
            router_weight.astype(bf16),
            norm_gains.astype(bf16),
            extra,
        ],
        axis=1,
    )
    pack = spread(pack, "a")

    to_dense = reorder_matrix(home, dense)
    x_dense = dot_nn(tokens, to_dense).astype(bf16)
    cot_dense = dot_nn(cotangent, to_dense).astype(bf16)
    positions, segment = doc_layout(doc_lengths.reshape(-1), rows)
    cosine, sine = rope_tables(positions, HEAD_DIMENSION)
    repeat = LANES // HEAD_DIMENSION
    cosine = jnp.concatenate([cosine, cosine] * repeat, axis=1)
    sine = jnp.concatenate([-sine, sine] * repeat, axis=1)
    row_index = jnp.arange(rows, dtype=jnp.int32)
    allowed = (segment[:, None] == segment[None, :]) & (row_index[None, :] <= row_index[:, None])
    allowed = allowed.astype(f32)
    used = jnp.any(
        routes[:, :, None] == jnp.arange(LANES, dtype=jnp.int32)[None, None, :], axis=1
    ).astype(f32)

    cot_expert = dot_nn(cotangent, reorder_matrix(home, expert)).astype(bf16)
    expert_pack = jnp.concatenate([in_weight.astype(bf16), down_weight.astype(bf16)], axis=2)
    to_expert = reorder_matrix(dense, expert)
    pieces = pieces_for(expert_pack, ("core", "a"))
    pack, x_dense, cot_dense, cosine, sine, allowed, used, to_expert, *pieces = (
        lax.optimization_barrier(
            (pack, x_dense, cot_dense, cosine, sine, allowed, used, to_expert, *pieces)
        )
    )
    pack = spread(pack, ("r", "exp"))
    expert_pack = exchange_aside(pieces, ("core", "a"))
    pack, expert_pack = lax.optimization_barrier((pack, expert_pack))
    cot_expert, expert_pack = lax.optimization_barrier((cot_expert, expert_pack))
    cot_group = spread_aside(spread_aside(cot_expert, "a"), "core")
    expert_full = lax.all_gather(expert_pack, ("exp", "r"), axis=0, tiled=True).reshape(
        n_e, width, 3 * FF
    )
    dense_full = spread(pack, "core")

    wide, qkv, sent = whole_call(
        functools.partial(attention_forward, experts, n_a),
        [
            shape((rows, width + 2 * LANES), f32),
            shape((rows, qkv_width + query_width), bf16),
            shape((n_a, rows, width + LANES), bf16),
        ],
        [x_dense, dense_full, cosine, sine, allowed, used, to_expert],
        flops=2 * rows * width * (qkv_width + 2 * width + 2 * rows),
    )

    arrived = exchange(sent, "a").reshape(n_a * rows, width + LANES)
    arrived = spread(arrived, "core")
    place = (lax.axis_index("core") * n_a + lax.axis_index("a")).astype(jnp.int32).reshape(1)
    out, inner = run_forward(place, arrived, expert_full, experts, local_count)
    back, inner_grad, activation = run_backward(
        place, arrived, cot_group, expert_full, inner, experts, local_count
    )
    out = collect_aside(out, "core").astype(bf16).reshape(n_a, rows, width)
    back = collect(back, "core").astype(bf16)

    factors = (arrived, inner_grad, cot_group, activation)
    expert_grads = list(weight_grads(factors, n_e, n_r))
    back = exchange(back.reshape(n_a, rows, width + LANES), "a")
    received = send_grads(expert_grads, n_e, n_r, width)
    back, out, expert_grads[-1] = lax.optimization_barrier((back, out, expert_grads[-1]))
    out = exchange(out, "a")

    from_expert = reorder_matrix(expert, dense)
    dense_grad, input_grad = whole_call(
        functools.partial(home_backward, experts),
        [shape((width, qkv_width + width + LANES), bf16), shape((rows, width), bf16)],
        [
            back,
            from_expert,
            cot_dense,
            wide,
            dense_full,
            qkv,
            x_dense,
            cosine,
            sine,
            allowed,
        ],
        earlier=expert_grads[-1:],
        flops=1,
        scratch=[pltpu.VMEM((rows, query_width), bf16), pltpu.VMEM((rows, qkv_width), bf16)],
    )
    dense_grad, out, received = lax.optimization_barrier((dense_grad, out, received))
    received = [send_onward(parts, way) for parts, way in zip(received, ("r", "exp"))]
    dense_grad = collect(dense_grad, "core").astype(bf16)
    dense_grad, received = lax.optimization_barrier((dense_grad, received))
    expert_grad = jnp.concatenate([add_parts(parts) for parts in received], axis=0)
    expert_grad = expert_grad.reshape(
        n_c * n_a, width // (n_r * n_c * n_a), 3 * FF
    )
    expert_grad = exchange_aside(
        pieces_for(expert_grad, ("core", "a")), ("core", "a")
    ).astype(f32)
    d_in = expert_grad[:, :, : 2 * FF]
    d_down = expert_grad[:, :, 2 * FF :]
    dense_grad = collect(dense_grad, ("r", "exp")).astype(bf16)
    dense_grad, out, input_grad = lax.optimization_barrier((dense_grad, out, input_grad))
    dense_grad = exchange(dense_grad.reshape((n_a, local_rows) + dense_grad.shape[1:]), "a")

    from_dense = reorder_matrix(dense, home)
    mixed = dot_nn(out[0], from_expert)
    for index in range(1, n_a):
        mixed = mixed + dot_nn(out[index], from_expert)
    block_out = dot_nn((wide[:, :width] + mixed).astype(bf16), from_dense).astype(bf16)
    input_grad = dot_nn(input_grad, from_dense).astype(bf16)
    dense_state = [
        qkv_weight,
        qkv_mean,
        qkv_square,
        out_weight,
        out_mean,
        out_square,
        router_weight.T,
        router_mean.T,
        router_square.T,
        norm_gains.T,
        gains_mean.T,
        gains_square.T,
    ]
    (
        new_qkv,
        new_qkv_mean,
        new_qkv_square,
        new_out,
        new_out_mean,
        new_out_square,
        new_router,
        new_router_mean,
        new_router_square,
        new_gains,
        new_gains_mean,
        new_gains_square,
    ) = whole_call(
        dense_update,
        [shape(item.shape, f32) for item in dense_state],
        [dense_grad] + dense_state,
        flops=20 * local_rows * (qkv_width + width),
    )
    new_router, new_router_mean, new_router_square = (
        item.T for item in (new_router, new_router_mean, new_router_square)
    )
    new_gains, new_gains_mean, new_gains_square = (
        item.T for item in (new_gains, new_gains_mean, new_gains_square)
    )
    new_in, new_in_mean, new_in_square = adamw(in_weight, d_in, in_mean, in_square, 0.1, decay_rate)
    new_down, new_down_mean, new_down_square = adamw(
        down_weight, d_down, down_mean, down_square, 1.0, decay_rate
    )
    return (
        block_out,
        input_grad,
        new_qkv,
        new_qkv_mean,
        new_qkv_square,
        new_out,
        new_out_mean,
        new_out_square,
        new_router,
        new_router_mean,
        new_router_square,
        new_gains,
        new_gains_mean,
        new_gains_square,
        new_in,
        new_in_mean,
        new_in_square,
        new_down,
        new_down_mean,
        new_down_square,
    )


def solution(mesh):
    n_dp, n_exp = mesh.shape["dp"], mesh.shape["exp"]
    n_a = EXPERTS // n_exp // 2
    mesh = Mesh(
        mesh.devices.reshape(n_a, n_dp // (2 * n_a), 2, n_exp), MESH_AXES
    )
    placed = (
        P(("a", "r", "core", "exp"), None),
        P(("a", "r", "core", "exp"), None),
        P(("a", "r", "core", "exp"), None),
        P(("a", "r", "core", "exp"), None),
        P(("a", "r", "core", "exp"), None),
        P(("a", "r", "core", "exp"), None),
        P(("a", "r", "core", "exp"), None),
        P(("a", "r", "core", "exp"), None),
        P(("a", "r", "core", "exp"), None),
        P(("a", "r", "core", "exp"), None),
        P(("a", "r", "core", "exp"), None),
        P(("a", "r", "core", "exp"), None),
        P(("a", "r", "core", "exp"), None),
        P(("a", "r", "core", "exp"), None),
        P(("a", "r", "core", "exp"), None),
        P(("a", "r", "core", "exp"), None),
        P("exp", ("a", "r", "core"), None),
        P("exp", ("a", "r", "core"), None),
        P("exp", ("a", "r", "core"), None),
        P("exp", ("a", "r", "core"), None),
        P("exp", ("a", "r", "core"), None),
        P("exp", ("a", "r", "core"), None),
    )
    return jax.shard_map(
        body,
        mesh=mesh,
        in_specs=placed,
        out_specs=(
            P(("a", "r", "core", "exp"), None),
            P(("a", "r", "core", "exp"), None),
            P(("a", "r", "core", "exp"), None),
            P(("a", "r", "core", "exp"), None),
            P(("a", "r", "core", "exp"), None),
            P(("a", "r", "core", "exp"), None),
            P(("a", "r", "core", "exp"), None),
            P(("a", "r", "core", "exp"), None),
            P(("a", "r", "core", "exp"), None),
            P(("a", "r", "core", "exp"), None),
            P(("a", "r", "core", "exp"), None),
            P(("a", "r", "core", "exp"), None),
            P(("a", "r", "core", "exp"), None),
            P(("a", "r", "core", "exp"), None),
            P("exp", ("a", "r", "core"), None),
            P("exp", ("a", "r", "core"), None),
            P("exp", ("a", "r", "core"), None),
            P("exp", ("a", "r", "core"), None),
            P("exp", ("a", "r", "core"), None),
            P("exp", ("a", "r", "core"), None),
        ),
        check_vma=False,
    )
```
